32 devices in a mesh: grp: 2 (over y), lon: 4 (over z), lat: 2 (over x), ta: 2 (over core).
Axes of the slice: x: 2, y: 2, z: 4, core: 2. Of those that a mesh axis runs over, the one named last changes fastest.
Arguments:
- swath: bfloat16 [1024, 128, 128], P(('grp', 'lon', 'lat'), 'ta'), parts along dimension 0, may hold values from -6 to 6
- obs_mask: int32 [1024, 128], P(('grp', 'lon', 'lat'), 'ta'), parts along dimension 0, may hold values 0 or 1
- target: int32 [1024], P(('grp', 'lon', 'lat')), parts along dimension 0, may hold values from 0 to 15
- send_list: int32 [16, 4, 32], P(('grp', 'lon', 'lat')), parts along dimension 0, may hold values from 0 to 63, as said below
- send_count: int32 [16, 4], P(('grp', 'lon', 'lat')), parts along dimension 0, may hold values from 0 to 32, as said below
- factor_space: float32 [96, 64, 512], P(None, ('grp', 'lat'), 'lon'), parts along dimension 1, may hold values from -0.6 to 0.6
- factor_time: float32 [256, 96], P(('grp', 'ta')), parts along dimension 0, may hold values from -0.625 to 0.625
Outputs:
- space_out: float32 [96, 64, 512], P(None, ('grp', 'lat'), 'lon'), parts along dimension 1
- time_out: float32 [256, 96], P(('grp', 'ta')), parts along dimension 0
The draws below stay inside these ranges and needn't reach their ends.
There are 2 independent parts, one for each index of `grp`. The reference program is written for one: setup_inputs(seed, part) draws one part's arguments, and reference() takes and returns one part's arrays. A program takes and returns all parts, laid end to end along the dimension named above; each array names one. Nothing has to cross between parts.
Inputs may be any that keep to these rules, and one draw needn't show every extreme that they name: Entries k < send_count[g, d] of send_list[g, d] name slots of shard g; over all d every slot of the shard is named exactly once; other entries are 0. `send_count`: counts of one shard sum to 64; in each latitude band one owner receives 32 blocks from every shard of the band.
All inputs are finite; a program needn't handle non-finite values. No bound on the sum of `obs_mask` on one device may be relied on, other than what follows from the above.
Results may differ from the reference program's by a relative error of at most 0.007.
The reference program's roundings to bfloat16 on the way count: a program that leaves them out, or rounds other values in their place, can miss the bound.
Values may be sent and summed in bfloat16 or wider, within the bound.
No kernel may reach another device: no remote copies, remote signals or barrier semaphores. Data moves between devices by JAX's collectives and lax.ppermute only.
A program may use at most 64 MiB of HBM per device.

```python
import jax
import jax.numpy as jnp
from jax import lax

RANK = 96
CLON = 128
CLAT = 16
SLOTS = 64
STEPS = 2
CAP = 32
SHARDS = 8
ALLSLOTS = 512
DAYS = 128
NLAT = 32
NLON = 512
N_LON = 4
N_LAT = 2


def route_tables(key):
    key_owner, key_heavy, key_shards = jax.random.split(key, 3)
    favoured = jax.random.randint(key_owner, (N_LAT,), 0, N_LON)
    heavy = jax.random.randint(key_heavy, (N_LAT, N_LON), 0, 4)
    shard_keys = jax.random.split(key_shards, SHARDS)
    token_ids = jnp.arange(N_LON * CAP, dtype=jnp.int32)
    owner_of = token_ids // CAP

    def one_shard(shard_key, shard):
        lat_band = shard % N_LAT
        noise_key, slot_key = jax.random.split(shard_key)
        noise = jax.random.randint(noise_key, (N_LON * CAP,), 0, 65536)
        score = noise + heavy[lat_band][owner_of] * 65536 + jnp.where(owner_of == favoured[lat_band], 4 * 65536, 0)
        ranked = jnp.argsort(-(score * (N_LON * CAP) + token_ids))
        chosen = ranked[:SLOTS]
        placed = jax.random.permutation(slot_key, SLOTS).astype(jnp.int32)
        slot_of = jnp.zeros((N_LON * CAP,), jnp.int32).at[chosen].set(placed)
        taken = jnp.zeros((N_LON * CAP,), jnp.int32).at[chosen].set(1)
        slot_grid = slot_of.reshape(N_LON, CAP)
        taken_grid = taken.reshape(N_LON, CAP)
        order = jnp.argsort((1 - taken_grid) * CAP + jnp.arange(CAP, dtype=jnp.int32)[None, :], axis=1)
        roster = jnp.take_along_axis(slot_grid, order, axis=1) * jnp.take_along_axis(taken_grid, order, axis=1)
        return (roster, jnp.sum(taken_grid, axis=1))
    return jax.vmap(one_shard)(shard_keys, jnp.arange(SHARDS, dtype=jnp.int32))


def draw_send_list(key, part):
    tables = route_tables(key)
    return tables[0].astype(jnp.int32)


def draw_send_count(key, part):
    tables = route_tables(key)
    return tables[1].astype(jnp.int32)


def with_ends(array, rng, least, top_value):
    index_at = [jax.random.randint(jax.random.fold_in(rng, axis), (), 0, length) for axis, length in enumerate(array.shape)]
    widest = array.shape.index(max(array.shape))
    next_to = index_at[:widest] + [(index_at[widest] + 1) % array.shape[widest]] + index_at[widest + 1:]
    return array.at[tuple(index_at)].set(least).at[tuple(next_to)].set(top_value)


def level_of(key, extent, shards, smallest, high):
    loudness, own = 1.0, jax.random.fold_in(key, 6)
    for dim, shards_of in shards:
        steps = jnp.exp(jax.random.uniform(jax.random.fold_in(own, dim), (shards_of,), jnp.float32, smallest / len(shards), high / len(shards)))
        loudness = loudness * jnp.repeat(steps, extent[dim] // shards_of).reshape([-1 if axis == dim else 1 for axis in range(len(extent))])
    return loudness


def normal_values(stream_key, shape, width, bound, pieces=(), held_as=jnp.bfloat16):
    level = level_of(stream_key, shape, pieces, -0.22, 0.18) if pieces else 1.0
    entries = jax.random.normal(stream_key, shape, jnp.float32) * width * level
    return jnp.minimum(jnp.maximum(entries, -bound), bound).astype(held_as)


def setup_inputs(seed: int = 0, part: int = 0) -> dict:
    seeds = jax.random.split(jax.random.key(seed), 8)
    part_splits = jax.random.split(jax.random.fold_in(seeds[7], part), 8)
    swath = normal_values(part_splits[0], (ALLSLOTS, DAYS, CLON), 1.0, 6.0, ((0, 8), (1, 2)))
    obs_mask = with_ends((jax.random.randint(part_splits[1], (ALLSLOTS, DAYS), 0, 3) < 2).astype(jnp.int32), jax.random.fold_in(part_splits[1], 1), 0, 1)
    target = with_ends(jax.random.randint(part_splits[2], (ALLSLOTS,), 0, CLAT), jax.random.fold_in(part_splits[2], 1), 0, CLAT - 1).astype(jnp.int32)
    send_list = draw_send_list(jax.random.fold_in(jax.random.fold_in(seeds[7], part), 71), part)
    send_count = draw_send_count(jax.random.fold_in(jax.random.fold_in(seeds[7], part), 71), part)
    factor_space = normal_values(part_splits[5], (RANK, NLAT, NLON), 0.1, 0.6, ((1, 2), (2, 4)), jnp.float32)
    factor_time = normal_values(part_splits[6], (DAYS, RANK), RANK ** -0.5, 0.625, ((0, 2),), jnp.float32)
    return dict(swath=swath, obs_mask=obs_mask, target=target, send_list=send_list, send_count=send_count, factor_space=factor_space, factor_time=factor_time)


SMOOTH = 2.0
ETA_SPACE = 0.08
RIDGE = 1.0
EPSILON = 1e-6


def laplace(surface):
    padded = jnp.pad(surface, ((0, 0), (1, 1), (0, 0)))
    beside_all = padded[:, 2:, :] + padded[:, :-2, :]
    beside_all = beside_all + jnp.roll(surface, 1, axis=2) + jnp.roll(surface, -1, axis=2)
    return 4.0 * surface - beside_all


def reference(swath, obs_mask, target, send_list, send_count, factor_space, factor_time):
    spatial = factor_space
    temporal = factor_time
    owners = jnp.repeat(jnp.arange(N_LON, dtype=jnp.int32), CAP)
    lane_ids = jnp.arange(CAP, dtype=jnp.int32)
    for sweep in range(STEPS):
        packed = spatial.astype(jnp.bfloat16).reshape(RANK, NLAT, N_LON, CLON)
        time_bf = temporal.astype(jnp.bfloat16).astype(jnp.float32)

        def visit(totals, shard):
            grad_space, grad_time, grad_diag = totals
            lat_band = shard % N_LAT
            filled = (lane_ids[None, :] < send_count[shard][:, None]).reshape(-1)
            slot_ids = (shard * SLOTS + send_list[shard]).reshape(-1).astype(jnp.int32)
            observed = swath[slot_ids].astype(jnp.float32)
            weights = (obs_mask[slot_ids] * filled[:, None].astype(jnp.int32)).astype(jnp.float32)
            tile_rows = (lat_band * CLAT + target[slot_ids]).astype(jnp.int32)
            blocks = packed[:, tile_rows, owners, :].astype(jnp.float32)
            predicted = jnp.einsum('dr,rbc->bdc', time_bf, blocks)
            residual = (weights[:, :, None] * (predicted - observed)).astype(jnp.bfloat16)
            residual = lax.optimization_barrier(residual).astype(jnp.float32)
            block_grad = jnp.einsum('dr,bdc->rbc', time_bf, residual)
            grad_space = grad_space.at[:, tile_rows, owners, :].add(block_grad)
            grad_time = grad_time + jnp.einsum('bdc,rbc->dr', residual, blocks)
            block_sq = jnp.sum(blocks * blocks, axis=2)
            grad_diag = grad_diag + jnp.einsum('bd,rb->dr', weights, block_sq, precision=lax.Precision.HIGHEST)
            return (grad_space, grad_time, grad_diag), None

        start = (jnp.zeros((RANK, NLAT, N_LON, CLON), jnp.float32), jnp.zeros((DAYS, RANK), jnp.float32), jnp.zeros((DAYS, RANK), jnp.float32))
        (grad_space, grad_time, grad_diag), _ = lax.scan(visit, start, jnp.arange(SHARDS, dtype=jnp.int32))
        grad_space = grad_space.reshape(RANK, NLAT, NLON)
        space_new = spatial - ETA_SPACE * (grad_space + SMOOTH * laplace(spatial))
        time_new = temporal - grad_time / (grad_diag + RIDGE)
        space_sq = jnp.sum(space_new * space_new, axis=(1, 2)) / (NLAT * NLON)
        time_sq = jnp.sum(time_new * time_new, axis=0) / DAYS
        rescale = ((time_sq + EPSILON) / (space_sq + EPSILON)) ** 0.25
        spatial = space_new * rescale[:, None, None]
        temporal = time_new / rescale[None, :]
    return spatial, temporal
```

```python
import functools

import jax
import jax.numpy as jnp
from jax import lax
from jax.experimental import pallas as pl
from jax.experimental.pallas import tpu as pltpu
from jax.sharding import PartitionSpec as P

SMOOTH = 2.0
ETA_SPACE = 0.08
RIDGE = 1.0
EPSILON = 1e-06

F32 = jnp.float32
BF16 = jnp.bfloat16
LANES = 128
TAIL = 16
COLS = 16
NORM = 8
VMEM_LIMIT = 56 * 1024 * 1024


def dot(a, b, contract):
    return lax.dot_general(a, b, ((contract[:1], contract[1:]), ((), ())), preferred_element_type=F32)


def route_kernel(n_lon, half, list_ref, count_ref, target_ref, swath_ref, mask_ref, *rest):
    outs, (place, total, seen) = rest[: 2 * n_lon], rest[2 * n_lon:]
    me, core = lax.axis_index("lon"), lax.axis_index("ta")
    slots, days, cells = swath_ref.shape

    def owner(d, carry):
        step = jnp.bitwise_xor(d, me)

        def entry(k, carry):
            slot = list_ref[0, d, k]
            row = target_ref[slot]
            far = jnp.bitwise_xor(lax.div(row, half), core)
            place[slot] = (far * n_lon + step) * half + lax.rem(row, half)
            return carry

        return lax.fori_loop(0, count_ref[0, d], entry, carry)

    lax.fori_loop(0, n_lon, owner, 0)
    total[...] = jnp.zeros(total.shape, F32)
    seen[...] = jnp.zeros(seen.shape, F32)
    mask = mask_ref[...].astype(F32)
    by_day = mask.T
    for slot in range(slots):
        at = place[slot]
        total[at] += swath_ref[slot].astype(F32) * by_day[:, slot:slot + 1]
        seen[pl.ds(at, 1), :days] += mask[slot:slot + 1, :]
    for piece, out in enumerate(outs):
        out[: half * days, :] = total[piece * half:(piece + 1) * half].reshape(half * days, cells).astype(BF16)
        out[half * days:, :] = seen[piece * half:piece * half + TAIL, :].astype(BF16)


def row_of(surface, row):
    return surface[:, row * LANES:(row + 1) * LANES]


def columns_as_rows(surface, half, flip, extra):
    rank = surface.shape[0]
    lane = lax.broadcasted_iota(jnp.int32, (rank, LANES), 1)
    block = jnp.zeros((rank, LANES), F32)
    for row in range(half):
        strip = row_of(surface, row)
        block = jnp.where(lane == row, strip[:, :1], block)
        block = jnp.where(lane == half + row, strip[:, LANES - 1:], block)
    if extra is not None:
        block = jnp.where(lane == COLS, extra, block)
    flip[...] = jnp.zeros(flip.shape, F32)
    flip[:rank, :] = block
    return flip[...].T[: COLS + NORM, :]


def rows_as_columns(rows, rank, flip):
    flip[...] = jnp.zeros(flip.shape, F32)
    flip[: rows.shape[0], :] = rows
    return flip[...].T[:rank, :]


def smoothed(surface, half, above, below, left_cols, right_cols):
    lane = lax.broadcasted_iota(jnp.int32, above.shape, 1)
    strips = []
    for row in range(half):
        here = row_of(surface, row)
        up = above if row == 0 else row_of(surface, row - 1)
        down = below if row == half - 1 else row_of(surface, row + 1)
        left = jnp.where(lane == 0, left_cols[:, half + row:half + row + 1], pltpu.roll(here, 1, 1))
        right = jnp.where(lane == LANES - 1, right_cols[:, row:row + 1], pltpu.roll(here, LANES - 1, 1))
        lap = 4.0 * here - (up + down + left + right)
        strips.append(here - (ETA_SPACE * SMOOTH) * lap)
    return strips


def prepare_kernel(half, space_ref, surface, edge_near, edge_far, cols, flip):
    core = lax.axis_index("ta")
    rank = surface.shape[0]
    height = space_ref.shape[0] // rank
    for row in range(half):
        surface[:, row * LANES:(row + 1) * LANES] = space_ref[pl.ds(core * half + row, rank, stride=height), :]
    edge_near[...] = space_ref[pl.ds(half - core, rank, stride=height), :]
    edge_far[...] = space_ref[pl.ds(core * (height - 1), rank, stride=height), :]
    cols[...] = columns_as_rows(surface[...], half, flip, None)


def pick(flag, a, b):
    return jnp.where(flag, a, b)


def model_kernel(half, surface, edge_near, edge_far, cols_a, cols_b, swap, time_own, time_other, base, predicted, packed, time_t, flip, days_all):
    core = lax.axis_index("ta")
    rank = surface.shape[0]
    days = time_own.shape[0]
    days_all[...] = jnp.zeros(days_all.shape, F32)
    days_all[:days, :rank] = time_own[...]
    days_all[days:, :rank] = time_other[...]
    time_full = days_all[...]
    time_t[...] = time_full.T[:rank, :]
    packed[...] = surface[...].astype(BF16)
    time_bf = time_full[:, :rank].astype(BF16)
    for at in range(0, half * LANES, 2 * LANES):
        predicted[:, at:at + 2 * LANES] = dot(time_bf, packed[:, at:at + 2 * LANES], (1, 0))
    above = pick(core == 0, edge_far[...], edge_near[...])
    below = pick(core == 0, edge_near[...], edge_far[...])
    odd = swap()
    left = rows_as_columns(pick(odd, cols_a[...], cols_b[...]), rank, flip)
    right = rows_as_columns(pick(odd, cols_b[...], cols_a[...]), rank, flip)
    for row, strip in enumerate(smoothed(surface[...], half, above, below, left, right)):
        base[:, row * LANES:(row + 1) * LANES] = strip


def gradients(half, base, predicted, packed, time_t, seen, summed, fresh, message, outgoing, edge_far, flip):
    core = lax.axis_index("ta")
    rank = time_t.shape[0]
    time_bf = time_t.astype(BF16)
    time_twice = jnp.concatenate([time_bf, time_bf], axis=1)
    seen_bf = seen.astype(BF16)
    width = 2 * LANES
    owner = lax.broadcasted_iota(jnp.int32, (TAIL, width), 0)
    lane = lax.broadcasted_iota(jnp.int32, (TAIL, width), 1)
    grad_time = jnp.zeros((rank, width), F32)
    grad_diag = jnp.zeros((rank, LANES), F32)
    norm = jnp.zeros((rank, 1), F32)
    for at in range(0, half * LANES, width):
        spread = (owner * LANES <= lane + at) & (lane + at < (owner + 1) * LANES)
        weight = dot(seen_bf, spread.astype(BF16), (0, 0))
        part = packed[:, at:at + width]
        residual = weight * predicted[:, at:at + width] - summed[:, at:at + width]
        high = residual.astype(BF16)
        low = (residual - high.astype(F32)).astype(BF16)
        both = jnp.concatenate([high, low], axis=0)
        grad_space = dot(time_twice, both, (1, 0))
        grad_time = grad_time + dot(part, both, (1, 1))
        new = base[:, at:at + width] - ETA_SPACE * grad_space
        fresh[:, at:at + width] = new
        norm = norm + jnp.sum(new * new, axis=1, keepdims=True)
        wide = part.astype(F32)
        for row in range(width // LANES):
            strip = row_of(wide, row)
            square = jnp.sum(strip * strip, axis=1, keepdims=True)
            grad_diag = grad_diag + square * seen[at // LANES + row:at // LANES + row + 1, :]
    grad_time = grad_time[:, :LANES] + grad_time[:, LANES:]
    message[:rank, :] = grad_time
    message[rank:2 * rank, :] = grad_diag
    last = columns_as_rows(fresh[...], half, flip, norm)
    message[2 * rank:, :] = last
    outgoing[:rank, :] = pltpu.roll(grad_time, LANES // 2, 1)
    outgoing[rank:2 * rank, :] = pltpu.roll(grad_diag, LANES // 2, 1)
    outgoing[2 * rank:2 * rank + COLS + NORM, :] = last
    first_row, last_row = fresh[:, :LANES], fresh[:, (half - 1) * LANES:]
    outgoing[2 * rank + COLS + NORM:, :] = pick(core == 0, last_row, first_row)
    edge_far[...] = pick(core == 0, first_row, last_row)


def first_kernel(half, n_lon, base, predicted, packed, time_t, *rest):
    near, far = rest[:n_lon], rest[n_lon:2 * n_lon]
    fresh, message, outgoing, edge_far, summed, seen, flip = rest[2 * n_lon:]
    days = (near[0].shape[0] - TAIL) // half
    for row in range(half):
        for first, parts in ((0, near), (days, far)):
            value = parts[0][row * days:(row + 1) * days, :].astype(F32)
            for piece in parts[1:]:
                value = value + piece[row * days:(row + 1) * days, :].astype(F32)
            summed[first:first + days, row * LANES:(row + 1) * LANES] = value

    def counts(parts):
        value = parts[0][half * days:, :].astype(F32)
        for piece in parts[1:]:
            value = value + piece[half * days:, :].astype(F32)
        return value

    seen[...] = counts(near) + pltpu.roll(counts(far), days, 1)
    gradients(half, base, predicted, packed, time_t[...], seen[...], summed, fresh, message, outgoing, edge_far, flip)


def settle(rank, day_count, cell_count, total, time_t):
    time_new = time_t - total[:rank, :] / (total[rank:2 * rank, :] + RIDGE)
    return time_new


def scaling(rank, day_count, cell_count, total, time_new, flip):
    space_sq = rows_as_columns(total[2 * rank + COLS:, :], rank, flip)[:, :1]
    square = time_new * time_new
    time_sq = 0.5 * jnp.sum(square + pltpu.roll(square, LANES // 2, 1), axis=1, keepdims=True)
    ratio = (time_sq / day_count + EPSILON) / (space_sq / cell_count + EPSILON)
    return jnp.sqrt(jnp.sqrt(ratio))


def total_of(parts):
    if len(parts) == 1:
        return parts[0][...]
    return (parts[0][...] + parts[1][...]) + (parts[2][...] + parts[3][...])


def second_kernel(half, counts, n_parts, swap, surface, time_t, summed, seen, edge_near, edge_far, *rest):
    parts, (cols_a, cols_b) = rest[:n_parts], rest[n_parts:n_parts + 2]
    fresh, time_out, message, outgoing, edge_out, flip, scaled, base, predicted, packed = rest[n_parts + 2:]
    core = lax.axis_index("ta")
    rank = surface.shape[0]
    total = total_of(parts)
    time_new = settle(rank, *counts, total, time_t[...])
    scale = scaling(rank, *counts, total, time_new, flip)
    time_now = time_new / scale
    time_out[...] = time_now
    scaled[...] = surface[...] * scale
    packed[...] = scaled[...].astype(BF16)
    time_bf = time_now.T.astype(BF16)
    for at in range(0, half * LANES, 2 * LANES):
        predicted[:, at:at + 2 * LANES] = dot(time_bf, packed[:, at:at + 2 * LANES], (1, 0))
    near, far = edge_near[...], edge_far[...]
    above = pick(core == 0, far, near) * scale
    below = pick(core == 0, near, far) * scale
    odd = swap()
    from_a, from_b = cols_a[2 * rank:2 * rank + COLS, :], cols_b[2 * rank:2 * rank + COLS, :]
    left = rows_as_columns(pick(odd, from_a, from_b), rank, flip) * scale
    right = rows_as_columns(pick(odd, from_b, from_a), rank, flip) * scale
    for row, strip in enumerate(smoothed(scaled[...], half, above, below, left, right)):
        base[:, row * LANES:(row + 1) * LANES] = strip
    gradients(half, base, predicted, packed, time_now, seen[...], summed, fresh, message, outgoing, edge_out, flip)


def last_kernel(half, counts, n_parts, surface, other, time_t, *rest):
    parts = rest[:n_parts]
    space_out, time_out, flip = rest[n_parts:]
    core = lax.axis_index("ta")
    rank = surface.shape[0]
    height = space_out.shape[0] // rank
    total = total_of(parts)
    time_new = settle(rank, *counts, total, time_t[...])
    scale = scaling(rank, *counts, total, time_new, flip)
    flip[...] = jnp.zeros(flip.shape, F32)
    flip[:rank, :] = time_new / scale
    time_out[...] = flip[...].T[: time_out.shape[0], :rank]
    for row in range(half):
        at = row * LANES
        space_out[pl.ds(core * half + row, rank, stride=height), :] = surface[:, at:at + LANES] * scale
        space_out[pl.ds((1 - core) * half + row, rank, stride=height), :] = other[:, at:at + LANES] * scale


def add_kernel(rank, mine, theirs, out):
    cols = slice(2 * rank, 2 * rank + COLS)
    out[: 2 * rank, :] = mine[: 2 * rank, :] + theirs[: 2 * rank, :]
    out[cols, :] = mine[cols, :]
    ends = slice(2 * rank + COLS, 2 * rank + COLS + NORM)
    out[ends, :] = mine[ends, :] + theirs[ends, :]


def shape(dims, dtype=F32):
    return jax.ShapeDtypeStruct(tuple(dims), dtype)


def call(kernel, out_shape, scratch=(), smem=0, flops=1_000_000):
    def run(*operands):
        return pl.pallas_call(
            kernel,
            out_shape=out_shape,
            in_specs=[pl.BlockSpec(memory_space=pltpu.SMEM)] * smem + [pl.BlockSpec(memory_space=pltpu.VMEM)] * (len(operands) - smem),
            out_specs=jax.tree.map(lambda _: pl.BlockSpec(memory_space=pltpu.VMEM), out_shape),
            scratch_shapes=list(scratch),
            compiler_params=pltpu.CompilerParams(vmem_limit_bytes=VMEM_LIMIT),
            cost_estimate=pl.CostEstimate(flops=flops, bytes_accessed=1_000_000, transcendentals=0),
        )(*operands)

    return run


def across(value, axis, step):
    peers = lax.axis_size(axis)
    return lax.ppermute(value, axis, [(i, i ^ step) for i in range(peers)])


def shards(swath, obs_mask, target, send_list, send_count, factor_space, factor_time):
    n_lon, n_lat, n_ta = (lax.axis_size(axis) for axis in ("lon", "lat", "ta"))
    slots, days, cells = swath.shape
    rank, height, _ = factor_space.shape
    half = height // n_ta
    wide = half * LANES
    counts = (float(days * n_ta), float(height * cells * n_lon * n_lat))
    message_rows = 2 * rank + COLS + NORM
    flip = pltpu.VMEM((LANES, LANES), F32)

    pieces = call(
        functools.partial(route_kernel, n_lon, half),
        [shape((half * days + TAIL, cells), BF16)] * (2 * n_lon),
        [pltpu.SMEM((slots,), jnp.int32), pltpu.VMEM((2 * n_lon * half, days, cells), F32), pltpu.VMEM((2 * n_lon * half + TAIL, LANES), F32)],
        smem=3,
    )(send_list, send_count, target, swath, obs_mask)
    near, far = pieces[:n_lon], pieces[n_lon:]
    order = sorted(range(1, n_lon), key=lambda step: (-((step + 1) // 2), step))
    near_in = {0: near[0]}
    for step in order:
        near_in[step] = across(near[step], "lon", step)
    far = [across(piece, "ta", 1) for piece in far]
    far_in = {0: far[0]}
    for step in order:
        far_in[step] = across(far[step], "lon", step)

    def bands(edge):
        there = [(2 * band + 1, 2 * band + 2) for band in range(n_lat - 1)]
        return lax.ppermute(edge, ("lat", "ta"), there + [(b, a) for a, b in there])

    paired = n_lon == 4

    def swap():
        return lax.rem(lax.axis_index("lon"), 2) == 1 if paired else jnp.bool_(True)

    def columns(value):
        if paired:
            return across(value, "lon", 1), across(value, "lon", 3)
        ring = [(i, (i + 1) % n_lon) for i in range(n_lon)]
        return lax.ppermute(value, "lon", ring), lax.ppermute(value, "lon", [(b, a) for a, b in ring])

    surface, edge_near, edge_far, cols = call(
        functools.partial(prepare_kernel, half),
        [shape((rank, wide)), shape((rank, LANES)), shape((rank, LANES)), shape((COLS + NORM, LANES))],
        [flip],
    )(factor_space.reshape(rank * height, cells))
    cols_a, cols_b = columns(cols)

    def model(*refs):
        model_kernel(half, *refs[:5], swap, *refs[5:])

    base, predicted, packed, time_t = call(
        model,
        [shape((rank, wide)), shape((2 * days, wide)), shape((rank, wide), BF16), shape((rank, LANES))],
        [flip, flip],
    )(surface, edge_near, bands(edge_far), cols_a, cols_b, factor_time, across(factor_time, "ta", 1))

    step_out = [shape((rank, wide)), shape((message_rows, LANES)), shape((message_rows + rank, LANES)), shape((rank, LANES))]
    surface, message, outgoing, edge_far, summed, seen = call(
        functools.partial(first_kernel, half, n_lon),
        step_out + [shape((2 * days, wide)), shape((TAIL, LANES))],
        [flip],
    )(base, predicted, packed, time_t, *[near_in[s] for s in range(n_lon)], *[far_in[s] for s in range(n_lon)])

    add = call(functools.partial(add_kernel, rank), shape((message_rows, LANES)))

    def gather(message, outgoing):
        incoming = across(outgoing, "ta", 1)
        total = add(message, incoming)
        step = 1
        while step < n_lat:
            total = add(total, across(total, "lat", step))
            step *= 2
        if paired:
            return incoming, [total] + [across(total, "lon", step) for step in (1, 2, 3)]
        step = 1
        own = total
        while step < n_lon:
            total = add(total, across(total, "lon", step))
            step *= 2
        return incoming, [total], own

    beside, *rest = gather(message, outgoing)
    parts = rest[0]
    if paired:
        cols_a, cols_b = parts[1], parts[3]
    else:
        cols_a, cols_b = columns(message)

    def second(*refs):
        second_kernel(half, counts, len(parts), swap, *refs)

    surface, time_t, message, outgoing, edge_far = call(
        second,
        [step_out[0], shape((rank, LANES))] + step_out[1:],
        [flip, pltpu.VMEM((rank, wide), F32), pltpu.VMEM((rank, wide), F32), pltpu.VMEM((2 * days, wide), F32), pltpu.VMEM((rank, wide), BF16)],
    )(surface, time_t, summed, seen, beside[message_rows:], bands(edge_far), *parts, cols_a, cols_b)

    other = across(surface, "ta", 1)
    parts = gather(message, outgoing)[1]
    space, time = call(
        functools.partial(last_kernel, half, counts, len(parts)),
        [shape((rank * height, cells)), shape(factor_time.shape)],
        [flip],
    )(surface, other, time_t, *parts)
    return space.reshape(rank, height, cells), time


def solution(mesh):
    in_specs = (
        P(("grp", "lon", "lat"), "ta", None),
        P(("grp", "lon", "lat"), "ta"),
        P(("grp", "lon", "lat")),
        P(("grp", "lon", "lat"), None, None),
        P(("grp", "lon", "lat"), None),
        P(None, ("grp", "lat"), "lon"),
        P(("grp", "ta"), None),
    )
    out_specs = (P(None, ("grp", "lat"), "lon"), P(("grp", "ta"), None))
    return jax.shard_map(shards, mesh=mesh, in_specs=in_specs, out_specs=out_specs, check_vma=False)
```

```python
import functools
import math

import jax
import jax.numpy as jnp
from jax import lax
from jax.experimental import pallas as pl
from jax.experimental.pallas import tpu as pltpu
from jax.sharding import PartitionSpec as P

SMOOTH = 2.0
ETA_SPACE = 0.08
RIDGE = 1.0
EPSILON = 1e-06

F32 = jnp.float32
BF16 = jnp.bfloat16
LANES = 128
TAIL = 16
COLS = 16
NORM = 8
SPARE = 2 * 1024 * 1024


def dot(a, b, contract):
    return lax.dot_general(a, b, ((contract[:1], contract[1:]), ((), ())), preferred_element_type=F32)


def route_kernel(n_lon, half, list_ref, count_ref, target_ref, swath_ref, mask_ref, *rest):
    outs, (place, total, seen) = rest[: 2 * n_lon], rest[2 * n_lon:]
    me, core = lax.axis_index("lon"), lax.axis_index("ta")
    slots, days, cells = swath_ref.shape

    def owner(d, carry):
        step = jnp.bitwise_xor(d, me)

        def entry(k, carry):
            slot = list_ref[0, d, k]
            row = target_ref[slot]
            far = jnp.bitwise_xor(lax.div(row, half), core)
            place[slot] = (far * n_lon + step) * half + lax.rem(row, half)
            return carry

        return lax.fori_loop(0, count_ref[0, d], entry, carry)

    lax.fori_loop(0, n_lon, owner, 0)
    total[...] = jnp.zeros(total.shape, F32)
    seen[...] = jnp.zeros(seen.shape, F32)
    mask = mask_ref[...].astype(F32)
    by_day = mask.T
    for slot in range(slots):
        at = place[slot]
        total[at] += swath_ref[slot].astype(F32) * by_day[:, slot:slot + 1]
        seen[pl.ds(at, 1), :days] += mask[slot:slot + 1, :]
    for piece, out in enumerate(outs):
        out[: half * days, :] = total[piece * half:(piece + 1) * half].reshape(half * days, cells).astype(BF16)
        out[half * days:, :] = seen[piece * half:piece * half + TAIL, :].astype(BF16)


def row_of(surface, row):
    return surface[:, row * LANES:(row + 1) * LANES]


def columns_as_rows(surface, half, flip, extra):
    rank = surface.shape[0]
    lane = lax.broadcasted_iota(jnp.int32, (rank, LANES), 1)
    block = jnp.zeros((rank, LANES), F32)
    for row in range(half):
        strip = row_of(surface, row)
        block = jnp.where(lane == row, strip[:, :1], block)
        block = jnp.where(lane == half + row, strip[:, LANES - 1:], block)
    if extra is not None:
        block = jnp.where(lane == COLS, extra, block)
    flip[...] = jnp.zeros(flip.shape, F32)
    flip[:rank, :] = block
    return flip[...].T[: COLS + NORM, :]


def rows_as_columns(rows, rank, flip):
    flip[...] = jnp.zeros(flip.shape, F32)
    flip[: rows.shape[0], :] = rows
    return flip[...].T[:rank, :]


def smoothed(surface, half, above, below, left_cols, right_cols):
    lane = lax.broadcasted_iota(jnp.int32, above.shape, 1)
    strips = []
    for row in range(half):
        here = row_of(surface, row)
        up = above if row == 0 else row_of(surface, row - 1)
        down = below if row == half - 1 else row_of(surface, row + 1)
        left = jnp.where(lane == 0, left_cols[:, half + row:half + row + 1], pltpu.roll(here, 1, 1))
        right = jnp.where(lane == LANES - 1, right_cols[:, row:row + 1], pltpu.roll(here, LANES - 1, 1))
        lap = 4.0 * here - (up + down + left + right)
        strips.append(here - (ETA_SPACE * SMOOTH) * lap)
    return strips


def prepare_kernel(half, space_ref, time_ref, after, surface, edge_near, edge_far, cols, time_own, flip):
    core = lax.axis_index("ta")
    rank = surface.shape[0]
    height = space_ref.shape[0] // rank
    for row in range(half):
        surface[:, row * LANES:(row + 1) * LANES] = space_ref[pl.ds(core * half + row, rank, stride=height), :]
    edge_near[...] = space_ref[pl.ds(half - core, rank, stride=height), :]
    edge_far[...] = space_ref[pl.ds(core * (height - 1), rank, stride=height), :]
    cols[...] = columns_as_rows(surface[...], half, flip, None)
    time_own[...] = time_ref[...]


def pick(flag, a, b):
    return jnp.where(flag, a, b)


def model_kernel(half, surface, edge_near, edge_far, cols_a, cols_b, swap, time_own, time_other, base, predicted, packed, time_t, flip, days_all):
    core = lax.axis_index("ta")
    rank = surface.shape[0]
    days = time_own.shape[0]
    days_all[...] = jnp.zeros(days_all.shape, F32)
    days_all[:days, :rank] = time_own[...]
    days_all[days:, :rank] = time_other[...]
    time_full = days_all[...]
    time_t[...] = time_full.T[:rank, :]
    packed[...] = surface[...].astype(BF16)
    time_bf = time_full[:, :rank].astype(BF16)
    for at in range(0, half * LANES, 2 * LANES):
        predicted[:, at:at + 2 * LANES] = dot(time_bf, packed[:, at:at + 2 * LANES], (1, 0))
    above = pick(core == 0, edge_far[...], edge_near[...])
    below = pick(core == 0, edge_near[...], edge_far[...])
    odd = swap()
    left = rows_as_columns(pick(odd, cols_a[...], cols_b[...]), rank, flip)
    right = rows_as_columns(pick(odd, cols_b[...], cols_a[...]), rank, flip)
    for row, strip in enumerate(smoothed(surface[...], half, above, below, left, right)):
        base[:, row * LANES:(row + 1) * LANES] = strip


def gradients(half, base, predicted, packed, time_t, seen, summed, fresh, message, outgoing, edge_far, flip):
    core = lax.axis_index("ta")
    rank = time_t.shape[0]
    time_bf = time_t.astype(BF16)
    time_twice = jnp.concatenate([time_bf, time_bf], axis=1)
    seen_bf = seen.astype(BF16)
    width = 2 * LANES
    owner = lax.broadcasted_iota(jnp.int32, (TAIL, width), 0)
    lane = lax.broadcasted_iota(jnp.int32, (TAIL, width), 1)
    grad_time = jnp.zeros((rank, width), F32)
    grad_diag = jnp.zeros((rank, LANES), F32)
    norm = jnp.zeros((rank, 1), F32)
    for at in range(0, half * LANES, width):
        spread = (owner * LANES <= lane + at) & (lane + at < (owner + 1) * LANES)
        weight = dot(seen_bf, spread.astype(BF16), (0, 0))
        part = packed[:, at:at + width]
        residual = weight * predicted[:, at:at + width] - summed[:, at:at + width]
        high = residual.astype(BF16)
        low = (residual - high.astype(F32)).astype(BF16)
        both = jnp.concatenate([high, low], axis=0)
        grad_space = dot(time_twice, both, (1, 0))
        grad_time = grad_time + dot(part, both, (1, 1))
        new = base[:, at:at + width] - ETA_SPACE * grad_space
        fresh[:, at:at + width] = new
        norm = norm + jnp.sum(new * new, axis=1, keepdims=True)
        wide = part.astype(F32)
        for row in range(width // LANES):
            strip = row_of(wide, row)
            square = jnp.sum(strip * strip, axis=1, keepdims=True)
            grad_diag = grad_diag + square * seen[at // LANES + row:at // LANES + row + 1, :]
    grad_time = grad_time[:, :LANES] + grad_time[:, LANES:]
    message[:rank, :] = grad_time
    message[rank:2 * rank, :] = grad_diag
    last = columns_as_rows(fresh[...], half, flip, norm)
    message[2 * rank:, :] = last
    outgoing[:rank, :] = pltpu.roll(grad_time, LANES // 2, 1)
    outgoing[rank:2 * rank, :] = pltpu.roll(grad_diag, LANES // 2, 1)
    outgoing[2 * rank:2 * rank + COLS + NORM, :] = last
    first_row, last_row = fresh[:, :LANES], fresh[:, (half - 1) * LANES:]
    outgoing[2 * rank + COLS + NORM:, :] = pick(core == 0, last_row, first_row)
    edge_far[...] = pick(core == 0, first_row, last_row)


def first_kernel(half, n_lon, base, predicted, packed, time_t, *rest):
    near, far = rest[:n_lon], rest[n_lon:2 * n_lon]
    fresh, message, outgoing, edge_far, summed, seen, flip = rest[2 * n_lon:]
    days = (near[0].shape[0] - TAIL) // half
    for row in range(half):
        for first, parts in ((0, near), (days, far)):
            value = parts[0][row * days:(row + 1) * days, :].astype(F32)
            for piece in parts[1:]:
                value = value + piece[row * days:(row + 1) * days, :].astype(F32)
            summed[first:first + days, row * LANES:(row + 1) * LANES] = value

    def counts(parts):
        value = parts[0][half * days:, :].astype(F32)
        for piece in parts[1:]:
            value = value + piece[half * days:, :].astype(F32)
        return value

    seen[...] = counts(near) + pltpu.roll(counts(far), days, 1)
    gradients(half, base, predicted, packed, time_t[...], seen[...], summed, fresh, message, outgoing, edge_far, flip)


def settle(rank, day_count, cell_count, total, time_t):
    time_new = time_t - total[:rank, :] / (total[rank:2 * rank, :] + RIDGE)
    return time_new


def scaling(rank, day_count, cell_count, total, time_new, flip):
    space_sq = rows_as_columns(total[2 * rank + COLS:, :], rank, flip)[:, :1]
    square = time_new * time_new
    time_sq = 0.5 * jnp.sum(square + pltpu.roll(square, LANES // 2, 1), axis=1, keepdims=True)
    ratio = (time_sq / day_count + EPSILON) / (space_sq / cell_count + EPSILON)
    return jnp.sqrt(jnp.sqrt(ratio))


def total_of(parts):
    if len(parts) == 1:
        return parts[0][...]
    return (parts[0][...] + parts[1][...]) + (parts[2][...] + parts[3][...])


def second_kernel(half, counts, n_parts, swap, surface, time_t, summed, seen, edge_near, edge_far, *rest):
    parts, (cols_a, cols_b) = rest[:n_parts], rest[n_parts:n_parts + 2]
    fresh, time_out, message, outgoing, edge_out, flip, scaled, base, predicted, packed = rest[n_parts + 2:]
    core = lax.axis_index("ta")
    rank = surface.shape[0]
    total = total_of(parts)
    time_new = settle(rank, *counts, total, time_t[...])
    scale = scaling(rank, *counts, total, time_new, flip)
    time_now = time_new / scale
    time_out[...] = time_now
    scaled[...] = surface[...] * scale
    packed[...] = scaled[...].astype(BF16)
    time_bf = time_now.T.astype(BF16)
    for at in range(0, half * LANES, 2 * LANES):
        predicted[:, at:at + 2 * LANES] = dot(time_bf, packed[:, at:at + 2 * LANES], (1, 0))
    near, far = edge_near[...], edge_far[...]
    above = pick(core == 0, far, near) * scale
    below = pick(core == 0, near, far) * scale
    odd = swap()
    from_a, from_b = cols_a[2 * rank:2 * rank + COLS, :], cols_b[2 * rank:2 * rank + COLS, :]
    left = rows_as_columns(pick(odd, from_a, from_b), rank, flip) * scale
    right = rows_as_columns(pick(odd, from_b, from_a), rank, flip) * scale
    for row, strip in enumerate(smoothed(scaled[...], half, above, below, left, right)):
        base[:, row * LANES:(row + 1) * LANES] = strip
    gradients(half, base, predicted, packed, time_now, seen[...], summed, fresh, message, outgoing, edge_out, flip)


def last_kernel(half, counts, n_parts, surface, other, time_t, *rest):
    parts = rest[:n_parts]
    space_out, time_out, flip = rest[n_parts:]
    core = lax.axis_index("ta")
    rank = surface.shape[0]
    height = space_out.shape[0] // rank
    total = total_of(parts)
    time_new = settle(rank, *counts, total, time_t[...])
    scale = scaling(rank, *counts, total, time_new, flip)
    flip[...] = jnp.zeros(flip.shape, F32)
    flip[:rank, :] = time_new / scale
    time_out[...] = flip[...].T[: time_out.shape[0], :rank]
    for row in range(half):
        at = row * LANES
        space_out[pl.ds(core * half + row, rank, stride=height), :] = surface[:, at:at + LANES] * scale
        space_out[pl.ds((1 - core) * half + row, rank, stride=height), :] = other[:, at:at + LANES] * scale


def add_kernel(rank, mine, theirs, out):
    cols = slice(2 * rank, 2 * rank + COLS)
    out[: 2 * rank, :] = mine[: 2 * rank, :] + theirs[: 2 * rank, :]
    out[cols, :] = mine[cols, :]
    ends = slice(2 * rank + COLS, 2 * rank + COLS + NORM)
    out[ends, :] = mine[ends, :] + theirs[ends, :]


def shape(dims, dtype=F32):
    return jax.ShapeDtypeStruct(tuple(dims), dtype)


def padded(ref):
    *outer, rows, lanes = (1, *ref.shape)
    return math.prod(outer) * -(-rows // 16) * 16 * -(-lanes // LANES) * LANES * jnp.dtype(ref.dtype).itemsize


def call(kernel, out_shape, scratch=(), smem=0, after=0, flops=1_000_000):
    def run(*operands):
        vmem = [*operands[smem:len(operands) - after], *jax.tree.leaves(out_shape), *scratch]
        specs = [pltpu.SMEM] * smem + [pltpu.VMEM] * (len(operands) - smem - after) + [pl.ANY] * after
        return pl.pallas_call(
            kernel,
            out_shape=out_shape,
            in_specs=[pl.BlockSpec(memory_space=space) for space in specs],
            out_specs=jax.tree.map(lambda _: pl.BlockSpec(memory_space=pltpu.VMEM), out_shape),
            scratch_shapes=list(scratch),
            compiler_params=pltpu.CompilerParams(vmem_limit_bytes=SPARE + sum(padded(ref) for ref in vmem if len(ref.shape) > 1)),
            cost_estimate=pl.CostEstimate(flops=flops, bytes_accessed=1_000_000, transcendentals=0),
        )(*operands)

    return run


def across(value, axis, step):
    return lax.ppermute(value, axis, [(i, i ^ step) for i in range(lax.axis_size(axis))])


def shards(swath, obs_mask, target, send_list, send_count, factor_space, factor_time):
    n_lon, n_lat, n_ta = (lax.axis_size(axis) for axis in ("lon", "lat", "ta"))
    slots, days, cells = swath.shape
    rank, height, _ = factor_space.shape
    half = height // n_ta
    wide = half * LANES
    counts = (float(days * n_ta), float(height * cells * n_lon * n_lat))
    message_rows = 2 * rank + COLS + NORM
    flip = pltpu.VMEM((LANES, LANES), F32)

    pieces = call(
        functools.partial(route_kernel, n_lon, half),
        [shape((half * days + TAIL, cells), BF16)] * (2 * n_lon),
        [pltpu.SMEM((slots,), jnp.int32), pltpu.VMEM((2 * n_lon * half, days, cells), F32), pltpu.VMEM((2 * n_lon * half + TAIL, LANES), F32)],
        smem=3,
    )(send_list, send_count, target, swath, obs_mask)
    near, far = pieces[:n_lon], pieces[n_lon:]
    near_in, far_in = {0: near[0]}, {}
    for step in (*range(n_lon // 2, n_lon), *range(n_lon // 2)):
        if step:
            near_in[step] = across(near[step], "lon", step)
        far_in[step] = across(far[step], ("lon", "ta"), 2 * step + 1)

    def bands(edge):
        there = [(2 * band + 1, 2 * band + 2) for band in range(n_lat - 1)]
        return lax.ppermute(edge, ("lat", "ta"), there + [(b, a) for a, b in there])

    paired = n_lon == 4

    def swap():
        return lax.rem(lax.axis_index("lon"), 2) == 1 if paired else jnp.bool_(True)

    def columns(value):
        if paired:
            return across(value, "lon", 1), across(value, "lon", 3)
        ring = [(i, (i + 1) % n_lon) for i in range(n_lon)]
        return lax.ppermute(value, "lon", ring), lax.ppermute(value, "lon", [(b, a) for a, b in ring])

    surface, edge_near, edge_far, cols, time_own = call(
        functools.partial(prepare_kernel, half),
        [shape((rank, wide)), shape((rank, LANES)), shape((rank, LANES)), shape((COLS + NORM, LANES)), shape(factor_time.shape)],
        [flip],
        after=1,
    )(factor_space.reshape(rank * height, cells), factor_time, near[0])
    cols_a, cols_b = columns(cols)

    def model(*refs):
        model_kernel(half, *refs[:5], swap, *refs[5:])

    base, predicted, packed, time_t = call(
        model,
        [shape((rank, wide)), shape((2 * days, wide)), shape((rank, wide), BF16), shape((rank, LANES))],
        [flip, flip],
    )(surface, edge_near, bands(edge_far), cols_a, cols_b, time_own, across(time_own, "ta", 1))

    step_out = [shape((rank, wide)), shape((message_rows, LANES)), shape((message_rows + rank, LANES)), shape((rank, LANES))]
    surface, message, outgoing, edge_far, summed, seen = call(
        functools.partial(first_kernel, half, n_lon),
        step_out + [shape((2 * days, wide)), shape((TAIL, LANES))],
        [flip],
    )(base, predicted, packed, time_t, *[near_in[s] for s in range(n_lon)], *[far_in[s] for s in range(n_lon)])

    add = call(functools.partial(add_kernel, rank), shape((message_rows, LANES)))

    def gather(message, outgoing):
        incoming = across(outgoing, "ta", 1)
        total = add(message, incoming)
        step = 1
        while step < n_lat:
            total = add(total, across(total, "lat", step))
            step *= 2
        if paired:
            return incoming, [total] + [across(total, "lon", step) for step in (1, 2, 3)]
        step = 1
        own = total
        while step < n_lon:
            total = add(total, across(total, "lon", step))
            step *= 2
        return incoming, [total], own

    beside, *rest = gather(message, outgoing)
    parts = rest[0]
    if paired:
        cols_a, cols_b = parts[1], parts[3]
    else:
        cols_a, cols_b = columns(message)

    def second(*refs):
        second_kernel(half, counts, len(parts), swap, *refs)

    surface, time_t, message, outgoing, edge_far = call(
        second,
        [step_out[0], shape((rank, LANES))] + step_out[1:],
        [flip, pltpu.VMEM((rank, wide), F32), pltpu.VMEM((rank, wide), F32), pltpu.VMEM((2 * days, wide), F32), pltpu.VMEM((rank, wide), BF16)],
    )(surface, time_t, summed, seen, beside[message_rows:], bands(edge_far), *parts, cols_a, cols_b)

    other = across(surface, "ta", 1)
    parts = gather(message, outgoing)[1]
    space, time = call(
        functools.partial(last_kernel, half, counts, len(parts)),
        [shape((rank * height, cells)), shape(factor_time.shape)],
        [flip],
    )(surface, other, time_t, *parts)
    return space.reshape(rank, height, cells), time


def solution(mesh):
    in_specs = (
        P(("grp", "lon", "lat"), "ta", None),
        P(("grp", "lon", "lat"), "ta"),
        P(("grp", "lon", "lat")),
        P(("grp", "lon", "lat"), None, None),
        P(("grp", "lon", "lat"), None),
        P(None, ("grp", "lat"), "lon"),
        P(("grp", "ta"), None),
    )
    out_specs = (P(None, ("grp", "lat"), "lon"), P(("grp", "ta"), None))
    return jax.shard_map(shards, mesh=mesh, in_specs=in_specs, out_specs=out_specs, check_vma=False)
```

```python
import functools
import math

import jax
import jax.numpy as jnp
from jax import lax
from jax.experimental import pallas as pl
from jax.experimental.pallas import tpu as pltpu
from jax.sharding import PartitionSpec as P

SMOOTH = 2.0
ETA_SPACE = 0.08
RIDGE = 1.0
EPSILON = 1e-06

F32 = jnp.float32
BF16 = jnp.bfloat16
LANES = 128
TAIL = 16
COLS = 16
NORM = 8
SPARE = 2 * 1024 * 1024
SWATH_COPIES = 4


def dot(a, b, contract):
    return lax.dot_general(a, b, ((contract[:1], contract[1:]), ((), ())), preferred_element_type=F32)


def route_kernel(half, sends, list_hbm, count_hbm, target_hbm, swath_hbm, mask_hbm, *rest):
    outs, rest = rest[: len(sends)], rest[len(sends):]
    list_ref, count_ref, target_ref, swath_ref, mask_ref, place, total, seen, arrived = rest
    me, core = lax.axis_index("lon"), lax.axis_index("ta")
    n_lon = list_ref.shape[1]
    slots, days, cells = swath_ref.shape
    chunk = slots // SWATH_COPIES
    small = [(list_hbm, list_ref), (count_hbm, count_ref), (target_hbm, target_ref), (mask_hbm, mask_ref)]
    large = [(swath_hbm.at[pl.ds(at, chunk)], swath_ref.at[pl.ds(at, chunk)]) for at in range(0, slots, chunk)]
    copies = [pltpu.make_async_copy(src, dst, arrived.at[i]) for i, (src, dst) in enumerate(small + large)]
    for copy in copies:
        copy.start()
    total[...] = jnp.zeros(total.shape, F32)
    seen[...] = jnp.zeros(seen.shape, F32)
    for copy in copies[: len(small)]:
        copy.wait()

    def owner(d, carry):
        step = jnp.bitwise_xor(d, me)

        def entry(k, carry):
            slot = list_ref[0, d, k]
            row = target_ref[slot]
            far = jnp.bitwise_xor(lax.div(row, half), core)
            place[slot] = (far * n_lon + step) * half + lax.rem(row, half)
            return carry

        return lax.fori_loop(0, count_ref[0, d], entry, carry)

    lax.fori_loop(0, n_lon, owner, 0)
    mask = mask_ref[...].astype(F32)
    by_day = mask.T
    for slot in range(slots):
        if slot % chunk == 0:
            copies[len(small) + slot // chunk].wait()
        at = place[slot]
        total[at] += swath_ref[slot].astype(F32) * by_day[:, slot:slot + 1]
        seen[pl.ds(at, 1), :days] += mask[slot:slot + 1, :]
    for (side, step), out in zip(sends, outs):
        at = (side * n_lon + step) * half
        out[: half * days, :] = total[at:at + half].reshape(half * days, cells).astype(BF16)
        out[half * days:, :] = seen[at:at + TAIL, :].astype(BF16)


def row_of(surface, row):
    return surface[:, row * LANES:(row + 1) * LANES]


def columns_as_rows(columns, flip):
    rank = columns[0].shape[0]
    lane = lax.broadcasted_iota(jnp.int32, (rank, LANES), 1)
    block = jnp.zeros((rank, LANES), F32)
    for at, column in enumerate(columns):
        block = jnp.where(lane == at, column, block)
    flip[...] = jnp.zeros(flip.shape, F32)
    flip[:rank, :] = block
    return flip[...].T


def border(surface, half):
    strips = [row_of(surface, row) for row in range(half)]
    return [strip[:, :1] for strip in strips] + [strip[:, LANES - 1:] for strip in strips]


def rows_as_columns(rows, rank, flip):
    flip[...] = jnp.zeros(flip.shape, F32)
    flip[: rows.shape[0], :] = rows
    return flip[...].T[:rank, :]


def smoothed(surface, half, above, below, left_cols, right_cols):
    lane = lax.broadcasted_iota(jnp.int32, above.shape, 1)
    strips = []
    for row in range(half):
        here = row_of(surface, row)
        up = above if row == 0 else row_of(surface, row - 1)
        down = below if row == half - 1 else row_of(surface, row + 1)
        left = jnp.where(lane == 0, left_cols[:, half + row:half + row + 1], pltpu.roll(here, 1, 1))
        right = jnp.where(lane == LANES - 1, right_cols[:, row:row + 1], pltpu.roll(here, LANES - 1, 1))
        lap = 4.0 * here - (up + down + left + right)
        strips.append(here - (ETA_SPACE * SMOOTH) * lap)
    return strips


def prepare_kernel(half, space_ref, time_ref, after, surface, edge_near, edge_far, cols, time_own, flip):
    core = lax.axis_index("ta")
    rank = surface.shape[0]
    height = space_ref.shape[0] // rank
    for row in range(half):
        surface[:, row * LANES:(row + 1) * LANES] = space_ref[pl.ds(core * half + row, rank, stride=height), :]
    edge_near[...] = space_ref[pl.ds(half - core, rank, stride=height), :]
    edge_far[...] = space_ref[pl.ds(core * (height - 1), rank, stride=height), :]
    cols[...] = columns_as_rows(border(surface[...], half), flip)[:COLS, :]
    time_own[...] = time_ref[...]


def pick(flag, a, b):
    return jnp.where(flag, a, b)


def model_kernel(half, surface, edge_near, edge_far, cols_a, cols_b, swap, time_own, time_other, base, predicted, packed, time_t, flip, days_all):
    core = lax.axis_index("ta")
    rank = surface.shape[0]
    days = time_own.shape[0]
    days_all[...] = jnp.zeros(days_all.shape, F32)
    days_all[:days, :rank] = time_own[...]
    days_all[days:, :rank] = time_other[...]
    time_full = days_all[...]
    time_t[...] = time_full.T[:rank, :]
    packed[...] = surface[...].astype(BF16)
    time_bf = time_full[:, :rank].astype(BF16)
    for at in range(0, half * LANES, 2 * LANES):
        predicted[:, at:at + 2 * LANES] = dot(time_bf, packed[:, at:at + 2 * LANES], (1, 0))
    above = pick(core == 0, edge_far[...], edge_near[...])
    below = pick(core == 0, edge_near[...], edge_far[...])
    odd = swap()
    left = rows_as_columns(pick(odd, cols_a[...], cols_b[...]), rank, flip)
    right = rows_as_columns(pick(odd, cols_b[...], cols_a[...]), rank, flip)
    for row, strip in enumerate(smoothed(surface[...], half, above, below, left, right)):
        base[:, row * LANES:(row + 1) * LANES] = strip


def gradients(half, base, predicted, packed, time_t, seen, summed, fresh):
    rank = time_t.shape[0]
    time_bf = time_t.astype(BF16)
    time_twice = jnp.concatenate([time_bf, time_bf], axis=1)
    seen_bf = seen.astype(BF16)
    width = 2 * LANES
    owner = lax.broadcasted_iota(jnp.int32, (TAIL, width), 0)
    lane = lax.broadcasted_iota(jnp.int32, (TAIL, width), 1)
    grad_time = jnp.zeros((rank, width), F32)
    grad_diag = jnp.zeros((rank, LANES), F32)
    norm = jnp.zeros((rank, 1), F32)
    for at in range(0, half * LANES, width):
        spread = (owner * LANES <= lane + at) & (lane + at < (owner + 1) * LANES)
        weight = dot(seen_bf, spread.astype(BF16), (0, 0))
        part = packed[:, at:at + width]
        residual = weight * predicted[:, at:at + width] - summed[:, at:at + width]
        high = residual.astype(BF16)
        low = (residual - high.astype(F32)).astype(BF16)
        both = jnp.concatenate([high, low], axis=0)
        grad_space = dot(time_twice, both, (1, 0))
        grad_time = grad_time + dot(part, both, (1, 1))
        new = base[:, at:at + width] - ETA_SPACE * grad_space
        fresh[:, at:at + width] = new
        norm = norm + jnp.sum(new * new, axis=1, keepdims=True)
        wide = part.astype(F32)
        for row in range(width // LANES):
            strip = row_of(wide, row)
            square = jnp.sum(strip * strip, axis=1, keepdims=True)
            grad_diag = grad_diag + square * seen[at // LANES + row:at // LANES + row + 1, :]
    return grad_time[:, :LANES] + grad_time[:, LANES:], grad_diag, norm


def post(half, sums, fresh, message, outgoing, edge_far, flip):
    grad_time, grad_diag, norm = sums
    core = lax.axis_index("ta")
    rank = norm.shape[0]
    columns = [norm] if edge_far is None else [norm] + [norm] * (NORM - 1) + border(fresh[...], half)
    last = columns_as_rows(columns, flip)[: message.shape[0] - 2 * rank, :]
    message[:rank, :] = grad_time
    message[rank:2 * rank, :] = grad_diag
    message[2 * rank:, :] = last
    outgoing[:rank, :] = pltpu.roll(grad_time, LANES // 2, 1)
    outgoing[rank:2 * rank, :] = pltpu.roll(grad_diag, LANES // 2, 1)
    outgoing[2 * rank:2 * rank + NORM, :] = last[:NORM, :]
    if edge_far is not None:
        first_row, last_row = fresh[:, :LANES], fresh[:, (half - 1) * LANES:]
        outgoing[2 * rank + NORM:, :] = pick(core == 0, last_row, first_row)
        edge_far[...] = pick(core == 0, first_row, last_row)


def first_kernel(half, n_lon, base, predicted, packed, time_t, *rest):
    near, far = rest[:n_lon], rest[n_lon:2 * n_lon]
    fresh, message, outgoing, edge_far, summed, seen, flip = rest[2 * n_lon:]
    days = (near[0].shape[0] - TAIL) // half
    for row in range(half):
        for first, parts in ((0, near), (days, far)):
            value = parts[0][row * days:(row + 1) * days, :].astype(F32)
            for piece in parts[1:]:
                value = value + piece[row * days:(row + 1) * days, :].astype(F32)
            summed[first:first + days, row * LANES:(row + 1) * LANES] = value

    def counts(parts):
        value = parts[0][half * days:, :].astype(F32)
        for piece in parts[1:]:
            value = value + piece[half * days:, :].astype(F32)
        return value

    seen[...] = counts(near) + pltpu.roll(counts(far), days, 1)
    sums = gradients(half, base, predicted, packed, time_t[...], seen[...], summed, fresh)
    post(half, sums, fresh, message, outgoing, edge_far, flip)


def settle(rank, counts, parts, time_t, flip):
    day_count, cell_count = counts
    total = parts[0][...].astype(F32)
    if len(parts) > 1:
        one, two, three = (part[...].astype(F32) for part in parts[1:])
        total = (total + one) + (two + three)
    time_new = time_t - total[:rank, :] / (total[rank:2 * rank, :] + RIDGE)
    norm = total[2 * rank:2 * rank + NORM, :]
    if parts[0].dtype == BF16:
        norm = norm + total[2 * rank + NORM:2 * rank + 2 * NORM, :]
    space_sq = rows_as_columns(norm, rank, flip)[:, :1]
    square = time_new * time_new
    time_sq = 0.5 * jnp.sum(square + pltpu.roll(square, LANES // 2, 1), axis=1, keepdims=True)
    ratio = (time_sq / day_count + EPSILON) / (space_sq / cell_count + EPSILON)
    return time_new, jnp.sqrt(jnp.sqrt(ratio))


def second_kernel(half, counts, n_parts, swap, surface, time_t, summed, seen, edge_near, edge_far, *rest):
    parts, (cols_a, cols_b) = rest[:n_parts], rest[n_parts:n_parts + 2]
    fresh, time_out, message, outgoing, flip, scaled, base, predicted, packed = rest[n_parts + 2:]
    core = lax.axis_index("ta")
    rank = surface.shape[0]
    time_new, scale = settle(rank, counts, parts, time_t[...], flip)
    time_now = time_new / scale
    time_out[...] = time_now
    scaled[...] = surface[...] * scale
    packed[...] = scaled[...].astype(BF16)
    time_bf = time_now.T.astype(BF16)
    for at in range(0, half * LANES, 2 * LANES):
        predicted[:, at:at + 2 * LANES] = dot(time_bf, packed[:, at:at + 2 * LANES], (1, 0))
    near, far = edge_near[...], edge_far[...]
    above = pick(core == 0, far, near) * scale
    below = pick(core == 0, near, far) * scale
    odd = swap()
    from_a, from_b = cols_a[cols_a.shape[0] - COLS:, :], cols_b[cols_b.shape[0] - COLS:, :]
    left = rows_as_columns(pick(odd, from_a, from_b), rank, flip) * scale
    right = rows_as_columns(pick(odd, from_b, from_a), rank, flip) * scale
    for row, strip in enumerate(smoothed(scaled[...], half, above, below, left, right)):
        base[:, row * LANES:(row + 1) * LANES] = strip
    sums = gradients(half, base, predicted, packed, time_now, seen[...], summed, fresh)
    post(half, sums, fresh, message, outgoing, None, flip)


def last_kernel(half, counts, n_parts, surface, other, time_t, *rest):
    parts = rest[:n_parts]
    space_out, time_out, flip = rest[n_parts:]
    core = lax.axis_index("ta")
    rank = surface.shape[0]
    height = space_out.shape[0] // rank
    time_new, scale = settle(rank, counts, parts, time_t[...], flip)
    flip[...] = jnp.zeros(flip.shape, F32)
    flip[:rank, :] = time_new / scale
    time_out[...] = flip[...].T[: time_out.shape[0], :rank]
    for row in range(half):
        at = row * LANES
        space_out[pl.ds(core * half + row, rank, stride=height), :] = surface[:, at:at + LANES] * scale
        space_out[pl.ds((1 - core) * half + row, rank, stride=height), :] = other[:, at:at + LANES] * scale


def core_kernel(rank, mine, theirs, edge_in, total, beside, edge_out):
    rows = total.shape[0]
    total[...] = mine[:rows, :] + theirs[:rows, :]
    beside[...] = theirs[rows:, :]
    edge_out[...] = edge_in[...]


def add_kernel(mine, theirs, total):
    rows = total.shape[0]
    total[...] = mine[:rows, :] + theirs[:rows, :]


def band_kernel(mine, theirs, message, after, total):
    rows = mine.shape[0]
    total[:rows, :] = mine[...] + theirs[...]
    total[rows:, :] = message[rows:, :]


def narrow_kernel(rank, mine, theirs, total):
    value = mine[...] + theirs[...]
    total[: 2 * rank, :] = value[: 2 * rank, :].astype(BF16)
    norm = value[2 * rank:, :]
    high = norm.astype(BF16).astype(F32)
    total[2 * rank:, :] = jnp.concatenate([high, norm - high], axis=0).astype(BF16)


def shape(dims, dtype=F32):
    return jax.ShapeDtypeStruct(tuple(dims), dtype)


def padded(ref):
    *outer, rows, lanes = (1, *ref.shape)
    return math.prod(outer) * -(-rows // 16) * 16 * -(-lanes // LANES) * LANES * jnp.dtype(ref.dtype).itemsize


def call(kernel, out_shape, scratch=(), hbm=0, after=0, flops=1_000_000):
    def run(*operands):
        vmem = [*operands[hbm:len(operands) - after], *jax.tree.leaves(out_shape), *scratch]
        specs = [pltpu.HBM] * hbm + [pltpu.VMEM] * (len(operands) - hbm - after) + [pl.ANY] * after
        return pl.pallas_call(
            kernel,
            out_shape=out_shape,
            in_specs=[pl.BlockSpec(memory_space=space) for space in specs],
            out_specs=jax.tree.map(lambda _: pl.BlockSpec(memory_space=pltpu.VMEM), out_shape),
            scratch_shapes=list(scratch),
            compiler_params=pltpu.CompilerParams(vmem_limit_bytes=SPARE + sum(padded(ref) for ref in vmem if len(ref.shape) > 1)),
            cost_estimate=pl.CostEstimate(flops=flops, bytes_accessed=1_000_000, transcendentals=0),
        )(*operands)

    return run


def across(value, axis, step):
    return lax.ppermute(value, axis, [(i, i ^ step) for i in range(lax.axis_size(axis))])


def shards(swath, obs_mask, target, send_list, send_count, factor_space, factor_time):
    n_lon, n_lat, n_ta = (lax.axis_size(axis) for axis in ("lon", "lat", "ta"))
    slots, days, cells = swath.shape
    rank, height, _ = factor_space.shape
    half = height // n_ta
    wide = half * LANES
    counts = (float(days * n_ta), float(height * cells * n_lon * n_lat))
    sum_rows = 2 * rank + NORM
    flip = pltpu.VMEM((LANES, LANES), F32)

    distant, close = range(n_lon // 2, n_lon), range(1, n_lon // 2)
    sends = [(side, step) for steps in (distant, close) for side in (0, 1) for step in steps] + [(1, 0), (0, 0)]
    pieces = call(
        functools.partial(route_kernel, half, sends),
        [shape((half * days + TAIL, cells), BF16)] * len(sends),
        [
            pltpu.SMEM(send_list.shape, jnp.int32),
            pltpu.SMEM(send_count.shape, jnp.int32),
            pltpu.SMEM(target.shape, jnp.int32),
            pltpu.VMEM(swath.shape, swath.dtype),
            pltpu.VMEM(obs_mask.shape, jnp.int32),
            pltpu.SMEM((slots,), jnp.int32),
            pltpu.VMEM((2 * n_lon * half, days, cells), F32),
            pltpu.VMEM((2 * n_lon * half + TAIL, LANES), F32),
            pltpu.SemaphoreType.DMA((4 + SWATH_COPIES,)),
        ],
        hbm=5,
    )(send_list, send_count, target, swath, obs_mask)
    near_in, far_in = {}, {}
    for (side, step), piece in zip(sends, pieces):
        if side:
            far_in[step] = across(piece, ("lon", "ta"), 2 * step + 1)
        else:
            near_in[step] = across(piece, "lon", step) if step else piece

    def bands(edge):
        there = [(2 * band + 1, 2 * band + 2) for band in range(n_lat - 1)]
        return lax.ppermute(edge, ("lat", "ta"), there + [(b, a) for a, b in there])

    paired = n_lon == 4

    def swap():
        return lax.rem(lax.axis_index("lon"), 2) == 1 if paired else jnp.bool_(True)

    def columns(value):
        if paired:
            return across(value, "lon", 1), across(value, "lon", 3)
        ring = [(i, (i + 1) % n_lon) for i in range(n_lon)]
        return lax.ppermute(value, "lon", ring), lax.ppermute(value, "lon", [(b, a) for a, b in ring])

    surface, edge_near, edge_far, cols, time_own = call(
        functools.partial(prepare_kernel, half),
        [shape((rank, wide)), shape((rank, LANES)), shape((rank, LANES)), shape((COLS, LANES)), shape(factor_time.shape)],
        [flip],
        after=1,
    )(factor_space.reshape(rank * height, cells), factor_time, near_in[1])
    cols_a, cols_b = columns(cols)

    def model(*refs):
        model_kernel(half, *refs[:5], swap, *refs[5:])

    base, predicted, packed, time_t = call(
        model,
        [shape((rank, wide)), shape((2 * days, wide)), shape((rank, wide), BF16), shape((rank, LANES))],
        [flip, flip],
    )(surface, edge_near, bands(edge_far), cols_a, cols_b, time_own, across(time_own, "ta", 1))

    fresh = shape((rank, wide))
    surface, message, outgoing, edge_far, summed, seen = call(
        functools.partial(first_kernel, half, n_lon),
        [fresh, shape((sum_rows + COLS, LANES)), shape((sum_rows + rank, LANES)), shape((rank, LANES)), shape((2 * days, wide)), shape((TAIL, LANES))],
        [flip],
    )(base, predicted, packed, time_t, *[near_in[s] for s in range(n_lon)], *[far_in[s] for s in range(n_lon)])

    sums = shape((sum_rows, LANES))
    add = call(add_kernel, sums)

    def over_bands(total, last):
        step = 1
        while 2 * step < n_lat:
            total = add(total, across(total, "lat", step))
            step *= 2
        return last(total, across(total, "lat", step))

    def over_lon(total):
        if paired:
            return [total] + [across(total, "lon", step) for step in (1, 2, 3)]
        step = 1
        while step < n_lon:
            total = add(total, across(total, "lon", step))
            step *= 2
        return [total]

    total, edge_near, edge_far = call(
        functools.partial(core_kernel, rank), [sums, shape((rank, LANES)), shape((rank, LANES))]
    )(message, across(outgoing, "ta", 1), edge_far)
    edge_far = bands(edge_far)
    if paired:
        last = call(band_kernel, shape((sum_rows + COLS, LANES)), after=1)
        parts = over_lon(over_bands(total, lambda mine, theirs: last(mine, theirs, message, edge_far)))
        cols_a, cols_b = parts[1], parts[3]
    else:
        parts = over_lon(over_bands(total, add))
        cols_a, cols_b = columns(message[sum_rows:])

    def second(*refs):
        second_kernel(half, counts, len(parts), swap, *refs)

    surface, time_t, message, outgoing = call(
        second,
        [fresh, shape((rank, LANES)), sums, sums],
        [flip, pltpu.VMEM((rank, wide), F32), pltpu.VMEM((rank, wide), F32), pltpu.VMEM((2 * days, wide), F32), pltpu.VMEM((rank, wide), BF16)],
    )(surface, time_t, summed, seen, edge_near, edge_far, *parts, cols_a, cols_b)

    total = add(message, across(outgoing, "ta", 1))
    other = across(surface, "ta", 1)
    narrow = call(functools.partial(narrow_kernel, rank), shape((sum_rows + NORM, LANES), BF16))
    parts = over_lon(over_bands(total, narrow if paired else add))
    space, time = call(
        functools.partial(last_kernel, half, counts, len(parts)),
        [shape((rank * height, cells)), shape(factor_time.shape)],
        [flip],
    )(surface, other, time_t, *parts)
    return space.reshape(rank, height, cells), time


def solution(mesh):
    in_specs = (
        P(("grp", "lon", "lat"), "ta", None),
        P(("grp", "lon", "lat"), "ta"),
        P(("grp", "lon", "lat")),
        P(("grp", "lon", "lat"), None, None),
        P(("grp", "lon", "lat"), None),
        P(None, ("grp", "lat"), "lon"),
        P(("grp", "ta"), None),
    )
    out_specs = (P(None, ("grp", "lat"), "lon"), P(("grp", "ta"), None))
    return jax.shard_map(shards, mesh=mesh, in_specs=in_specs, out_specs=out_specs, check_vma=False)
```

```python
import functools
import math

import jax
import jax.numpy as jnp
from jax import lax
from jax.experimental import pallas as pl
from jax.experimental.pallas import tpu as pltpu
from jax.sharding import PartitionSpec as P

SMOOTH = 2.0
ETA_SPACE = 0.08
RIDGE = 1.0
EPSILON = 1e-06

F32 = jnp.float32
BF16 = jnp.bfloat16
LANES = 128
TAIL = 16
COLS = 16
NORM = 8
SPARE = 2 * 1024 * 1024
SWATH_COPIES = 4


def dot(a, b, contract):
    return lax.dot_general(a, b, ((contract[:1], contract[1:]), ((), ())), preferred_element_type=F32)


def route_kernel(half, sends, paired, list_hbm, count_hbm, target_hbm, swath_hbm, mask_hbm, space_hbm, time_hbm, *rest):
    outs, rest = rest[: len(sends)], rest[len(sends):]
    surface, edge_near, edge_far, cols, rest = *rest[:4], rest[4:]
    list_ref, count_ref, target_ref, swath_ref, mask_ref, space_ref, time_ref, place, total, seen, flip, arrived = rest
    me, core = lax.axis_index("lon"), lax.axis_index("ta")
    n_lon = list_ref.shape[1]
    slots, days, cells = swath_ref.shape
    chunk = slots // SWATH_COPIES
    small = [(list_hbm, list_ref), (count_hbm, count_ref), (target_hbm, target_ref), (mask_hbm, mask_ref)]
    large = [(swath_hbm.at[pl.ds(at, chunk)], swath_ref.at[pl.ds(at, chunk)]) for at in range(0, slots, chunk)]
    model = [(space_hbm, space_ref), (time_hbm, time_ref)]
    copies = [pltpu.make_async_copy(src, dst, arrived.at[i]) for i, (src, dst) in enumerate(small + large + model)]
    for copy in copies:
        copy.start()
    total[...] = jnp.zeros(total.shape, F32)
    seen[...] = jnp.zeros(seen.shape, F32)
    for copy in copies[: len(small)]:
        copy.wait()

    def owner(d, carry):
        step = jnp.bitwise_xor(d, me)

        def entry(k, carry):
            slot = list_ref[0, d, k]
            row = target_ref[slot]
            far = jnp.bitwise_xor(lax.div(row, half), core)
            place[slot] = (far * n_lon + step) * half + lax.rem(row, half)
            return carry

        return lax.fori_loop(0, count_ref[0, d], entry, carry)

    lax.fori_loop(0, n_lon, owner, 0)
    mask = mask_ref[...].astype(F32)
    by_day = mask.T
    for slot in range(slots):
        if slot % chunk == 0:
            copies[len(small) + slot // chunk].wait()
        at = place[slot]
        total[at] += swath_ref[slot].astype(F32) * by_day[:, slot:slot + 1]
        seen[pl.ds(at, 1), :days] += mask[slot:slot + 1, :]
    for copy in copies[len(small) + len(large):]:
        copy.wait()
    rank = surface.shape[0]
    height = space_ref.shape[0] // rank
    for row in range(half):
        surface[:, row * LANES:(row + 1) * LANES] = space_ref[pl.ds(core * half + row, rank, stride=height), :]
    edge_near[...] = space_ref[pl.ds(half - core, rank, stride=height), :]
    edge_far[...] = space_ref[pl.ds(core * (height - 1), rank, stride=height), :]
    cols[...] = columns_as_rows(border(surface[...], half), flip)[:COLS, :]
    for (side, step), out in zip(sends, outs):
        at = (side * n_lon + step) * half
        end = half * days + TAIL
        out[: half * days, :] = total[at:at + half].reshape(half * days, cells).astype(BF16)
        out[half * days:end, :] = seen[at:at + TAIL, :].astype(BF16)
        if (side, step) == (1, 0):
            left = time_ref[...]
            for part in range(end, end + 3 * days, days):
                value = left.astype(BF16)
                out[part:part + days, :] = jnp.zeros((days, LANES), BF16)
                out[part:part + days, :rank] = value
                left = left - value.astype(F32)
        elif paired and side == 0 and step in (1, 3):
            out[end:, :] = cols[...].astype(BF16)


def row_of(surface, row):
    return surface[:, row * LANES:(row + 1) * LANES]


def columns_as_rows(columns, flip):
    rank = columns[0].shape[0]
    lane = lax.broadcasted_iota(jnp.int32, (rank, LANES), 1)
    block = jnp.zeros((rank, LANES), F32)
    for at, column in enumerate(columns):
        block = jnp.where(lane == at, column, block)
    flip[...] = jnp.zeros(flip.shape, F32)
    flip[:rank, :] = block
    return flip[...].T


def border(surface, half):
    strips = [row_of(surface, row) for row in range(half)]
    return [strip[:, :1] for strip in strips] + [strip[:, LANES - 1:] for strip in strips]


def rows_as_columns(rows, rank, flip):
    flip[...] = jnp.zeros(flip.shape, F32)
    flip[: rows.shape[0], :] = rows
    return flip[...].T[:rank, :]


def smoothed(surface, half, above, below, left_cols, right_cols):
    lane = lax.broadcasted_iota(jnp.int32, above.shape, 1)
    strips = []
    for row in range(half):
        here = row_of(surface, row)
        up = above if row == 0 else row_of(surface, row - 1)
        down = below if row == half - 1 else row_of(surface, row + 1)
        left = jnp.where(lane == 0, left_cols[:, half + row:half + row + 1], pltpu.roll(here, 1, 1))
        right = jnp.where(lane == LANES - 1, right_cols[:, row:row + 1], pltpu.roll(here, LANES - 1, 1))
        lap = 4.0 * here - (up + down + left + right)
        strips.append(here - (ETA_SPACE * SMOOTH) * lap)
    return strips


def pick(flag, a, b):
    return jnp.where(flag, a, b)


def model_kernel(half, surface, time_own, piece, predicted, packed, time_t, days_all):
    rank = surface.shape[0]
    days = time_own.shape[0]
    at = half * days + TAIL
    high, middle, low = (piece[first:first + days, :].astype(F32) for first in range(at, at + 3 * days, days))
    days_all[...] = jnp.zeros(days_all.shape, F32)
    days_all[:days, :rank] = time_own[...]
    days_all[days:, :] = (high + middle) + low
    time_full = days_all[...]
    time_t[...] = time_full.T[:rank, :]
    packed[...] = surface[...].astype(BF16)
    time_bf = time_full[:, :rank].astype(BF16)
    for at in range(0, half * LANES, 2 * LANES):
        predicted[:, at:at + 2 * LANES] = dot(time_bf, packed[:, at:at + 2 * LANES], (1, 0))


def smooth(half, odd, surface, edge_near, edge_far, cols_a, cols_b, scale, base, flip):
    core = lax.axis_index("ta")
    rank = surface.shape[0]
    above = pick(core == 0, edge_far, edge_near)
    below = pick(core == 0, edge_near, edge_far)
    left = rows_as_columns(pick(odd, cols_a, cols_b), rank, flip)
    right = rows_as_columns(pick(odd, cols_b, cols_a), rank, flip)
    if scale is not None:
        above, below, left, right = above * scale, below * scale, left * scale, right * scale
    for row, strip in enumerate(smoothed(surface, half, above, below, left, right)):
        base[:, row * LANES:(row + 1) * LANES] = strip


def gradients(half, base, predicted, packed, time_t, seen, summed, fresh):
    rank = time_t.shape[0]
    time_bf = time_t.astype(BF16)
    time_twice = jnp.concatenate([time_bf, time_bf], axis=1)
    seen_bf = seen.astype(BF16)
    width = 2 * LANES
    owner = lax.broadcasted_iota(jnp.int32, (TAIL, width), 0)
    lane = lax.broadcasted_iota(jnp.int32, (TAIL, width), 1)
    grad_time = jnp.zeros((rank, width), F32)
    grad_diag = jnp.zeros((rank, LANES), F32)
    norm = jnp.zeros((rank, 1), F32)
    for at in range(0, half * LANES, width):
        spread = (owner * LANES <= lane + at) & (lane + at < (owner + 1) * LANES)
        weight = dot(seen_bf, spread.astype(BF16), (0, 0))
        part = packed[:, at:at + width]
        residual = weight * predicted[:, at:at + width] - summed[:, at:at + width]
        high = residual.astype(BF16)
        low = (residual - high.astype(F32)).astype(BF16)
        both = jnp.concatenate([high, low], axis=0)
        grad_space = dot(time_twice, both, (1, 0))
        grad_time = grad_time + dot(part, both, (1, 1))
        new = base[:, at:at + width] - ETA_SPACE * grad_space
        fresh[:, at:at + width] = new
        norm = norm + jnp.sum(new * new, axis=1, keepdims=True)
        wide = part.astype(F32)
        for row in range(width // LANES):
            strip = row_of(wide, row)
            square = jnp.sum(strip * strip, axis=1, keepdims=True)
            grad_diag = grad_diag + square * seen[at // LANES + row:at // LANES + row + 1, :]
    return grad_time[:, :LANES] + grad_time[:, LANES:], grad_diag, norm


def post(half, sums, fresh, message, outgoing, edge_far, flip):
    grad_time, grad_diag, norm = sums
    core = lax.axis_index("ta")
    rank = norm.shape[0]
    columns = [norm] if edge_far is None else [norm] + [norm] * (NORM - 1) + border(fresh[...], half)
    last = columns_as_rows(columns, flip)[: message.shape[0] - 2 * rank, :]
    message[:rank, :] = grad_time
    message[rank:2 * rank, :] = grad_diag
    message[2 * rank:, :] = last
    outgoing[:rank, :] = pltpu.roll(grad_time, LANES // 2, 1)
    outgoing[rank:2 * rank, :] = pltpu.roll(grad_diag, LANES // 2, 1)
    outgoing[2 * rank:2 * rank + NORM, :] = last[:NORM, :]
    if edge_far is not None:
        first_row, last_row = fresh[:, :LANES], fresh[:, (half - 1) * LANES:]
        outgoing[2 * rank + NORM:, :] = pick(core == 0, last_row, first_row)
        edge_far[...] = pick(core == 0, first_row, last_row)


def first_kernel(half, days, order, paired, swap, surface, edge_near, predicted, packed, time_t, *rest):
    pieces, rest = dict(zip(order, rest)), rest[len(order):]
    edge_far_in, rest = rest[0], rest[1:]
    if paired:
        at = half * days + TAIL
        cols = [pieces[0, step][at:, :].astype(F32) for step in (1, 3)]
    else:
        cols, rest = [ref[...] for ref in rest[:2]], rest[2:]
    fresh, message, outgoing, edge_far, summed, seen, flip, base = rest
    smooth(half, swap(), surface[...], edge_near[...], edge_far_in[...], *cols, None, base, flip)
    sides = [[pieces[key] for key in sorted(pieces) if key[0] == side] for side in (0, 1)]

    def add_up(parts, rows):
        value = parts[0][rows, :].astype(F32)
        for piece in parts[1:]:
            value = value + piece[rows, :].astype(F32)
        return value

    for row in range(half):
        for first, parts in zip((0, days), sides):
            summed[first:first + days, row * LANES:(row + 1) * LANES] = add_up(parts, slice(row * days, (row + 1) * days))
    near, far = (add_up(parts, slice(half * days, half * days + TAIL)) for parts in sides)
    seen[...] = near + pltpu.roll(far, days, 1)
    sums = gradients(half, base, predicted, packed, time_t[...], seen[...], summed, fresh)
    post(half, sums, fresh, message, outgoing, edge_far, flip)


def settle(rank, counts, parts, time_t, flip):
    day_count, cell_count = counts
    total = parts[0][...].astype(F32)
    if len(parts) > 1:
        one, two, three = (part[...].astype(F32) for part in parts[1:])
        total = (total + one) + (two + three)
    time_new = time_t - total[:rank, :] / (total[rank:2 * rank, :] + RIDGE)
    norm = total[2 * rank:2 * rank + NORM, :]
    if parts[0].dtype == BF16:
        norm = norm + total[2 * rank + NORM:2 * rank + 2 * NORM, :]
    space_sq = rows_as_columns(norm, rank, flip)[:, :1]
    square = time_new * time_new
    time_sq = 0.5 * jnp.sum(square + pltpu.roll(square, LANES // 2, 1), axis=1, keepdims=True)
    ratio = (time_sq / day_count + EPSILON) / (space_sq / cell_count + EPSILON)
    return time_new, jnp.sqrt(jnp.sqrt(ratio))


def second_kernel(half, counts, n_parts, swap, surface, time_t, summed, seen, edge_near, edge_far, *rest):
    parts, (cols_a, cols_b) = rest[:n_parts], rest[n_parts:n_parts + 2]
    fresh, time_out, message, outgoing, flip, scaled, base, predicted, packed = rest[n_parts + 2:]
    rank = surface.shape[0]
    time_new, scale = settle(rank, counts, parts, time_t[...], flip)
    time_now = time_new / scale
    time_out[...] = time_now
    scaled[...] = surface[...] * scale
    packed[...] = scaled[...].astype(BF16)
    time_bf = time_now.T.astype(BF16)
    for at in range(0, half * LANES, 2 * LANES):
        predicted[:, at:at + 2 * LANES] = dot(time_bf, packed[:, at:at + 2 * LANES], (1, 0))
    cols = [ref[ref.shape[0] - COLS:, :] for ref in (cols_a, cols_b)]
    smooth(half, swap(), scaled[...], edge_near[...], edge_far[...], *cols, scale, base, flip)
    sums = gradients(half, base, predicted, packed, time_now, seen[...], summed, fresh)
    post(half, sums, fresh, message, outgoing, None, flip)


def last_kernel(half, counts, n_parts, surface, other, time_t, *rest):
    parts = rest[:n_parts]
    space_out, time_out, flip = rest[n_parts:]
    core = lax.axis_index("ta")
    rank = surface.shape[0]
    height = space_out.shape[0] // rank
    time_new, scale = settle(rank, counts, parts, time_t[...], flip)
    flip[...] = jnp.zeros(flip.shape, F32)
    flip[:rank, :] = time_new / scale
    time_out[...] = flip[...].T[: time_out.shape[0], :rank]
    for row in range(half):
        at = row * LANES
        space_out[pl.ds(core * half + row, rank, stride=height), :] = surface[:, at:at + LANES] * scale
        space_out[pl.ds((1 - core) * half + row, rank, stride=height), :] = other[:, at:at + LANES] * scale


def core_kernel(rank, mine, theirs, edge_in, total, beside, edge_out):
    rows = total.shape[0]
    total[...] = mine[:rows, :] + theirs[:rows, :]
    beside[...] = theirs[rows:, :]
    edge_out[...] = edge_in[...]


def add_kernel(mine, theirs, total):
    rows = total.shape[0]
    total[...] = mine[:rows, :] + theirs[:rows, :]


def band_kernel(mine, theirs, message, after, total):
    rows = mine.shape[0]
    total[:rows, :] = mine[...] + theirs[...]
    total[rows:, :] = message[rows:, :]


def narrow_kernel(rank, mine, theirs, total):
    value = mine[...] + theirs[...]
    total[: 2 * rank, :] = value[: 2 * rank, :].astype(BF16)
    norm = value[2 * rank:, :]
    high = norm.astype(BF16).astype(F32)
    total[2 * rank:, :] = jnp.concatenate([high, norm - high], axis=0).astype(BF16)


def shape(dims, dtype=F32):
    return jax.ShapeDtypeStruct(tuple(dims), dtype)


def padded(ref):
    *outer, rows, lanes = (1, *ref.shape)
    return math.prod(outer) * -(-rows // 16) * 16 * -(-lanes // LANES) * LANES * jnp.dtype(ref.dtype).itemsize


def call(kernel, out_shape, scratch=(), hbm=0, after=0, flops=1_000_000):
    def run(*operands):
        operands = [pltpu.with_memory_space_constraint(x, pltpu.HBM) if i < hbm else x for i, x in enumerate(operands)]
        vmem = [*operands[hbm:len(operands) - after], *jax.tree.leaves(out_shape), *scratch]
        specs = [pltpu.HBM] * hbm + [pltpu.VMEM] * (len(operands) - hbm - after) + [pl.ANY] * after
        return pl.pallas_call(
            kernel,
            out_shape=out_shape,
            in_specs=[pl.BlockSpec(memory_space=space) for space in specs],
            out_specs=jax.tree.map(lambda _: pl.BlockSpec(memory_space=pltpu.VMEM), out_shape),
            scratch_shapes=list(scratch),
            compiler_params=pltpu.CompilerParams(vmem_limit_bytes=SPARE + sum(padded(ref) for ref in vmem if len(ref.shape) > 1)),
            cost_estimate=pl.CostEstimate(flops=flops, bytes_accessed=1_000_000, transcendentals=0),
        )(*operands)

    return run


def across(value, axis, step):
    return lax.ppermute(value, axis, [(i, i ^ step) for i in range(lax.axis_size(axis))])


def shards(swath, obs_mask, target, send_list, send_count, factor_space, factor_time):
    n_lon, n_lat, n_ta = (lax.axis_size(axis) for axis in ("lon", "lat", "ta"))
    slots, days, cells = swath.shape
    rank, height, _ = factor_space.shape
    half = height // n_ta
    wide = half * LANES
    counts = (float(days * n_ta), float(height * cells * n_lon * n_lat))
    sum_rows = 2 * rank + NORM
    flip = pltpu.VMEM((LANES, LANES), F32)

    paired = n_lon == 4

    distant, close = range(n_lon // 2, n_lon), range(1, n_lon // 2)
    sends = [(0, step) for step in distant] + [(1, 0)] + [(1, step) for step in distant]
    sends += [(side, step) for side in (0, 1) for step in close] + [(0, 0)]

    def piece_rows(side, step):
        more = 3 * days if (side, step) == (1, 0) else COLS if paired and side == 0 and step in (1, 3) else 0
        return half * days + TAIL + more

    operands = (send_list, send_count, target, swath, obs_mask, factor_space.reshape(rank * height, cells), factor_time)
    *pieces, surface, edge_near, edge_far, cols = call(
        functools.partial(route_kernel, half, sends, paired),
        [shape((piece_rows(*key), cells), BF16) for key in sends]
        + [shape((rank, wide)), shape((rank, LANES)), shape((rank, LANES)), shape((COLS, LANES))],
        [pltpu.SMEM(ref.shape, jnp.int32) for ref in operands[:3]]
        + [pltpu.VMEM(ref.shape, ref.dtype) for ref in operands[3:]]
        + [
            pltpu.SMEM((slots,), jnp.int32),
            pltpu.VMEM((2 * n_lon * half, days, cells), F32),
            pltpu.VMEM((2 * n_lon * half + TAIL, LANES), F32),
            flip,
            pltpu.SemaphoreType.DMA((len(operands) - 1 + SWATH_COPIES,)),
        ],
        hbm=len(operands),
    )(*operands)

    def arrived(key, piece):
        side, step = key
        if side:
            return across(piece, ("lon", "ta"), 2 * step + 1)
        return across(piece, "lon", step) if step else piece

    pieces = {key: arrived(key, piece) for key, piece in zip(sends, pieces)}

    def bands(edge):
        there = [(2 * band + 1, 2 * band + 2) for band in range(n_lat - 1)]
        return lax.ppermute(edge, ("lat", "ta"), there + [(b, a) for a, b in there])

    def swap():
        return lax.rem(lax.axis_index("lon"), 2) == 1 if paired else jnp.bool_(True)

    def columns(value):
        if paired:
            return across(value, "lon", 1), across(value, "lon", 3)
        ring = [(i, (i + 1) % n_lon) for i in range(n_lon)]
        return lax.ppermute(value, "lon", ring), lax.ppermute(value, "lon", [(b, a) for a, b in ring])

    predicted, packed, time_t = call(
        functools.partial(model_kernel, half),
        [shape((2 * days, wide)), shape((rank, wide), BF16), shape((rank, LANES))],
        [flip],
    )(surface, factor_time, pieces[1, 0])

    fresh = shape((rank, wide))
    surface, message, outgoing, edge_far, summed, seen = call(
        functools.partial(first_kernel, half, days, sends, paired, swap),
        [fresh, shape((sum_rows + COLS, LANES)), shape((sum_rows + rank, LANES)), shape((rank, LANES)), shape((2 * days, wide)), shape((TAIL, LANES))],
        [flip, pltpu.VMEM((rank, wide), F32)],
    )(surface, edge_near, predicted, packed, time_t, *[pieces[key] for key in sends], bands(edge_far), *(() if paired else columns(cols)))

    sums = shape((sum_rows, LANES))
    add = call(add_kernel, sums)

    def over_bands(total, last):
        step = 1
        while 2 * step < n_lat:
            total = add(total, across(total, "lat", step))
            step *= 2
        return last(total, across(total, "lat", step))

    def over_lon(total):
        if paired:
            return [total] + [across(total, "lon", step) for step in (1, 2, 3)]
        step = 1
        while step < n_lon:
            total = add(total, across(total, "lon", step))
            step *= 2
        return [total]

    total, edge_near, edge_far = call(
        functools.partial(core_kernel, rank), [sums, shape((rank, LANES)), shape((rank, LANES))]
    )(message, across(outgoing, "ta", 1), edge_far)
    edge_far = bands(edge_far)
    if paired:
        last = call(band_kernel, shape((sum_rows + COLS, LANES)), after=1)
        parts = over_lon(over_bands(total, lambda mine, theirs: last(mine, theirs, message, edge_far)))
        cols_a, cols_b = parts[1], parts[3]
    else:
        parts = over_lon(over_bands(total, add))
        cols_a, cols_b = columns(message[sum_rows:])

    def second(*refs):
        second_kernel(half, counts, len(parts), swap, *refs)

    surface, time_t, message, outgoing = call(
        second,
        [fresh, shape((rank, LANES)), sums, sums],
        [flip, pltpu.VMEM((rank, wide), F32), pltpu.VMEM((rank, wide), F32), pltpu.VMEM((2 * days, wide), F32), pltpu.VMEM((rank, wide), BF16)],
    )(surface, time_t, summed, seen, edge_near, edge_far, *parts, cols_a, cols_b)

    total = add(message, across(outgoing, "ta", 1))
    other = across(surface, "ta", 1)
    narrow = call(functools.partial(narrow_kernel, rank), shape((sum_rows + NORM, LANES), BF16))
    parts = over_lon(over_bands(total, narrow if paired else add))
    space, time = call(
        functools.partial(last_kernel, half, counts, len(parts)),
        [shape((rank * height, cells)), shape(factor_time.shape)],
        [flip],
    )(surface, other, time_t, *parts)
    return space.reshape(rank, height, cells), time


def solution(mesh):
    in_specs = (
        P(("grp", "lon", "lat"), "ta", None),
        P(("grp", "lon", "lat"), "ta"),
        P(("grp", "lon", "lat")),
        P(("grp", "lon", "lat"), None, None),
        P(("grp", "lon", "lat"), None),
        P(None, ("grp", "lat"), "lon"),
        P(("grp", "ta"), None),
    )
    out_specs = (P(None, ("grp", "lat"), "lon"), P(("grp", "ta"), None))
    return jax.shard_map(shards, mesh=mesh, in_specs=in_specs, out_specs=out_specs, check_vma=False)
```

```python
import functools
import math

import jax
import jax.numpy as jnp
from jax import lax
from jax.experimental import pallas as pl
from jax.experimental.pallas import tpu as pltpu
from jax.sharding import PartitionSpec as P

SMOOTH = 2.0
ETA_SPACE = 0.08
RIDGE = 1.0
EPSILON = 1e-06

F32 = jnp.float32
BF16 = jnp.bfloat16
LANES = 128
TAIL = 16
COLS = 16
NORM = 8
SPARE = 2 * 1024 * 1024
SWATH_COPIES = 4


def dot(a, b, contract):
    return lax.dot_general(a, b, ((contract[:1], contract[1:]), ((), ())), preferred_element_type=F32)


def route_kernel(half, sends, paired, list_hbm, count_hbm, target_hbm, swath_hbm, mask_hbm, space_hbm, time_hbm, *rest):
    outs, rest = rest[: len(sends)], rest[len(sends):]
    surface, edge_near, edge_far, cols, rest = *rest[:4], rest[4:]
    list_ref, count_ref, target_ref, swath_ref, mask_ref, space_ref, time_ref, place, total, seen, flip, arrived = rest
    me, core = lax.axis_index("lon"), lax.axis_index("ta")
    n_lon = list_ref.shape[1]
    slots, days, cells = swath_ref.shape
    chunk = slots // SWATH_COPIES
    small = [(list_hbm, list_ref), (count_hbm, count_ref), (target_hbm, target_ref), (mask_hbm, mask_ref)]
    large = [(swath_hbm.at[pl.ds(at, chunk)], swath_ref.at[pl.ds(at, chunk)]) for at in range(0, slots, chunk)]
    model = [(space_hbm, space_ref), (time_hbm, time_ref)]
    copies = [pltpu.make_async_copy(src, dst, arrived.at[i]) for i, (src, dst) in enumerate(small + large + model)]
    for copy in copies:
        copy.start()
    total[...] = jnp.zeros(total.shape, F32)
    seen[...] = jnp.zeros(seen.shape, F32)
    for copy in copies[: len(small)]:
        copy.wait()

    def owner(d, carry):
        step = jnp.bitwise_xor(d, me)

        def entry(k, carry):
            slot = list_ref[0, d, k]
            row = target_ref[slot]
            far = jnp.bitwise_xor(lax.div(row, half), core)
            place[slot] = (far * n_lon + step) * half + lax.rem(row, half)
            return carry

        return lax.fori_loop(0, count_ref[0, d], entry, carry)

    lax.fori_loop(0, n_lon, owner, 0)
    mask = mask_ref[...].astype(F32)
    by_day = mask.T
    for slot in range(slots):
        if slot % chunk == 0:
            copies[len(small) + slot // chunk].wait()
        at = place[slot]
        total[at] += swath_ref[slot].astype(F32) * by_day[:, slot:slot + 1]
        seen[pl.ds(at, 1), :days] += mask[slot:slot + 1, :]
    for copy in copies[len(small) + len(large):]:
        copy.wait()
    rank = surface.shape[0]
    height = space_ref.shape[0] // rank
    for row in range(half):
        surface[:, row * LANES:(row + 1) * LANES] = space_ref[pl.ds(core * half + row, rank, stride=height), :]
    edge_near[...] = space_ref[pl.ds(half - core, rank, stride=height), :]
    edge_far[...] = space_ref[pl.ds(core * (height - 1), rank, stride=height), :]
    cols[...] = columns_as_rows(border(surface[...], half), flip)[:COLS, :]
    for (side, step), out in zip(sends, outs):
        at = (side * n_lon + step) * half
        end = half * days + TAIL
        out[: half * days, :] = total[at:at + half].reshape(half * days, cells).astype(BF16)
        out[half * days:end, :] = seen[at:at + TAIL, :].astype(BF16)
        if (side, step) == (1, 0):
            left = time_ref[...]
            for part in range(end, end + 3 * days, days):
                value = left.astype(BF16)
                out[part:part + days, :] = jnp.zeros((days, LANES), BF16)
                out[part:part + days, :rank] = value
                left = left - value.astype(F32)
        elif paired and side == 0 and step in (1, 3):
            out[end:, :] = cols[...].astype(BF16)


def row_of(surface, row):
    return surface[:, row * LANES:(row + 1) * LANES]


def columns_as_rows(columns, flip):
    rank = columns[0].shape[0]
    lane = lax.broadcasted_iota(jnp.int32, (rank, LANES), 1)
    block = jnp.zeros((rank, LANES), F32)
    for at, column in enumerate(columns):
        block = jnp.where(lane == at, column, block)
    flip[...] = jnp.zeros(flip.shape, F32)
    flip[:rank, :] = block
    return flip[...].T


def border(surface, half):
    strips = [row_of(surface, row) for row in range(half)]
    return [strip[:, :1] for strip in strips] + [strip[:, LANES - 1:] for strip in strips]


def rows_as_columns(rows, rank, flip):
    flip[...] = jnp.zeros(flip.shape, F32)
    flip[: rows.shape[0], :] = rows
    return flip[...].T[:rank, :]


def smoothed(surface, half, above, below, left_cols, right_cols):
    lane = lax.broadcasted_iota(jnp.int32, above.shape, 1)
    strips = []
    for row in range(half):
        here = row_of(surface, row)
        up = above if row == 0 else row_of(surface, row - 1)
        down = below if row == half - 1 else row_of(surface, row + 1)
        left = jnp.where(lane == 0, left_cols[:, half + row:half + row + 1], pltpu.roll(here, 1, 1))
        right = jnp.where(lane == LANES - 1, right_cols[:, row:row + 1], pltpu.roll(here, LANES - 1, 1))
        lap = 4.0 * here - (up + down + left + right)
        strips.append(here - (ETA_SPACE * SMOOTH) * lap)
    return strips


def pick(flag, a, b):
    return jnp.where(flag, a, b)


def model_kernel(half, surface, time_own, piece, predicted, packed, time_t, days_all):
    rank = surface.shape[0]
    days = time_own.shape[0]
    at = half * days + TAIL
    high, middle, low = (piece[first:first + days, :].astype(F32) for first in range(at, at + 3 * days, days))
    days_all[...] = jnp.zeros(days_all.shape, F32)
    days_all[:days, :rank] = time_own[...]
    days_all[days:, :] = (high + middle) + low
    time_full = days_all[...]
    time_t[...] = time_full.T[:rank, :]
    packed[...] = surface[...].astype(BF16)
    time_bf = time_full[:, :rank].astype(BF16)
    for at in range(0, half * LANES, 2 * LANES):
        predicted[:, at:at + 2 * LANES] = dot(time_bf, packed[:, at:at + 2 * LANES], (1, 0))


def smooth(half, odd, surface, edge_near, edge_far, cols_a, cols_b, scale, base, flip):
    core = lax.axis_index("ta")
    rank = surface.shape[0]
    above = pick(core == 0, edge_far, edge_near)
    below = pick(core == 0, edge_near, edge_far)
    left = rows_as_columns(pick(odd, cols_a, cols_b), rank, flip)
    right = rows_as_columns(pick(odd, cols_b, cols_a), rank, flip)
    if scale is not None:
        above, below, left, right = above * scale, below * scale, left * scale, right * scale
    for row, strip in enumerate(smoothed(surface, half, above, below, left, right)):
        base[:, row * LANES:(row + 1) * LANES] = strip


def gradients(half, base, predicted, packed, time_t, seen, summed, fresh):
    rank = time_t.shape[0]
    time_bf = time_t.astype(BF16)
    time_twice = jnp.concatenate([time_bf, time_bf], axis=1)
    seen_bf = seen.astype(BF16)
    width = 2 * LANES
    owner = lax.broadcasted_iota(jnp.int32, (TAIL, width), 0)
    lane = lax.broadcasted_iota(jnp.int32, (TAIL, width), 1)
    grad_time = jnp.zeros((rank, width), F32)
    grad_diag = jnp.zeros((rank, LANES), F32)
    norm = jnp.zeros((rank, 1), F32)
    for at in range(0, half * LANES, width):
        spread = (owner * LANES <= lane + at) & (lane + at < (owner + 1) * LANES)
        weight = dot(seen_bf, spread.astype(BF16), (0, 0))
        part = packed[:, at:at + width]
        residual = weight * predicted[:, at:at + width] - summed[:, at:at + width]
        high = residual.astype(BF16)
        low = (residual - high.astype(F32)).astype(BF16)
        both = jnp.concatenate([high, low], axis=0)
        grad_space = dot(time_twice, both, (1, 0))
        grad_time = grad_time + dot(part, both, (1, 1))
        new = base[:, at:at + width] - ETA_SPACE * grad_space
        fresh[:, at:at + width] = new
        norm = norm + jnp.sum(new * new, axis=1, keepdims=True)
        wide = part.astype(F32)
        for row in range(width // LANES):
            strip = row_of(wide, row)
            square = jnp.sum(strip * strip, axis=1, keepdims=True)
            grad_diag = grad_diag + square * seen[at // LANES + row:at // LANES + row + 1, :]
    return grad_time[:, :LANES] + grad_time[:, LANES:], grad_diag, norm


def post(half, sums, fresh, message, outgoing, edge_far, flip):
    grad_time, grad_diag, norm = sums
    core = lax.axis_index("ta")
    rank = norm.shape[0]
    columns = [norm] if edge_far is None else [norm] + [norm] * (NORM - 1) + border(fresh[...], half)
    last = columns_as_rows(columns, flip)[: message.shape[0] - 2 * rank, :]
    message[:rank, :] = grad_time
    message[rank:2 * rank, :] = grad_diag
    message[2 * rank:, :] = last
    outgoing[:rank, :] = pltpu.roll(grad_time, LANES // 2, 1)
    outgoing[rank:2 * rank, :] = pltpu.roll(grad_diag, LANES // 2, 1)
    outgoing[2 * rank:2 * rank + NORM, :] = last[:NORM, :]
    if edge_far is not None:
        first_row, last_row = fresh[:, :LANES], fresh[:, (half - 1) * LANES:]
        outgoing[2 * rank + NORM:, :] = pick(core == 0, last_row, first_row)
        edge_far[...] = pick(core == 0, first_row, last_row)


def first_kernel(half, days, order, paired, swap, surface, edge_near, predicted, packed, time_t, *rest):
    pieces, rest = dict(zip(order, rest)), rest[len(order):]
    edge_far_in, rest = rest[0], rest[1:]
    if paired:
        at = half * days + TAIL
        cols = [pieces[0, step][at:, :].astype(F32) for step in (1, 3)]
    else:
        cols, rest = [ref[...] for ref in rest[:2]], rest[2:]
    fresh, message, outgoing, edge_far, summed, seen, flip, base = rest
    smooth(half, swap(), surface[...], edge_near[...], edge_far_in[...], *cols, None, base, flip)
    sides = [[pieces[key] for key in sorted(pieces) if key[0] == side] for side in (0, 1)]

    def add_up(parts, rows):
        value = parts[0][rows, :].astype(F32)
        for piece in parts[1:]:
            value = value + piece[rows, :].astype(F32)
        return value

    for row in range(half):
        for first, parts in zip((0, days), sides):
            summed[first:first + days, row * LANES:(row + 1) * LANES] = add_up(parts, slice(row * days, (row + 1) * days))
    near, far = (add_up(parts, slice(half * days, half * days + TAIL)) for parts in sides)
    seen[...] = near + pltpu.roll(far, days, 1)
    sums = gradients(half, base, predicted, packed, time_t[...], seen[...], summed, fresh)
    post(half, sums, fresh, message, outgoing, edge_far, flip)


def settle(rank, counts, parts, time_t, flip):
    day_count, cell_count = counts
    total = parts[0][...].astype(F32)
    if len(parts) > 1:
        one, two, three = (part[...].astype(F32) for part in parts[1:])
        total = (total + one) + (two + three)
    time_new = time_t - total[:rank, :] / (total[rank:2 * rank, :] + RIDGE)
    norm = total[2 * rank:2 * rank + NORM, :]
    if parts[0].dtype == BF16:
        norm = norm + total[2 * rank + NORM:2 * rank + 2 * NORM, :]
    space_sq = rows_as_columns(norm, rank, flip)[:, :1]
    square = time_new * time_new
    time_sq = 0.5 * jnp.sum(square + pltpu.roll(square, LANES // 2, 1), axis=1, keepdims=True)
    ratio = (time_sq / day_count + EPSILON) / (space_sq / cell_count + EPSILON)
    return time_new, jnp.sqrt(jnp.sqrt(ratio))


def second_kernel(half, counts, n_parts, swap, surface, time_t, summed, seen, edge_near, edge_far, *rest):
    parts, (cols_a, cols_b) = rest[:n_parts], rest[n_parts:n_parts + 2]
    fresh, time_out, message, outgoing, flip, scaled, base, predicted, packed = rest[n_parts + 2:]
    rank = surface.shape[0]
    time_new, scale = settle(rank, counts, parts, time_t[...], flip)
    time_now = time_new / scale
    time_out[...] = time_now
    scaled[...] = surface[...] * scale
    packed[...] = scaled[...].astype(BF16)
    time_bf = time_now.T.astype(BF16)
    for at in range(0, half * LANES, 2 * LANES):
        predicted[:, at:at + 2 * LANES] = dot(time_bf, packed[:, at:at + 2 * LANES], (1, 0))
    cols = [ref[ref.shape[0] - COLS:, :] for ref in (cols_a, cols_b)]
    smooth(half, swap(), scaled[...], edge_near[...], edge_far[...], *cols, scale, base, flip)
    sums = gradients(half, base, predicted, packed, time_now, seen[...], summed, fresh)
    post(half, sums, fresh, message, outgoing, None, flip)


def last_kernel(half, counts, n_parts, surface, other, time_t, *rest):
    parts = rest[:n_parts]
    space_out, time_out, flip = rest[n_parts:]
    core = lax.axis_index("ta")
    rank = surface.shape[0]
    height = space_out.shape[0] // rank
    time_new, scale = settle(rank, counts, parts, time_t[...], flip)
    flip[...] = jnp.zeros(flip.shape, F32)
    flip[:rank, :] = time_new / scale
    time_out[...] = flip[...].T[: time_out.shape[0], :rank]
    for row in range(half):
        at = row * LANES
        space_out[pl.ds(core * half + row, rank, stride=height), :] = surface[:, at:at + LANES] * scale
        space_out[pl.ds((1 - core) * half + row, rank, stride=height), :] = other[:, at:at + LANES] * scale


def core_kernel(rank, mine, theirs, edge_in, total, beside, edge_out):
    rows = total.shape[0]
    total[...] = mine[:rows, :] + theirs[:rows, :]
    beside[...] = theirs[rows:, :]
    edge_out[...] = edge_in[...]


def merge_kernel(mine, theirs, out):
    out[...] = (mine[...].astype(F32) + theirs[...].astype(F32)).astype(BF16)


def add_kernel(mine, theirs, total):
    rows = total.shape[0]
    total[...] = mine[:rows, :] + theirs[:rows, :]


def band_kernel(mine, theirs, message, after, total):
    rows = mine.shape[0]
    total[:rows, :] = mine[...] + theirs[...]
    total[rows:, :] = message[rows:, :]


def narrow_kernel(rank, mine, theirs, total):
    value = mine[...] + theirs[...]
    total[: 2 * rank, :] = value[: 2 * rank, :].astype(BF16)
    norm = value[2 * rank:, :]
    high = norm.astype(BF16).astype(F32)
    total[2 * rank:, :] = jnp.concatenate([high, norm - high], axis=0).astype(BF16)


def shape(dims, dtype=F32):
    return jax.ShapeDtypeStruct(tuple(dims), dtype)


def padded(ref):
    *outer, rows, lanes = (1, *ref.shape)
    return math.prod(outer) * -(-rows // 16) * 16 * -(-lanes // LANES) * LANES * jnp.dtype(ref.dtype).itemsize


def call(kernel, out_shape, scratch=(), hbm=0, after=0, flops=1_000_000):
    def run(*operands):
        operands = [pltpu.with_memory_space_constraint(x, pltpu.HBM) if i < hbm else x for i, x in enumerate(operands)]
        vmem = [*operands[hbm:len(operands) - after], *jax.tree.leaves(out_shape), *scratch]
        specs = [pltpu.HBM] * hbm + [pltpu.VMEM] * (len(operands) - hbm - after) + [pl.ANY] * after
        return pl.pallas_call(
            kernel,
            out_shape=out_shape,
            in_specs=[pl.BlockSpec(memory_space=space) for space in specs],
            out_specs=jax.tree.map(lambda _: pl.BlockSpec(memory_space=pltpu.VMEM), out_shape),
            scratch_shapes=list(scratch),
            compiler_params=pltpu.CompilerParams(vmem_limit_bytes=SPARE + sum(padded(ref) for ref in vmem if len(ref.shape) > 1)),
            cost_estimate=pl.CostEstimate(flops=flops, bytes_accessed=1_000_000, transcendentals=0),
        )(*operands)

    return run


def across(value, axis, step):
    return lax.ppermute(value, axis, [(i, i ^ step) for i in range(lax.axis_size(axis))])


def shards(swath, obs_mask, target, send_list, send_count, factor_space, factor_time):
    n_lon, n_lat, n_ta = (lax.axis_size(axis) for axis in ("lon", "lat", "ta"))
    slots, days, cells = swath.shape
    rank, height, _ = factor_space.shape
    half = height // n_ta
    wide = half * LANES
    counts = (float(days * n_ta), float(height * cells * n_lon * n_lat))
    sum_rows = 2 * rank + NORM
    flip = pltpu.VMEM((LANES, LANES), F32)

    paired = n_lon == 4

    distant, close = range(n_lon // 2, n_lon), range(1, n_lon // 2)
    sends = [(1, step) for step in reversed(distant)] + [(0, step) for step in distant] + [(1, 0)]
    sends += [(side, step) for side in (0, 1) for step in close] + [(0, 0)]

    def piece_rows(side, step):
        more = 3 * days if (side, step) == (1, 0) else COLS if paired and side == 0 and step in (1, 3) else 0
        return half * days + TAIL + more

    operands = (send_list, send_count, target, swath, obs_mask, factor_space.reshape(rank * height, cells), factor_time)
    *pieces, surface, edge_near, edge_far, cols = call(
        functools.partial(route_kernel, half, sends, paired),
        [shape((piece_rows(*key), cells), BF16) for key in sends]
        + [shape((rank, wide)), shape((rank, LANES)), shape((rank, LANES)), shape((COLS, LANES))],
        [pltpu.SMEM(ref.shape, jnp.int32) for ref in operands[:3]]
        + [pltpu.VMEM(ref.shape, ref.dtype) for ref in operands[3:]]
        + [
            pltpu.SMEM((slots,), jnp.int32),
            pltpu.VMEM((2 * n_lon * half, days, cells), F32),
            pltpu.VMEM((2 * n_lon * half + TAIL, LANES), F32),
            flip,
            pltpu.SemaphoreType.DMA((len(operands) - 1 + SWATH_COPIES,)),
        ],
        hbm=len(operands),
    )(*operands)

    def arrived(key, piece):
        side, step = key
        if side:
            return across(piece, ("lon", "ta"), 2 * step + 1)
        return across(piece, "lon", step) if step else piece

    pieces = dict(zip(sends, pieces))
    if paired:
        passing = across(pieces.pop((1, 3)), "lon", 1)
        pieces[1, 2] = call(merge_kernel, shape(passing.shape, BF16))(pieces[1, 2], passing)
    pieces = {key: arrived(key, piece) for key, piece in pieces.items()}
    order = list(pieces)

    def bands(edge):
        there = [(2 * band + 1, 2 * band + 2) for band in range(n_lat - 1)]
        return lax.ppermute(edge, ("lat", "ta"), there + [(b, a) for a, b in there])

    def swap():
        return lax.rem(lax.axis_index("lon"), 2) == 1 if paired else jnp.bool_(True)

    def columns(value):
        if paired:
            return across(value, "lon", 1), across(value, "lon", 3)
        ring = [(i, (i + 1) % n_lon) for i in range(n_lon)]
        return lax.ppermute(value, "lon", ring), lax.ppermute(value, "lon", [(b, a) for a, b in ring])

    predicted, packed, time_t = call(
        functools.partial(model_kernel, half),
        [shape((2 * days, wide)), shape((rank, wide), BF16), shape((rank, LANES))],
        [flip],
    )(surface, factor_time, pieces[1, 0])

    fresh = shape((rank, wide))
    surface, message, outgoing, edge_far, summed, seen = call(
        functools.partial(first_kernel, half, days, order, paired, swap),
        [fresh, shape((sum_rows + COLS, LANES)), shape((sum_rows + rank, LANES)), shape((rank, LANES)), shape((2 * days, wide)), shape((TAIL, LANES))],
        [flip, pltpu.VMEM((rank, wide), F32)],
    )(surface, edge_near, predicted, packed, time_t, *[pieces[key] for key in order], bands(edge_far), *(() if paired else columns(cols)))

    sums = shape((sum_rows, LANES))
    add = call(add_kernel, sums)

    def over_bands(total, last):
        step = 1
        while 2 * step < n_lat:
            total = add(total, across(total, "lat", step))
            step *= 2
        return last(total, across(total, "lat", step))

    def over_lon(total):
        if paired:
            return [total] + [across(total, "lon", step) for step in (1, 2, 3)]
        step = 1
        while step < n_lon:
            total = add(total, across(total, "lon", step))
            step *= 2
        return [total]

    total, edge_near, edge_far = call(
        functools.partial(core_kernel, rank), [sums, shape((rank, LANES)), shape((rank, LANES))]
    )(message, across(outgoing, "ta", 1), edge_far)
    edge_far = bands(edge_far)
    if paired:
        last = call(band_kernel, shape((sum_rows + COLS, LANES)), after=1)
        parts = over_lon(over_bands(total, lambda mine, theirs: last(mine, theirs, message, edge_far)))
        cols_a, cols_b = parts[1], parts[3]
    else:
        parts = over_lon(over_bands(total, add))
        cols_a, cols_b = columns(message[sum_rows:])

    def second(*refs):
        second_kernel(half, counts, len(parts), swap, *refs)

    surface, time_t, message, outgoing = call(
        second,
        [fresh, shape((rank, LANES)), sums, sums],
        [flip, pltpu.VMEM((rank, wide), F32), pltpu.VMEM((rank, wide), F32), pltpu.VMEM((2 * days, wide), F32), pltpu.VMEM((rank, wide), BF16)],
    )(surface, time_t, summed, seen, edge_near, edge_far, *parts, cols_a, cols_b)

    total = add(message, across(outgoing, "ta", 1))
    other = across(surface, "ta", 1)
    narrow = call(functools.partial(narrow_kernel, rank), shape((sum_rows + NORM, LANES), BF16))
    parts = over_lon(over_bands(total, narrow if paired else add))
    space, time = call(
        functools.partial(last_kernel, half, counts, len(parts)),
        [shape((rank * height, cells)), shape(factor_time.shape)],
        [flip],
    )(surface, other, time_t, *parts)
    return space.reshape(rank, height, cells), time


def solution(mesh):
    in_specs = (
        P(("grp", "lon", "lat"), "ta", None),
        P(("grp", "lon", "lat"), "ta"),
        P(("grp", "lon", "lat")),
        P(("grp", "lon", "lat"), None, None),
        P(("grp", "lon", "lat"), None),
        P(None, ("grp", "lat"), "lon"),
        P(("grp", "ta"), None),
    )
    out_specs = (P(None, ("grp", "lat"), "lon"), P(("grp", "ta"), None))
    return jax.shard_map(shards, mesh=mesh, in_specs=in_specs, out_specs=out_specs, check_vma=False)
```

```python
import functools
import math

import jax
import jax.numpy as jnp
from jax import lax
from jax.experimental import pallas as pl
from jax.experimental.pallas import tpu as pltpu
from jax.sharding import PartitionSpec as P

SMOOTH = 2.0
ETA_SPACE = 0.08
RIDGE = 1.0
EPSILON = 1e-06

F32 = jnp.float32
BF16 = jnp.bfloat16
LANES = 128
TAIL = 16
COLS = 16
NORM = 8
SPARE = 2 * 1024 * 1024
SWATH_COPIES = 4


def dot(a, b, contract):
    return lax.dot_general(a, b, ((contract[:1], contract[1:]), ((), ())), preferred_element_type=F32)


def route_kernel(half, sends, paired, list_hbm, count_hbm, target_hbm, swath_hbm, mask_hbm, space_hbm, time_hbm, *rest):
    outs, rest = rest[: len(sends)], rest[len(sends):]
    surface, edge_near, edge_far, cols, rest = *rest[:4], rest[4:]
    list_ref, count_ref, target_ref, swath_ref, mask_ref, space_ref, time_ref, place, total, seen, flip, arrived = rest
    me, core = lax.axis_index("lon"), lax.axis_index("ta")
    n_lon = list_ref.shape[1]
    slots, days, cells = swath_ref.shape
    chunk = slots // SWATH_COPIES
    small = [(list_hbm, list_ref), (count_hbm, count_ref), (target_hbm, target_ref), (mask_hbm, mask_ref)]
    large = [(swath_hbm.at[pl.ds(at, chunk)], swath_ref.at[pl.ds(at, chunk)]) for at in range(0, slots, chunk)]
    model = [(space_hbm, space_ref), (time_hbm, time_ref)]
    copies = [pltpu.make_async_copy(src, dst, arrived.at[i]) for i, (src, dst) in enumerate(small + large + model)]
    for copy in copies:
        copy.start()
    total[...] = jnp.zeros(total.shape, F32)
    seen[...] = jnp.zeros(seen.shape, F32)
    for copy in copies[: len(small)]:
        copy.wait()

    def owner(d, carry):
        step = jnp.bitwise_xor(d, me)

        def entry(k, carry):
            slot = list_ref[0, d, k]
            row = target_ref[slot]
            far = jnp.bitwise_xor(lax.div(row, half), core)
            place[slot] = (far * n_lon + step) * half + lax.rem(row, half)
            return carry

        return lax.fori_loop(0, count_ref[0, d], entry, carry)

    lax.fori_loop(0, n_lon, owner, 0)
    mask = mask_ref[...].astype(F32)
    by_day = mask.T
    for slot in range(slots):
        if slot % chunk == 0:
            copies[len(small) + slot // chunk].wait()
        at = place[slot]
        total[at] += swath_ref[slot].astype(F32) * by_day[:, slot:slot + 1]
        seen[pl.ds(at, 1), :days] += mask[slot:slot + 1, :]
    for copy in copies[len(small) + len(large):]:
        copy.wait()
    rank = surface.shape[0]
    height = space_ref.shape[0] // rank
    for row in range(half):
        surface[:, row * LANES:(row + 1) * LANES] = space_ref[pl.ds(core * half + row, rank, stride=height), :]
    edge_near[...] = space_ref[pl.ds(half - core, rank, stride=height), :]
    edge_far[...] = space_ref[pl.ds(core * (height - 1), rank, stride=height), :]
    cols[...] = columns_as_rows(border(surface[...], half), flip)[:COLS, :]
    for (side, step), out in zip(sends, outs):
        at = (side * n_lon + step) * half
        end = half * days + TAIL
        out[: half * days, :] = total[at:at + half].reshape(half * days, cells).astype(BF16)
        out[half * days:end, :] = seen[at:at + TAIL, :].astype(BF16)
        if (side, step) == (1, 0):
            left = time_ref[...]
            for part in range(end, end + 3 * days, days):
                value = left.astype(BF16)
                out[part:part + days, :] = jnp.zeros((days, LANES), BF16)
                out[part:part + days, :rank] = value
                left = left - value.astype(F32)
        elif paired and side == 0 and step in (1, 3):
            out[end:, :] = cols[...].astype(BF16)


def row_of(surface, row):
    return surface[:, row * LANES:(row + 1) * LANES]


def columns_as_rows(columns, flip):
    rank = columns[0].shape[0]
    lane = lax.broadcasted_iota(jnp.int32, (rank, LANES), 1)
    block = jnp.zeros((rank, LANES), F32)
    for at, column in enumerate(columns):
        block = jnp.where(lane == at, column, block)
    flip[...] = jnp.zeros(flip.shape, F32)
    flip[:rank, :] = block
    return flip[...].T


def border(surface, half):
    strips = [row_of(surface, row) for row in range(half)]
    return [strip[:, :1] for strip in strips] + [strip[:, LANES - 1:] for strip in strips]


def rows_as_columns(rows, rank, flip):
    flip[...] = jnp.zeros(flip.shape, F32)
    flip[: rows.shape[0], :] = rows
    return flip[...].T[:rank, :]


def smoothed(surface, half, above, below, left_cols, right_cols):
    lane = lax.broadcasted_iota(jnp.int32, above.shape, 1)
    strips = []
    for row in range(half):
        here = row_of(surface, row)
        up = above if row == 0 else row_of(surface, row - 1)
        down = below if row == half - 1 else row_of(surface, row + 1)
        left = jnp.where(lane == 0, left_cols[:, half + row:half + row + 1], pltpu.roll(here, 1, 1))
        right = jnp.where(lane == LANES - 1, right_cols[:, row:row + 1], pltpu.roll(here, LANES - 1, 1))
        lap = 4.0 * here - (up + down + left + right)
        strips.append(here - (ETA_SPACE * SMOOTH) * lap)
    return strips


def pick(flag, a, b):
    return jnp.where(flag, a, b)


def model_kernel(half, surface, time_own, piece, predicted, packed, time_t, days_all):
    rank = surface.shape[0]
    days = time_own.shape[0]
    at = half * days + TAIL
    high, middle, low = (piece[first:first + days, :].astype(F32) for first in range(at, at + 3 * days, days))
    days_all[...] = jnp.zeros(days_all.shape, F32)
    days_all[:days, :rank] = time_own[...]
    days_all[days:, :] = (high + middle) + low
    time_full = days_all[...]
    time_t[...] = time_full.T[:rank, :]
    packed[...] = surface[...].astype(BF16)
    time_bf = time_full[:, :rank].astype(BF16)
    for at in range(0, half * LANES, 2 * LANES):
        predicted[:, at:at + 2 * LANES] = dot(time_bf, packed[:, at:at + 2 * LANES], (1, 0))


def smooth(half, odd, surface, edge_near, edge_far, cols_a, cols_b, scale, base, flip):
    core = lax.axis_index("ta")
    rank = surface.shape[0]
    above = pick(core == 0, edge_far, edge_near)
    below = pick(core == 0, edge_near, edge_far)
    left = rows_as_columns(pick(odd, cols_a, cols_b), rank, flip)
    right = rows_as_columns(pick(odd, cols_b, cols_a), rank, flip)
    if scale is not None:
        above, below, left, right = above * scale, below * scale, left * scale, right * scale
    for row, strip in enumerate(smoothed(surface, half, above, below, left, right)):
        base[:, row * LANES:(row + 1) * LANES] = strip


def gradients(half, base, predicted, packed, time_t, seen, summed, fresh):
    rank = time_t.shape[0]
    time_bf = time_t.astype(BF16)
    time_twice = jnp.concatenate([time_bf, time_bf], axis=1)
    seen_bf = seen.astype(BF16)
    width = 2 * LANES
    owner = lax.broadcasted_iota(jnp.int32, (TAIL, width), 0)
    lane = lax.broadcasted_iota(jnp.int32, (TAIL, width), 1)
    grad_time = jnp.zeros((rank, width), F32)
    grad_diag = jnp.zeros((rank, LANES), F32)
    norm = jnp.zeros((rank, 1), F32)
    for at in range(0, half * LANES, width):
        spread = (owner * LANES <= lane + at) & (lane + at < (owner + 1) * LANES)
        weight = dot(seen_bf, spread.astype(BF16), (0, 0))
        part = packed[:, at:at + width]
        residual = weight * predicted[:, at:at + width] - summed[:, at:at + width]
        high = residual.astype(BF16)
        low = (residual - high.astype(F32)).astype(BF16)
        both = jnp.concatenate([high, low], axis=0)
        grad_space = dot(time_twice, both, (1, 0))
        grad_time = grad_time + dot(part, both, (1, 1))
        new = base[:, at:at + width] - ETA_SPACE * grad_space
        fresh[:, at:at + width] = new
        norm = norm + jnp.sum(new * new, axis=1, keepdims=True)
        wide = part.astype(F32)
        for row in range(width // LANES):
            strip = row_of(wide, row)
            square = jnp.sum(strip * strip, axis=1, keepdims=True)
            grad_diag = grad_diag + square * seen[at // LANES + row:at // LANES + row + 1, :]
    return grad_time[:, :LANES] + grad_time[:, LANES:], grad_diag, norm


def post_own(half, sums, fresh, message, outgoing, edge_far, flip):
    grad_time, grad_diag, norm = sums
    core = lax.axis_index("ta")
    rank = norm.shape[0]
    days = LANES // 2
    own = lax.broadcasted_iota(jnp.int32, grad_time.shape, 1) < days
    last = columns_as_rows([norm] * NORM + border(fresh[...], half), flip)
    message[:rank, :] = jnp.where(own, grad_time, pltpu.roll(grad_diag, days, 1))
    message[rank:, :] = last[: NORM + COLS, :]
    outgoing[:rank, :] = jnp.where(own, pltpu.roll(grad_time, days, 1), grad_diag)
    outgoing[rank:rank + NORM, :] = last[:NORM, :]
    first_row, last_row = fresh[:, :LANES], fresh[:, (half - 1) * LANES:]
    outgoing[rank + NORM:, :] = pick(core == 0, last_row, first_row)
    edge_far[...] = pick(core == 0, first_row, last_row)


def post_all(sums, message, outgoing, flip):
    grad_time, grad_diag, norm = sums
    rank = norm.shape[0]
    last = columns_as_rows([norm], flip)[:NORM, :]
    message[:rank, :] = grad_time
    message[rank:2 * rank, :] = grad_diag
    message[2 * rank:, :] = last
    outgoing[:rank, :] = pltpu.roll(grad_time, LANES // 2, 1)
    outgoing[rank:2 * rank, :] = pltpu.roll(grad_diag, LANES // 2, 1)
    outgoing[2 * rank:, :] = last


def first_kernel(half, days, order, paired, swap, surface, edge_near, predicted, packed, time_t, *rest):
    pieces, rest = dict(zip(order, rest)), rest[len(order):]
    edge_far_in, rest = rest[0], rest[1:]
    if paired:
        at = half * days + TAIL
        cols = [pieces[0, step][at:, :].astype(F32) for step in (1, 3)]
    else:
        cols, rest = [ref[...] for ref in rest[:2]], rest[2:]
    fresh, message, outgoing, edge_far, summed, seen, flip, base = rest
    smooth(half, swap(), surface[...], edge_near[...], edge_far_in[...], *cols, None, base, flip)
    sides = [[pieces[key] for key in sorted(pieces) if key[0] == side] for side in (0, 1)]

    def add_up(parts, rows):
        value = parts[0][rows, :].astype(F32)
        for piece in parts[1:]:
            value = value + piece[rows, :].astype(F32)
        return value

    for row in range(half):
        for first, parts in zip((0, days), sides):
            summed[first:first + days, row * LANES:(row + 1) * LANES] = add_up(parts, slice(row * days, (row + 1) * days))
    near, far = (add_up(parts, slice(half * days, half * days + TAIL)) for parts in sides)
    seen[...] = near + pltpu.roll(far, days, 1)
    sums = gradients(half, base, predicted, packed, time_t[...], seen[...], summed, fresh)
    post_own(half, sums, fresh, message, outgoing, edge_far, flip)


def total_of(parts):
    total = parts[0][...].astype(F32)
    if len(parts) > 1:
        one, two, three = (part[...].astype(F32) for part in parts[1:])
        total = (total + one) + (two + three)
    return total


def own_kernel(n_parts, time_t, *rest):
    parts, (time_own, norm) = rest[:n_parts], rest[n_parts:]
    rank = time_t.shape[0]
    days = LANES // 2
    total = total_of(parts)
    block = total[:rank, :]
    own = lax.broadcasted_iota(jnp.int32, block.shape, 1) < days
    time_own[...] = jnp.where(own, time_t[...] - block / (pltpu.roll(block, days, 1) + RIDGE), 0.0)
    norm[...] = total[rank:rank + NORM, :]


def rescaling(counts, norm, time_new, flip):
    day_count, cell_count = counts
    space_sq = rows_as_columns(norm, time_new.shape[0], flip)[:, :1]
    square = time_new * time_new
    time_sq = 0.5 * jnp.sum(square + pltpu.roll(square, LANES // 2, 1), axis=1, keepdims=True)
    ratio = (time_sq / day_count + EPSILON) / (space_sq / cell_count + EPSILON)
    return jnp.sqrt(jnp.sqrt(ratio))


def second_kernel(half, counts, swap, surface, time_own, time_other, norm, summed, seen, edge_near, edge_far, cols_a, cols_b, *rest):
    fresh, time_out, message, outgoing, flip, scaled, base, predicted, packed = rest
    rank = surface.shape[0]
    time_new = time_own[...] + pltpu.roll(time_other[...], LANES // 2, 1)
    scale = rescaling(counts, norm[...], time_new, flip)
    time_now = time_new / scale
    time_out[...] = time_now
    scaled[...] = surface[...] * scale
    packed[...] = scaled[...].astype(BF16)
    time_bf = time_now.T.astype(BF16)
    for at in range(0, half * LANES, 2 * LANES):
        predicted[:, at:at + 2 * LANES] = dot(time_bf, packed[:, at:at + 2 * LANES], (1, 0))
    cols = [ref[ref.shape[0] - COLS:, :] for ref in (cols_a, cols_b)]
    smooth(half, swap(), scaled[...], edge_near[...], edge_far[...], *cols, scale, base, flip)
    sums = gradients(half, base, predicted, packed, time_now, seen[...], summed, fresh)
    post_all(sums, message, outgoing, flip)


def last_kernel(half, counts, n_parts, surface, other, time_t, *rest):
    parts = rest[:n_parts]
    space_out, time_out, flip = rest[n_parts:]
    core = lax.axis_index("ta")
    rank = surface.shape[0]
    height = space_out.shape[0] // rank
    total = total_of(parts)
    time_new = time_t[...] - total[:rank, :] / (total[rank:2 * rank, :] + RIDGE)
    norm = total[2 * rank:2 * rank + NORM, :]
    if parts[0].dtype == BF16:
        norm = norm + total[2 * rank + NORM:, :]
    scale = rescaling(counts, norm, time_new, flip)
    flip[...] = jnp.zeros(flip.shape, F32)
    flip[:rank, :] = time_new / scale
    time_out[...] = flip[...].T[: time_out.shape[0], :rank]
    for row in range(half):
        at = row * LANES
        space_out[pl.ds(core * half + row, rank, stride=height), :] = surface[:, at:at + LANES] * scale
        space_out[pl.ds((1 - core) * half + row, rank, stride=height), :] = other[:, at:at + LANES] * scale


def core_kernel(mine, theirs, total, beside):
    rows = total.shape[0]
    total[...] = mine[:rows, :] + theirs[:rows, :]
    beside[...] = theirs[rows:, :]


def merge_kernel(mine, theirs, out):
    out[...] = (mine[...].astype(F32) + theirs[...].astype(F32)).astype(BF16)


def add_kernel(mine, theirs, total):
    rows = total.shape[0]
    total[...] = mine[:rows, :] + theirs[:rows, :]


def band_kernel(mine, theirs, message, total):
    rows = mine.shape[0]
    total[:rows, :] = mine[...] + theirs[...]
    total[rows:, :] = message[rows:, :]


def narrow_kernel(rank, mine, theirs, total):
    value = mine[...] + theirs[...]
    total[: 2 * rank, :] = value[: 2 * rank, :].astype(BF16)
    norm = value[2 * rank:, :]
    high = norm.astype(BF16).astype(F32)
    total[2 * rank:, :] = jnp.concatenate([high, norm - high], axis=0).astype(BF16)


def shape(dims, dtype=F32):
    return jax.ShapeDtypeStruct(tuple(dims), dtype)


def padded(ref):
    *outer, rows, lanes = (1, *ref.shape)
    return math.prod(outer) * -(-rows // 16) * 16 * -(-lanes // LANES) * LANES * jnp.dtype(ref.dtype).itemsize


def call(kernel, out_shape, scratch=(), hbm=0, after=0, flops=1_000_000):
    def run(*operands):
        operands = [pltpu.with_memory_space_constraint(x, pltpu.HBM) if i < hbm else x for i, x in enumerate(operands)]
        vmem = [*operands[hbm:len(operands) - after], *jax.tree.leaves(out_shape), *scratch]
        specs = [pltpu.HBM] * hbm + [pltpu.VMEM] * (len(operands) - hbm - after) + [pl.ANY] * after
        return pl.pallas_call(
            kernel,
            out_shape=out_shape,
            in_specs=[pl.BlockSpec(memory_space=space) for space in specs],
            out_specs=jax.tree.map(lambda _: pl.BlockSpec(memory_space=pltpu.VMEM), out_shape),
            scratch_shapes=list(scratch),
            compiler_params=pltpu.CompilerParams(vmem_limit_bytes=SPARE + sum(padded(ref) for ref in vmem if len(ref.shape) > 1)),
            cost_estimate=pl.CostEstimate(flops=flops, bytes_accessed=1_000_000, transcendentals=0),
        )(*operands)

    return run


def across(value, axis, step):
    return lax.ppermute(value, axis, [(i, i ^ step) for i in range(lax.axis_size(axis))])


def shards(swath, obs_mask, target, send_list, send_count, factor_space, factor_time):
    n_lon, n_lat, n_ta = (lax.axis_size(axis) for axis in ("lon", "lat", "ta"))
    slots, days, cells = swath.shape
    rank, height, _ = factor_space.shape
    half = height // n_ta
    wide = half * LANES
    counts = (float(days * n_ta), float(height * cells * n_lon * n_lat))
    own_rows, sum_rows = rank + NORM, 2 * rank + NORM
    flip = pltpu.VMEM((LANES, LANES), F32)

    paired = n_lon == 4

    distant, close = range(n_lon // 2, n_lon), range(1, n_lon // 2)
    sends = [(1, step) for step in reversed(distant)] + [(0, step) for step in distant] + [(1, 0)]
    sends += [(side, step) for side in (0, 1) for step in close] + [(0, 0)]

    def piece_rows(side, step):
        more = 3 * days if (side, step) == (1, 0) else COLS if paired and side == 0 and step in (1, 3) else 0
        return half * days + TAIL + more

    operands = (send_list, send_count, target, swath, obs_mask, factor_space.reshape(rank * height, cells), factor_time)
    *pieces, surface, edge_near, edge_far, cols = call(
        functools.partial(route_kernel, half, sends, paired),
        [shape((piece_rows(*key), cells), BF16) for key in sends]
        + [shape((rank, wide)), shape((rank, LANES)), shape((rank, LANES)), shape((COLS, LANES))],
        [pltpu.SMEM(ref.shape, jnp.int32) for ref in operands[:3]]
        + [pltpu.VMEM(ref.shape, ref.dtype) for ref in operands[3:]]
        + [
            pltpu.SMEM((slots,), jnp.int32),
            pltpu.VMEM((2 * n_lon * half, days, cells), F32),
            pltpu.VMEM((2 * n_lon * half + TAIL, LANES), F32),
            flip,
            pltpu.SemaphoreType.DMA((len(operands) - 1 + SWATH_COPIES,)),
        ],
        hbm=len(operands),
    )(*operands)

    def arrived(key, piece):
        side, step = key
        if side:
            return across(piece, ("lon", "ta"), 2 * step + 1)
        return across(piece, "lon", step) if step else piece

    pieces = dict(zip(sends, pieces))
    if paired:
        passing = across(pieces.pop((1, 3)), "lon", 1)
        pieces[1, 2] = call(merge_kernel, shape(passing.shape, BF16))(pieces[1, 2], passing)
    pieces = {key: arrived(key, piece) for key, piece in pieces.items()}
    order = list(pieces)

    def bands(edge):
        there = [(2 * band + 1, 2 * band + 2) for band in range(n_lat - 1)]
        return lax.ppermute(edge, ("lat", "ta"), there + [(b, a) for a, b in there])

    def swap():
        return lax.rem(lax.axis_index("lon"), 2) == 1 if paired else jnp.bool_(True)

    def columns(value):
        if paired:
            return across(value, "lon", 1), across(value, "lon", 3)
        ring = [(i, (i + 1) % n_lon) for i in range(n_lon)]
        return lax.ppermute(value, "lon", ring), lax.ppermute(value, "lon", [(b, a) for a, b in ring])

    predicted, packed, time_t = call(
        functools.partial(model_kernel, half),
        [shape((2 * days, wide)), shape((rank, wide), BF16), shape((rank, LANES))],
        [flip],
    )(surface, factor_time, pieces[1, 0])

    fresh, edge = shape((rank, wide)), shape((rank, LANES))
    surface, message, outgoing, edge_far, summed, seen = call(
        functools.partial(first_kernel, half, days, order, paired, swap),
        [fresh, shape((own_rows + COLS, LANES)), shape((own_rows + rank, LANES)), edge, shape((2 * days, wide)), shape((TAIL, LANES))],
        [flip, pltpu.VMEM((rank, wide), F32)],
    )(surface, edge_near, predicted, packed, time_t, *[pieces[key] for key in order], bands(edge_far), *(() if paired else columns(cols)))

    def add(mine, theirs):
        return call(add_kernel, shape(theirs.shape))(mine, theirs)

    def over_bands(total, last):
        step = 1
        while 2 * step < n_lat:
            total = add(total, across(total, "lat", step))
            step *= 2
        return last(total, across(total, "lat", step))

    def over_lon(total):
        if paired:
            return [total] + [across(total, "lon", step) for step in (1, 2, 3)]
        step = 1
        while step < n_lon:
            total = add(total, across(total, "lon", step))
            step *= 2
        return [total]

    total, edge_near = call(core_kernel, [shape((own_rows, LANES)), edge])(message, across(outgoing, "ta", 1))
    if paired:
        last = call(band_kernel, shape(message.shape))
        parts = over_lon(over_bands(total, lambda mine, theirs: last(mine, theirs, message)))
        cols = parts[1], parts[3]
    else:
        parts = over_lon(over_bands(total, add))
        cols = columns(message[own_rows:])
    time_own, norm = call(functools.partial(own_kernel, len(parts)), [edge, shape((NORM, LANES))])(time_t, *parts)

    surface, time_t, message, outgoing = call(
        functools.partial(second_kernel, half, counts, swap),
        [fresh, edge, shape((sum_rows, LANES)), shape((sum_rows, LANES))],
        [flip, pltpu.VMEM((rank, wide), F32), pltpu.VMEM((rank, wide), F32), pltpu.VMEM((2 * days, wide), F32), pltpu.VMEM((rank, wide), BF16)],
    )(surface, time_own, across(time_own, "ta", 1), norm, summed, seen, edge_near, bands(edge_far), *cols)

    total = add(message, across(outgoing, "ta", 1))
    other = across(surface, "ta", 1)
    narrow = call(functools.partial(narrow_kernel, rank), shape((sum_rows + NORM, LANES), BF16))
    parts = over_lon(over_bands(total, narrow if paired else add))
    space, time = call(
        functools.partial(last_kernel, half, counts, len(parts)),
        [shape((rank * height, cells)), shape(factor_time.shape)],
        [flip],
    )(surface, other, time_t, *parts)
    return space.reshape(rank, height, cells), time


def solution(mesh):
    in_specs = (
        P(("grp", "lon", "lat"), "ta", None),
        P(("grp", "lon", "lat"), "ta"),
        P(("grp", "lon", "lat")),
        P(("grp", "lon", "lat"), None, None),
        P(("grp", "lon", "lat"), None),
        P(None, ("grp", "lat"), "lon"),
        P(("grp", "ta"), None),
    )
    out_specs = (P(None, ("grp", "lat"), "lon"), P(("grp", "ta"), None))
    return jax.shard_map(shards, mesh=mesh, in_specs=in_specs, out_specs=out_specs, check_vma=False)
```

```python
import functools
import math

import jax
import jax.numpy as jnp
from jax import lax
from jax.experimental import pallas as pl
from jax.experimental.pallas import tpu as pltpu
from jax.sharding import PartitionSpec as P

SMOOTH = 2.0
ETA_SPACE = 0.08
RIDGE = 1.0
EPSILON = 1e-06

F32 = jnp.float32
BF16 = jnp.bfloat16
LANES = 128
TAIL = 16
COLS = 16
NORM = 8
SPARE = 2 * 1024 * 1024
SWATH_COPIES = 4


def dot(a, b, contract):
    return lax.dot_general(a, b, ((contract[:1], contract[1:]), ((), ())), preferred_element_type=F32)


def route_kernel(half, sends, paired, list_hbm, count_hbm, target_hbm, swath_hbm, mask_hbm, space_hbm, time_hbm, *rest):
    outs, rest = rest[: len(sends)], rest[len(sends):]
    surface, edge_near, edge_far, cols, rest = *rest[:4], rest[4:]
    list_ref, count_ref, target_ref, swath_ref, mask_ref, space_ref, time_ref, place, total, seen, flip, arrived = rest
    me, core = lax.axis_index("lon"), lax.axis_index("ta")
    n_lon = list_ref.shape[1]
    slots, days, cells = swath_ref.shape
    chunk = slots // SWATH_COPIES
    small = [(list_hbm, list_ref), (count_hbm, count_ref), (target_hbm, target_ref), (mask_hbm, mask_ref)]
    large = [(swath_hbm.at[pl.ds(at, chunk)], swath_ref.at[pl.ds(at, chunk)]) for at in range(0, slots, chunk)]
    model = [(space_hbm, space_ref), (time_hbm, time_ref)]
    copies = [pltpu.make_async_copy(src, dst, arrived.at[i]) for i, (src, dst) in enumerate(small + large + model)]
    for copy in copies:
        copy.start()
    total[...] = jnp.zeros(total.shape, F32)
    seen[...] = jnp.zeros(seen.shape, F32)
    for copy in copies[: len(small)]:
        copy.wait()

    def owner(d, carry):
        step = jnp.bitwise_xor(d, me)

        def entry(k, carry):
            slot = list_ref[0, d, k]
            row = target_ref[slot]
            far = jnp.bitwise_xor(lax.div(row, half), core)
            place[slot] = (far * n_lon + step) * half + lax.rem(row, half)
            return carry

        return lax.fori_loop(0, count_ref[0, d], entry, carry)

    lax.fori_loop(0, n_lon, owner, 0)
    mask = mask_ref[...].astype(F32)
    by_day = mask.T
    for slot in range(slots):
        if slot % chunk == 0:
            copies[len(small) + slot // chunk].wait()
        at = place[slot]
        total[at] += swath_ref[slot].astype(F32) * by_day[:, slot:slot + 1]
        seen[pl.ds(at, 1), :days] += mask[slot:slot + 1, :]
    for copy in copies[len(small) + len(large):]:
        copy.wait()
    rank = surface.shape[0]
    height = space_ref.shape[0] // rank
    for row in range(half):
        surface[:, row * LANES:(row + 1) * LANES] = space_ref[pl.ds(core * half + row, rank, stride=height), :]
    edge_near[...] = space_ref[pl.ds(half - core, rank, stride=height), :]
    edge_far[...] = space_ref[pl.ds(core * (height - 1), rank, stride=height), :]
    cols[...] = columns_as_rows(border(surface[...], half), flip)[:COLS, :]
    for (side, step), out in zip(sends, outs):
        at = (side * n_lon + step) * half
        end = half * days + TAIL
        out[: half * days, :] = total[at:at + half].reshape(half * days, cells).astype(BF16)
        out[half * days:end, :] = seen[at:at + TAIL, :].astype(BF16)
        if (side, step) == (1, 0):
            left = time_ref[...]
            for part in range(end, end + 3 * days, days):
                value = left.astype(BF16)
                out[part:part + days, :] = jnp.zeros((days, LANES), BF16)
                out[part:part + days, :rank] = value
                left = left - value.astype(F32)
        elif paired and side == 0 and step in (1, 3):
            out[end:, :] = cols[...].astype(BF16)


def row_of(surface, row):
    return surface[:, row * LANES:(row + 1) * LANES]


def columns_as_rows(columns, flip):
    rank = columns[0].shape[0]
    lane = lax.broadcasted_iota(jnp.int32, (rank, LANES), 1)
    block = jnp.zeros((rank, LANES), F32)
    for at, column in enumerate(columns):
        block = jnp.where(lane == at, column, block)
    flip[...] = jnp.zeros(flip.shape, F32)
    flip[:rank, :] = block
    return flip[...].T


def border(surface, half):
    strips = [row_of(surface, row) for row in range(half)]
    return [strip[:, :1] for strip in strips] + [strip[:, LANES - 1:] for strip in strips]


def rows_as_columns(rows, rank, flip):
    flip[...] = jnp.zeros(flip.shape, F32)
    flip[: rows.shape[0], :] = rows
    return flip[...].T[:rank, :]


def smoothed(surface, half, above, below, left_cols, right_cols):
    lane = lax.broadcasted_iota(jnp.int32, above.shape, 1)
    strips = []
    for row in range(half):
        here = row_of(surface, row)
        up = above if row == 0 else row_of(surface, row - 1)
        down = below if row == half - 1 else row_of(surface, row + 1)
        left = jnp.where(lane == 0, left_cols[:, half + row:half + row + 1], pltpu.roll(here, 1, 1))
        right = jnp.where(lane == LANES - 1, right_cols[:, row:row + 1], pltpu.roll(here, LANES - 1, 1))
        lap = 4.0 * here - (up + down + left + right)
        strips.append(here - (ETA_SPACE * SMOOTH) * lap)
    return strips


def pick(flag, a, b):
    return jnp.where(flag, a, b)


def model_kernel(half, surface, time_own, piece, predicted, packed, time_t, days_all):
    rank = surface.shape[0]
    days = time_own.shape[0]
    at = half * days + TAIL
    high, middle, low = (piece[first:first + days, :].astype(F32) for first in range(at, at + 3 * days, days))
    days_all[...] = jnp.zeros(days_all.shape, F32)
    days_all[:days, :rank] = time_own[...]
    days_all[days:, :] = (high + middle) + low
    time_full = days_all[...]
    time_t[...] = time_full.T[:rank, :]
    packed[...] = surface[...].astype(BF16)
    time_bf = time_full[:, :rank].astype(BF16)
    for at in range(0, half * LANES, 2 * LANES):
        predicted[:, at:at + 2 * LANES] = dot(time_bf, packed[:, at:at + 2 * LANES], (1, 0))


def smooth(half, odd, surface, edge_near, edge_far, cols_a, cols_b, scale, base, flip):
    core = lax.axis_index("ta")
    rank = surface.shape[0]
    above = pick(core == 0, edge_far, edge_near)
    below = pick(core == 0, edge_near, edge_far)
    left = rows_as_columns(pick(odd, cols_a, cols_b), rank, flip)
    right = rows_as_columns(pick(odd, cols_b, cols_a), rank, flip)
    if scale is not None:
        above, below, left, right = above * scale, below * scale, left * scale, right * scale
    for row, strip in enumerate(smoothed(surface, half, above, below, left, right)):
        base[:, row * LANES:(row + 1) * LANES] = strip


def gradients(half, base, predicted, packed, time_t, seen, summed, fresh):
    rank = time_t.shape[0]
    time_bf = time_t.astype(BF16)
    time_twice = jnp.concatenate([time_bf, time_bf], axis=1)
    seen_bf = seen.astype(BF16)
    width = 2 * LANES
    owner = lax.broadcasted_iota(jnp.int32, (TAIL, width), 0)
    lane = lax.broadcasted_iota(jnp.int32, (TAIL, width), 1)
    grad_time = jnp.zeros((rank, width), F32)
    grad_diag = jnp.zeros((rank, LANES), F32)
    norm = jnp.zeros((rank, 1), F32)
    for at in range(0, half * LANES, width):
        spread = (owner * LANES <= lane + at) & (lane + at < (owner + 1) * LANES)
        weight = dot(seen_bf, spread.astype(BF16), (0, 0))
        part = packed[:, at:at + width]
        residual = weight * predicted[:, at:at + width] - summed[:, at:at + width]
        high = residual.astype(BF16)
        low = (residual - high.astype(F32)).astype(BF16)
        both = jnp.concatenate([high, low], axis=0)
        grad_space = dot(time_twice, both, (1, 0))
        grad_time = grad_time + dot(part, both, (1, 1))
        new = base[:, at:at + width] - ETA_SPACE * grad_space
        fresh[:, at:at + width] = new
        norm = norm + jnp.sum(new * new, axis=1, keepdims=True)
        wide = part.astype(F32)
        for row in range(width // LANES):
            strip = row_of(wide, row)
            square = jnp.sum(strip * strip, axis=1, keepdims=True)
            grad_diag = grad_diag + square * seen[at // LANES + row:at // LANES + row + 1, :]
    return grad_time[:, :LANES] + grad_time[:, LANES:], grad_diag, norm


def post_own(half, sums, fresh, message, outgoing, edge_far, flip):
    grad_time, grad_diag, norm = sums
    core = lax.axis_index("ta")
    rank = norm.shape[0]
    days = LANES // 2
    own = lax.broadcasted_iota(jnp.int32, grad_time.shape, 1) < days
    last = columns_as_rows([norm] * NORM + border(fresh[...], half), flip)
    message[:rank, :] = jnp.where(own, grad_time, pltpu.roll(grad_diag, days, 1))
    message[rank:, :] = last[: NORM + COLS, :]
    outgoing[:rank, :] = jnp.where(own, pltpu.roll(grad_time, days, 1), grad_diag)
    outgoing[rank:rank + NORM, :] = last[:NORM, :]
    first_row, last_row = fresh[:, :LANES], fresh[:, (half - 1) * LANES:]
    outgoing[rank + NORM:, :] = pick(core == 0, last_row, first_row)
    edge_far[...] = pick(core == 0, first_row, last_row)


def post_all(sums, message, outgoing, flip):
    grad_time, grad_diag, norm = sums
    rank = norm.shape[0]
    last = columns_as_rows([norm], flip)[:NORM, :]
    message[:rank, :] = grad_time
    message[rank:2 * rank, :] = grad_diag
    message[2 * rank:, :] = last
    outgoing[:rank, :] = pltpu.roll(grad_time, LANES // 2, 1)
    outgoing[rank:2 * rank, :] = pltpu.roll(grad_diag, LANES // 2, 1)
    outgoing[2 * rank:, :] = last


def first_kernel(half, days, order, paired, swap, surface, edge_near, predicted, packed, time_t, *rest):
    pieces, rest = dict(zip(order, rest)), rest[len(order):]
    edge_far_in, rest = rest[0], rest[1:]
    if paired:
        at = half * days + TAIL
        cols = [pieces[0, step][at:, :].astype(F32) for step in (1, 3)]
    else:
        cols, rest = [ref[...] for ref in rest[:2]], rest[2:]
    fresh, message, outgoing, edge_far, summed, seen, flip, base = rest
    smooth(half, swap(), surface[...], edge_near[...], edge_far_in[...], *cols, None, base, flip)
    sides = [[pieces[key] for key in sorted(pieces) if key[0] == side] for side in (0, 1)]

    def add_up(parts, rows):
        value = parts[0][rows, :].astype(F32)
        for piece in parts[1:]:
            value = value + piece[rows, :].astype(F32)
        return value

    for row in range(half):
        for first, parts in zip((0, days), sides):
            summed[first:first + days, row * LANES:(row + 1) * LANES] = add_up(parts, slice(row * days, (row + 1) * days))
    near, far = (add_up(parts, slice(half * days, half * days + TAIL)) for parts in sides)
    seen[...] = near + pltpu.roll(far, days, 1)
    sums = gradients(half, base, predicted, packed, time_t[...], seen[...], summed, fresh)
    post_own(half, sums, fresh, message, outgoing, edge_far, flip)


def total_of(parts):
    total = parts[0][...].astype(F32)
    if len(parts) > 1:
        one, two, three = (part[...].astype(F32) for part in parts[1:])
        total = (total + one) + (two + three)
    return total


def own_kernel(n_parts, time_t, *rest):
    parts, (time_own, norm) = rest[:n_parts], rest[n_parts:]
    rank = time_t.shape[0]
    days = LANES // 2
    total = total_of(parts)
    block = total[:rank, :]
    own = lax.broadcasted_iota(jnp.int32, block.shape, 1) < days
    time_own[...] = jnp.where(own, time_t[...] - block / (pltpu.roll(block, days, 1) + RIDGE), 0.0)
    norm[...] = total[rank:rank + NORM, :]


def rescaling(counts, norm, time_new, flip):
    day_count, cell_count = counts
    space_sq = rows_as_columns(norm, time_new.shape[0], flip)[:, :1]
    square = time_new * time_new
    time_sq = 0.5 * jnp.sum(square + pltpu.roll(square, LANES // 2, 1), axis=1, keepdims=True)
    ratio = (time_sq / day_count + EPSILON) / (space_sq / cell_count + EPSILON)
    return jnp.sqrt(jnp.sqrt(ratio))


def second_kernel(half, counts, swap, surface, time_own, time_other, norm, summed, seen, edge_near, edge_far, cols_a, cols_b, *rest):
    fresh, time_out, message, outgoing, flip, scaled, base, predicted, packed = rest
    rank = surface.shape[0]
    time_new = time_own[...] + pltpu.roll(time_other[...], LANES // 2, 1)
    scale = rescaling(counts, norm[...], time_new, flip)
    time_now = time_new / scale
    time_out[...] = time_now
    scaled[...] = surface[...] * scale
    packed[...] = scaled[...].astype(BF16)
    time_bf = time_now.T.astype(BF16)
    for at in range(0, half * LANES, 2 * LANES):
        predicted[:, at:at + 2 * LANES] = dot(time_bf, packed[:, at:at + 2 * LANES], (1, 0))
    cols = [ref[ref.shape[0] - COLS:, :] for ref in (cols_a, cols_b)]
    smooth(half, swap(), scaled[...], edge_near[...], edge_far[...], *cols, scale, base, flip)
    sums = gradients(half, base, predicted, packed, time_now, seen[...], summed, fresh)
    post_all(sums, message, outgoing, flip)


def last_kernel(half, counts, n_parts, surface, other, time_t, *rest):
    parts = rest[:n_parts]
    space_out, time_out, flip = rest[n_parts:]
    core = lax.axis_index("ta")
    rank = surface.shape[0]
    height = space_out.shape[0] // rank
    total = total_of(parts)
    time_new = time_t[...] - total[:rank, :] / (total[rank:2 * rank, :] + RIDGE)
    norm = total[2 * rank:2 * rank + NORM, :]
    if parts[0].dtype == BF16:
        norm = norm + total[2 * rank + NORM:, :]
    scale = rescaling(counts, norm, time_new, flip)
    flip[...] = jnp.zeros(flip.shape, F32)
    flip[:rank, :] = time_new / scale
    time_out[...] = flip[...].T[: time_out.shape[0], :rank]
    for row in range(half):
        at = row * LANES
        space_out[pl.ds(core * half + row, rank, stride=height), :] = surface[:, at:at + LANES] * scale
        space_out[pl.ds((1 - core) * half + row, rank, stride=height), :] = other[:, at:at + LANES] * scale


def core_kernel(mine, theirs, total, beside):
    rows = total.shape[0]
    total[...] = mine[:rows, :] + theirs[:rows, :]
    beside[...] = theirs[rows:, :]


def merge_kernel(mine, theirs, edge_in, out, edge_out):
    edge_out[...] = edge_in[...]
    out[...] = (mine[...].astype(F32) + theirs[...].astype(F32)).astype(BF16)


def add_kernel(mine, theirs, total):
    rows = total.shape[0]
    total[...] = mine[:rows, :] + theirs[:rows, :]


def band_kernel(mine, theirs, message, total):
    rows = mine.shape[0]
    total[:rows, :] = mine[...] + theirs[...]
    total[rows:, :] = message[rows:, :]


def narrow_kernel(rank, mine, theirs, total):
    value = mine[...] + theirs[...]
    total[: 2 * rank, :] = value[: 2 * rank, :].astype(BF16)
    norm = value[2 * rank:, :]
    high = norm.astype(BF16).astype(F32)
    total[2 * rank:, :] = jnp.concatenate([high, norm - high], axis=0).astype(BF16)


def shape(dims, dtype=F32):
    return jax.ShapeDtypeStruct(tuple(dims), dtype)


def padded(ref):
    *outer, rows, lanes = (1, *ref.shape)
    return math.prod(outer) * -(-rows // 16) * 16 * -(-lanes // LANES) * LANES * jnp.dtype(ref.dtype).itemsize


def call(kernel, out_shape, scratch=(), hbm=0, after=0, flops=1_000_000):
    def run(*operands):
        operands = [pltpu.with_memory_space_constraint(x, pltpu.HBM) if i < hbm else x for i, x in enumerate(operands)]
        vmem = [*operands[hbm:len(operands) - after], *jax.tree.leaves(out_shape), *scratch]
        specs = [pltpu.HBM] * hbm + [pltpu.VMEM] * (len(operands) - hbm - after) + [pl.ANY] * after
        return pl.pallas_call(
            kernel,
            out_shape=out_shape,
            in_specs=[pl.BlockSpec(memory_space=space) for space in specs],
            out_specs=jax.tree.map(lambda _: pl.BlockSpec(memory_space=pltpu.VMEM), out_shape),
            scratch_shapes=list(scratch),
            compiler_params=pltpu.CompilerParams(vmem_limit_bytes=SPARE + sum(padded(ref) for ref in vmem if len(ref.shape) > 1)),
            cost_estimate=pl.CostEstimate(flops=flops, bytes_accessed=1_000_000, transcendentals=0),
        )(*operands)

    return run


def across(value, axis, step):
    return lax.ppermute(value, axis, [(i, i ^ step) for i in range(lax.axis_size(axis))])


def shards(swath, obs_mask, target, send_list, send_count, factor_space, factor_time):
    n_lon, n_lat, n_ta = (lax.axis_size(axis) for axis in ("lon", "lat", "ta"))
    slots, days, cells = swath.shape
    rank, height, _ = factor_space.shape
    half = height // n_ta
    wide = half * LANES
    counts = (float(days * n_ta), float(height * cells * n_lon * n_lat))
    own_rows, sum_rows = rank + NORM, 2 * rank + NORM
    flip = pltpu.VMEM((LANES, LANES), F32)

    paired = n_lon == 4

    distant, close = range(n_lon // 2, n_lon), range(1, n_lon // 2)
    sends = [(1, step) for step in reversed(distant)] + [(0, step) for step in distant] + [(1, 0)]
    sends += [(side, step) for side in (0, 1) for step in close] + [(0, 0)]

    def piece_rows(side, step):
        more = 3 * days if (side, step) == (1, 0) else COLS if paired and side == 0 and step in (1, 3) else 0
        return half * days + TAIL + more

    operands = (send_list, send_count, target, swath, obs_mask, factor_space.reshape(rank * height, cells), factor_time)
    *pieces, surface, edge_near, edge_far, cols = call(
        functools.partial(route_kernel, half, sends, paired),
        [shape((piece_rows(*key), cells), BF16) for key in sends]
        + [shape((rank, wide)), shape((rank, LANES)), shape((rank, LANES)), shape((COLS, LANES))],
        [pltpu.SMEM(ref.shape, jnp.int32) for ref in operands[:3]]
        + [pltpu.VMEM(ref.shape, ref.dtype) for ref in operands[3:]]
        + [
            pltpu.SMEM((slots,), jnp.int32),
            pltpu.VMEM((2 * n_lon * half, days, cells), F32),
            pltpu.VMEM((2 * n_lon * half + TAIL, LANES), F32),
            flip,
            pltpu.SemaphoreType.DMA((len(operands) - 1 + SWATH_COPIES,)),
        ],
        hbm=len(operands),
    )(*operands)

    def arrived(key, piece):
        side, step = key
        if side:
            return across(piece, ("lon", "ta"), 2 * step + 1)
        return across(piece, "lon", step) if step else piece

    pieces = dict(zip(sends, pieces))
    if paired:
        passing = across(pieces.pop((1, 3)), "lon", 1)
        outs = [shape(passing.shape, BF16), shape(edge_far.shape)]
        pieces[1, 2], edge_far = call(merge_kernel, outs)(pieces[1, 2], passing, edge_far)
    pieces = {key: arrived(key, piece) for key, piece in pieces.items()}
    order = list(pieces)

    def bands(edge):
        there = [(2 * band + 1, 2 * band + 2) for band in range(n_lat - 1)]
        return lax.ppermute(edge, ("lat", "ta"), there + [(b, a) for a, b in there])

    def swap():
        return lax.rem(lax.axis_index("lon"), 2) == 1 if paired else jnp.bool_(True)

    def columns(value):
        if paired:
            return across(value, "lon", 1), across(value, "lon", 3)
        ring = [(i, (i + 1) % n_lon) for i in range(n_lon)]
        return lax.ppermute(value, "lon", ring), lax.ppermute(value, "lon", [(b, a) for a, b in ring])

    predicted, packed, time_t = call(
        functools.partial(model_kernel, half),
        [shape((2 * days, wide)), shape((rank, wide), BF16), shape((rank, LANES))],
        [flip],
    )(surface, factor_time, pieces[1, 0])

    fresh, edge = shape((rank, wide)), shape((rank, LANES))
    surface, message, outgoing, edge_far, summed, seen = call(
        functools.partial(first_kernel, half, days, order, paired, swap),
        [fresh, shape((own_rows + COLS, LANES)), shape((own_rows + rank, LANES)), edge, shape((2 * days, wide)), shape((TAIL, LANES))],
        [flip, pltpu.VMEM((rank, wide), F32)],
    )(surface, edge_near, predicted, packed, time_t, *[pieces[key] for key in order], bands(edge_far), *(() if paired else columns(cols)))

    def add(mine, theirs):
        return call(add_kernel, shape(theirs.shape))(mine, theirs)

    def over_bands(total, last):
        step = 1
        while 2 * step < n_lat:
            total = add(total, across(total, "lat", step))
            step *= 2
        return last(total, across(total, "lat", step))

    def over_lon(total):
        if paired:
            return [total] + [across(total, "lon", step) for step in (1, 2, 3)]
        step = 1
        while step < n_lon:
            total = add(total, across(total, "lon", step))
            step *= 2
        return [total]

    total, edge_near = call(core_kernel, [shape((own_rows, LANES)), edge])(message, across(outgoing, "ta", 1))
    if paired:
        last = call(band_kernel, shape(message.shape))
        parts = over_lon(over_bands(total, lambda mine, theirs: last(mine, theirs, message)))
        cols = parts[1], parts[3]
    else:
        parts = over_lon(over_bands(total, add))
        cols = columns(message[own_rows:])
    time_own, norm = call(functools.partial(own_kernel, len(parts)), [edge, shape((NORM, LANES))])(time_t, *parts)

    surface, time_t, message, outgoing = call(
        functools.partial(second_kernel, half, counts, swap),
        [fresh, edge, shape((sum_rows, LANES)), shape((sum_rows, LANES))],
        [flip, pltpu.VMEM((rank, wide), F32), pltpu.VMEM((rank, wide), F32), pltpu.VMEM((2 * days, wide), F32), pltpu.VMEM((rank, wide), BF16)],
    )(surface, time_own, across(time_own, "ta", 1), norm, summed, seen, edge_near, bands(edge_far), *cols)

    total = add(message, across(outgoing, "ta", 1))
    other = across(surface, "ta", 1)
    narrow = call(functools.partial(narrow_kernel, rank), shape((sum_rows + NORM, LANES), BF16))
    parts = over_lon(over_bands(total, narrow if paired else add))
    space, time = call(
        functools.partial(last_kernel, half, counts, len(parts)),
        [shape((rank * height, cells)), shape(factor_time.shape)],
        [flip],
    )(surface, other, time_t, *parts)
    return space.reshape(rank, height, cells), time


def solution(mesh):
    in_specs = (
        P(("grp", "lon", "lat"), "ta", None),
        P(("grp", "lon", "lat"), "ta"),
        P(("grp", "lon", "lat")),
        P(("grp", "lon", "lat"), None, None),
        P(("grp", "lon", "lat"), None),
        P(None, ("grp", "lat"), "lon"),
        P(("grp", "ta"), None),
    )
    out_specs = (P(None, ("grp", "lat"), "lon"), P(("grp", "ta"), None))
    return jax.shard_map(shards, mesh=mesh, in_specs=in_specs, out_specs=out_specs, check_vma=False)
```

```python
import functools
import math

import jax
import jax.numpy as jnp
from jax import lax
from jax.experimental import pallas as pl
from jax.experimental.pallas import tpu as pltpu
from jax.sharding import PartitionSpec as P

SMOOTH = 2.0
ETA_SPACE = 0.08
RIDGE = 1.0
EPSILON = 1e-06

F32 = jnp.float32
BF16 = jnp.bfloat16
LANES = 128
TAIL = 16
COLS = 16
NORM = 8
SPARE = 2 * 1024 * 1024
SWATH_COPIES = 4


def dot(a, b, contract):
    return lax.dot_general(a, b, ((contract[:1], contract[1:]), ((), ())), preferred_element_type=F32)


def route_kernel(half, sends, paired, list_hbm, count_hbm, target_hbm, swath_hbm, mask_hbm, space_hbm, time_hbm, *rest):
    outs, rest = rest[: len(sends)], rest[len(sends):]
    surface, edge_near, edge_far, cols, rest = *rest[:4], rest[4:]
    list_ref, count_ref, target_ref, swath_ref, mask_ref, space_ref, time_ref, place, total, seen, flip, arrived = rest
    me, core = lax.axis_index("lon"), lax.axis_index("ta")
    n_lon = list_ref.shape[1]
    slots, days, cells = swath_ref.shape
    chunk = slots // SWATH_COPIES
    small = [(list_hbm, list_ref), (count_hbm, count_ref), (target_hbm, target_ref), (mask_hbm, mask_ref)]
    large = [(swath_hbm.at[pl.ds(at, chunk)], swath_ref.at[pl.ds(at, chunk)]) for at in range(0, slots, chunk)]
    model = [(space_hbm, space_ref), (time_hbm, time_ref)]
    copies = [pltpu.make_async_copy(src, dst, arrived.at[i]) for i, (src, dst) in enumerate(small + large + model)]
    for copy in copies:
        copy.start()
    total[...] = jnp.zeros(total.shape, F32)
    seen[...] = jnp.zeros(seen.shape, F32)
    for copy in copies[: len(small)]:
        copy.wait()

    def owner(d, carry):
        step = jnp.bitwise_xor(d, me)

        def entry(k, carry):
            slot = list_ref[0, d, k]
            row = target_ref[slot]
            far = jnp.bitwise_xor(lax.div(row, half), core)
            place[slot] = (far * n_lon + step) * half + lax.rem(row, half)
            return carry

        return lax.fori_loop(0, count_ref[0, d], entry, carry)

    lax.fori_loop(0, n_lon, owner, 0)
    mask = mask_ref[...].astype(F32)
    by_day = mask.T
    for slot in range(slots):
        if slot % chunk == 0:
            copies[len(small) + slot // chunk].wait()
        at = place[slot]
        total[at] += swath_ref[slot].astype(F32) * by_day[:, slot:slot + 1]
        seen[pl.ds(at, 1), :days] += mask[slot:slot + 1, :]
    for copy in copies[len(small) + len(large):]:
        copy.wait()
    rank = surface.shape[0]
    height = space_ref.shape[0] // rank
    for row in range(half):
        surface[:, row * LANES:(row + 1) * LANES] = space_ref[pl.ds(core * half + row, rank, stride=height), :]
    edge_near[...] = space_ref[pl.ds(half - core, rank, stride=height), :]
    edge_far[...] = space_ref[pl.ds(core * (height - 1), rank, stride=height), :]
    cols[...] = columns_as_rows(border(surface[...], half), flip)[:COLS, :]
    for (side, step), out in zip(sends, outs):
        at = (side * n_lon + step) * half
        end = half * days + TAIL
        out[: half * days, :] = total[at:at + half].reshape(half * days, cells).astype(BF16)
        out[half * days:end, :] = seen[at:at + TAIL, :].astype(BF16)
        if (side, step) == (1, 0):
            left = time_ref[...]
            for part in range(end, end + 3 * days, days):
                value = left.astype(BF16)
                out[part:part + days, :] = jnp.zeros((days, LANES), BF16)
                out[part:part + days, :rank] = value
                left = left - value.astype(F32)
        elif paired and side == 0 and step in (1, 3):
            out[end:, :] = cols[...].astype(BF16)


def row_of(surface, row):
    return surface[:, row * LANES:(row + 1) * LANES]


def columns_as_rows(columns, flip):
    rank = columns[0].shape[0]
    lane = lax.broadcasted_iota(jnp.int32, (rank, LANES), 1)
    block = jnp.zeros((rank, LANES), F32)
    for at, column in enumerate(columns):
        block = jnp.where(lane == at, column, block)
    flip[...] = jnp.zeros(flip.shape, F32)
    flip[:rank, :] = block
    return flip[...].T


def border(surface, half):
    strips = [row_of(surface, row) for row in range(half)]
    return [strip[:, :1] for strip in strips] + [strip[:, LANES - 1:] for strip in strips]


def rows_as_columns(rows, rank, flip):
    flip[...] = jnp.zeros(flip.shape, F32)
    flip[: rows.shape[0], :] = rows
    return flip[...].T[:rank, :]


def smoothed(surface, half, above, below, left_cols, right_cols):
    lane = lax.broadcasted_iota(jnp.int32, above.shape, 1)
    strips = []
    for row in range(half):
        here = row_of(surface, row)
        up = above if row == 0 else row_of(surface, row - 1)
        down = below if row == half - 1 else row_of(surface, row + 1)
        left = jnp.where(lane == 0, left_cols[:, half + row:half + row + 1], pltpu.roll(here, 1, 1))
        right = jnp.where(lane == LANES - 1, right_cols[:, row:row + 1], pltpu.roll(here, LANES - 1, 1))
        lap = 4.0 * here - (up + down + left + right)
        strips.append(here - (ETA_SPACE * SMOOTH) * lap)
    return strips


def pick(flag, a, b):
    return jnp.where(flag, a, b)


def model_kernel(half, surface, time_own, piece, predicted, packed, time_t, days_all):
    rank = surface.shape[0]
    days = time_own.shape[0]
    at = half * days + TAIL
    high, middle, low = (piece[first:first + days, :].astype(F32) for first in range(at, at + 3 * days, days))
    days_all[...] = jnp.zeros(days_all.shape, F32)
    days_all[:days, :rank] = time_own[...]
    days_all[days:, :] = (high + middle) + low
    time_full = days_all[...]
    time_t[...] = time_full.T[:rank, :]
    packed[...] = surface[...].astype(BF16)
    time_bf = time_full[:, :rank].astype(BF16)
    for at in range(0, half * LANES, 2 * LANES):
        predicted[:, at:at + 2 * LANES] = dot(time_bf, packed[:, at:at + 2 * LANES], (1, 0))


def smooth(half, odd, surface, edge_near, edge_far, cols_a, cols_b, scale, base, flip):
    core = lax.axis_index("ta")
    rank = surface.shape[0]
    above = pick(core == 0, edge_far, edge_near)
    below = pick(core == 0, edge_near, edge_far)
    left = rows_as_columns(pick(odd, cols_a, cols_b), rank, flip)
    right = rows_as_columns(pick(odd, cols_b, cols_a), rank, flip)
    if scale is not None:
        above, below, left, right = above * scale, below * scale, left * scale, right * scale
    for row, strip in enumerate(smoothed(surface, half, above, below, left, right)):
        base[:, row * LANES:(row + 1) * LANES] = strip


def gradients(half, base, predicted, packed, time_t, seen, summed, fresh):
    rank = time_t.shape[0]
    time_bf = time_t.astype(BF16)
    time_twice = jnp.concatenate([time_bf, time_bf], axis=1)
    seen_bf = seen.astype(BF16)
    width = 2 * LANES
    owner = lax.broadcasted_iota(jnp.int32, (TAIL, width), 0)
    lane = lax.broadcasted_iota(jnp.int32, (TAIL, width), 1)
    grad_time = jnp.zeros((rank, width), F32)
    grad_diag = jnp.zeros((rank, LANES), F32)
    norm = jnp.zeros((rank, 1), F32)
    for at in range(0, half * LANES, width):
        spread = (owner * LANES <= lane + at) & (lane + at < (owner + 1) * LANES)
        weight = dot(seen_bf, spread.astype(BF16), (0, 0))
        part = packed[:, at:at + width]
        residual = weight * predicted[:, at:at + width] - summed[:, at:at + width]
        high = residual.astype(BF16)
        low = (residual - high.astype(F32)).astype(BF16)
        both = jnp.concatenate([high, low], axis=0)
        grad_space = dot(time_twice, both, (1, 0))
        grad_time = grad_time + dot(part, both, (1, 1))
        new = base[:, at:at + width] - ETA_SPACE * grad_space
        fresh[:, at:at + width] = new
        norm = norm + jnp.sum(new * new, axis=1, keepdims=True)
        wide = part.astype(F32)
        for row in range(width // LANES):
            strip = row_of(wide, row)
            square = jnp.sum(strip * strip, axis=1, keepdims=True)
            grad_diag = grad_diag + square * seen[at // LANES + row:at // LANES + row + 1, :]
    return grad_time[:, :LANES] + grad_time[:, LANES:], grad_diag, norm


def post_own(half, sums, fresh, message, outgoing, edge_far, flip):
    grad_time, grad_diag, norm = sums
    core = lax.axis_index("ta")
    rank = norm.shape[0]
    days = LANES // 2
    own = lax.broadcasted_iota(jnp.int32, grad_time.shape, 1) < days
    last = columns_as_rows([norm] * NORM + border(fresh[...], half), flip)
    message[:rank, :] = jnp.where(own, grad_time, pltpu.roll(grad_diag, days, 1))
    message[rank:, :] = last[: NORM + COLS, :]
    outgoing[:rank, :] = jnp.where(own, pltpu.roll(grad_time, days, 1), grad_diag)
    outgoing[rank:rank + NORM, :] = last[:NORM, :]
    first_row, last_row = fresh[:, :LANES], fresh[:, (half - 1) * LANES:]
    outgoing[rank + NORM:, :] = pick(core == 0, last_row, first_row)
    edge_far[...] = pick(core == 0, first_row, last_row)


def post_all(sums, message, outgoing, flip):
    grad_time, grad_diag, norm = sums
    rank = norm.shape[0]
    last = columns_as_rows([norm], flip)[:NORM, :]
    message[:rank, :] = grad_time
    message[rank:2 * rank, :] = grad_diag
    message[2 * rank:, :] = last
    outgoing[:rank, :] = pltpu.roll(grad_time, LANES // 2, 1)
    outgoing[rank:2 * rank, :] = pltpu.roll(grad_diag, LANES // 2, 1)
    outgoing[2 * rank:, :] = last


def first_kernel(half, days, order, paired, swap, surface, edge_near, predicted, packed, time_t, *rest):
    pieces, rest = dict(zip(order, rest)), rest[len(order):]
    edge_far_in, rest = rest[0], rest[1:]
    if paired:
        at = half * days + TAIL
        cols = [pieces[0, step][at:, :].astype(F32) for step in (1, 3)]
    else:
        cols, rest = [ref[...] for ref in rest[:2]], rest[2:]
    fresh, message, outgoing, edge_far, summed, seen, flip, base = rest
    smooth(half, swap(), surface[...], edge_near[...], edge_far_in[...], *cols, None, base, flip)
    sides = [[pieces[key] for key in sorted(pieces) if key[0] == side] for side in (0, 1)]

    def add_up(parts, rows):
        value = parts[0][rows, :].astype(F32)
        for piece in parts[1:]:
            value = value + piece[rows, :].astype(F32)
        return value

    for row in range(half):
        for first, parts in zip((0, days), sides):
            summed[first:first + days, row * LANES:(row + 1) * LANES] = add_up(parts, slice(row * days, (row + 1) * days))
    near, far = (add_up(parts, slice(half * days, half * days + TAIL)) for parts in sides)
    seen[...] = near + pltpu.roll(far, days, 1)
    sums = gradients(half, base, predicted, packed, time_t[...], seen[...], summed, fresh)
    post_own(half, sums, fresh, message, outgoing, edge_far, flip)


def total_of(parts):
    total = parts[0][...].astype(F32)
    if len(parts) > 1:
        one, two, three = (part[...].astype(F32) for part in parts[1:])
        total = (total + one) + (two + three)
    return total


def own_kernel(n_parts, time_t, *rest):
    parts, (time_own, norm) = rest[:n_parts], rest[n_parts:]
    rank = time_t.shape[0]
    days = LANES // 2
    total = total_of(parts)
    block = total[:rank, :]
    own = lax.broadcasted_iota(jnp.int32, block.shape, 1) < days
    time_own[...] = jnp.where(own, time_t[...] - block / (pltpu.roll(block, days, 1) + RIDGE), 0.0)
    norm[...] = total[rank:rank + NORM, :]


def rescaling(counts, norm, time_new, flip):
    day_count, cell_count = counts
    space_sq = rows_as_columns(norm, time_new.shape[0], flip)[:, :1]
    square = time_new * time_new
    time_sq = 0.5 * jnp.sum(square + pltpu.roll(square, LANES // 2, 1), axis=1, keepdims=True)
    ratio = (time_sq / day_count + EPSILON) / (space_sq / cell_count + EPSILON)
    return jnp.sqrt(jnp.sqrt(ratio))


def second_kernel(half, counts, swap, surface, time_own, time_other, norm, summed, seen, edge_near, edge_far, cols_a, cols_b, *rest):
    fresh, time_out, message, outgoing, flip, scaled, base, predicted, packed = rest
    rank = surface.shape[0]
    time_new = time_own[...] + pltpu.roll(time_other[...], LANES // 2, 1)
    scale = rescaling(counts, norm[...], time_new, flip)
    time_now = time_new / scale
    time_out[...] = time_now
    scaled[...] = surface[...] * scale
    packed[...] = scaled[...].astype(BF16)
    time_bf = time_now.T.astype(BF16)
    for at in range(0, half * LANES, 2 * LANES):
        predicted[:, at:at + 2 * LANES] = dot(time_bf, packed[:, at:at + 2 * LANES], (1, 0))
    cols = [ref[ref.shape[0] - COLS:, :] for ref in (cols_a, cols_b)]
    smooth(half, swap(), scaled[...], edge_near[...], edge_far[...], *cols, scale, base, flip)
    sums = gradients(half, base, predicted, packed, time_now, seen[...], summed, fresh)
    post_all(sums, message, outgoing, flip)


def last_kernel(half, counts, n_parts, surface, other, time_t, *rest):
    parts = rest[:n_parts]
    space_out, time_out, flip = rest[n_parts:]
    core = lax.axis_index("ta")
    rank = surface.shape[0]
    height = space_out.shape[0] // rank
    total = total_of(parts)
    time_new = time_t[...] - total[:rank, :] / (total[rank:2 * rank, :] + RIDGE)
    norm = total[2 * rank:2 * rank + NORM, :]
    if parts[0].dtype == BF16:
        norm = norm + total[2 * rank + NORM:, :]
    scale = rescaling(counts, norm, time_new, flip)
    flip[...] = jnp.zeros(flip.shape, F32)
    flip[:rank, :] = time_new / scale
    time_out[...] = flip[...].T[: time_out.shape[0], :rank]
    for row in range(half):
        at = row * LANES
        space_out[pl.ds(core * half + row, rank, stride=height), :] = surface[:, at:at + LANES] * scale
        space_out[pl.ds((1 - core) * half + row, rank, stride=height), :] = other[:, at:at + LANES] * scale


def core_kernel(mine, theirs, total, beside):
    rows = total.shape[0]
    total[...] = mine[:rows, :] + theirs[:rows, :]
    beside[...] = theirs[rows:, :]


def merge_kernel(mine, theirs, piece_in, edge_in, out, piece_out, edge_out):
    piece_out[...] = piece_in[...]
    edge_out[...] = edge_in[...]
    out[...] = (mine[...].astype(F32) + theirs[...].astype(F32)).astype(BF16)


def add_kernel(mine, theirs, total):
    rows = total.shape[0]
    total[...] = mine[:rows, :] + theirs[:rows, :]


def band_kernel(mine, theirs, message, total):
    rows = mine.shape[0]
    total[:rows, :] = mine[...] + theirs[...]
    total[rows:, :] = message[rows:, :]


def narrow_kernel(rank, mine, theirs, total):
    value = mine[...] + theirs[...]
    total[: 2 * rank, :] = value[: 2 * rank, :].astype(BF16)
    norm = value[2 * rank:, :]
    high = norm.astype(BF16).astype(F32)
    total[2 * rank:, :] = jnp.concatenate([high, norm - high], axis=0).astype(BF16)


def shape(dims, dtype=F32):
    return jax.ShapeDtypeStruct(tuple(dims), dtype)


def padded(ref):
    *outer, rows, lanes = (1, *ref.shape)
    return math.prod(outer) * -(-rows // 16) * 16 * -(-lanes // LANES) * LANES * jnp.dtype(ref.dtype).itemsize


def call(kernel, out_shape, scratch=(), hbm=0, after=0, flops=1_000_000):
    def run(*operands):
        operands = [pltpu.with_memory_space_constraint(x, pltpu.HBM) if i < hbm else x for i, x in enumerate(operands)]
        vmem = [*operands[hbm:len(operands) - after], *jax.tree.leaves(out_shape), *scratch]
        specs = [pltpu.HBM] * hbm + [pltpu.VMEM] * (len(operands) - hbm - after) + [pl.ANY] * after
        return pl.pallas_call(
            kernel,
            out_shape=out_shape,
            in_specs=[pl.BlockSpec(memory_space=space) for space in specs],
            out_specs=jax.tree.map(lambda _: pl.BlockSpec(memory_space=pltpu.VMEM), out_shape),
            scratch_shapes=list(scratch),
            compiler_params=pltpu.CompilerParams(vmem_limit_bytes=SPARE + sum(padded(ref) for ref in vmem if len(ref.shape) > 1)),
            cost_estimate=pl.CostEstimate(flops=flops, bytes_accessed=1_000_000, transcendentals=0),
        )(*operands)

    return run


def across(value, axis, step):
    return lax.ppermute(value, axis, [(i, i ^ step) for i in range(lax.axis_size(axis))])


def shards(swath, obs_mask, target, send_list, send_count, factor_space, factor_time):
    n_lon, n_lat, n_ta = (lax.axis_size(axis) for axis in ("lon", "lat", "ta"))
    slots, days, cells = swath.shape
    rank, height, _ = factor_space.shape
    half = height // n_ta
    wide = half * LANES
    counts = (float(days * n_ta), float(height * cells * n_lon * n_lat))
    own_rows, sum_rows = rank + NORM, 2 * rank + NORM
    flip = pltpu.VMEM((LANES, LANES), F32)

    paired = n_lon == 4

    distant, close = range(n_lon // 2, n_lon), range(1, n_lon // 2)
    sends = [(1, step) for step in reversed(distant)] + [(0, step) for step in distant] + [(1, 0)]
    sends += [(side, step) for side in (0, 1) for step in close] + [(0, 0)]

    def piece_rows(side, step):
        more = 3 * days if (side, step) == (1, 0) else COLS if paired and side == 0 and step in (1, 3) else 0
        return half * days + TAIL + more

    operands = (send_list, send_count, target, swath, obs_mask, factor_space.reshape(rank * height, cells), factor_time)
    *pieces, surface, edge_near, edge_far, cols = call(
        functools.partial(route_kernel, half, sends, paired),
        [shape((piece_rows(*key), cells), BF16) for key in sends]
        + [shape((rank, wide)), shape((rank, LANES)), shape((rank, LANES)), shape((COLS, LANES))],
        [pltpu.SMEM(ref.shape, jnp.int32) for ref in operands[:3]]
        + [pltpu.VMEM(ref.shape, ref.dtype) for ref in operands[3:]]
        + [
            pltpu.SMEM((slots,), jnp.int32),
            pltpu.VMEM((2 * n_lon * half, days, cells), F32),
            pltpu.VMEM((2 * n_lon * half + TAIL, LANES), F32),
            flip,
            pltpu.SemaphoreType.DMA((len(operands) - 1 + SWATH_COPIES,)),
        ],
        hbm=len(operands),
    )(*operands)

    def arrived(key, piece):
        side, step = key
        if side:
            return across(piece, ("lon", "ta"), 2 * step + 1)
        return across(piece, "lon", step) if step else piece

    pieces = dict(zip(sends, pieces))
    if paired:
        passing = across(pieces.pop((1, 3)), "lon", 1)
        outs = [shape(passing.shape, BF16), shape(passing.shape, BF16), shape(edge_far.shape)]
        pieces[1, 2], pieces[1, 1], edge_far = call(merge_kernel, outs)(pieces[1, 2], passing, pieces[1, 1], edge_far)
    pieces = {key: arrived(key, piece) for key, piece in pieces.items()}
    order = list(pieces)

    def bands(edge):
        there = [(2 * band + 1, 2 * band + 2) for band in range(n_lat - 1)]
        return lax.ppermute(edge, ("lat", "ta"), there + [(b, a) for a, b in there])

    def swap():
        return lax.rem(lax.axis_index("lon"), 2) == 1 if paired else jnp.bool_(True)

    def columns(value):
        if paired:
            return across(value, "lon", 1), across(value, "lon", 3)
        ring = [(i, (i + 1) % n_lon) for i in range(n_lon)]
        return lax.ppermute(value, "lon", ring), lax.ppermute(value, "lon", [(b, a) for a, b in ring])

    predicted, packed, time_t = call(
        functools.partial(model_kernel, half),
        [shape((2 * days, wide)), shape((rank, wide), BF16), shape((rank, LANES))],
        [flip],
    )(surface, factor_time, pieces[1, 0])

    fresh, edge = shape((rank, wide)), shape((rank, LANES))
    surface, message, outgoing, edge_far, summed, seen = call(
        functools.partial(first_kernel, half, days, order, paired, swap),
        [fresh, shape((own_rows + COLS, LANES)), shape((own_rows + rank, LANES)), edge, shape((2 * days, wide)), shape((TAIL, LANES))],
        [flip, pltpu.VMEM((rank, wide), F32)],
    )(surface, edge_near, predicted, packed, time_t, *[pieces[key] for key in order], bands(edge_far), *(() if paired else columns(cols)))

    def add(mine, theirs):
        return call(add_kernel, shape(theirs.shape))(mine, theirs)

    def over_bands(total, last):
        step = 1
        while 2 * step < n_lat:
            total = add(total, across(total, "lat", step))
            step *= 2
        return last(total, across(total, "lat", step))

    def over_lon(total):
        if paired:
            return [total] + [across(total, "lon", step) for step in (1, 2, 3)]
        step = 1
        while step < n_lon:
            total = add(total, across(total, "lon", step))
            step *= 2
        return [total]

    total, edge_near = call(core_kernel, [shape((own_rows, LANES)), edge])(message, across(outgoing, "ta", 1))
    if paired:
        last = call(band_kernel, shape(message.shape))
        parts = over_lon(over_bands(total, lambda mine, theirs: last(mine, theirs, message)))
        cols = parts[1], parts[3]
    else:
        parts = over_lon(over_bands(total, add))
        cols = columns(message[own_rows:])
    time_own, norm = call(functools.partial(own_kernel, len(parts)), [edge, shape((NORM, LANES))])(time_t, *parts)

    surface, time_t, message, outgoing = call(
        functools.partial(second_kernel, half, counts, swap),
        [fresh, edge, shape((sum_rows, LANES)), shape((sum_rows, LANES))],
        [flip, pltpu.VMEM((rank, wide), F32), pltpu.VMEM((rank, wide), F32), pltpu.VMEM((2 * days, wide), F32), pltpu.VMEM((rank, wide), BF16)],
    )(surface, time_own, across(time_own, "ta", 1), norm, summed, seen, edge_near, bands(edge_far), *cols)

    total = add(message, across(outgoing, "ta", 1))
    other = across(surface, "ta", 1)
    narrow = call(functools.partial(narrow_kernel, rank), shape((sum_rows + NORM, LANES), BF16))
    parts = over_lon(over_bands(total, narrow if paired else add))
    space, time = call(
        functools.partial(last_kernel, half, counts, len(parts)),
        [shape((rank * height, cells)), shape(factor_time.shape)],
        [flip],
    )(surface, other, time_t, *parts)
    return space.reshape(rank, height, cells), time


def solution(mesh):
    in_specs = (
        P(("grp", "lon", "lat"), "ta", None),
        P(("grp", "lon", "lat"), "ta"),
        P(("grp", "lon", "lat")),
        P(("grp", "lon", "lat"), None, None),
        P(("grp", "lon", "lat"), None),
        P(None, ("grp", "lat"), "lon"),
        P(("grp", "ta"), None),
    )
    out_specs = (P(None, ("grp", "lat"), "lon"), P(("grp", "ta"), None))
    return jax.shard_map(shards, mesh=mesh, in_specs=in_specs, out_specs=out_specs, check_vma=False)
```

```python
import functools
import math

import jax
import jax.numpy as jnp
from jax import lax
from jax.experimental import pallas as pl
from jax.experimental.pallas import tpu as pltpu
from jax.sharding import PartitionSpec as P

SMOOTH = 2.0
ETA_SPACE = 0.08
RIDGE = 1.0
EPSILON = 1e-06

F32 = jnp.float32
BF16 = jnp.bfloat16
LANES = 128
TAIL = 16
COLS = 16
NORM = 8
SPARE = 2 * 1024 * 1024
SWATH_COPIES = 4


def dot(a, b, contract):
    return lax.dot_general(a, b, ((contract[:1], contract[1:]), ((), ())), preferred_element_type=F32)


def route_kernel(half, sends, paired, list_hbm, count_hbm, target_hbm, swath_hbm, mask_hbm, space_hbm, time_hbm, *rest):
    outs, rest = rest[: len(sends)], rest[len(sends):]
    surface, edge_near, edge_far, cols, rest = *rest[:4], rest[4:]
    list_ref, count_ref, target_ref, swath_ref, mask_ref, space_ref, time_ref, place, total, seen, flip, arrived = rest
    me, core = lax.axis_index("lon"), lax.axis_index("ta")
    n_lon = list_ref.shape[1]
    slots, days, cells = swath_ref.shape
    chunk = slots // SWATH_COPIES
    small = [(list_hbm, list_ref), (count_hbm, count_ref), (target_hbm, target_ref), (mask_hbm, mask_ref)]
    large = [(swath_hbm.at[pl.ds(at, chunk)], swath_ref.at[pl.ds(at, chunk)]) for at in range(0, slots, chunk)]
    model = [(space_hbm, space_ref), (time_hbm, time_ref)]
    copies = [pltpu.make_async_copy(src, dst, arrived.at[i]) for i, (src, dst) in enumerate(small + large + model)]
    for copy in copies:
        copy.start()
    total[...] = jnp.zeros(total.shape, F32)
    seen[...] = jnp.zeros(seen.shape, F32)
    for copy in copies[: len(small)]:
        copy.wait()

    def owner(d, carry):
        step = jnp.bitwise_xor(d, me)

        def entry(k, carry):
            slot = list_ref[0, d, k]
            row = target_ref[slot]
            far = jnp.bitwise_xor(lax.div(row, half), core)
            place[slot] = (far * n_lon + step) * half + lax.rem(row, half)
            return carry

        return lax.fori_loop(0, count_ref[0, d], entry, carry)

    lax.fori_loop(0, n_lon, owner, 0)
    mask = mask_ref[...].astype(F32)
    by_day = mask.T
    for slot in range(slots):
        if slot % chunk == 0:
            copies[len(small) + slot // chunk].wait()
        at = place[slot]
        total[at] += swath_ref[slot].astype(F32) * by_day[:, slot:slot + 1]
        seen[pl.ds(at, 1), :days] += mask[slot:slot + 1, :]
    for copy in copies[len(small) + len(large):]:
        copy.wait()
    rank = surface.shape[0]
    height = space_ref.shape[0] // rank
    for row in range(half):
        surface[:, row * LANES:(row + 1) * LANES] = space_ref[pl.ds(core * half + row, rank, stride=height), :]
    edge_near[...] = space_ref[pl.ds(half - core, rank, stride=height), :]
    edge_far[...] = space_ref[pl.ds(core * (height - 1), rank, stride=height), :]
    cols[...] = columns_as_rows(border(surface[...], half), flip)[:COLS, :]
    for (side, step), out in zip(sends, outs):
        at = (side * n_lon + step) * half
        end = half * days + TAIL
        out[: half * days, :] = total[at:at + half].reshape(half * days, cells).astype(BF16)
        out[half * days:end, :] = seen[at:at + TAIL, :].astype(BF16)
        if (side, step) == (1, 0):
            left = time_ref[...]
            for part in range(end, end + 3 * days, days):
                value = left.astype(BF16)
                out[part:part + days, :] = jnp.zeros((days, LANES), BF16)
                out[part:part + days, :rank] = value
                left = left - value.astype(F32)
        elif paired and side == 0 and step in (1, 3):
            out[end:, :] = cols[...].astype(BF16)


def row_of(surface, row):
    return surface[:, row * LANES:(row + 1) * LANES]


def columns_as_rows(columns, flip):
    rank = columns[0].shape[0]
    lane = lax.broadcasted_iota(jnp.int32, (rank, LANES), 1)
    block = jnp.zeros((rank, LANES), F32)
    for at, column in enumerate(columns):
        block = jnp.where(lane == at, column, block)
    flip[...] = jnp.zeros(flip.shape, F32)
    flip[:rank, :] = block
    return flip[...].T


def border(surface, half):
    strips = [row_of(surface, row) for row in range(half)]
    return [strip[:, :1] for strip in strips] + [strip[:, LANES - 1:] for strip in strips]


def rows_as_columns(rows, rank, flip):
    flip[...] = jnp.zeros(flip.shape, F32)
    flip[: rows.shape[0], :] = rows
    return flip[...].T[:rank, :]


def smoothed(surface, half, above, below, left_cols, right_cols):
    lane = lax.broadcasted_iota(jnp.int32, above.shape, 1)
    strips = []
    for row in range(half):
        here = row_of(surface, row)
        up = above if row == 0 else row_of(surface, row - 1)
        down = below if row == half - 1 else row_of(surface, row + 1)
        left = jnp.where(lane == 0, left_cols[:, half + row:half + row + 1], pltpu.roll(here, 1, 1))
        right = jnp.where(lane == LANES - 1, right_cols[:, row:row + 1], pltpu.roll(here, LANES - 1, 1))
        lap = 4.0 * here - (up + down + left + right)
        strips.append(here - (ETA_SPACE * SMOOTH) * lap)
    return strips


def pick(flag, a, b):
    return jnp.where(flag, a, b)


def model_kernel(half, surface, time_own, piece, predicted, packed, time_t, days_all):
    rank = surface.shape[0]
    days = time_own.shape[0]
    at = half * days + TAIL
    high, middle, low = (piece[first:first + days, :].astype(F32) for first in range(at, at + 3 * days, days))
    days_all[...] = jnp.zeros(days_all.shape, F32)
    days_all[:days, :rank] = time_own[...]
    days_all[days:, :] = (high + middle) + low
    time_full = days_all[...]
    time_t[...] = time_full.T[:rank, :]
    packed[...] = surface[...].astype(BF16)
    time_bf = time_full[:, :rank].astype(BF16)
    for at in range(0, half * LANES, 2 * LANES):
        predicted[:, at:at + 2 * LANES] = dot(time_bf, packed[:, at:at + 2 * LANES], (1, 0))


def smooth(half, odd, surface, edge_near, edge_far, cols_a, cols_b, scale, base, flip):
    core = lax.axis_index("ta")
    rank = surface.shape[0]
    above = pick(core == 0, edge_far, edge_near)
    below = pick(core == 0, edge_near, edge_far)
    left = rows_as_columns(pick(odd, cols_a, cols_b), rank, flip)
    right = rows_as_columns(pick(odd, cols_b, cols_a), rank, flip)
    if scale is not None:
        above, below, left, right = above * scale, below * scale, left * scale, right * scale
    for row, strip in enumerate(smoothed(surface, half, above, below, left, right)):
        base[:, row * LANES:(row + 1) * LANES] = strip


def gradients(half, base, predicted, packed, time_t, seen, summed, fresh):
    rank = time_t.shape[0]
    time_bf = time_t.astype(BF16)
    time_twice = jnp.concatenate([time_bf, time_bf], axis=1)
    seen_bf = seen.astype(BF16)
    width = 2 * LANES
    owner = lax.broadcasted_iota(jnp.int32, (TAIL, width), 0)
    lane = lax.broadcasted_iota(jnp.int32, (TAIL, width), 1)
    grad_time = jnp.zeros((rank, width), F32)
    grad_diag = jnp.zeros((rank, LANES), F32)
    norm = jnp.zeros((rank, 1), F32)
    for at in range(0, half * LANES, width):
        spread = (owner * LANES <= lane + at) & (lane + at < (owner + 1) * LANES)
        weight = dot(seen_bf, spread.astype(BF16), (0, 0))
        part = packed[:, at:at + width]
        residual = weight * predicted[:, at:at + width] - summed[:, at:at + width]
        high = residual.astype(BF16)
        low = (residual - high.astype(F32)).astype(BF16)
        both = jnp.concatenate([high, low], axis=0)
        grad_space = dot(time_twice, both, (1, 0))
        grad_time = grad_time + dot(part, both, (1, 1))
        new = base[:, at:at + width] - ETA_SPACE * grad_space
        fresh[:, at:at + width] = new
        norm = norm + jnp.sum(new * new, axis=1, keepdims=True)
        wide = part.astype(F32)
        for row in range(width // LANES):
            strip = row_of(wide, row)
            square = jnp.sum(strip * strip, axis=1, keepdims=True)
            grad_diag = grad_diag + square * seen[at // LANES + row:at // LANES + row + 1, :]
    return grad_time[:, :LANES] + grad_time[:, LANES:], grad_diag, norm


def post_own(half, sums, fresh, message, crossing, outgoing, edge_far, flip):
    grad_time, grad_diag, norm = sums
    core = lax.axis_index("ta")
    rank = norm.shape[0]
    days = LANES // 2
    own = lax.broadcasted_iota(jnp.int32, grad_time.shape, 1) < days
    last = columns_as_rows([norm] * NORM + border(fresh[...], half), flip)
    message[:rank, :] = jnp.where(own, grad_time, pltpu.roll(grad_diag, days, 1))
    message[rank:, :] = last[: NORM + COLS, :]
    for out in (crossing, outgoing):
        out[:rank, :] = jnp.where(own, pltpu.roll(grad_time, days, 1), grad_diag)
        out[rank:rank + NORM, :] = last[:NORM, :]
    first_row, last_row = fresh[:, :LANES], fresh[:, (half - 1) * LANES:]
    outgoing[rank + NORM:, :] = pick(core == 0, last_row, first_row)
    edge_far[...] = pick(core == 0, first_row, last_row)


def narrow(value, rank):
    high = value[2 * rank:, :].astype(BF16)
    low = (value[2 * rank:, :] - high.astype(F32)).astype(BF16)
    return value[: 2 * rank, :].astype(BF16), jnp.concatenate([high.astype(F32), low.astype(F32)], axis=0).astype(BF16)


def widened(value, rank):
    value = value.astype(F32)
    return jnp.concatenate([value[: 2 * rank, :], value[2 * rank:2 * rank + NORM, :] + value[2 * rank + NORM:, :]], axis=0)


def post_all(sums, message, outgoing, flip):
    grad_time, grad_diag, norm = sums
    rank = norm.shape[0]
    last = columns_as_rows([norm], flip)[:NORM, :]
    for out, shift in ((message, 0), (outgoing, LANES // 2)):
        parts = [pltpu.roll(part, shift, 1) if shift else part for part in (grad_time, grad_diag)]
        out[: 2 * rank, :], out[2 * rank:, :] = narrow(jnp.concatenate([*parts, last], axis=0), rank)


def first_kernel(half, days, order, paired, swap, surface, edge_near, predicted, packed, time_t, *rest):
    pieces, rest = dict(zip(order, rest)), rest[len(order):]
    edge_far_in, rest = rest[0], rest[1:]
    if paired:
        at = half * days + TAIL
        cols = [pieces[0, step][at:, :].astype(F32) for step in (1, 3)]
    else:
        cols, rest = [ref[...] for ref in rest[:2]], rest[2:]
    fresh, message, crossing, outgoing, edge_far, summed, seen, flip, base = rest
    smooth(half, swap(), surface[...], edge_near[...], edge_far_in[...], *cols, None, base, flip)
    sides = [[pieces[key] for key in sorted(pieces) if key[0] == side] for side in (0, 1)]

    def add_up(parts, rows):
        value = parts[0][rows, :].astype(F32)
        for piece in parts[1:]:
            value = value + piece[rows, :].astype(F32)
        return value

    for row in range(half):
        for first, parts in zip((0, days), sides):
            summed[first:first + days, row * LANES:(row + 1) * LANES] = add_up(parts, slice(row * days, (row + 1) * days))
    near, far = (add_up(parts, slice(half * days, half * days + TAIL)) for parts in sides)
    seen[...] = near + pltpu.roll(far, days, 1)
    sums = gradients(half, base, predicted, packed, time_t[...], seen[...], summed, fresh)
    post_own(half, sums, fresh, message, crossing, outgoing, edge_far, flip)


def total_of(parts):
    total = parts[0][...].astype(F32)
    if len(parts) > 1:
        one, two, three = (part[...].astype(F32) for part in parts[1:])
        total = (total + one) + (two + three)
    return total


def own_kernel(n_parts, time_t, *rest):
    parts, (time_own, norm) = rest[:n_parts], rest[n_parts:]
    rank = time_t.shape[0]
    days = LANES // 2
    total = total_of(parts)
    block = total[:rank, :]
    own = lax.broadcasted_iota(jnp.int32, block.shape, 1) < days
    time_own[...] = jnp.where(own, time_t[...] - block / (pltpu.roll(block, days, 1) + RIDGE), 0.0)
    norm[...] = total[rank:rank + NORM, :]


def rescaling(counts, norm, time_new, flip):
    day_count, cell_count = counts
    space_sq = rows_as_columns(norm, time_new.shape[0], flip)[:, :1]
    square = time_new * time_new
    time_sq = 0.5 * jnp.sum(square + pltpu.roll(square, LANES // 2, 1), axis=1, keepdims=True)
    ratio = (time_sq / day_count + EPSILON) / (space_sq / cell_count + EPSILON)
    return jnp.sqrt(jnp.sqrt(ratio))


def second_kernel(half, counts, swap, surface, time_own, time_other, norm, summed, seen, edge_near, edge_far, cols_a, cols_b, *rest):
    fresh, time_out, message, outgoing, flip, scaled, base, predicted, packed = rest
    rank = surface.shape[0]
    time_new = time_own[...] + pltpu.roll(time_other[...], LANES // 2, 1)
    scale = rescaling(counts, norm[...], time_new, flip)
    time_now = time_new / scale
    time_out[...] = time_now
    scaled[...] = surface[...] * scale
    packed[...] = scaled[...].astype(BF16)
    time_bf = time_now.T.astype(BF16)
    for at in range(0, half * LANES, 2 * LANES):
        predicted[:, at:at + 2 * LANES] = dot(time_bf, packed[:, at:at + 2 * LANES], (1, 0))
    cols = [ref[ref.shape[0] - COLS:, :] for ref in (cols_a, cols_b)]
    smooth(half, swap(), scaled[...], edge_near[...], edge_far[...], *cols, scale, base, flip)
    sums = gradients(half, base, predicted, packed, time_now, seen[...], summed, fresh)
    post_all(sums, message, outgoing, flip)


def last_kernel(half, counts, n_parts, surface, other, time_t, *rest):
    parts = rest[:n_parts]
    space_out, time_out, flip = rest[n_parts:]
    core = lax.axis_index("ta")
    rank = surface.shape[0]
    height = space_out.shape[0] // rank
    total = total_of(parts)
    if parts[0].dtype == BF16:
        total = widened(total, rank)
    time_new = time_t[...] - total[:rank, :] / (total[rank:2 * rank, :] + RIDGE)
    scale = rescaling(counts, total[2 * rank:, :], time_new, flip)
    flip[...] = jnp.zeros(flip.shape, F32)
    flip[:rank, :] = time_new / scale
    time_out[...] = flip[...].T[: time_out.shape[0], :rank]
    for row in range(half):
        at = row * LANES
        space_out[pl.ds(core * half + row, rank, stride=height), :] = surface[:, at:at + LANES] * scale
        space_out[pl.ds((1 - core) * half + row, rank, stride=height), :] = other[:, at:at + LANES] * scale


def merge_kernel(mine, theirs, piece_in, edge_in, out, piece_out, edge_out):
    piece_out[...] = piece_in[...]
    edge_out[...] = edge_in[...]
    out[...] = (mine[...].astype(F32) + theirs[...].astype(F32)).astype(BF16)


def add_kernel(mine, theirs, total):
    total[...] = mine[...] + theirs[...]


def own_sum_kernel(mine, core, band, both, total, beside):
    rows = both.shape[0]
    total[:rows, :] = (mine[:rows, :] + core[:rows, :]) + (band[:rows, :] + both[...])
    total[rows:, :] = mine[rows:, :]
    beside[...] = core[rows:, :]


def all_sum_kernel(rank, mine, core, band, both, total):
    one, two, three, four = (widened(part[...], rank) for part in (mine, core, band, both))
    value = (one + two) + (three + four)
    if total.dtype == BF16:
        total[: 2 * rank, :], total[2 * rank:, :] = narrow(value, rank)
    else:
        total[...] = value


def shape(dims, dtype=F32):
    return jax.ShapeDtypeStruct(tuple(dims), dtype)


def padded(ref):
    *outer, rows, lanes = (1, *ref.shape)
    return math.prod(outer) * -(-rows // 16) * 16 * -(-lanes // LANES) * LANES * jnp.dtype(ref.dtype).itemsize


def call(kernel, out_shape, scratch=(), hbm=0, after=0, flops=1_000_000):
    def run(*operands):
        operands = [pltpu.with_memory_space_constraint(x, pltpu.HBM) if i < hbm else x for i, x in enumerate(operands)]
        vmem = [*operands[hbm:len(operands) - after], *jax.tree.leaves(out_shape), *scratch]
        specs = [pltpu.HBM] * hbm + [pltpu.VMEM] * (len(operands) - hbm - after) + [pl.ANY] * after
        return pl.pallas_call(
            kernel,
            out_shape=out_shape,
            in_specs=[pl.BlockSpec(memory_space=space) for space in specs],
            out_specs=jax.tree.map(lambda _: pl.BlockSpec(memory_space=pltpu.VMEM), out_shape),
            scratch_shapes=list(scratch),
            compiler_params=pltpu.CompilerParams(vmem_limit_bytes=SPARE + sum(padded(ref) for ref in vmem if len(ref.shape) > 1)),
            cost_estimate=pl.CostEstimate(flops=flops, bytes_accessed=1_000_000, transcendentals=0),
        )(*operands)

    return run


def across(value, axis, step):
    return lax.ppermute(value, axis, [(i, i ^ step) for i in range(lax.axis_size(axis))])


def shards(swath, obs_mask, target, send_list, send_count, factor_space, factor_time):
    n_lon, n_lat, n_ta = (lax.axis_size(axis) for axis in ("lon", "lat", "ta"))
    slots, days, cells = swath.shape
    rank, height, _ = factor_space.shape
    half = height // n_ta
    wide = half * LANES
    counts = (float(days * n_ta), float(height * cells * n_lon * n_lat))
    own_rows, sum_rows = rank + NORM, 2 * rank + NORM
    flip = pltpu.VMEM((LANES, LANES), F32)

    paired = n_lon == 4

    distant, close = range(n_lon // 2, n_lon), range(1, n_lon // 2)
    sends = [(1, step) for step in reversed(distant)] + [(0, step) for step in distant] + [(1, 0)]
    sends += [(side, step) for side in (0, 1) for step in close] + [(0, 0)]

    def piece_rows(side, step):
        more = 3 * days if (side, step) == (1, 0) else COLS if paired and side == 0 and step in (1, 3) else 0
        return half * days + TAIL + more

    operands = (send_list, send_count, target, swath, obs_mask, factor_space.reshape(rank * height, cells), factor_time)
    *pieces, surface, edge_near, edge_far, cols = call(
        functools.partial(route_kernel, half, sends, paired),
        [shape((piece_rows(*key), cells), BF16) for key in sends]
        + [shape((rank, wide)), shape((rank, LANES)), shape((rank, LANES)), shape((COLS, LANES))],
        [pltpu.SMEM(ref.shape, jnp.int32) for ref in operands[:3]]
        + [pltpu.VMEM(ref.shape, ref.dtype) for ref in operands[3:]]
        + [
            pltpu.SMEM((slots,), jnp.int32),
            pltpu.VMEM((2 * n_lon * half, days, cells), F32),
            pltpu.VMEM((2 * n_lon * half + TAIL, LANES), F32),
            flip,
            pltpu.SemaphoreType.DMA((len(operands) - 1 + SWATH_COPIES,)),
        ],
        hbm=len(operands),
    )(*operands)

    def arrived(key, piece):
        side, step = key
        if side:
            return across(piece, ("lon", "ta"), 2 * step + 1)
        return across(piece, "lon", step) if step else piece

    pieces = dict(zip(sends, pieces))
    if paired:
        passing = across(pieces.pop((1, 3)), "lon", 1)
        outs = [shape(passing.shape, BF16), shape(passing.shape, BF16), shape(edge_far.shape)]
        pieces[1, 2], pieces[1, 1], edge_far = call(merge_kernel, outs)(pieces[1, 2], passing, pieces[1, 1], edge_far)
    pieces = {key: arrived(key, piece) for key, piece in pieces.items()}
    order = list(pieces)

    def bands(edge):
        there = [(2 * band + 1, 2 * band + 2) for band in range(n_lat - 1)]
        return lax.ppermute(edge, ("lat", "ta"), there + [(b, a) for a, b in there])

    def swap():
        return lax.rem(lax.axis_index("lon"), 2) == 1 if paired else jnp.bool_(True)

    def columns(value):
        if paired:
            return across(value, "lon", 1), across(value, "lon", 3)
        ring = [(i, (i + 1) % n_lon) for i in range(n_lon)]
        return lax.ppermute(value, "lon", ring), lax.ppermute(value, "lon", [(b, a) for a, b in ring])

    predicted, packed, time_t = call(
        functools.partial(model_kernel, half),
        [shape((2 * days, wide)), shape((rank, wide), BF16), shape((rank, LANES))],
        [flip],
    )(surface, factor_time, pieces[1, 0])

    fresh, edge = shape((rank, wide)), shape((rank, LANES))
    surface, message, crossing, outgoing, edge_far, summed, seen = call(
        functools.partial(first_kernel, half, days, order, paired, swap),
        [fresh, shape((own_rows + COLS, LANES)), shape((own_rows, LANES)), shape((own_rows + rank, LANES)), edge, shape((2 * days, wide)), shape((TAIL, LANES))],
        [flip, pltpu.VMEM((rank, wide), F32)],
    )(surface, edge_near, predicted, packed, time_t, *[pieces[key] for key in order], bands(edge_far), *(() if paired else columns(cols)))

    narrowed = shape((sum_rows + NORM, LANES), BF16)

    def add(mine, theirs):
        return call(add_kernel, shape(mine.shape))(mine, theirs)

    def doubled(total, axis, step):
        while step < lax.axis_size(axis):
            total = add(total, across(total, axis, step))
            step *= 2
        return total

    def over_lon(total):
        if paired:
            return [total] + [across(total, "lon", step) for step in (1, 2, 3)]
        return [doubled(total, "lon", 1)]

    def around(mine, core, both):
        return mine, across(core, "ta", 1), across(mine, "lat", 1), across(both, ("lat", "ta"), 3)

    total, edge_near = call(own_sum_kernel, [shape(message.shape), edge])(*around(message, outgoing, crossing))
    parts = over_lon(doubled(total, "lat", 2))
    cols = (parts[1], parts[3]) if paired else columns(message[own_rows:])
    time_own, norm = call(functools.partial(own_kernel, len(parts)), [edge, shape((NORM, LANES))])(time_t, *parts)

    surface, time_t, message, outgoing = call(
        functools.partial(second_kernel, half, counts, swap),
        [fresh, edge, narrowed, narrowed],
        [flip, pltpu.VMEM((rank, wide), F32), pltpu.VMEM((rank, wide), F32), pltpu.VMEM((2 * days, wide), F32), pltpu.VMEM((rank, wide), BF16)],
    )(surface, time_own, across(time_own, "ta", 1), norm, summed, seen, edge_near, bands(edge_far), *cols)

    other = across(surface, "ta", 1)
    total = narrowed if paired and n_lat == 2 else shape((sum_rows, LANES))
    total = call(functools.partial(all_sum_kernel, rank), total)(*around(message, outgoing, outgoing))
    parts = over_lon(doubled(total, "lat", 2))
    space, time = call(
        functools.partial(last_kernel, half, counts, len(parts)),
        [shape((rank * height, cells)), shape(factor_time.shape)],
        [flip],
    )(surface, other, time_t, *parts)
    return space.reshape(rank, height, cells), time


def solution(mesh):
    in_specs = (
        P(("grp", "lon", "lat"), "ta", None),
        P(("grp", "lon", "lat"), "ta"),
        P(("grp", "lon", "lat")),
        P(("grp", "lon", "lat"), None, None),
        P(("grp", "lon", "lat"), None),
        P(None, ("grp", "lat"), "lon"),
        P(("grp", "ta"), None),
    )
    out_specs = (P(None, ("grp", "lat"), "lon"), P(("grp", "ta"), None))
    return jax.shard_map(shards, mesh=mesh, in_specs=in_specs, out_specs=out_specs, check_vma=False)
```

```python
import functools
import math

import jax
import jax.numpy as jnp
from jax import lax
from jax.experimental import pallas as pl
from jax.experimental.pallas import tpu as pltpu
from jax.sharding import PartitionSpec as P

SMOOTH = 2.0
ETA_SPACE = 0.08
RIDGE = 1.0
EPSILON = 1e-06

F32 = jnp.float32
BF16 = jnp.bfloat16
LANES = 128
TAIL = 16
COLS = 16
NORM = 8
SPARE = 2 * 1024 * 1024
SWATH_COPIES = 1
UNROLL = 4


def dot(a, b, contract):
    return lax.dot_general(a, b, ((contract[:1], contract[1:]), ((), ())), preferred_element_type=F32)


def route_kernel(half, sends, paired, list_hbm, count_hbm, target_hbm, swath_hbm, mask_hbm, space_hbm, time_hbm, *rest):
    outs, rest = rest[: len(sends)], rest[len(sends):]
    surface, edge_near, edge_far, cols, rest = *rest[:4], rest[4:]
    list_ref, count_ref, target_ref, swath_ref, mask_ref, space_ref, time_ref, place, total, seen, flip, arrived = rest
    me, core = lax.axis_index("lon"), lax.axis_index("ta")
    n_lon = list_ref.shape[1]
    slots, days, cells = swath_ref.shape
    chunk = slots // SWATH_COPIES
    small = [(list_hbm, list_ref), (count_hbm, count_ref), (target_hbm, target_ref), (mask_hbm, mask_ref)]
    large = [(swath_hbm.at[pl.ds(at, chunk)], swath_ref.at[pl.ds(at, chunk)]) for at in range(0, slots, chunk)]
    model = [(space_hbm, space_ref), (time_hbm, time_ref)]
    copies = [pltpu.make_async_copy(src, dst, arrived.at[i]) for i, (src, dst) in enumerate(small + large + model)]
    for copy in copies:
        copy.start()
    total[...] = jnp.zeros(total.shape, F32)
    seen[...] = jnp.zeros(seen.shape, F32)
    for copy in copies[: len(small)]:
        copy.wait()

    def owner(d, carry):
        first = jnp.bitwise_xor(d, me) * half
        count = count_ref[0, d]

        def entries(i, carry):
            for k in range(UNROLL):
                k = i * UNROLL + k
                slot = list_ref[0, d, k]
                row = target_ref[slot]
                far = jnp.bitwise_xor(lax.shift_right_logical(row, half.bit_length() - 1), core)
                place[jnp.where(k < count, slot, slots)] = far * (n_lon * half) + first + jnp.bitwise_and(row, half - 1)
            return carry

        return lax.fori_loop(0, lax.div(count + UNROLL - 1, UNROLL), entries, carry)

    lax.fori_loop(0, n_lon, owner, 0)
    mask = mask_ref[...].astype(F32)
    by_day = mask.T.astype(BF16)
    for slot in range(slots):
        if slot % chunk == 0:
            copies[len(small) + slot // chunk].wait()
        at = place[slot]
        total[at] += (swath_ref[slot] * by_day[:, slot:slot + 1]).astype(F32)
        seen[pl.ds(at, 1), :days] += mask[slot:slot + 1, :]
    for copy in copies[len(small) + len(large):]:
        copy.wait()
    rank = surface.shape[0]
    height = space_ref.shape[0] // rank
    for row in range(half):
        surface[:, row * LANES:(row + 1) * LANES] = space_ref[pl.ds(core * half + row, rank, stride=height), :]
    edge_near[...] = space_ref[pl.ds(half - core, rank, stride=height), :]
    edge_far[...] = space_ref[pl.ds(core * (height - 1), rank, stride=height), :]
    cols[...] = jnp.zeros(cols.shape, F32)
    cols[:, :rank] = border(surface[...], half)
    for (side, step), out in zip(sends, outs):
        at = (side * n_lon + step) * half
        end = half * days + TAIL
        out[: half * days, :] = total[at:at + half].reshape(half * days, cells).astype(BF16)
        out[half * days:end, :] = seen[at:at + TAIL, :].astype(BF16)
        if (side, step) == (1, 0):
            left = time_ref[...]
            for part in range(end, end + 3 * days, days):
                value = left.astype(BF16)
                out[part:part + days, :] = jnp.zeros((days, LANES), BF16)
                out[part:part + days, :rank] = value
                left = left - value.astype(F32)
        elif paired and side == 0 and step in (1, 3):
            out[end:, :] = cols[...].astype(BF16)


def row_of(surface, row):
    return surface[:, row * LANES:(row + 1) * LANES]


def column_as_row(column, flip):
    rank = column.shape[0]
    flip[...] = jnp.zeros(flip.shape, F32)
    flip[:rank, :] = jnp.broadcast_to(column, (rank, LANES))
    return flip[...].T[:NORM, :]


def border(surface, half):
    line = lax.broadcasted_iota(jnp.int32, (COLS, half * LANES), 0)
    lane = lax.broadcasted_iota(jnp.int32, (COLS, half * LANES), 1)
    pick_lane = jnp.where(line < half, line * LANES, (line - half) * LANES + LANES - 1)
    return dot((lane == pick_lane).astype(BF16), surface.astype(BF16), (1, 1))


def rows_as_columns(rows, rank, flip):
    flip[...] = jnp.zeros(flip.shape, F32)
    flip[: rows.shape[0], :] = rows
    return flip[...].T[:rank, :]


def smoothed(surface, half, above, below, left_cols, right_cols):
    lane = lax.broadcasted_iota(jnp.int32, above.shape, 1)
    strips = []
    for row in range(half):
        here = row_of(surface, row)
        up = above if row == 0 else row_of(surface, row - 1)
        down = below if row == half - 1 else row_of(surface, row + 1)
        left = jnp.where(lane == 0, left_cols[:, half + row:half + row + 1], pltpu.roll(here, 1, 1))
        right = jnp.where(lane == LANES - 1, right_cols[:, row:row + 1], pltpu.roll(here, LANES - 1, 1))
        lap = 4.0 * here - (up + down + left + right)
        strips.append(here - (ETA_SPACE * SMOOTH) * lap)
    return strips


def pick(flag, a, b):
    return jnp.where(flag, a, b)


def model_kernel(half, surface, time_own, piece, predicted, packed, time_t, days_all):
    rank = surface.shape[0]
    days = time_own.shape[0]
    at = half * days + TAIL
    high, middle, low = (piece[first:first + days, :].astype(F32) for first in range(at, at + 3 * days, days))
    days_all[...] = jnp.zeros(days_all.shape, F32)
    days_all[:days, :rank] = time_own[...]
    days_all[days:, :] = (high + middle) + low
    time_full = days_all[...]
    time_t[...] = time_full.T[:rank, :]
    packed[...] = surface[...].astype(BF16)
    time_bf = time_full[:, :rank].astype(BF16)
    for at in range(0, half * LANES, 2 * LANES):
        predicted[:, at:at + 2 * LANES] = dot(time_bf, packed[:, at:at + 2 * LANES], (1, 0))


def smooth(half, odd, surface, edge_near, edge_far, cols_a, cols_b, scale, base, flip):
    core = lax.axis_index("ta")
    rank = surface.shape[0]
    above = pick(core == 0, edge_far, edge_near)
    below = pick(core == 0, edge_near, edge_far)
    left = rows_as_columns(pick(odd, cols_a, cols_b), rank, flip)
    right = rows_as_columns(pick(odd, cols_b, cols_a), rank, flip)
    if scale is not None:
        above, below, left, right = above * scale, below * scale, left * scale, right * scale
    for row, strip in enumerate(smoothed(surface, half, above, below, left, right)):
        base[:, row * LANES:(row + 1) * LANES] = strip


def gradients(half, base, predicted, packed, time_t, seen, summed, fresh):
    rank = time_t.shape[0]
    time_bf = time_t.astype(BF16)
    time_twice = jnp.concatenate([time_bf, time_bf], axis=1)
    seen_bf = seen.astype(BF16)
    width = 2 * LANES
    owner = lax.broadcasted_iota(jnp.int32, (TAIL, width), 0)
    lane = lax.broadcasted_iota(jnp.int32, (TAIL, width), 1)
    grad_time = jnp.zeros((rank, width), F32)
    grad_diag = jnp.zeros((rank, LANES), F32)
    norm = jnp.zeros((rank, 1), F32)
    for at in range(0, half * LANES, width):
        spread = (owner * LANES <= lane + at) & (lane + at < (owner + 1) * LANES)
        weight = dot(seen_bf, spread.astype(BF16), (0, 0))
        part = packed[:, at:at + width]
        residual = weight * predicted[:, at:at + width] - summed[:, at:at + width]
        high = residual.astype(BF16)
        low = (residual - high.astype(F32)).astype(BF16)
        both = jnp.concatenate([high, low], axis=0)
        grad_space = dot(time_twice, both, (1, 0))
        grad_time = grad_time + dot(part, both, (1, 1))
        new = base[:, at:at + width] - ETA_SPACE * grad_space
        fresh[:, at:at + width] = new
        norm = norm + jnp.sum(new * new, axis=1, keepdims=True)
        wide = part.astype(F32)
        for row in range(width // LANES):
            strip = row_of(wide, row)
            square = jnp.sum(strip * strip, axis=1, keepdims=True)
            grad_diag = grad_diag + square * seen[at // LANES + row:at // LANES + row + 1, :]
    return grad_time[:, :LANES] + grad_time[:, LANES:], grad_diag, norm


def post_own(half, sums, fresh, message, crossing, outgoing, edge_far, flip):
    grad_time, grad_diag, norm = sums
    core = lax.axis_index("ta")
    rank = norm.shape[0]
    days = LANES // 2
    own = lax.broadcasted_iota(jnp.int32, grad_time.shape, 1) < days
    last = column_as_row(norm, flip)
    message[:rank, :] = jnp.where(own, grad_time, pltpu.roll(grad_diag, days, 1))
    message[rank:rank + NORM, :] = last
    message[rank + NORM:, :] = jnp.zeros((COLS, LANES), F32)
    message[rank + NORM:, :rank] = border(fresh[...], half)
    for out in (crossing, outgoing):
        out[:rank, :] = jnp.where(own, pltpu.roll(grad_time, days, 1), grad_diag)
        out[rank:rank + NORM, :] = last
    first_row, last_row = fresh[:, :LANES], fresh[:, (half - 1) * LANES:]
    outgoing[rank + NORM:, :] = pick(core == 0, last_row, first_row)
    edge_far[...] = pick(core == 0, first_row, last_row)


def narrow(value, rank):
    high = value[2 * rank:, :].astype(BF16)
    low = (value[2 * rank:, :] - high.astype(F32)).astype(BF16)
    return value[: 2 * rank, :].astype(BF16), jnp.concatenate([high.astype(F32), low.astype(F32)], axis=0).astype(BF16)


def widened(value, rank):
    value = value.astype(F32)
    return jnp.concatenate([value[: 2 * rank, :], value[2 * rank:2 * rank + NORM, :] + value[2 * rank + NORM:, :]], axis=0)


def post_all(sums, message, outgoing, flip):
    grad_time, grad_diag, norm = sums
    rank = norm.shape[0]
    last = column_as_row(norm, flip)
    for out, shift in ((message, 0), (outgoing, LANES // 2)):
        parts = [pltpu.roll(part, shift, 1) if shift else part for part in (grad_time, grad_diag)]
        out[: 2 * rank, :], out[2 * rank:, :] = narrow(jnp.concatenate([*parts, last], axis=0), rank)


def first_kernel(half, days, order, paired, swap, surface, edge_near, predicted, packed, time_t, *rest):
    pieces, rest = dict(zip(order, rest)), rest[len(order):]
    edge_far_in, rest = rest[0], rest[1:]
    if paired:
        at = half * days + TAIL
        cols = [pieces[0, step][at:, :].astype(F32) for step in (1, 3)]
    else:
        cols, rest = [ref[...] for ref in rest[:2]], rest[2:]
    fresh, message, crossing, outgoing, edge_far, summed, seen, flip, base = rest
    smooth(half, swap(), surface[...], edge_near[...], edge_far_in[...], *cols, None, base, flip)
    sides = [[pieces[key] for key in sorted(pieces) if key[0] == side] for side in (0, 1)]

    def add_up(parts, rows):
        value = parts[0][rows, :].astype(F32)
        for piece in parts[1:]:
            value = value + piece[rows, :].astype(F32)
        return value

    for row in range(half):
        for first, parts in zip((0, days), sides):
            summed[first:first + days, row * LANES:(row + 1) * LANES] = add_up(parts, slice(row * days, (row + 1) * days))
    near, far = (add_up(parts, slice(half * days, half * days + TAIL)) for parts in sides)
    seen[...] = near + pltpu.roll(far, days, 1)
    sums = gradients(half, base, predicted, packed, time_t[...], seen[...], summed, fresh)
    post_own(half, sums, fresh, message, crossing, outgoing, edge_far, flip)


def total_of(parts):
    total = parts[0][...].astype(F32)
    if len(parts) > 1:
        one, two, three = (part[...].astype(F32) for part in parts[1:])
        total = (total + one) + (two + three)
    return total


def own_kernel(n_parts, time_t, *rest):
    parts, (time_own, norm) = rest[:n_parts], rest[n_parts:]
    rank = time_t.shape[0]
    days = LANES // 2
    total = total_of(parts)
    block = total[:rank, :]
    own = lax.broadcasted_iota(jnp.int32, block.shape, 1) < days
    time_own[...] = jnp.where(own, time_t[...] - block / (pltpu.roll(block, days, 1) + RIDGE), 0.0)
    norm[...] = total[rank:rank + NORM, :]


def rescaling(counts, norm, time_new, flip):
    day_count, cell_count = counts
    space_sq = rows_as_columns(norm, time_new.shape[0], flip)[:, :1]
    square = time_new * time_new
    time_sq = 0.5 * jnp.sum(square + pltpu.roll(square, LANES // 2, 1), axis=1, keepdims=True)
    ratio = (time_sq / day_count + EPSILON) / (space_sq / cell_count + EPSILON)
    return jnp.sqrt(jnp.sqrt(ratio))


def second_kernel(half, counts, swap, surface, time_own, time_other, norm, summed, seen, edge_near, edge_far, cols_a, cols_b, *rest):
    fresh, time_out, message, outgoing, flip, scaled, base, predicted, packed = rest
    rank = surface.shape[0]
    time_new = time_own[...] + pltpu.roll(time_other[...], LANES // 2, 1)
    scale = rescaling(counts, norm[...], time_new, flip)
    time_now = time_new / scale
    time_out[...] = time_now
    scaled[...] = surface[...] * scale
    packed[...] = scaled[...].astype(BF16)
    time_bf = time_now.T.astype(BF16)
    for at in range(0, half * LANES, 2 * LANES):
        predicted[:, at:at + 2 * LANES] = dot(time_bf, packed[:, at:at + 2 * LANES], (1, 0))
    cols = [ref[ref.shape[0] - COLS:, :] for ref in (cols_a, cols_b)]
    smooth(half, swap(), scaled[...], edge_near[...], edge_far[...], *cols, scale, base, flip)
    sums = gradients(half, base, predicted, packed, time_now, seen[...], summed, fresh)
    post_all(sums, message, outgoing, flip)


def last_kernel(half, counts, n_parts, surface, other, time_t, *rest):
    parts = rest[:n_parts]
    space_out, time_out, flip = rest[n_parts:]
    core = lax.axis_index("ta")
    rank = surface.shape[0]
    height = space_out.shape[0] // rank
    total = total_of(parts)
    if parts[0].dtype == BF16:
        total = widened(total, rank)
    time_new = time_t[...] - total[:rank, :] / (total[rank:2 * rank, :] + RIDGE)
    scale = rescaling(counts, total[2 * rank:, :], time_new, flip)
    flip[...] = jnp.zeros(flip.shape, F32)
    flip[:rank, :] = time_new / scale
    time_out[...] = flip[...].T[: time_out.shape[0], :rank]
    for row in range(half):
        at = row * LANES
        space_out[pl.ds(core * half + row, rank, stride=height), :] = surface[:, at:at + LANES] * scale
        space_out[pl.ds((1 - core) * half + row, rank, stride=height), :] = other[:, at:at + LANES] * scale


def merge_kernel(mine, theirs, piece_in, edge_in, out, piece_out, edge_out):
    piece_out[...] = piece_in[...]
    edge_out[...] = edge_in[...]
    out[...] = (mine[...].astype(F32) + theirs[...].astype(F32)).astype(BF16)


def add_kernel(mine, theirs, total):
    total[...] = mine[...] + theirs[...]


def own_sum_kernel(mine, core, band, both, total, beside):
    rows = both.shape[0]
    total[:rows, :] = (mine[:rows, :] + core[:rows, :]) + (band[:rows, :] + both[...])
    total[rows:, :] = mine[rows:, :]
    beside[...] = core[rows:, :]


def all_sum_kernel(rank, mine, core, band, both, total):
    one, two, three, four = (widened(part[...], rank) for part in (mine, core, band, both))
    value = (one + two) + (three + four)
    if total.dtype == BF16:
        total[: 2 * rank, :], total[2 * rank:, :] = narrow(value, rank)
    else:
        total[...] = value


def shape(dims, dtype=F32):
    return jax.ShapeDtypeStruct(tuple(dims), dtype)


def padded(ref):
    *outer, rows, lanes = (1, *ref.shape)
    return math.prod(outer) * -(-rows // 16) * 16 * -(-lanes // LANES) * LANES * jnp.dtype(ref.dtype).itemsize


def call(kernel, out_shape, scratch=(), hbm=0, after=0, flops=1_000_000):
    def run(*operands):
        operands = [pltpu.with_memory_space_constraint(x, pltpu.HBM) if i < hbm else x for i, x in enumerate(operands)]
        vmem = [*operands[hbm:len(operands) - after], *jax.tree.leaves(out_shape), *scratch]
        specs = [pltpu.HBM] * hbm + [pltpu.VMEM] * (len(operands) - hbm - after) + [pl.ANY] * after
        return pl.pallas_call(
            kernel,
            out_shape=out_shape,
            in_specs=[pl.BlockSpec(memory_space=space) for space in specs],
            out_specs=jax.tree.map(lambda _: pl.BlockSpec(memory_space=pltpu.VMEM), out_shape),
            scratch_shapes=list(scratch),
            compiler_params=pltpu.CompilerParams(vmem_limit_bytes=SPARE + sum(padded(ref) for ref in vmem if len(ref.shape) > 1)),
            cost_estimate=pl.CostEstimate(flops=flops, bytes_accessed=1_000_000, transcendentals=0),
        )(*operands)

    return run


def across(value, axis, step):
    return lax.ppermute(value, axis, [(i, i ^ step) for i in range(lax.axis_size(axis))])


def shards(swath, obs_mask, target, send_list, send_count, factor_space, factor_time):
    n_lon, n_lat, n_ta = (lax.axis_size(axis) for axis in ("lon", "lat", "ta"))
    slots, days, cells = swath.shape
    rank, height, _ = factor_space.shape
    half = height // n_ta
    wide = half * LANES
    counts = (float(days * n_ta), float(height * cells * n_lon * n_lat))
    own_rows, sum_rows = rank + NORM, 2 * rank + NORM
    flip = pltpu.VMEM((LANES, LANES), F32)

    paired = n_lon == 4

    distant, close = range(n_lon // 2, n_lon), range(1, n_lon // 2)
    sends = [(1, step) for step in reversed(distant)] + [(0, step) for step in distant] + [(1, 0)]
    sends += [(side, step) for side in (0, 1) for step in close] + [(0, 0)]

    def piece_rows(side, step):
        more = 3 * days if (side, step) == (1, 0) else COLS if paired and side == 0 and step in (1, 3) else 0
        return half * days + TAIL + more

    operands = (send_list, send_count, target, swath, obs_mask, factor_space.reshape(rank * height, cells), factor_time)
    *pieces, surface, edge_near, edge_far, cols = call(
        functools.partial(route_kernel, half, sends, paired),
        [shape((piece_rows(*key), cells), BF16) for key in sends]
        + [shape((rank, wide)), shape((rank, LANES)), shape((rank, LANES)), shape((COLS, LANES))],
        [pltpu.SMEM(ref.shape, jnp.int32) for ref in operands[:3]]
        + [pltpu.VMEM(ref.shape, ref.dtype) for ref in operands[3:]]
        + [
            pltpu.SMEM((slots + 1,), jnp.int32),
            pltpu.VMEM((2 * n_lon * half, days, cells), F32),
            pltpu.VMEM((2 * n_lon * half + TAIL, LANES), F32),
            flip,
            pltpu.SemaphoreType.DMA((len(operands) - 1 + SWATH_COPIES,)),
        ],
        hbm=len(operands),
    )(*operands)

    def arrived(key, piece):
        side, step = key
        if side:
            return across(piece, ("lon", "ta"), 2 * step + 1)
        return across(piece, "lon", step) if step else piece

    pieces = dict(zip(sends, pieces))
    if paired:
        passing = across(pieces.pop((1, 3)), "lon", 1)
        outs = [shape(passing.shape, BF16), shape(passing.shape, BF16), shape(edge_far.shape)]
        pieces[1, 2], pieces[1, 1], edge_far = call(merge_kernel, outs)(pieces[1, 2], passing, pieces[1, 1], edge_far)
    pieces = {key: arrived(key, piece) for key, piece in pieces.items()}
    order = list(pieces)

    def bands(edge):
        there = [(2 * band + 1, 2 * band + 2) for band in range(n_lat - 1)]
        return lax.ppermute(edge, ("lat", "ta"), there + [(b, a) for a, b in there])

    def swap():
        return lax.rem(lax.axis_index("lon"), 2) == 1 if paired else jnp.bool_(True)

    def columns(value):
        if paired:
            return across(value, "lon", 1), across(value, "lon", 3)
        ring = [(i, (i + 1) % n_lon) for i in range(n_lon)]
        return lax.ppermute(value, "lon", ring), lax.ppermute(value, "lon", [(b, a) for a, b in ring])

    predicted, packed, time_t = call(
        functools.partial(model_kernel, half),
        [shape((2 * days, wide)), shape((rank, wide), BF16), shape((rank, LANES))],
        [flip],
    )(surface, factor_time, pieces[1, 0])

    fresh, edge = shape((rank, wide)), shape((rank, LANES))
    surface, message, crossing, outgoing, edge_far, summed, seen = call(
        functools.partial(first_kernel, half, days, order, paired, swap),
        [fresh, shape((own_rows + COLS, LANES)), shape((own_rows, LANES)), shape((own_rows + rank, LANES)), edge, shape((2 * days, wide)), shape((TAIL, LANES))],
        [flip, pltpu.VMEM((rank, wide), F32)],
    )(surface, edge_near, predicted, packed, time_t, *[pieces[key] for key in order], bands(edge_far), *(() if paired else columns(cols)))

    narrowed = shape((sum_rows + NORM, LANES), BF16)

    def add(mine, theirs):
        return call(add_kernel, shape(mine.shape))(mine, theirs)

    def doubled(total, axis, step):
        while step < lax.axis_size(axis):
            total = add(total, across(total, axis, step))
            step *= 2
        return total

    def over_lon(total):
        if paired:
            return [total] + [across(total, "lon", step) for step in (1, 2, 3)]
        return [doubled(total, "lon", 1)]

    def around(mine, core, both):
        return mine, across(core, "ta", 1), across(mine, "lat", 1), across(both, ("lat", "ta"), 3)

    total, edge_near = call(own_sum_kernel, [shape(message.shape), edge])(*around(message, outgoing, crossing))
    parts = over_lon(doubled(total, "lat", 2))
    cols = (parts[1], parts[3]) if paired else columns(message[own_rows:])
    time_own, norm = call(functools.partial(own_kernel, len(parts)), [edge, shape((NORM, LANES))])(time_t, *parts)

    surface, time_t, message, outgoing = call(
        functools.partial(second_kernel, half, counts, swap),
        [fresh, edge, narrowed, narrowed],
        [flip, pltpu.VMEM((rank, wide), F32), pltpu.VMEM((rank, wide), F32), pltpu.VMEM((2 * days, wide), F32), pltpu.VMEM((rank, wide), BF16)],
    )(surface, time_own, across(time_own, "ta", 1), norm, summed, seen, edge_near, bands(edge_far), *cols)

    other = across(surface, "ta", 1)
    total = narrowed if paired and n_lat == 2 else shape((sum_rows, LANES))
    total = call(functools.partial(all_sum_kernel, rank), total)(*around(message, outgoing, outgoing))
    parts = over_lon(doubled(total, "lat", 2))
    space, time = call(
        functools.partial(last_kernel, half, counts, len(parts)),
        [shape((rank * height, cells)), shape(factor_time.shape)],
        [flip],
    )(surface, other, time_t, *parts)
    return space.reshape(rank, height, cells), time


def solution(mesh):
    in_specs = (
        P(("grp", "lon", "lat"), "ta", None),
        P(("grp", "lon", "lat"), "ta"),
        P(("grp", "lon", "lat")),
        P(("grp", "lon", "lat"), None, None),
        P(("grp", "lon", "lat"), None),
        P(None, ("grp", "lat"), "lon"),
        P(("grp", "ta"), None),
    )
    out_specs = (P(None, ("grp", "lat"), "lon"), P(("grp", "ta"), None))
    return jax.shard_map(shards, mesh=mesh, in_specs=in_specs, out_specs=out_specs, check_vma=False)
```

```python
import functools
import math

import jax
import jax.numpy as jnp
from jax import lax
from jax.experimental import pallas as pl
from jax.experimental.pallas import tpu as pltpu
from jax.sharding import PartitionSpec as P

SMOOTH = 2.0
ETA_SPACE = 0.08
RIDGE = 1.0
EPSILON = 1e-06

F32 = jnp.float32
BF16 = jnp.bfloat16
LANES = 128
WIDTH = 512
TAIL = 16
COLS = 16
NORM = 8
SPARE = 2 * 1024 * 1024
SWATH_COPIES = 1
UNROLL = 4


def dot(a, b, contract):
    return lax.dot_general(a, b, ((contract[:1], contract[1:]), ((), ())), preferred_element_type=F32)


def route_kernel(half, sends, paired, list_hbm, count_hbm, target_hbm, swath_hbm, mask_hbm, space_hbm, time_hbm, *rest):
    outs, rest = rest[: len(sends)], rest[len(sends):]
    surface, edge_near, edge_far, cols, rest = *rest[:4], rest[4:]
    list_ref, count_ref, target_ref, swath_ref, mask_ref, space_ref, time_ref, place, total, seen, arrived = rest
    me, core = lax.axis_index("lon"), lax.axis_index("ta")
    n_lon = list_ref.shape[1]
    slots, days, cells = swath_ref.shape
    chunk = slots // SWATH_COPIES
    small = [(list_hbm, list_ref), (count_hbm, count_ref), (target_hbm, target_ref), (mask_hbm, mask_ref)]
    large = [(swath_hbm.at[pl.ds(at, chunk)], swath_ref.at[pl.ds(at, chunk)]) for at in range(0, slots, chunk)]
    model = [(space_hbm, space_ref), (time_hbm, time_ref)]
    copies = [pltpu.make_async_copy(src, dst, arrived.at[i]) for i, (src, dst) in enumerate(small + large + model)]
    for copy in copies:
        copy.start()
    total[...] = jnp.zeros(total.shape, F32)
    seen[...] = jnp.zeros(seen.shape, F32)
    for copy in copies[: len(small)]:
        copy.wait()

    def owner(d, carry):
        first = jnp.bitwise_xor(d, me) * half
        count = count_ref[0, d]

        def entries(i, carry):
            for k in range(UNROLL):
                k = i * UNROLL + k
                slot = list_ref[0, d, k]
                row = target_ref[slot]
                far = jnp.bitwise_xor(lax.shift_right_logical(row, half.bit_length() - 1), core)
                place[jnp.where(k < count, slot, slots)] = far * (n_lon * half) + first + jnp.bitwise_and(row, half - 1)
            return carry

        return lax.fori_loop(0, lax.div(count + UNROLL - 1, UNROLL), entries, carry)

    lax.fori_loop(0, n_lon, owner, 0)
    mask = mask_ref[...].astype(F32)
    by_day = mask.T.astype(BF16)
    for slot in range(slots):
        if slot % chunk == 0:
            copies[len(small) + slot // chunk].wait()
        at = place[slot]
        total[at] += (swath_ref[slot] * by_day[:, slot:slot + 1]).astype(F32)
        seen[pl.ds(at, 1), :days] += mask[slot:slot + 1, :]
    for copy in copies[len(small) + len(large):]:
        copy.wait()
    rank = surface.shape[0]
    height = space_ref.shape[0] // rank
    for row in range(half):
        surface[:, row * LANES:(row + 1) * LANES] = space_ref[pl.ds(core * half + row, rank, stride=height), :]
    edge_near[...] = space_ref[pl.ds(half - core, rank, stride=height), :]
    edge_far[...] = space_ref[pl.ds(core * (height - 1), rank, stride=height), :]
    cols[...] = jnp.zeros(cols.shape, F32)
    cols[:, :rank] = border(surface[...], half)
    for (side, step), out in zip(sends, outs):
        at = (side * n_lon + step) * half
        end = half * days + TAIL
        out[: half * days, :] = total[at:at + half].reshape(half * days, cells).astype(BF16)
        out[half * days:end, :] = seen[at:at + TAIL, :].astype(BF16)
        if (side, step) == (1, 0):
            left = time_ref[...]
            for part in range(end, end + 3 * days, days):
                value = left.astype(BF16)
                out[part:part + days, :] = jnp.zeros((days, LANES), BF16)
                out[part:part + days, :rank] = value
                left = left - value.astype(F32)
        elif paired and side == 0 and step in (1, 3):
            out[end:, :] = cols[...].astype(BF16)


def row_of(surface, row):
    return surface[:, row * LANES:(row + 1) * LANES]


def diagonal(value, rank):
    row = lax.broadcasted_iota(jnp.int32, (rank, LANES), 0)
    lane = lax.broadcasted_iota(jnp.int32, (rank, LANES), 1)
    return jnp.where(row == lane, value, 0.0)


def column_as_row(column):
    row = jnp.sum(diagonal(column, column.shape[0]), axis=0, keepdims=True)
    return jnp.broadcast_to(row, (NORM, LANES))


def row_as_column(row, rank):
    return jnp.sum(diagonal(row, rank), axis=1, keepdims=True)


def border(surface, half):
    line = lax.broadcasted_iota(jnp.int32, (COLS, half * LANES), 0)
    lane = lax.broadcasted_iota(jnp.int32, (COLS, half * LANES), 1)
    pick_lane = jnp.where(line < half, line * LANES, (line - half) * LANES + LANES - 1)
    return dot((lane == pick_lane).astype(BF16), surface.astype(BF16), (1, 1))


def smoothed(surface, half, above, below, sides):
    lane = lax.broadcasted_iota(jnp.int32, above.shape, 1)
    strips = []
    for row in range(half):
        here = row_of(surface, row)
        up = above if row == 0 else row_of(surface, row - 1)
        down = below if row == half - 1 else row_of(surface, row + 1)
        left = jnp.where(lane == 0, 0.0, pltpu.roll(here, 1, 1))
        right = jnp.where(lane == LANES - 1, 0.0, pltpu.roll(here, LANES - 1, 1))
        lap = 4.0 * here - (up + down + left + right + row_of(sides, row))
        strips.append(here - (ETA_SPACE * SMOOTH) * lap)
    return strips


def pick(flag, a, b):
    return jnp.where(flag, a, b)


def model_kernel(half, surface, time_own, piece, predicted, packed, time_t, days_all):
    rank = surface.shape[0]
    days = time_own.shape[0]
    at = half * days + TAIL
    high, middle, low = (piece[first:first + days, :].astype(F32) for first in range(at, at + 3 * days, days))
    days_all[...] = jnp.zeros(days_all.shape, F32)
    days_all[:days, :rank] = time_own[...]
    days_all[days:, :] = (high + middle) + low
    time_full = days_all[...]
    time_t[...] = time_full.T[:rank, :]
    packed[...] = surface[...].astype(BF16)
    time_bf = time_full[:, :rank].astype(BF16)
    for at in range(0, half * LANES, 2 * LANES):
        predicted[:, at:at + 2 * LANES] = dot(time_bf, packed[:, at:at + 2 * LANES], (1, 0))


def smooth(half, odd, surface, edge_near, edge_far, cols_a, cols_b, scale, base):
    core = lax.axis_index("ta")
    rank = surface.shape[0]
    above = pick(core == 0, edge_far, edge_near)
    below = pick(core == 0, edge_near, edge_far)
    cols = jnp.concatenate([pick(odd, cols_a, cols_b), pick(odd, cols_b, cols_a)], axis=0)
    line = lax.broadcasted_iota(jnp.int32, (2 * COLS, half * LANES), 0)
    lane = lax.broadcasted_iota(jnp.int32, (2 * COLS, half * LANES), 1)
    from_left = (line >= half) & (line < 2 * half) & (lane == (line - half) * LANES)
    from_right = (line >= COLS) & (line < COLS + half) & (lane == (line - COLS) * LANES + LANES - 1)
    sides = dot(cols[:, :rank].astype(BF16), (from_left | from_right).astype(BF16), (0, 0))
    if scale is not None:
        above, below, sides = above * scale, below * scale, sides * scale
    for row, strip in enumerate(smoothed(surface, half, above, below, sides)):
        base[:, row * LANES:(row + 1) * LANES] = strip


def gradients(half, base, predicted, packed, time_t, seen, summed, fresh):
    rank = time_t.shape[0]
    time_bf = time_t.astype(BF16)
    time_twice = jnp.concatenate([time_bf, time_bf], axis=1)
    seen_bf = seen.astype(BF16)
    width = WIDTH
    owner = lax.broadcasted_iota(jnp.int32, (TAIL, width), 0)
    lane = lax.broadcasted_iota(jnp.int32, (TAIL, width), 1)
    grad_time = jnp.zeros((rank, 2 * LANES), F32)
    grad_diag = jnp.zeros((rank, LANES), F32)
    norm = jnp.zeros((rank, 1), F32)
    for at in range(0, half * LANES, width):
        spread = (owner * LANES <= lane + at) & (lane + at < (owner + 1) * LANES)
        weight = dot(seen_bf, spread.astype(BF16), (0, 0))
        part = packed[:, at:at + width]
        residual = weight * predicted[:, at:at + width] - summed[:, at:at + width]
        high = residual.astype(BF16)
        low = (residual - high.astype(F32)).astype(BF16)
        both = jnp.concatenate([high, low], axis=0)
        grad_space = dot(time_twice, both, (1, 0))
        grad_time = grad_time + dot(part, both, (1, 1))
        new = base[:, at:at + width] - ETA_SPACE * grad_space
        fresh[:, at:at + width] = new
        norm = norm + jnp.sum(new * new, axis=1, keepdims=True)
        wide = part.astype(F32)
        for row in range(width // LANES):
            strip = row_of(wide, row)
            square = jnp.sum(strip * strip, axis=1, keepdims=True)
            grad_diag = grad_diag + square * seen[at // LANES + row:at // LANES + row + 1, :]
    return grad_time[:, :LANES] + grad_time[:, LANES:], grad_diag, norm


def post_own(half, sums, fresh, message, crossing, edge_near, edge_far):
    grad_time, grad_diag, norm = sums
    core = lax.axis_index("ta")
    rank = norm.shape[0]
    days = LANES // 2
    own = lax.broadcasted_iota(jnp.int32, grad_time.shape, 1) < days
    last = column_as_row(norm)
    message[:rank, :] = jnp.where(own, grad_time, pltpu.roll(grad_diag, days, 1))
    message[rank:rank + NORM, :] = last
    message[rank + NORM:, :] = jnp.zeros((COLS, LANES), F32)
    message[rank + NORM:, :rank] = border(fresh[...], half)
    crossing[:rank, :] = jnp.where(own, pltpu.roll(grad_time, days, 1), grad_diag)
    crossing[rank:, :] = last
    first_row, last_row = fresh[:, :LANES], fresh[:, (half - 1) * LANES:]
    edge_near[...] = pick(core == 0, last_row, first_row)
    edge_far[...] = pick(core == 0, first_row, last_row)


def narrow(value, rank):
    high = value[2 * rank:, :].astype(BF16)
    low = (value[2 * rank:, :] - high.astype(F32)).astype(BF16)
    return value[: 2 * rank, :].astype(BF16), jnp.concatenate([high.astype(F32), low.astype(F32)], axis=0).astype(BF16)


def widened(value, rank):
    value = value.astype(F32)
    return jnp.concatenate([value[: 2 * rank, :], value[2 * rank:2 * rank + NORM, :] + value[2 * rank + NORM:, :]], axis=0)


def post_all(sums, message, outgoing):
    grad_time, grad_diag, norm = sums
    rank = norm.shape[0]
    last = column_as_row(norm)
    for out, shift in ((message, 0), (outgoing, LANES // 2)):
        parts = [pltpu.roll(part, shift, 1) if shift else part for part in (grad_time, grad_diag)]
        out[: 2 * rank, :], out[2 * rank:, :] = narrow(jnp.concatenate([*parts, last], axis=0), rank)


def first_kernel(half, days, order, paired, swap, surface, edge_near, predicted, packed, time_t, *rest):
    pieces, rest = dict(zip(order, rest)), rest[len(order):]
    edge_far_in, rest = rest[0], rest[1:]
    if paired:
        at = half * days + TAIL
        cols = [pieces[0, step][at:, :].astype(F32) for step in (1, 3)]
    else:
        cols, rest = [ref[...] for ref in rest[:2]], rest[2:]
    fresh, message, crossing, edge_out, edge_far, summed, seen, base = rest
    smooth(half, swap(), surface[...], edge_near[...], edge_far_in[...], *cols, None, base)
    sides = [[pieces[key] for key in sorted(pieces) if key[0] == side] for side in (0, 1)]

    def add_up(parts, rows):
        value = parts[0][rows, :].astype(F32)
        for piece in parts[1:]:
            value = value + piece[rows, :].astype(F32)
        return value

    for row in range(half):
        for first, parts in zip((0, days), sides):
            summed[first:first + days, row * LANES:(row + 1) * LANES] = add_up(parts, slice(row * days, (row + 1) * days))
    near, far = (add_up(parts, slice(half * days, half * days + TAIL)) for parts in sides)
    seen[...] = near + pltpu.roll(far, days, 1)
    sums = gradients(half, base, predicted, packed, time_t[...], seen[...], summed, fresh)
    post_own(half, sums, fresh, message, crossing, edge_out, edge_far)


def total_of(parts):
    total = parts[0][...].astype(F32)
    if len(parts) > 1:
        one, two, three = (part[...].astype(F32) for part in parts[1:])
        total = (total + one) + (two + three)
    return total


def own_kernel(n_parts, time_t, *rest):
    parts, (time_own, norm) = rest[:n_parts], rest[n_parts:]
    rank = time_t.shape[0]
    days = LANES // 2
    total = total_of(parts)
    block = total[:rank, :]
    own = lax.broadcasted_iota(jnp.int32, block.shape, 1) < days
    time_own[...] = jnp.where(own, time_t[...] - block / (pltpu.roll(block, days, 1) + RIDGE), 0.0)
    norm[...] = total[rank:rank + NORM, :]


def rescaling(counts, norm, time_new):
    day_count, cell_count = counts
    space_sq = row_as_column(norm[:1, :], time_new.shape[0])
    square = time_new * time_new
    time_sq = 0.5 * jnp.sum(square + pltpu.roll(square, LANES // 2, 1), axis=1, keepdims=True)
    ratio = (time_sq / day_count + EPSILON) / (space_sq / cell_count + EPSILON)
    return jnp.sqrt(jnp.sqrt(ratio))


def second_kernel(half, counts, swap, surface, time_own, time_other, norm, summed, seen, edge_near, edge_far, cols_a, cols_b, *rest):
    fresh, time_out, message, outgoing, scaled, base, predicted, packed = rest
    rank = surface.shape[0]
    time_new = time_own[...] + pltpu.roll(time_other[...], LANES // 2, 1)
    scale = rescaling(counts, norm[...], time_new)
    time_now = time_new / scale
    time_out[...] = time_now
    scaled[...] = surface[...] * scale
    packed[...] = scaled[...].astype(BF16)
    time_bf = time_now.astype(BF16)
    for at in range(0, half * LANES, WIDTH):
        predicted[:, at:at + WIDTH] = dot(time_bf, packed[:, at:at + WIDTH], (0, 0))
    cols = [ref[ref.shape[0] - COLS:, :] for ref in (cols_a, cols_b)]
    smooth(half, swap(), scaled[...], edge_near[...], edge_far[...], *cols, scale, base)
    sums = gradients(half, base, predicted, packed, time_now, seen[...], summed, fresh)
    post_all(sums, message, outgoing)


def last_kernel(half, counts, n_parts, surface, other, time_t, *rest):
    parts = rest[:n_parts]
    space_out, time_out, flip = rest[n_parts:]
    core = lax.axis_index("ta")
    rank = surface.shape[0]
    height = space_out.shape[0] // rank
    total = total_of(parts)
    if parts[0].dtype == BF16:
        total = widened(total, rank)
    time_new = time_t[...] - total[:rank, :] / (total[rank:2 * rank, :] + RIDGE)
    scale = rescaling(counts, total[2 * rank:, :], time_new)
    flip[...] = jnp.zeros(flip.shape, F32)
    flip[:rank, :] = time_new / scale
    time_out[...] = flip[...].T[: time_out.shape[0], :rank]
    for row in range(half):
        at = row * LANES
        space_out[pl.ds(core * half + row, rank, stride=height), :] = surface[:, at:at + LANES] * scale
        space_out[pl.ds((1 - core) * half + row, rank, stride=height), :] = other[:, at:at + LANES] * scale


def merge_kernel(mine, theirs, piece_in, edge_in, out, piece_out, edge_out):
    piece_out[...] = piece_in[...]
    edge_out[...] = edge_in[...]
    out[...] = (mine[...].astype(F32) + theirs[...].astype(F32)).astype(BF16)


def add_kernel(mine, theirs, total):
    total[...] = mine[...] + theirs[...]


def own_sum_kernel(mine, core, band, both, total):
    rows = both.shape[0]
    total[:rows, :] = (mine[:rows, :] + core[...]) + (band[:rows, :] + both[...])
    total[rows:, :] = mine[rows:, :]


def all_sum_kernel(rank, mine, core, band, both, total):
    one, two, three, four = (widened(part[...], rank) for part in (mine, core, band, both))
    value = (one + two) + (three + four)
    if total.dtype == BF16:
        total[: 2 * rank, :], total[2 * rank:, :] = narrow(value, rank)
    else:
        total[...] = value


def shape(dims, dtype=F32):
    return jax.ShapeDtypeStruct(tuple(dims), dtype)


def padded(ref):
    *outer, rows, lanes = (1, *ref.shape)
    return math.prod(outer) * -(-rows // 16) * 16 * -(-lanes // LANES) * LANES * jnp.dtype(ref.dtype).itemsize


def call(kernel, out_shape, scratch=(), hbm=0, after=0, flops=1_000_000):
    def run(*operands):
        operands = [pltpu.with_memory_space_constraint(x, pltpu.HBM) if i < hbm else x for i, x in enumerate(operands)]
        vmem = [*operands[hbm:len(operands) - after], *jax.tree.leaves(out_shape), *scratch]
        specs = [pltpu.HBM] * hbm + [pltpu.VMEM] * (len(operands) - hbm - after) + [pl.ANY] * after
        return pl.pallas_call(
            kernel,
            out_shape=out_shape,
            in_specs=[pl.BlockSpec(memory_space=space) for space in specs],
            out_specs=jax.tree.map(lambda _: pl.BlockSpec(memory_space=pltpu.VMEM), out_shape),
            scratch_shapes=list(scratch),
            compiler_params=pltpu.CompilerParams(vmem_limit_bytes=SPARE + sum(padded(ref) for ref in vmem if len(ref.shape) > 1)),
            cost_estimate=pl.CostEstimate(flops=flops, bytes_accessed=1_000_000, transcendentals=0),
        )(*operands)

    return run


def across(value, axis, step):
    return lax.ppermute(value, axis, [(i, i ^ step) for i in range(lax.axis_size(axis))])


def shards(swath, obs_mask, target, send_list, send_count, factor_space, factor_time):
    n_lon, n_lat, n_ta = (lax.axis_size(axis) for axis in ("lon", "lat", "ta"))
    slots, days, cells = swath.shape
    rank, height, _ = factor_space.shape
    half = height // n_ta
    wide = half * LANES
    counts = (float(days * n_ta), float(height * cells * n_lon * n_lat))
    own_rows, sum_rows = rank + NORM, 2 * rank + NORM
    flip = pltpu.VMEM((LANES, LANES), F32)

    paired = n_lon == 4

    distant, close = range(n_lon // 2, n_lon), range(1, n_lon // 2)
    sends = [(1, step) for step in reversed(distant)] + [(0, step) for step in distant] + [(1, 0)]
    sends += [(side, step) for side in (0, 1) for step in close] + [(0, 0)]

    def piece_rows(side, step):
        more = 3 * days if (side, step) == (1, 0) else COLS if paired and side == 0 and step in (1, 3) else 0
        return half * days + TAIL + more

    operands = (send_list, send_count, target, swath, obs_mask, factor_space.reshape(rank * height, cells), factor_time)
    *pieces, surface, edge_near, edge_far, cols = call(
        functools.partial(route_kernel, half, sends, paired),
        [shape((piece_rows(*key), cells), BF16) for key in sends]
        + [shape((rank, wide)), shape((rank, LANES)), shape((rank, LANES)), shape((COLS, LANES))],
        [pltpu.SMEM(ref.shape, jnp.int32) for ref in operands[:3]]
        + [pltpu.VMEM(ref.shape, ref.dtype) for ref in operands[3:]]
        + [
            pltpu.SMEM((slots + 1,), jnp.int32),
            pltpu.VMEM((2 * n_lon * half, days, cells), F32),
            pltpu.VMEM((2 * n_lon * half + TAIL, LANES), F32),
            pltpu.SemaphoreType.DMA((len(operands) - 1 + SWATH_COPIES,)),
        ],
        hbm=len(operands),
    )(*operands)

    def arrived(key, piece):
        side, step = key
        if side:
            return across(piece, ("lon", "ta"), 2 * step + 1)
        return across(piece, "lon", step) if step else piece

    pieces = dict(zip(sends, pieces))
    if paired:
        passing = across(pieces.pop((1, 3)), "lon", 1)
        outs = [shape(passing.shape, BF16), shape(passing.shape, BF16), shape(edge_far.shape)]
        pieces[1, 2], pieces[1, 1], edge_far = call(merge_kernel, outs)(pieces[1, 2], passing, pieces[1, 1], edge_far)
    pieces = {key: arrived(key, piece) for key, piece in pieces.items()}
    order = list(pieces)

    def bands(edge):
        there = [(2 * band + 1, 2 * band + 2) for band in range(n_lat - 1)]
        return lax.ppermute(edge, ("lat", "ta"), there + [(b, a) for a, b in there])

    def swap():
        return lax.rem(lax.axis_index("lon"), 2) == 1 if paired else jnp.bool_(True)

    def columns(value):
        if paired:
            return across(value, "lon", 1), across(value, "lon", 3)
        ring = [(i, (i + 1) % n_lon) for i in range(n_lon)]
        return lax.ppermute(value, "lon", ring), lax.ppermute(value, "lon", [(b, a) for a, b in ring])

    predicted, packed, time_t = call(
        functools.partial(model_kernel, half),
        [shape((2 * days, wide)), shape((rank, wide), BF16), shape((rank, LANES))],
        [flip],
    )(surface, factor_time, pieces[1, 0])

    fresh, edge = shape((rank, wide)), shape((rank, LANES))
    surface, message, crossing, edge_near, edge_far, summed, seen = call(
        functools.partial(first_kernel, half, days, order, paired, swap),
        [fresh, shape((own_rows + COLS, LANES)), shape((own_rows, LANES)), edge, edge, shape((2 * days, wide)), shape((TAIL, LANES))],
        [pltpu.VMEM((rank, wide), F32)],
    )(surface, edge_near, predicted, packed, time_t, *[pieces[key] for key in order], bands(edge_far), *(() if paired else columns(cols)))

    narrowed = shape((sum_rows + NORM, LANES), BF16)

    def add(mine, theirs):
        return call(add_kernel, shape(mine.shape))(mine, theirs)

    def doubled(total, axis, step):
        while step < lax.axis_size(axis):
            total = add(total, across(total, axis, step))
            step *= 2
        return total

    def over_lon(total):
        if paired:
            return [total] + [across(total, "lon", step) for step in (1, 2, 3)]
        return [doubled(total, "lon", 1)]

    def around(mine, core, both):
        return mine, across(core, "ta", 1), across(mine, "lat", 1), across(both, ("lat", "ta"), 3)

    total = call(own_sum_kernel, shape(message.shape))(*around(message, crossing, crossing))
    parts = over_lon(doubled(total, "lat", 2))
    cols = (parts[1], parts[3]) if paired else columns(message[own_rows:])
    time_own, norm = call(functools.partial(own_kernel, len(parts)), [edge, shape((NORM, LANES))])(time_t, *parts)

    surface, time_t, message, outgoing = call(
        functools.partial(second_kernel, half, counts, swap),
        [fresh, edge, narrowed, narrowed],
        [pltpu.VMEM((rank, wide), F32), pltpu.VMEM((rank, wide), F32), pltpu.VMEM((2 * days, wide), F32), pltpu.VMEM((rank, wide), BF16)],
    )(surface, time_own, across(time_own, "ta", 1), norm, summed, seen, across(edge_near, "ta", 1), bands(edge_far), *cols)

    other = across(surface, "ta", 1)
    total = narrowed if paired and n_lat == 2 else shape((sum_rows, LANES))
    total = call(functools.partial(all_sum_kernel, rank), total)(*around(message, outgoing, outgoing))
    parts = over_lon(doubled(total, "lat", 2))
    space, time = call(
        functools.partial(last_kernel, half, counts, len(parts)),
        [shape((rank * height, cells)), shape(factor_time.shape)],
        [flip],
    )(surface, other, time_t, *parts)
    return space.reshape(rank, height, cells), time


def solution(mesh):
    in_specs = (
        P(("grp", "lon", "lat"), "ta", None),
        P(("grp", "lon", "lat"), "ta"),
        P(("grp", "lon", "lat")),
        P(("grp", "lon", "lat"), None, None),
        P(("grp", "lon", "lat"), None),
        P(None, ("grp", "lat"), "lon"),
        P(("grp", "ta"), None),
    )
    out_specs = (P(None, ("grp", "lat"), "lon"), P(("grp", "ta"), None))
    return jax.shard_map(shards, mesh=mesh, in_specs=in_specs, out_specs=out_specs, check_vma=False)
```

```python
import functools
import math

import jax
import jax.numpy as jnp
from jax import lax
from jax.experimental import pallas as pl
from jax.experimental.pallas import tpu as pltpu
from jax.sharding import PartitionSpec as P

SMOOTH = 2.0
ETA_SPACE = 0.08
RIDGE = 1.0
EPSILON = 1e-06

F32 = jnp.float32
BF16 = jnp.bfloat16
LANES = 128
WIDTH = 512
TAIL = 16
COLS = 16
NORM = 8
SPARE = 2 * 1024 * 1024
SWATH_COPIES = 1
UNROLL = 4


def dot(a, b, contract):
    return lax.dot_general(a, b, ((contract[:1], contract[1:]), ((), ())), preferred_element_type=F32)


def route_kernel(half, sends, paired, list_hbm, count_hbm, target_hbm, swath_hbm, mask_hbm, space_hbm, time_hbm, *rest):
    outs, rest = rest[: len(sends)], rest[len(sends):]
    surface, edge_near, edge_far, cols, rest = *rest[:4], rest[4:]
    list_ref, count_ref, target_ref, swath_ref, mask_ref, space_ref, time_ref, place, total, seen, arrived = rest
    me, core = lax.axis_index("lon"), lax.axis_index("ta")
    n_lon = list_ref.shape[1]
    slots, days, cells = swath_ref.shape
    chunk = slots // SWATH_COPIES
    small = [(list_hbm, list_ref), (count_hbm, count_ref), (target_hbm, target_ref), (mask_hbm, mask_ref)]
    large = [(swath_hbm.at[pl.ds(at, chunk)], swath_ref.at[pl.ds(at, chunk)]) for at in range(0, slots, chunk)]
    model = [(space_hbm, space_ref), (time_hbm, time_ref)]
    copies = [pltpu.make_async_copy(src, dst, arrived.at[i]) for i, (src, dst) in enumerate(small + model + large)]
    for copy in copies:
        copy.start()
    total[...] = jnp.zeros(total.shape, F32)
    seen[...] = jnp.zeros(seen.shape, F32)
    for copy in copies[: len(small)]:
        copy.wait()

    def owner(d, carry):
        first = jnp.bitwise_xor(d, me) * half
        count = count_ref[0, d]

        def entries(i, carry):
            for k in range(UNROLL):
                k = i * UNROLL + k
                slot = list_ref[0, d, k]
                row = target_ref[slot]
                far = jnp.bitwise_xor(lax.shift_right_logical(row, half.bit_length() - 1), core)
                place[jnp.where(k < count, slot, slots)] = far * (n_lon * half) + first + jnp.bitwise_and(row, half - 1)
            return carry

        return lax.fori_loop(0, lax.div(count + UNROLL - 1, UNROLL), entries, carry)

    lax.fori_loop(0, n_lon, owner, 0)
    for copy in copies[len(small):len(small) + len(model)]:
        copy.wait()
    rank = surface.shape[0]
    height = space_ref.shape[0] // rank
    for row in range(half):
        surface[:, row * LANES:(row + 1) * LANES] = space_ref[pl.ds(core * half + row, rank, stride=height), :]
    edge_near[...] = space_ref[pl.ds(half - core, rank, stride=height), :]
    edge_far[...] = space_ref[pl.ds(core * (height - 1), rank, stride=height), :]
    cols[...] = jnp.zeros(cols.shape, F32)
    cols[:, :rank] = border(surface[...], half)
    mask = mask_ref[...].astype(F32)
    by_day = mask.T.astype(BF16)
    for slot in range(slots):
        if slot % chunk == 0:
            copies[len(small) + len(model) + slot // chunk].wait()
        at = place[slot]
        total[at] += (swath_ref[slot] * by_day[:, slot:slot + 1]).astype(F32)
        seen[pl.ds(at, 1), :days] += mask[slot:slot + 1, :]
    for (side, step), out in zip(sends, outs):
        at = (side * n_lon + step) * half
        end = half * days + TAIL
        out[: half * days, :] = total[at:at + half].reshape(half * days, cells).astype(BF16)
        out[half * days:end, :] = seen[at:at + TAIL, :].astype(BF16)
        if (side, step) == (1, 0):
            left = time_ref[...]
            for part in range(end, end + 3 * days, days):
                value = left.astype(BF16)
                out[part:part + days, :] = jnp.zeros((days, LANES), BF16)
                out[part:part + days, :rank] = value
                left = left - value.astype(F32)
        elif paired and (side, step) == (0, 3):
            out[end:, :] = cols[...].astype(BF16)


def row_of(surface, row):
    return surface[:, row * LANES:(row + 1) * LANES]


def diagonal(value, rank):
    row = lax.broadcasted_iota(jnp.int32, (rank, LANES), 0)
    lane = lax.broadcasted_iota(jnp.int32, (rank, LANES), 1)
    return jnp.where(row == lane, value, 0.0)


def column_as_row(column):
    row = jnp.sum(diagonal(column, column.shape[0]), axis=0, keepdims=True)
    return jnp.broadcast_to(row, (NORM, LANES))


def row_as_column(row, rank):
    return jnp.sum(diagonal(row, rank), axis=1, keepdims=True)


def border(surface, half):
    line = lax.broadcasted_iota(jnp.int32, (COLS, half * LANES), 0)
    lane = lax.broadcasted_iota(jnp.int32, (COLS, half * LANES), 1)
    pick_lane = jnp.where(line < half, line * LANES, (line - half) * LANES + LANES - 1)
    return dot((lane == pick_lane).astype(BF16), surface.astype(BF16), (1, 1))


def smoothed(surface, half, above, below, sides):
    lane = lax.broadcasted_iota(jnp.int32, above.shape, 1)
    strips = []
    for row in range(half):
        here = row_of(surface, row)
        up = above if row == 0 else row_of(surface, row - 1)
        down = below if row == half - 1 else row_of(surface, row + 1)
        left = jnp.where(lane == 0, 0.0, pltpu.roll(here, 1, 1))
        right = jnp.where(lane == LANES - 1, 0.0, pltpu.roll(here, LANES - 1, 1))
        lap = 4.0 * here - (up + down + left + right + row_of(sides, row))
        strips.append(here - (ETA_SPACE * SMOOTH) * lap)
    return strips


def pick(flag, a, b):
    return jnp.where(flag, a, b)


def model_kernel(half, surface, time_own, piece, predicted, packed, time_t, days_all):
    rank = surface.shape[0]
    days = time_own.shape[0]
    at = half * days + TAIL
    high, middle, low = (piece[first:first + days, :].astype(F32) for first in range(at, at + 3 * days, days))
    days_all[...] = jnp.zeros(days_all.shape, F32)
    days_all[:days, :rank] = time_own[...]
    days_all[days:, :] = (high + middle) + low
    time_full = days_all[...]
    time_t[...] = time_full.T[:rank, :]
    packed[...] = surface[...].astype(BF16)
    time_bf = time_full[:, :rank].astype(BF16)
    for at in range(0, half * LANES, 2 * LANES):
        predicted[:, at:at + 2 * LANES] = dot(time_bf, packed[:, at:at + 2 * LANES], (1, 0))


def smooth(half, odd, surface, edge_near, edge_far, cols_a, cols_b, scale, base):
    core = lax.axis_index("ta")
    rank = surface.shape[0]
    above = pick(core == 0, edge_far, edge_near)
    below = pick(core == 0, edge_near, edge_far)
    cols = jnp.concatenate([pick(odd, cols_a, cols_b), pick(odd, cols_b, cols_a)], axis=0)
    line = lax.broadcasted_iota(jnp.int32, (2 * COLS, half * LANES), 0)
    lane = lax.broadcasted_iota(jnp.int32, (2 * COLS, half * LANES), 1)
    from_left = (line >= half) & (line < 2 * half) & (lane == (line - half) * LANES)
    from_right = (line >= COLS) & (line < COLS + half) & (lane == (line - COLS) * LANES + LANES - 1)
    sides = dot(cols[:, :rank].astype(BF16), (from_left | from_right).astype(BF16), (0, 0))
    if scale is not None:
        above, below, sides = above * scale, below * scale, sides * scale
    for row, strip in enumerate(smoothed(surface, half, above, below, sides)):
        base[:, row * LANES:(row + 1) * LANES] = strip


def gradients(half, base, predicted, packed, time_t, seen, summed, fresh):
    rank = time_t.shape[0]
    time_bf = time_t.astype(BF16)
    time_twice = jnp.concatenate([time_bf, time_bf], axis=1)
    seen_bf = seen.astype(BF16)
    width = WIDTH
    owner = lax.broadcasted_iota(jnp.int32, (TAIL, width), 0)
    lane = lax.broadcasted_iota(jnp.int32, (TAIL, width), 1)
    grad_time = jnp.zeros((rank, 2 * LANES), F32)
    grad_diag = jnp.zeros((rank, LANES), F32)
    norm = jnp.zeros((rank, 1), F32)
    for at in range(0, half * LANES, width):
        spread = (owner * LANES <= lane + at) & (lane + at < (owner + 1) * LANES)
        weight = dot(seen_bf, spread.astype(BF16), (0, 0))
        part = packed[:, at:at + width]
        residual = weight * predicted[:, at:at + width] - summed[:, at:at + width]
        high = residual.astype(BF16)
        low = (residual - high.astype(F32)).astype(BF16)
        both = jnp.concatenate([high, low], axis=0)
        grad_space = dot(time_twice, both, (1, 0))
        grad_time = grad_time + dot(part, both, (1, 1))
        new = base[:, at:at + width] - ETA_SPACE * grad_space
        fresh[:, at:at + width] = new
        norm = norm + jnp.sum(new * new, axis=1, keepdims=True)
        wide = part.astype(F32)
        for row in range(width // LANES):
            strip = row_of(wide, row)
            square = jnp.sum(strip * strip, axis=1, keepdims=True)
            grad_diag = grad_diag + square * seen[at // LANES + row:at // LANES + row + 1, :]
    return grad_time[:, :LANES] + grad_time[:, LANES:], grad_diag, norm


def post_own(half, sums, fresh, message, crossing, edge_near, edge_far):
    grad_time, grad_diag, norm = sums
    core = lax.axis_index("ta")
    rank = norm.shape[0]
    days = LANES // 2
    own = lax.broadcasted_iota(jnp.int32, grad_time.shape, 1) < days
    last = column_as_row(norm)
    message[:rank, :] = jnp.where(own, grad_time, pltpu.roll(grad_diag, days, 1))
    message[rank:rank + NORM, :] = last
    message[rank + NORM:, :] = jnp.zeros((COLS, LANES), F32)
    message[rank + NORM:, :rank] = border(fresh[...], half)
    crossing[:rank, :] = jnp.where(own, pltpu.roll(grad_time, days, 1), grad_diag)
    crossing[rank:, :] = last
    first_row, last_row = fresh[:, :LANES], fresh[:, (half - 1) * LANES:]
    edge_near[...] = pick(core == 0, last_row, first_row)
    edge_far[...] = pick(core == 0, first_row, last_row)


def narrow(value, rank):
    high = value[2 * rank:, :].astype(BF16)
    low = (value[2 * rank:, :] - high.astype(F32)).astype(BF16)
    return value[: 2 * rank, :].astype(BF16), jnp.concatenate([high.astype(F32), low.astype(F32)], axis=0).astype(BF16)


def widened(value, rank):
    value = value.astype(F32)
    return jnp.concatenate([value[: 2 * rank, :], value[2 * rank:2 * rank + NORM, :] + value[2 * rank + NORM:, :]], axis=0)


def post_all(sums, message, outgoing):
    grad_time, grad_diag, norm = sums
    rank = norm.shape[0]
    last = column_as_row(norm)
    for out, shift in ((message, 0), (outgoing, LANES // 2)):
        parts = [pltpu.roll(part, shift, 1) if shift else part for part in (grad_time, grad_diag)]
        out[: 2 * rank, :], out[2 * rank:, :] = narrow(jnp.concatenate([*parts, last], axis=0), rank)


def first_kernel(half, days, order, paired, swap, surface, edge_near, predicted, packed, time_t, *rest):
    pieces, rest = dict(zip(order, rest)), rest[len(order):]
    edge_far_in, rest = rest[0], rest[1:]
    if paired:
        at = half * days + TAIL
        cols = [ref[at:, :].astype(F32) for ref in (rest[0], pieces[0, 2])]
        rest = rest[1:]
    else:
        cols, rest = [ref[...] for ref in rest[:2]], rest[2:]
    fresh, message, crossing, edge_out, edge_far, summed, seen, base = rest
    smooth(half, swap(), surface[...], edge_near[...], edge_far_in[...], *cols, None, base)
    sides = [[pieces[key] for key in sorted(pieces) if key[0] == side] for side in (0, 1)]

    def add_up(parts, rows):
        value = parts[0][rows, :].astype(F32)
        for piece in parts[1:]:
            value = value + piece[rows, :].astype(F32)
        return value

    for row in range(half):
        for first, parts in zip((0, days), sides):
            summed[first:first + days, row * LANES:(row + 1) * LANES] = add_up(parts, slice(row * days, (row + 1) * days))
    near, far = (add_up(parts, slice(half * days, half * days + TAIL)) for parts in sides)
    seen[...] = near + pltpu.roll(far, days, 1)
    sums = gradients(half, base, predicted, packed, time_t[...], seen[...], summed, fresh)
    post_own(half, sums, fresh, message, crossing, edge_out, edge_far)


def total_of(parts):
    total = parts[0][...].astype(F32)
    if len(parts) > 1:
        one, two, three = (part[...].astype(F32) for part in parts[1:])
        total = (total + one) + (two + three)
    return total


def own_kernel(n_parts, time_t, *rest):
    parts, (time_own, norm) = rest[:n_parts], rest[n_parts:]
    rank = time_t.shape[0]
    days = LANES // 2
    total = total_of(parts)
    block = total[:rank, :]
    own = lax.broadcasted_iota(jnp.int32, block.shape, 1) < days
    time_own[...] = jnp.where(own, time_t[...] - block / (pltpu.roll(block, days, 1) + RIDGE), 0.0)
    norm[...] = total[rank:rank + NORM, :]


def rescaling(counts, norm, time_new):
    day_count, cell_count = counts
    space_sq = row_as_column(norm[:1, :], time_new.shape[0])
    square = time_new * time_new
    time_sq = 0.5 * jnp.sum(square + pltpu.roll(square, LANES // 2, 1), axis=1, keepdims=True)
    ratio = (time_sq / day_count + EPSILON) / (space_sq / cell_count + EPSILON)
    return jnp.sqrt(jnp.sqrt(ratio))


def second_kernel(half, counts, swap, surface, time_own, time_other, norm, summed, seen, edge_near, edge_far, cols_a, cols_b, *rest):
    fresh, time_out, message, outgoing, scaled, base, predicted, packed = rest
    rank = surface.shape[0]
    time_new = time_own[...] + pltpu.roll(time_other[...], LANES // 2, 1)
    scale = rescaling(counts, norm[...], time_new)
    time_now = time_new / scale
    time_out[...] = time_now
    scaled[...] = surface[...] * scale
    packed[...] = scaled[...].astype(BF16)
    time_bf = time_now.astype(BF16)
    for at in range(0, half * LANES, WIDTH):
        predicted[:, at:at + WIDTH] = dot(time_bf, packed[:, at:at + WIDTH], (0, 0))
    cols = [ref[ref.shape[0] - COLS:, :] for ref in (cols_a, cols_b)]
    smooth(half, swap(), scaled[...], edge_near[...], edge_far[...], *cols, scale, base)
    sums = gradients(half, base, predicted, packed, time_now, seen[...], summed, fresh)
    post_all(sums, message, outgoing)


def last_kernel(half, counts, n_parts, surface, other, time_t, *rest):
    parts = rest[:n_parts]
    space_out, time_out, flip = rest[n_parts:]
    core = lax.axis_index("ta")
    rank = surface.shape[0]
    height = space_out.shape[0] // rank
    total = total_of(parts)
    if parts[0].dtype == BF16:
        total = widened(total, rank)
    time_new = time_t[...] - total[:rank, :] / (total[rank:2 * rank, :] + RIDGE)
    scale = rescaling(counts, total[2 * rank:, :], time_new)
    flip[...] = jnp.zeros(flip.shape, F32)
    flip[:rank, :] = time_new / scale
    time_out[...] = flip[...].T[: time_out.shape[0], :rank]
    for row in range(half):
        at = row * LANES
        space_out[pl.ds(core * half + row, rank, stride=height), :] = surface[:, at:at + LANES] * scale
        space_out[pl.ds((1 - core) * half + row, rank, stride=height), :] = other[:, at:at + LANES] * scale


def near_merge_kernel(mine, theirs, out):
    rows = mine.shape[0]
    out[:rows, :] = (mine[...].astype(F32) + theirs[:rows, :].astype(F32)).astype(BF16)
    out[rows:, :] = theirs[rows:, :]


def far_merge_kernel(mine, theirs, piece_in, edge_in, out, piece_out, edge_out):
    piece_out[...] = piece_in[...]
    edge_out[...] = edge_in[...]
    out[...] = (mine[...].astype(F32) + theirs[...].astype(F32)).astype(BF16)


def add_kernel(mine, theirs, total):
    total[...] = mine[...] + theirs[...]


def core_sum_kernel(mine, core, total):
    total[...] = mine[: total.shape[0], :] + core[...]


def band_sum_kernel(mine, band, message, total):
    rows = mine.shape[0]
    total[:rows, :] = mine[...] + band[...]
    total[rows:, :] = message[rows:, :]


def all_sum_kernel(rank, mine, core, band, both, total):
    one, two, three, four = (widened(part[...], rank) for part in (mine, core, band, both))
    value = (one + two) + (three + four)
    if total.dtype == BF16:
        total[: 2 * rank, :], total[2 * rank:, :] = narrow(value, rank)
    else:
        total[...] = value


def shape(dims, dtype=F32):
    return jax.ShapeDtypeStruct(tuple(dims), dtype)


def padded(ref):
    *outer, rows, lanes = (1, *ref.shape)
    return math.prod(outer) * -(-rows // 16) * 16 * -(-lanes // LANES) * LANES * jnp.dtype(ref.dtype).itemsize


def call(kernel, out_shape, scratch=(), hbm=0, after=0, flops=1_000_000):
    def run(*operands):
        operands = [pltpu.with_memory_space_constraint(x, pltpu.HBM) if i < hbm else x for i, x in enumerate(operands)]
        vmem = [*operands[hbm:len(operands) - after], *jax.tree.leaves(out_shape), *scratch]
        specs = [pltpu.HBM] * hbm + [pltpu.VMEM] * (len(operands) - hbm - after) + [pl.ANY] * after
        return pl.pallas_call(
            kernel,
            out_shape=out_shape,
            in_specs=[pl.BlockSpec(memory_space=space) for space in specs],
            out_specs=jax.tree.map(lambda _: pl.BlockSpec(memory_space=pltpu.VMEM), out_shape),
            scratch_shapes=list(scratch),
            compiler_params=pltpu.CompilerParams(vmem_limit_bytes=SPARE + sum(padded(ref) for ref in vmem if len(ref.shape) > 1)),
            cost_estimate=pl.CostEstimate(flops=flops, bytes_accessed=1_000_000, transcendentals=0),
        )(*operands)

    return run


def across(value, axis, step):
    return lax.ppermute(value, axis, [(i, i ^ step) for i in range(lax.axis_size(axis))])


def shards(swath, obs_mask, target, send_list, send_count, factor_space, factor_time):
    n_lon, n_lat, n_ta = (lax.axis_size(axis) for axis in ("lon", "lat", "ta"))
    slots, days, cells = swath.shape
    rank, height, _ = factor_space.shape
    half = height // n_ta
    wide = half * LANES
    counts = (float(days * n_ta), float(height * cells * n_lon * n_lat))
    own_rows, sum_rows = rank + NORM, 2 * rank + NORM
    flip = pltpu.VMEM((LANES, LANES), F32)

    paired = n_lon == 4

    distant, close = range(n_lon // 2, n_lon), range(1, n_lon // 2)
    sends = [(side, step) for step in reversed(distant) for side in (0, 1)] + [(1, 0)]
    sends += [(side, step) for side in (0, 1) for step in close] + [(0, 0)]

    def piece_rows(side, step):
        more = 3 * days if (side, step) == (1, 0) else COLS if paired and (side, step) == (0, 3) else 0
        return half * days + TAIL + more

    operands = (send_list, send_count, target, swath, obs_mask, factor_space.reshape(rank * height, cells), factor_time)
    *pieces, surface, edge_near, edge_far, cols = call(
        functools.partial(route_kernel, half, sends, paired),
        [shape((piece_rows(*key), cells), BF16) for key in sends]
        + [shape((rank, wide)), shape((rank, LANES)), shape((rank, LANES)), shape((COLS, LANES))],
        [pltpu.SMEM(ref.shape, jnp.int32) for ref in operands[:3]]
        + [pltpu.VMEM(ref.shape, ref.dtype) for ref in operands[3:]]
        + [
            pltpu.SMEM((slots + 1,), jnp.int32),
            pltpu.VMEM((2 * n_lon * half, days, cells), F32),
            pltpu.VMEM((2 * n_lon * half + TAIL, LANES), F32),
            pltpu.SemaphoreType.DMA((len(operands) - 1 + SWATH_COPIES,)),
        ],
        hbm=len(operands),
    )(*operands)

    def arrived(key, piece):
        side, step = key
        if side:
            return across(piece, ("lon", "ta"), 2 * step + 1)
        return across(piece, "lon", step) if step else piece

    pieces = dict(zip(sends, pieces))
    borders = ()
    if paired:
        near, far = (across(pieces.pop((side, 3)), "lon", 1) for side in (0, 1))
        borders = (near,)
        pieces[0, 2] = call(near_merge_kernel, shape(near.shape, BF16))(pieces[0, 2], near)
        outs = [shape(far.shape, BF16), shape(far.shape, BF16), shape(edge_far.shape)]
        pieces[1, 2], pieces[1, 1], edge_far = call(far_merge_kernel, outs)(pieces[1, 2], far, pieces[1, 1], edge_far)
    pieces = {key: arrived(key, piece) for key, piece in pieces.items()}
    order = list(pieces)

    def bands(edge):
        there = [(2 * band + 1, 2 * band + 2) for band in range(n_lat - 1)]
        return lax.ppermute(edge, ("lat", "ta"), there + [(b, a) for a, b in there])

    def swap():
        return lax.rem(lax.axis_index("lon"), 2) == 1 if paired else jnp.bool_(True)

    def columns(value):
        if paired:
            return across(value, "lon", 1), across(value, "lon", 3)
        ring = [(i, (i + 1) % n_lon) for i in range(n_lon)]
        return lax.ppermute(value, "lon", ring), lax.ppermute(value, "lon", [(b, a) for a, b in ring])

    predicted, packed, time_t = call(
        functools.partial(model_kernel, half),
        [shape((2 * days, wide)), shape((rank, wide), BF16), shape((rank, LANES))],
        [flip],
    )(surface, factor_time, pieces[1, 0])

    fresh, edge = shape((rank, wide)), shape((rank, LANES))
    surface, message, crossing, edge_near, edge_far, summed, seen = call(
        functools.partial(first_kernel, half, days, order, paired, swap),
        [fresh, shape((own_rows + COLS, LANES)), shape((own_rows, LANES)), edge, edge, shape((2 * days, wide)), shape((TAIL, LANES))],
        [pltpu.VMEM((rank, wide), F32)],
    )(surface, edge_near, predicted, packed, time_t, *[pieces[key] for key in order], bands(edge_far), *(borders if paired else columns(cols)))

    narrowed = shape((sum_rows + NORM, LANES), BF16)

    def add(mine, theirs):
        return call(add_kernel, shape(mine.shape))(mine, theirs)

    def doubled(total, axis, step):
        while step < lax.axis_size(axis):
            total = add(total, across(total, axis, step))
            step *= 2
        return total

    def over_lon(total):
        if paired:
            return [total] + [across(total, "lon", step) for step in (1, 2, 3)]
        return [doubled(total, "lon", 1)]

    def around(mine, core, both):
        return mine, across(core, "ta", 1), across(mine, "lat", 1), across(both, ("lat", "ta"), 3)

    total = call(core_sum_kernel, shape(crossing.shape))(message, across(crossing, "ta", 1))
    total = call(band_sum_kernel, shape(message.shape))(total, across(total, "lat", 1), message)
    parts = over_lon(doubled(total, "lat", 2))
    cols = (parts[1], parts[3]) if paired else columns(message[own_rows:])
    time_own, norm = call(functools.partial(own_kernel, len(parts)), [edge, shape((NORM, LANES))])(time_t, *parts)

    surface, time_t, message, outgoing = call(
        functools.partial(second_kernel, half, counts, swap),
        [fresh, edge, narrowed, narrowed],
        [pltpu.VMEM((rank, wide), F32), pltpu.VMEM((rank, wide), F32), pltpu.VMEM((2 * days, wide), F32), pltpu.VMEM((rank, wide), BF16)],
    )(surface, time_own, across(time_own, "ta", 1), norm, summed, seen, across(edge_near, "ta", 1), bands(edge_far), *cols)

    other = across(surface, "ta", 1)
    total = narrowed if paired and n_lat == 2 else shape((sum_rows, LANES))
    total = call(functools.partial(all_sum_kernel, rank), total)(*around(message, outgoing, outgoing))
    parts = over_lon(doubled(total, "lat", 2))
    space, time = call(
        functools.partial(last_kernel, half, counts, len(parts)),
        [shape((rank * height, cells)), shape(factor_time.shape)],
        [flip],
    )(surface, other, time_t, *parts)
    return space.reshape(rank, height, cells), time


def solution(mesh):
    in_specs = (
        P(("grp", "lon", "lat"), "ta", None),
        P(("grp", "lon", "lat"), "ta"),
        P(("grp", "lon", "lat")),
        P(("grp", "lon", "lat"), None, None),
        P(("grp", "lon", "lat"), None),
        P(None, ("grp", "lat"), "lon"),
        P(("grp", "ta"), None),
    )
    out_specs = (P(None, ("grp", "lat"), "lon"), P(("grp", "ta"), None))
    return jax.shard_map(shards, mesh=mesh, in_specs=in_specs, out_specs=out_specs, check_vma=False)
```

```python
import functools
import math

import jax
import jax.numpy as jnp
from jax import lax
from jax.experimental import pallas as pl
from jax.experimental.pallas import tpu as pltpu
from jax.sharding import PartitionSpec as P

SMOOTH = 2.0
ETA_SPACE = 0.08
RIDGE = 1.0
EPSILON = 1e-06

F32 = jnp.float32
BF16 = jnp.bfloat16
LANES = 128
WIDTH = 512
TAIL = 16
COLS = 16
NORM = 8
SPARE = 2 * 1024 * 1024
SWATH_COPIES = 1
UNROLL = 4


def dot(a, b, contract):
    return lax.dot_general(a, b, ((contract[:1], contract[1:]), ((), ())), preferred_element_type=F32)


def route_kernel(half, sends, paired, list_hbm, count_hbm, target_hbm, swath_hbm, mask_hbm, space_hbm, time_hbm, *rest):
    outs, rest = rest[: len(sends)], rest[len(sends):]
    surface, edge_near, edge_far, cols, rest = *rest[:4], rest[4:]
    list_ref, count_ref, target_ref, swath_ref, mask_ref, space_ref, time_ref, place, total, seen, arrived = rest
    me, core = lax.axis_index("lon"), lax.axis_index("ta")
    n_lon = list_ref.shape[1]
    slots, days, cells = swath_ref.shape
    chunk = slots // SWATH_COPIES
    small = [(list_hbm, list_ref), (count_hbm, count_ref), (target_hbm, target_ref), (mask_hbm, mask_ref)]
    large = [(swath_hbm.at[pl.ds(at, chunk)], swath_ref.at[pl.ds(at, chunk)]) for at in range(0, slots, chunk)]
    model = [(space_hbm, space_ref), (time_hbm, time_ref)]
    copies = [pltpu.make_async_copy(src, dst, arrived.at[i]) for i, (src, dst) in enumerate(small + model + large)]
    for copy in copies:
        copy.start()
    total[...] = jnp.zeros(total.shape, F32)
    seen[...] = jnp.zeros(seen.shape, F32)
    for copy in copies[: len(small)]:
        copy.wait()

    def owner(d, carry):
        first = jnp.bitwise_xor(d, me) * half
        count = count_ref[0, d]

        def entries(i, carry):
            for k in range(UNROLL):
                k = i * UNROLL + k
                slot = list_ref[0, d, k]
                row = target_ref[slot]
                far = jnp.bitwise_xor(lax.shift_right_logical(row, half.bit_length() - 1), core)
                place[jnp.where(k < count, slot, slots)] = far * (n_lon * half) + first + jnp.bitwise_and(row, half - 1)
            return carry

        return lax.fori_loop(0, lax.div(count + UNROLL - 1, UNROLL), entries, carry)

    lax.fori_loop(0, n_lon, owner, 0)
    for copy in copies[len(small):len(small) + len(model)]:
        copy.wait()
    rank = surface.shape[0]
    height = space_ref.shape[0] // rank
    for row in range(half):
        surface[:, row * LANES:(row + 1) * LANES] = space_ref[pl.ds(core * half + row, rank, stride=height), :]
    edge_near[...] = space_ref[pl.ds(half - core, rank, stride=height), :]
    edge_far[...] = space_ref[pl.ds(core * (height - 1), rank, stride=height), :]
    cols[...] = jnp.zeros(cols.shape, F32)
    cols[:, :rank] = border(surface[...], half)
    mask = mask_ref[...].astype(F32)
    by_day = mask.T.astype(BF16)
    for slot in range(slots):
        if slot % chunk == 0:
            copies[len(small) + len(model) + slot // chunk].wait()
        at = place[slot]
        total[at] += (swath_ref[slot] * by_day[:, slot:slot + 1]).astype(F32)
        seen[pl.ds(at, 1), :days] += mask[slot:slot + 1, :]
    for (side, step), out in zip(sends, outs):
        at = (side * n_lon + step) * half
        end = half * days + TAIL
        out[: half * days, :] = total[at:at + half].reshape(half * days, cells).astype(BF16)
        out[half * days:end, :] = seen[at:at + TAIL, :].astype(BF16)
        if (side, step) == (1, 0):
            left = time_ref[...]
            for part in range(end, end + 3 * days, days):
                value = left.astype(BF16)
                out[part:part + days, :] = jnp.zeros((days, LANES), BF16)
                out[part:part + days, :rank] = value
                left = left - value.astype(F32)
        elif paired and (side, step) == (0, 3):
            out[end:, :] = cols[...].astype(BF16)


def row_of(surface, row):
    return surface[:, row * LANES:(row + 1) * LANES]


def diagonal(value, rank):
    row = lax.broadcasted_iota(jnp.int32, (rank, LANES), 0)
    lane = lax.broadcasted_iota(jnp.int32, (rank, LANES), 1)
    return jnp.where(row == lane, value, 0.0)


def column_as_row(column):
    row = jnp.sum(diagonal(column, column.shape[0]), axis=0, keepdims=True)
    return jnp.broadcast_to(row, (NORM, LANES))


def row_as_column(row, rank):
    return jnp.sum(diagonal(row, rank), axis=1, keepdims=True)


def border(surface, half):
    line = lax.broadcasted_iota(jnp.int32, (COLS, half * LANES), 0)
    lane = lax.broadcasted_iota(jnp.int32, (COLS, half * LANES), 1)
    pick_lane = jnp.where(line < half, line * LANES, (line - half) * LANES + LANES - 1)
    return dot((lane == pick_lane).astype(BF16), surface.astype(BF16), (1, 1))


def smoothed(surface, half, above, below, sides):
    lane = lax.broadcasted_iota(jnp.int32, above.shape, 1)
    strips = []
    for row in range(half):
        here = row_of(surface, row)
        up = above if row == 0 else row_of(surface, row - 1)
        down = below if row == half - 1 else row_of(surface, row + 1)
        left = jnp.where(lane == 0, 0.0, pltpu.roll(here, 1, 1))
        right = jnp.where(lane == LANES - 1, 0.0, pltpu.roll(here, LANES - 1, 1))
        lap = 4.0 * here - (up + down + left + right + row_of(sides, row))
        strips.append(here - (ETA_SPACE * SMOOTH) * lap)
    return strips


def pick(flag, a, b):
    return jnp.where(flag, a, b)


def in_order(odd, a, b):
    return pick(odd, a, b), pick(odd, b, a)


def model_kernel(half, surface, time_own, piece, predicted, packed, time_t, days_all):
    rank = surface.shape[0]
    days = time_own.shape[0]
    at = half * days + TAIL
    high, middle, low = (piece[first:first + days, :].astype(F32) for first in range(at, at + 3 * days, days))
    days_all[...] = jnp.zeros(days_all.shape, F32)
    days_all[:days, :rank] = time_own[...]
    days_all[days:, :] = (high + middle) + low
    time_full = days_all[...]
    time_t[...] = time_full.T[:rank, :]
    packed[...] = surface[...].astype(BF16)
    time_bf = time_full[:, :rank].astype(BF16)
    for at in range(0, half * LANES, 2 * LANES):
        predicted[:, at:at + 2 * LANES] = dot(time_bf, packed[:, at:at + 2 * LANES], (1, 0))


def smooth(half, surface, edge_near, edge_far, left, right, scale, base):
    core = lax.axis_index("ta")
    rank = surface.shape[0]
    band = lax.axis_index("lat")
    outer = pick(core == 0, band == 0, band == lax.axis_size("lat") - 1)
    edge_far = jnp.where(outer, 0.0, edge_far)
    above = pick(core == 0, edge_far, edge_near)
    below = pick(core == 0, edge_near, edge_far)
    line = lax.broadcasted_iota(jnp.int32, (2 * half, half * LANES), 0)
    lane = lax.broadcasted_iota(jnp.int32, (2 * half, half * LANES), 1)
    place = jnp.where(line < half, line * LANES, (line - half) * LANES + LANES - 1)
    cols = jnp.concatenate([left, right], axis=0)
    sides = dot(cols[:, :rank].astype(BF16), (lane == place).astype(BF16), (0, 0))
    if scale is not None:
        above, below, sides = above * scale, below * scale, sides * scale
    for row, strip in enumerate(smoothed(surface, half, above, below, sides)):
        base[:, row * LANES:(row + 1) * LANES] = strip


def gradients(half, base, predicted, packed, time_t, seen, near, far, fresh):
    rank = time_t.shape[0]
    time_bf = time_t.astype(BF16)
    time_twice = jnp.concatenate([time_bf, time_bf], axis=1)
    seen_bf = seen.astype(BF16)
    width = WIDTH
    owner = lax.broadcasted_iota(jnp.int32, (TAIL, width), 0)
    lane = lax.broadcasted_iota(jnp.int32, (TAIL, width), 1)
    grad_time = jnp.zeros((rank, 2 * LANES), F32)
    grad_diag = jnp.zeros((rank, LANES), F32)
    norm = jnp.zeros((rank, 1), F32)
    for at in range(0, half * LANES, width):
        spread = (owner * LANES <= lane + at) & (lane + at < (owner + 1) * LANES)
        weight = dot(seen_bf, spread.astype(BF16), (0, 0))
        part = packed[:, at:at + width]
        summed = jnp.concatenate([near[:, at:at + width], far[:, at:at + width]], axis=0)
        residual = weight * predicted[:, at:at + width] - summed
        high = residual.astype(BF16)
        low = (residual - high.astype(F32)).astype(BF16)
        both = jnp.concatenate([high, low], axis=0)
        grad_space = dot(time_twice, both, (1, 0))
        grad_time = grad_time + dot(part, both, (1, 1))
        new = base[:, at:at + width] - ETA_SPACE * grad_space
        fresh[:, at:at + width] = new
        norm = norm + jnp.sum(new * new, axis=1, keepdims=True)
        wide = part.astype(F32)
        for row in range(width // LANES):
            strip = row_of(wide, row)
            square = jnp.sum(strip * strip, axis=1, keepdims=True)
            grad_diag = grad_diag + square * seen[at // LANES + row:at // LANES + row + 1, :]
    return grad_time[:, :LANES] + grad_time[:, LANES:], grad_diag, norm


def side_gradients(half, first, predicted, packed, time_t, seen, summed, take):
    rank, days = time_t.shape[0], summed.shape[0]
    below = lax.broadcasted_iota(jnp.int32, time_t.shape, 1) < days
    moved = pltpu.roll(time_t, days, 1)
    time_twice = (jnp.where(below, moved, time_t) if first else jnp.where(below, time_t, moved)).astype(BF16)
    seen_bf = seen[:, :days].astype(BF16)
    owner = lax.broadcasted_iota(jnp.int32, (TAIL, WIDTH), 0)
    lane = lax.broadcasted_iota(jnp.int32, (TAIL, WIDTH), 1)
    grad_time = jnp.zeros((rank, LANES), F32)
    grad_diag = jnp.zeros((rank, LANES), F32)
    for at in range(0, half * LANES, WIDTH):
        spread = (owner * LANES <= lane + at) & (lane + at < (owner + 1) * LANES)
        weight = dot(seen_bf, spread.astype(BF16), (0, 0))
        part = packed[:, at:at + WIDTH]
        residual = weight * predicted[first:first + days, at:at + WIDTH] - summed[:, at:at + WIDTH]
        high = residual.astype(BF16)
        low = (residual - high.astype(F32)).astype(BF16)
        both = jnp.concatenate([high, low], axis=0)
        take(at, dot(time_twice, both, (1, 0)))
        grad_time = grad_time + dot(part, both, (1, 1))
        wide = part.astype(F32)
        for row in range(WIDTH // LANES):
            strip = row_of(wide, row)
            square = jnp.sum(strip * strip, axis=1, keepdims=True)
            grad_diag = grad_diag + square * seen[at // LANES + row:at // LANES + row + 1, :]
    return jnp.where(below, grad_time + pltpu.roll(grad_time, days, 1), pltpu.roll(grad_diag, days, 1))


def add_up(parts, rows):
    value = parts[0][rows, :].astype(F32)
    for piece in parts[1:]:
        value = value + piece[rows, :].astype(F32)
    return value


def unpack_pieces(half, parts, summed, seen):
    days = summed.shape[0]
    for row in range(half):
        summed[:, row * LANES:(row + 1) * LANES] = add_up(parts, slice(row * days, (row + 1) * days))
    seen[...] = add_up(parts, slice(half * days, half * days + TAIL))


def narrow(value, rank):
    high = value[2 * rank:, :].astype(BF16)
    low = (value[2 * rank:, :] - high.astype(F32)).astype(BF16)
    return value[: 2 * rank, :].astype(BF16), jnp.concatenate([high.astype(F32), low.astype(F32)], axis=0).astype(BF16)


def widened(value, rank):
    value = value.astype(F32)
    return jnp.concatenate([value[: 2 * rank, :], value[2 * rank:2 * rank + NORM, :] + value[2 * rank + NORM:, :]], axis=0)


def post_all(sums, message, outgoing):
    grad_time, grad_diag, norm = sums
    rank = norm.shape[0]
    last = column_as_row(norm)
    for out, shift in ((message, 0), (outgoing, LANES // 2)):
        parts = [pltpu.roll(part, shift, 1) if shift else part for part in (grad_time, grad_diag)]
        out[: 2 * rank, :], out[2 * rank:, :] = narrow(jnp.concatenate([*parts, last], axis=0), rank)


def near_kernel(half, days, order, paired, swap, surface, edge_near, predicted, packed, time_t, edge_far, *rest):
    pieces, rest = dict(zip(order, rest)), rest[len(order):]
    cols, (base, block, summed, seen) = rest[:-4], rest[-4:]
    if paired:
        at = half * days + TAIL
        cols = in_order(swap(), *[ref[at:, :].astype(F32) for ref in (cols[0], pieces[0, 2])])
    left, right = (ref[...] for ref in cols)
    smooth(half, surface[...], edge_near[...], edge_far[...], left[half:, :], right[:half, :], None, base)
    unpack_pieces(half, [pieces[key] for key in sorted(pieces)], summed, seen)

    def take(at, grad_space):
        base[:, at:at + WIDTH] = base[:, at:at + WIDTH] - ETA_SPACE * grad_space

    block[...] = side_gradients(half, 0, predicted, packed, time_t[...], seen, summed, take)


def far_kernel(half, days, n_lon, base, predicted, packed, time_t, block, *rest):
    parts, rest = rest[:n_lon], rest[n_lon:]
    fresh, message, crossing, cols, edge_near, edge_far, summed, seen = rest
    core = lax.axis_index("ta")
    rank = block.shape[0]
    unpack_pieces(half, parts, summed, seen)

    def take(at, grad_space):
        fresh[:, at:at + WIDTH] = base[:, at:at + WIDTH] - ETA_SPACE * grad_space

    crossing[:rank, :] = side_gradients(half, days, predicted, packed, time_t[...], seen, summed, take)
    message[:rank, :] = block[...]
    new = fresh[...]
    norm = column_as_row(jnp.sum(new * new, axis=1, keepdims=True))
    message[rank:, :] = norm
    crossing[rank:, :] = norm
    cols[...] = jnp.zeros(cols.shape, F32)
    cols[:, :rank] = border(new, half)
    first_row, last_row = row_of(new, 0), row_of(new, half - 1)
    edge_near[...] = pick(core == 0, last_row, first_row)
    edge_far[...] = pick(core == 0, first_row, last_row)


def total_of(parts):
    total = parts[0][...].astype(F32)
    if len(parts) > 1:
        one, two, three = (part[...].astype(F32) for part in parts[1:])
        total = (total + one) + (two + three)
    return total


def packed_norm(norm, cols, rank):
    free = LANES - rank
    line = lax.broadcasted_iota(jnp.int32, cols.shape, 0)
    lane = lax.broadcasted_iota(jnp.int32, cols.shape, 1)
    for part in range(rank // free):
        moved = pltpu.roll(norm, rank - part * free, 1)
        cols = jnp.where((lane >= rank) & (line == part), moved, cols)
    return cols


def unpacked(block, rank):
    free = LANES - rank
    line = lax.broadcasted_iota(jnp.int32, block.shape, 0)
    lane = lax.broadcasted_iota(jnp.int32, block.shape, 1)
    norm = jnp.zeros(block.shape, F32)
    for part in range(rank // free):
        row = jnp.where((lane >= rank) & (line == part), block, 0.0)
        norm = norm + pltpu.roll(row, LANES - rank + part * free, 1)
    return jnp.broadcast_to(jnp.sum(norm, axis=0, keepdims=True), block.shape)


def own_kernel(n_parts, time_t, *rest):
    parts, (time_own, norm) = rest[:n_parts], rest[n_parts:]
    rank = time_t.shape[0]
    days = LANES // 2
    total = total_of(parts)
    block = total[:rank, :]
    own = lax.broadcasted_iota(jnp.int32, block.shape, 1) < days
    time_own[...] = jnp.where(own, time_t[...] - block / (pltpu.roll(block, days, 1) + RIDGE), 0.0)
    norm[...] = unpacked(total[rank:, :], rank) if n_parts > 1 else total[rank:, :]


def rescaling(counts, norm, time_new):
    day_count, cell_count = counts
    space_sq = row_as_column(norm[:1, :], time_new.shape[0])
    square = time_new * time_new
    time_sq = 0.5 * jnp.sum(square + pltpu.roll(square, LANES // 2, 1), axis=1, keepdims=True)
    ratio = (time_sq / day_count + EPSILON) / (space_sq / cell_count + EPSILON)
    return jnp.sqrt(jnp.sqrt(ratio))


def second_kernel(half, counts, paired, swap, surface, time_own, time_other, norm, near, far, seen_near, seen_far, edge_near, edge_far, cols_a, cols_b, *rest):
    fresh, time_out, message, outgoing, scaled, base, predicted, packed = rest
    rank = surface.shape[0]
    time_new = time_own[...] + pltpu.roll(time_other[...], LANES // 2, 1)
    scale = rescaling(counts, norm[...], time_new)
    time_now = time_new / scale
    time_out[...] = time_now
    scaled[...] = surface[...] * scale
    packed[...] = scaled[...].astype(BF16)
    time_bf = time_now.astype(BF16)
    for at in range(0, half * LANES, WIDTH):
        predicted[:, at:at + WIDTH] = dot(time_bf, packed[:, at:at + WIDTH], (0, 0))
    if paired:
        left, right = in_order(swap(), cols_a[rank:, :], cols_b[rank:, :])
    else:
        left, right = cols_a[half:, :], cols_b[:half, :]
    smooth(half, scaled[...], edge_near[...], edge_far[...], left, right, scale, base)
    seen = seen_near[...] + pltpu.roll(seen_far[...], LANES // 2, 1)
    sums = gradients(half, base, predicted, packed, time_now, seen, near, far, fresh)
    post_all(sums, message, outgoing)


def last_kernel(half, counts, n_parts, surface, other, time_t, *rest):
    parts = rest[:n_parts]
    space_out, time_out, flip = rest[n_parts:]
    core = lax.axis_index("ta")
    rank = surface.shape[0]
    height = space_out.shape[0] // rank
    total = total_of(parts)
    if parts[0].dtype == BF16:
        total = widened(total, rank)
    time_new = time_t[...] - total[:rank, :] / (total[rank:2 * rank, :] + RIDGE)
    scale = rescaling(counts, total[2 * rank:, :], time_new)
    flip[...] = jnp.zeros(flip.shape, F32)
    flip[:rank, :] = time_new / scale
    time_out[...] = flip[...].T[: time_out.shape[0], :rank]
    for row in range(half):
        at = row * LANES
        space_out[pl.ds(core * half + row, rank, stride=height), :] = surface[:, at:at + LANES] * scale
        space_out[pl.ds((1 - core) * half + row, rank, stride=height), :] = other[:, at:at + LANES] * scale


def near_merge_kernel(mine, theirs, out):
    rows = mine.shape[0]
    out[:rows, :] = (mine[...].astype(F32) + theirs[:rows, :].astype(F32)).astype(BF16)
    out[rows:, :] = theirs[rows:, :]


def far_merge_kernel(mine, theirs, piece_in, edge_in, out, piece_out, edge_out):
    piece_out[...] = piece_in[...]
    edge_out[...] = edge_in[...]
    out[...] = (mine[...].astype(F32) + theirs[...].astype(F32)).astype(BF16)


def add_kernel(mine, theirs, total):
    total[...] = mine[...] + theirs[...]


def core_sum_kernel(mine, core, total):
    total[...] = mine[: total.shape[0], :] + core[...]


def band_sum_kernel(half, swap, mine, band, cols, *totals):
    rank = mine.shape[0] - NORM
    value = mine[...] + band[...]
    borders = in_order(swap(), cols[:half, :], cols[half:, :])
    for total, lines in zip(totals, borders):
        total[:rank, :] = value[:rank, :]
        total[rank:, :] = value[rank:, :] if len(totals) == 1 else packed_norm(value[rank:, :], lines, rank)


def all_sum_kernel(rank, mine, core, band, both, total):
    one, two, three, four = (widened(part[...], rank) for part in (mine, core, band, both))
    value = (one + two) + (three + four)
    if total.dtype == BF16:
        total[: 2 * rank, :], total[2 * rank:, :] = narrow(value, rank)
    else:
        total[...] = value


def shape(dims, dtype=F32):
    return jax.ShapeDtypeStruct(tuple(dims), dtype)


def padded(ref):
    *outer, rows, lanes = (1, *ref.shape)
    return math.prod(outer) * -(-rows // 16) * 16 * -(-lanes // LANES) * LANES * jnp.dtype(ref.dtype).itemsize


def call(kernel, out_shape, scratch=(), hbm=0, after=0, flops=1_000_000):
    def run(*operands):
        operands = [pltpu.with_memory_space_constraint(x, pltpu.HBM) if i < hbm else x for i, x in enumerate(operands)]
        vmem = [*operands[hbm:len(operands) - after], *jax.tree.leaves(out_shape), *scratch]
        specs = [pltpu.HBM] * hbm + [pltpu.VMEM] * (len(operands) - hbm - after) + [pl.ANY] * after
        return pl.pallas_call(
            kernel,
            out_shape=out_shape,
            in_specs=[pl.BlockSpec(memory_space=space) for space in specs],
            out_specs=jax.tree.map(lambda _: pl.BlockSpec(memory_space=pltpu.VMEM), out_shape),
            scratch_shapes=list(scratch),
            compiler_params=pltpu.CompilerParams(vmem_limit_bytes=SPARE + sum(padded(ref) for ref in vmem if len(ref.shape) > 1)),
            cost_estimate=pl.CostEstimate(flops=flops, bytes_accessed=1_000_000, transcendentals=0),
        )(*operands)

    return run


def across(value, axis, step):
    return lax.ppermute(value, axis, [(i, i ^ step) for i in range(lax.axis_size(axis))])


def shards(swath, obs_mask, target, send_list, send_count, factor_space, factor_time):
    n_lon, n_lat, n_ta = (lax.axis_size(axis) for axis in ("lon", "lat", "ta"))
    slots, days, cells = swath.shape
    rank, height, _ = factor_space.shape
    half = height // n_ta
    wide = half * LANES
    counts = (float(days * n_ta), float(height * cells * n_lon * n_lat))
    own_rows, sum_rows = rank + NORM, 2 * rank + NORM
    flip = pltpu.VMEM((LANES, LANES), F32)

    paired = n_lon == 4

    distant, close = range(n_lon // 2, n_lon), range(1, n_lon // 2)
    sends = [(side, step) for step in reversed(distant) for side in (0, 1)] + [(1, 0)]
    sends += [(side, step) for side in (0, 1) for step in close] + [(0, 0)]

    def piece_rows(side, step):
        more = 3 * days if (side, step) == (1, 0) else COLS if paired and (side, step) == (0, 3) else 0
        return half * days + TAIL + more

    operands = (send_list, send_count, target, swath, obs_mask, factor_space.reshape(rank * height, cells), factor_time)
    *pieces, surface, edge_near, edge_far, cols = call(
        functools.partial(route_kernel, half, sends, paired),
        [shape((piece_rows(*key), cells), BF16) for key in sends]
        + [shape((rank, wide)), shape((rank, LANES)), shape((rank, LANES)), shape((COLS, LANES))],
        [pltpu.SMEM(ref.shape, jnp.int32) for ref in operands[:3]]
        + [pltpu.VMEM(ref.shape, ref.dtype) for ref in operands[3:]]
        + [
            pltpu.SMEM((slots + 1,), jnp.int32),
            pltpu.VMEM((2 * n_lon * half, days, cells), F32),
            pltpu.VMEM((2 * n_lon * half + TAIL, LANES), F32),
            pltpu.SemaphoreType.DMA((len(operands) - 1 + SWATH_COPIES,)),
        ],
        hbm=len(operands),
    )(*operands)

    def arrived(key, piece):
        side, step = key
        if side:
            return across(piece, ("lon", "ta"), 2 * step + 1)
        return across(piece, "lon", step) if step else piece

    pieces = dict(zip(sends, pieces))
    borders = ()
    if paired:
        near, far = (across(pieces.pop((side, 3)), "lon", 1) for side in (0, 1))
        borders = (near,)
        pieces[0, 2] = call(near_merge_kernel, shape(near.shape, BF16))(pieces[0, 2], near)
        outs = [shape(far.shape, BF16), shape(far.shape, BF16), shape(edge_far.shape)]
        pieces[1, 2], pieces[1, 1], edge_far = call(far_merge_kernel, outs)(pieces[1, 2], far, pieces[1, 1], edge_far)
    pieces = {key: arrived(key, piece) for key, piece in pieces.items()}
    order = list(pieces)

    def bands(edge):
        there = [(2 * band + 1, (2 * band + 2) % (2 * n_lat)) for band in range(n_lat)]
        return lax.ppermute(edge, ("lat", "ta"), there + [(b, a) for a, b in there])

    def swap():
        return lax.rem(lax.axis_index("lon"), 2) == 1 if paired else jnp.bool_(True)

    def columns(value):
        if paired:
            return across(value, "lon", 1), across(value, "lon", 3)
        ring = [(i, (i + 1) % n_lon) for i in range(n_lon)]
        return lax.ppermute(value, "lon", ring), lax.ppermute(value, "lon", [(b, a) for a, b in ring])

    predicted, packed, time_t = call(
        functools.partial(model_kernel, half),
        [shape((2 * days, wide)), shape((rank, wide), BF16), shape((rank, LANES))],
        [flip],
    )(surface, factor_time, pieces[1, 0])

    fresh, edge = shape((rank, wide)), shape((rank, LANES))
    sides = [[key for key in order if key[0] == side] for side in (0, 1)]
    side_out = [shape((days, wide)), shape((TAIL, LANES))]
    base, block, near, seen_near = call(
        functools.partial(near_kernel, half, days, sides[0], paired, swap),
        [fresh, edge, *side_out],
    )(surface, edge_near, predicted, packed, time_t, bands(edge_far), *[pieces[key] for key in sides[0]], *(borders if paired else columns(cols)))
    surface, message, crossing, cols, edge_near, edge_far, far, seen_far = call(
        functools.partial(far_kernel, half, days, len(sides[1])),
        [fresh, shape((own_rows, LANES)), shape((own_rows, LANES)), shape((COLS, LANES)), edge, edge, *side_out],
    )(base, predicted, packed, time_t, block, *[pieces[key] for key in sides[1]])

    narrowed = shape((sum_rows + NORM, LANES), BF16)

    def add(mine, theirs):
        return call(add_kernel, shape(mine.shape))(mine, theirs)

    def doubled(total, axis, step):
        while step < lax.axis_size(axis):
            total = add(total, across(total, axis, step))
            step *= 2
        return total

    def over_lon(total):
        if paired:
            return [total] + [across(total, "lon", step) for step in (1, 2, 3)]
        return [doubled(total, "lon", 1)]

    def around(mine, core, both):
        return mine, across(core, "ta", 1), across(mine, "lat", 1), across(both, ("lat", "ta"), 3)

    total = call(core_sum_kernel, shape(crossing.shape))(message, across(crossing, "ta", 1))
    direct = paired and n_lat == 2
    band_sum = functools.partial(band_sum_kernel, half, swap)
    total, *again = call(band_sum, [shape(crossing.shape)] * (1 + direct))(total, across(total, "lat", 1), cols)
    if direct:
        parts = [total] + [across(value, "lon", step) for step, value in ((1, total), (2, again[0]), (3, again[0]))]
        cols = parts[1], parts[3]
    else:
        parts = [doubled(doubled(total, "lat", 2), "lon", 1)]
        cols = columns(cols)
    time_own, norm = call(functools.partial(own_kernel, len(parts)), [edge, shape((NORM, LANES))])(time_t, *parts)

    surface, time_t, message, outgoing = call(
        functools.partial(second_kernel, half, counts, direct, swap),
        [fresh, edge, narrowed, narrowed],
        [pltpu.VMEM((rank, wide), F32), pltpu.VMEM((rank, wide), F32), pltpu.VMEM((2 * days, wide), F32), pltpu.VMEM((rank, wide), BF16)],
    )(surface, time_own, across(time_own, "ta", 1), norm, near, far, seen_near, seen_far, across(edge_near, "ta", 1), bands(edge_far), *cols)

    other = across(surface, "ta", 1)
    total = narrowed if paired and n_lat == 2 else shape((sum_rows, LANES))
    total = call(functools.partial(all_sum_kernel, rank), total)(*around(message, outgoing, outgoing))
    parts = over_lon(doubled(total, "lat", 2))
    space, time = call(
        functools.partial(last_kernel, half, counts, len(parts)),
        [shape((rank * height, cells)), shape(factor_time.shape)],
        [flip],
    )(surface, other, time_t, *parts)
    return space.reshape(rank, height, cells), time


def solution(mesh):
    in_specs = (
        P(("grp", "lon", "lat"), "ta", None),
        P(("grp", "lon", "lat"), "ta"),
        P(("grp", "lon", "lat")),
        P(("grp", "lon", "lat"), None, None),
        P(("grp", "lon", "lat"), None),
        P(None, ("grp", "lat"), "lon"),
        P(("grp", "ta"), None),
    )
    out_specs = (P(None, ("grp", "lat"), "lon"), P(("grp", "ta"), None))
    return jax.shard_map(shards, mesh=mesh, in_specs=in_specs, out_specs=out_specs, check_vma=False)
```

```python
import functools
import math

import jax
import jax.numpy as jnp
from jax import lax
from jax.experimental import pallas as pl
from jax.experimental.pallas import tpu as pltpu
from jax.sharding import PartitionSpec as P

SMOOTH = 2.0
ETA_SPACE = 0.08
RIDGE = 1.0
EPSILON = 1e-06

F32 = jnp.float32
BF16 = jnp.bfloat16
LANES = 128
WIDTH = 512
TAIL = 16
COLS = 16
NORM = 8
SPARE = 2 * 1024 * 1024
SWATH_COPIES = 1
UNROLL = 4


def dot(a, b, contract):
    return lax.dot_general(a, b, ((contract[:1], contract[1:]), ((), ())), preferred_element_type=F32)


def route_kernel(half, early, paired, list_hbm, count_hbm, target_hbm, swath_hbm, mask_hbm, space_hbm, time_hbm, *rest):
    piece, total, seen, surface, space_ref, time_ref, *rest = rest
    cols = rest.pop(-1 if paired else 0)
    list_ref, count_ref, target_ref, swath_ref, mask_ref, place, arrived = rest
    me, core = lax.axis_index("lon"), lax.axis_index("ta")
    n_lon = list_ref.shape[1]
    slots, days, cells = swath_ref.shape
    chunk = slots // SWATH_COPIES
    small = [(list_hbm, list_ref), (count_hbm, count_ref), (target_hbm, target_ref), (mask_hbm, mask_ref)]
    large = [(swath_hbm.at[pl.ds(at, chunk)], swath_ref.at[pl.ds(at, chunk)]) for at in range(0, slots, chunk)]
    model = [(space_hbm, space_ref), (time_hbm, time_ref)]
    copies = [pltpu.make_async_copy(src, dst, arrived.at[i]) for i, (src, dst) in enumerate(small + model + large)]
    for copy in copies:
        copy.start()
    total[...] = jnp.zeros(total.shape, F32)
    seen[...] = jnp.zeros(seen.shape, F32)
    for copy in copies[: len(small)]:
        copy.wait()

    def owner(d, carry):
        first = jnp.bitwise_xor(d, me) * half
        count = count_ref[0, d]

        def entries(i, carry):
            for k in range(UNROLL):
                k = i * UNROLL + k
                slot = list_ref[0, d, k]
                row = target_ref[slot]
                far = jnp.bitwise_xor(lax.shift_right_logical(row, half.bit_length() - 1), core)
                place[jnp.where(k < count, slot, slots)] = far * (n_lon * half) + first + jnp.bitwise_and(row, half - 1)
            return carry

        return lax.fori_loop(0, lax.div(count + UNROLL - 1, UNROLL), entries, carry)

    lax.fori_loop(0, n_lon, owner, 0)
    for copy in copies[len(small):len(small) + len(model)]:
        copy.wait()
    rank = surface.shape[0]
    height = space_ref.shape[0] // rank
    for row in range(half):
        surface[:, row * LANES:(row + 1) * LANES] = space_ref[pl.ds(core * half + row, rank, stride=height), :]
    cols[...] = jnp.zeros(cols.shape, F32)
    cols[:, :rank] = border(surface[...], half)
    mask = mask_ref[...].astype(F32)
    by_day = mask.T.astype(BF16)
    for slot in range(slots):
        if slot % chunk == 0:
            copies[len(small) + len(model) + slot // chunk].wait()
        at = place[slot]
        total[at] += (swath_ref[slot] * by_day[:, slot:slot + 1]).astype(F32)
        seen[pl.ds(at, 1), :days] += mask[slot:slot + 1, :]
    pack(half, n_lon, early, total, seen, piece)
    end = half * days + TAIL
    if piece.shape[0] > end:
        piece[end:, :] = cols[...].astype(BF16)


def pack(half, n_lon, key, total, seen, out):
    side, step = key
    at = (side * n_lon + step) * half
    end = half * total.shape[1]
    out[:end, :] = total[at:at + half].reshape(end, LANES).astype(BF16)
    out[end:end + TAIL, :] = seen[at:at + TAIL, :].astype(BF16)


def pack_kernel(half, n_lon, sends, total, seen, space_ref, time_ref, *rest):
    outs, (edge_near, edge_far) = rest[: len(sends)], rest[len(sends):]
    core = lax.axis_index("ta")
    days = total.shape[1]
    end = half * days + TAIL
    rank = edge_near.shape[0]
    height = space_ref.shape[0] // rank
    edge_near[...] = space_ref[pl.ds(half - core, rank, stride=height), :]
    edge_far[...] = space_ref[pl.ds(core * (height - 1), rank, stride=height), :]
    for key, out in zip(sends, outs):
        pack(half, n_lon, key, total, seen, out)
        if key == (1, 0):
            left = time_ref[...]
            for part in range(end, end + 3 * days, days):
                value = left.astype(BF16)
                out[part:part + days, :] = jnp.zeros((days, LANES), BF16)
                out[part:part + days, :rank] = value
                left = left - value.astype(F32)


def row_of(surface, row):
    return surface[:, row * LANES:(row + 1) * LANES]


def diagonal(value, rank):
    row = lax.broadcasted_iota(jnp.int32, (rank, LANES), 0)
    lane = lax.broadcasted_iota(jnp.int32, (rank, LANES), 1)
    return jnp.where(row == lane, value, 0.0)


def column_as_row(column):
    row = jnp.sum(diagonal(column, column.shape[0]), axis=0, keepdims=True)
    return jnp.broadcast_to(row, (NORM, LANES))


def row_as_column(row, rank):
    return jnp.sum(diagonal(row, rank), axis=1, keepdims=True)


def border(surface, half):
    line = lax.broadcasted_iota(jnp.int32, (COLS, half * LANES), 0)
    lane = lax.broadcasted_iota(jnp.int32, (COLS, half * LANES), 1)
    pick_lane = jnp.where(line < half, line * LANES, (line - half) * LANES + LANES - 1)
    return dot((lane == pick_lane).astype(BF16), surface.astype(BF16), (1, 1))


def smoothed(surface, half, above, below, sides):
    lane = lax.broadcasted_iota(jnp.int32, above.shape, 1)
    strips = []
    for row in range(half):
        here = row_of(surface, row)
        up = above if row == 0 else row_of(surface, row - 1)
        down = below if row == half - 1 else row_of(surface, row + 1)
        left = jnp.where(lane == 0, 0.0, pltpu.roll(here, 1, 1))
        right = jnp.where(lane == LANES - 1, 0.0, pltpu.roll(here, LANES - 1, 1))
        lap = 4.0 * here - (up + down + left + right + row_of(sides, row))
        strips.append(here - (ETA_SPACE * SMOOTH) * lap)
    return strips


def pick(flag, a, b):
    return jnp.where(flag, a, b)


def in_order(odd, a, b):
    return pick(odd, a, b), pick(odd, b, a)


def model_kernel(half, surface, time_own, piece, predicted, packed, time_t, days_all):
    rank = surface.shape[0]
    days = time_own.shape[0]
    at = half * days + TAIL
    high, middle, low = (piece[first:first + days, :].astype(F32) for first in range(at, at + 3 * days, days))
    days_all[...] = jnp.zeros(days_all.shape, F32)
    days_all[:days, :rank] = time_own[...]
    days_all[days:, :] = (high + middle) + low
    time_full = days_all[...]
    time_t[...] = time_full.T[:rank, :]
    packed[...] = surface[...].astype(BF16)
    time_bf = time_full[:, :rank].astype(BF16)
    for at in range(0, half * LANES, 2 * LANES):
        predicted[:, at:at + 2 * LANES] = dot(time_bf, packed[:, at:at + 2 * LANES], (1, 0))


def smooth(half, surface, edge_near, edge_far, left, right, scale, base):
    core = lax.axis_index("ta")
    rank = surface.shape[0]
    band = lax.axis_index("lat")
    outer = pick(core == 0, band == 0, band == lax.axis_size("lat") - 1)
    edge_far = jnp.where(outer, 0.0, edge_far)
    above = pick(core == 0, edge_far, edge_near)
    below = pick(core == 0, edge_near, edge_far)
    line = lax.broadcasted_iota(jnp.int32, (2 * half, half * LANES), 0)
    lane = lax.broadcasted_iota(jnp.int32, (2 * half, half * LANES), 1)
    place = jnp.where(line < half, line * LANES, (line - half) * LANES + LANES - 1)
    cols = jnp.concatenate([left, right], axis=0)
    sides = dot(cols[:, :rank].astype(BF16), (lane == place).astype(BF16), (0, 0))
    if scale is not None:
        above, below, sides = above * scale, below * scale, sides * scale
    for row, strip in enumerate(smoothed(surface, half, above, below, sides)):
        base[:, row * LANES:(row + 1) * LANES] = strip


def gradients(half, base, predicted, packed, time_t, seen, near, far, fresh):
    rank = time_t.shape[0]
    time_bf = time_t.astype(BF16)
    time_twice = jnp.concatenate([time_bf, time_bf], axis=1)
    seen_bf = seen.astype(BF16)
    width = WIDTH
    owner = lax.broadcasted_iota(jnp.int32, (TAIL, width), 0)
    lane = lax.broadcasted_iota(jnp.int32, (TAIL, width), 1)
    grad_time = jnp.zeros((rank, 2 * LANES), F32)
    grad_diag = jnp.zeros((rank, LANES), F32)
    norm = jnp.zeros((rank, 1), F32)
    for at in range(0, half * LANES, width):
        spread = (owner * LANES <= lane + at) & (lane + at < (owner + 1) * LANES)
        weight = dot(seen_bf, spread.astype(BF16), (0, 0))
        part = packed[:, at:at + width]
        summed = jnp.concatenate([near[:, at:at + width], far[:, at:at + width]], axis=0)
        residual = weight * predicted[:, at:at + width] - summed
        high = residual.astype(BF16)
        low = (residual - high.astype(F32)).astype(BF16)
        both = jnp.concatenate([high, low], axis=0)
        grad_space = dot(time_twice, both, (1, 0))
        grad_time = grad_time + dot(part, both, (1, 1))
        new = base[:, at:at + width] - ETA_SPACE * grad_space
        fresh[:, at:at + width] = new
        norm = norm + jnp.sum(new * new, axis=1, keepdims=True)
        wide = part.astype(F32)
        for row in range(width // LANES):
            strip = row_of(wide, row)
            square = jnp.sum(strip * strip, axis=1, keepdims=True)
            grad_diag = grad_diag + square * seen[at // LANES + row:at // LANES + row + 1, :]
    return grad_time[:, :LANES] + grad_time[:, LANES:], grad_diag, norm


def side_gradients(half, first, predicted, packed, time_t, seen, summed, take):
    rank, days = time_t.shape[0], summed.shape[0]
    below = lax.broadcasted_iota(jnp.int32, time_t.shape, 1) < days
    moved = pltpu.roll(time_t, days, 1)
    time_twice = (jnp.where(below, moved, time_t) if first else jnp.where(below, time_t, moved)).astype(BF16)
    seen_bf = seen[:, :days].astype(BF16)
    owner = lax.broadcasted_iota(jnp.int32, (TAIL, WIDTH), 0)
    lane = lax.broadcasted_iota(jnp.int32, (TAIL, WIDTH), 1)
    grad_time = jnp.zeros((rank, LANES), F32)
    grad_diag = jnp.zeros((rank, LANES), F32)
    for at in range(0, half * LANES, WIDTH):
        spread = (owner * LANES <= lane + at) & (lane + at < (owner + 1) * LANES)
        weight = dot(seen_bf, spread.astype(BF16), (0, 0))
        part = packed[:, at:at + WIDTH]
        residual = weight * predicted[first:first + days, at:at + WIDTH] - summed[:, at:at + WIDTH]
        high = residual.astype(BF16)
        low = (residual - high.astype(F32)).astype(BF16)
        both = jnp.concatenate([high, low], axis=0)
        take(at, dot(time_twice, both, (1, 0)))
        grad_time = grad_time + dot(part, both, (1, 1))
        wide = part.astype(F32)
        for row in range(WIDTH // LANES):
            strip = row_of(wide, row)
            square = jnp.sum(strip * strip, axis=1, keepdims=True)
            grad_diag = grad_diag + square * seen[at // LANES + row:at // LANES + row + 1, :]
    return jnp.where(below, grad_time + pltpu.roll(grad_time, days, 1), pltpu.roll(grad_diag, days, 1))


def add_up(parts, rows):
    value = parts[0][rows, :].astype(F32)
    for piece in parts[1:]:
        value = value + piece[rows, :].astype(F32)
    return value


def unpack_pieces(half, parts, summed, seen):
    days = summed.shape[0]
    for row in range(half):
        summed[:, row * LANES:(row + 1) * LANES] = add_up(parts, slice(row * days, (row + 1) * days))
    seen[...] = add_up(parts, slice(half * days, half * days + TAIL))


def narrow(value, rank):
    high = value[2 * rank:, :].astype(BF16)
    low = (value[2 * rank:, :] - high.astype(F32)).astype(BF16)
    return value[: 2 * rank, :].astype(BF16), jnp.concatenate([high.astype(F32), low.astype(F32)], axis=0).astype(BF16)


def widened(value, rank):
    value = value.astype(F32)
    return jnp.concatenate([value[: 2 * rank, :], value[2 * rank:2 * rank + NORM, :] + value[2 * rank + NORM:, :]], axis=0)


def post_all(sums, message, outgoing):
    grad_time, grad_diag, norm = sums
    rank = norm.shape[0]
    last = column_as_row(norm)
    for out, shift in ((message, 0), (outgoing, LANES // 2)):
        parts = [pltpu.roll(part, shift, 1) if shift else part for part in (grad_time, grad_diag)]
        out[: 2 * rank, :], out[2 * rank:, :] = narrow(jnp.concatenate([*parts, last], axis=0), rank)


def near_kernel(half, days, order, paired, swap, surface, edge_near, predicted, packed, time_t, edge_far, *rest):
    pieces, rest = dict(zip(order, rest)), rest[len(order):]
    cols, (base, block, summed, seen) = rest[:-4], rest[-4:]
    if paired:
        at = half * days + TAIL
        cols = in_order(swap(), *[ref[at:, :].astype(F32) for ref in (cols[0], pieces[0, 2])])
    left, right = (ref[...] for ref in cols)
    smooth(half, surface[...], edge_near[...], edge_far[...], left[half:, :], right[:half, :], None, base)
    unpack_pieces(half, [pieces[key] for key in sorted(pieces)], summed, seen)

    def take(at, grad_space):
        base[:, at:at + WIDTH] = base[:, at:at + WIDTH] - ETA_SPACE * grad_space

    block[...] = side_gradients(half, 0, predicted, packed, time_t[...], seen, summed, take)


def far_kernel(half, days, n_lon, base, predicted, packed, time_t, block, *rest):
    parts, rest = rest[:n_lon], rest[n_lon:]
    fresh, message, crossing, cols, edge_near, edge_far, summed, seen = rest
    core = lax.axis_index("ta")
    rank = block.shape[0]
    unpack_pieces(half, parts, summed, seen)

    def take(at, grad_space):
        fresh[:, at:at + WIDTH] = base[:, at:at + WIDTH] - ETA_SPACE * grad_space

    crossing[:rank, :] = side_gradients(half, days, predicted, packed, time_t[...], seen, summed, take)
    message[:rank, :] = block[...]
    new = fresh[...]
    norm = column_as_row(jnp.sum(new * new, axis=1, keepdims=True))
    message[rank:, :] = norm
    crossing[rank:, :] = norm
    cols[...] = jnp.zeros(cols.shape, F32)
    cols[:, :rank] = border(new, half)
    first_row, last_row = row_of(new, 0), row_of(new, half - 1)
    edge_near[...] = pick(core == 0, last_row, first_row)
    edge_far[...] = pick(core == 0, first_row, last_row)


def total_of(parts):
    total = parts[0][...].astype(F32)
    if len(parts) > 1:
        one, two, three = (part[...].astype(F32) for part in parts[1:])
        total = (total + one) + (two + three)
    return total


def packed_norm(norm, cols, rank):
    free = LANES - rank
    line = lax.broadcasted_iota(jnp.int32, cols.shape, 0)
    lane = lax.broadcasted_iota(jnp.int32, cols.shape, 1)
    for part in range(rank // free):
        moved = pltpu.roll(norm, rank - part * free, 1)
        cols = jnp.where((lane >= rank) & (line == part), moved, cols)
    return cols


def unpacked(block, rank):
    free = LANES - rank
    line = lax.broadcasted_iota(jnp.int32, block.shape, 0)
    lane = lax.broadcasted_iota(jnp.int32, block.shape, 1)
    norm = jnp.zeros(block.shape, F32)
    for part in range(rank // free):
        row = jnp.where((lane >= rank) & (line == part), block, 0.0)
        norm = norm + pltpu.roll(row, LANES - rank + part * free, 1)
    return jnp.broadcast_to(jnp.sum(norm, axis=0, keepdims=True), block.shape)


def own_kernel(n_parts, time_t, *rest):
    parts, (time_own, norm) = rest[:n_parts], rest[n_parts:]
    rank = time_t.shape[0]
    days = LANES // 2
    total = total_of(parts)
    block = total[:rank, :]
    own = lax.broadcasted_iota(jnp.int32, block.shape, 1) < days
    time_own[...] = jnp.where(own, time_t[...] - block / (pltpu.roll(block, days, 1) + RIDGE), 0.0)
    norm[...] = unpacked(total[rank:, :], rank) if n_parts > 1 else total[rank:, :]


def rescaling(counts, norm, time_new):
    day_count, cell_count = counts
    space_sq = row_as_column(norm[:1, :], time_new.shape[0])
    square = time_new * time_new
    time_sq = 0.5 * jnp.sum(square + pltpu.roll(square, LANES // 2, 1), axis=1, keepdims=True)
    ratio = (time_sq / day_count + EPSILON) / (space_sq / cell_count + EPSILON)
    return jnp.sqrt(jnp.sqrt(ratio))


def second_kernel(half, counts, paired, swap, surface, time_own, time_other, norm, near, far, seen_near, seen_far, edge_near, edge_far, cols_a, cols_b, *rest):
    fresh, time_out, message, outgoing, scaled, base, predicted, packed = rest
    rank = surface.shape[0]
    time_new = time_own[...] + pltpu.roll(time_other[...], LANES // 2, 1)
    scale = rescaling(counts, norm[...], time_new)
    time_now = time_new / scale
    time_out[...] = time_now
    scaled[...] = surface[...] * scale
    packed[...] = scaled[...].astype(BF16)
    time_bf = time_now.astype(BF16)
    for at in range(0, half * LANES, WIDTH):
        predicted[:, at:at + WIDTH] = dot(time_bf, packed[:, at:at + WIDTH], (0, 0))
    if paired:
        left, right = in_order(swap(), cols_a[rank:, :], cols_b[rank:, :])
    else:
        left, right = cols_a[half:, :], cols_b[:half, :]
    smooth(half, scaled[...], edge_near[...], edge_far[...], left, right, scale, base)
    seen = seen_near[...] + pltpu.roll(seen_far[...], LANES // 2, 1)
    sums = gradients(half, base, predicted, packed, time_now, seen, near, far, fresh)
    post_all(sums, message, outgoing)


def last_kernel(half, counts, n_parts, surface, other, time_t, *rest):
    parts = rest[:n_parts]
    space_out, time_out, flip = rest[n_parts:]
    core = lax.axis_index("ta")
    rank = surface.shape[0]
    height = space_out.shape[0] // rank
    total = total_of(parts)
    if parts[0].dtype == BF16:
        total = widened(total, rank)
    time_new = time_t[...] - total[:rank, :] / (total[rank:2 * rank, :] + RIDGE)
    scale = rescaling(counts, total[2 * rank:, :], time_new)
    flip[...] = jnp.zeros(flip.shape, F32)
    flip[:rank, :] = time_new / scale
    time_out[...] = flip[...].T[: time_out.shape[0], :rank]
    for row in range(half):
        at = row * LANES
        space_out[pl.ds(core * half + row, rank, stride=height), :] = surface[:, at:at + LANES] * scale
        space_out[pl.ds((1 - core) * half + row, rank, stride=height), :] = other[:, at:at + LANES] * scale


def near_merge_kernel(mine, theirs, out):
    rows = mine.shape[0]
    out[:rows, :] = (mine[...].astype(F32) + theirs[:rows, :].astype(F32)).astype(BF16)
    out[rows:, :] = theirs[rows:, :]


def far_merge_kernel(mine, theirs, piece_in, edge_in, out, piece_out, edge_out):
    piece_out[...] = piece_in[...]
    edge_out[...] = edge_in[...]
    out[...] = (mine[...].astype(F32) + theirs[...].astype(F32)).astype(BF16)


def add_kernel(mine, theirs, total):
    total[...] = mine[...] + theirs[...]


def core_sum_kernel(mine, core, total):
    total[...] = mine[: total.shape[0], :] + core[...]


def band_sum_kernel(half, swap, mine, band, cols, *totals):
    rank = mine.shape[0] - NORM
    value = mine[...] + band[...]
    borders = in_order(swap(), cols[:half, :], cols[half:, :])
    for total, lines in zip(totals, borders):
        total[:rank, :] = value[:rank, :]
        total[rank:, :] = value[rank:, :] if len(totals) == 1 else packed_norm(value[rank:, :], lines, rank)


def all_sum_kernel(rank, mine, core, band, both, total):
    one, two, three, four = (widened(part[...], rank) for part in (mine, core, band, both))
    value = (one + two) + (three + four)
    if total.dtype == BF16:
        total[: 2 * rank, :], total[2 * rank:, :] = narrow(value, rank)
    else:
        total[...] = value


def shape(dims, dtype=F32):
    return jax.ShapeDtypeStruct(tuple(dims), dtype)


def padded(ref):
    *outer, rows, lanes = (1, *ref.shape)
    return math.prod(outer) * -(-rows // 16) * 16 * -(-lanes // LANES) * LANES * jnp.dtype(ref.dtype).itemsize


def call(kernel, out_shape, scratch=(), hbm=0, after=0, flops=1_000_000):
    def run(*operands):
        operands = [pltpu.with_memory_space_constraint(x, pltpu.HBM) if i < hbm else x for i, x in enumerate(operands)]
        vmem = [*operands[hbm:len(operands) - after], *jax.tree.leaves(out_shape), *scratch]
        specs = [pltpu.HBM] * hbm + [pltpu.VMEM] * (len(operands) - hbm - after) + [pl.ANY] * after
        return pl.pallas_call(
            kernel,
            out_shape=out_shape,
            in_specs=[pl.BlockSpec(memory_space=space) for space in specs],
            out_specs=jax.tree.map(lambda _: pl.BlockSpec(memory_space=pltpu.VMEM), out_shape),
            scratch_shapes=list(scratch),
            compiler_params=pltpu.CompilerParams(vmem_limit_bytes=SPARE + sum(padded(ref) for ref in vmem if len(ref.shape) > 1)),
            cost_estimate=pl.CostEstimate(flops=flops, bytes_accessed=1_000_000, transcendentals=0),
        )(*operands)

    return run


def across(value, axis, step):
    return lax.ppermute(value, axis, [(i, i ^ step) for i in range(lax.axis_size(axis))])


def shards(swath, obs_mask, target, send_list, send_count, factor_space, factor_time):
    n_lon, n_lat, n_ta = (lax.axis_size(axis) for axis in ("lon", "lat", "ta"))
    slots, days, cells = swath.shape
    rank, height, _ = factor_space.shape
    half = height // n_ta
    wide = half * LANES
    counts = (float(days * n_ta), float(height * cells * n_lon * n_lat))
    own_rows, sum_rows = rank + NORM, 2 * rank + NORM
    flip = pltpu.VMEM((LANES, LANES), F32)

    paired = n_lon == 4

    distant, close = range(n_lon // 2, n_lon), range(1, n_lon // 2)
    sends = [(side, step) for step in reversed(distant) for side in (0, 1)] + [(1, 0)]
    sends += [(side, step) for side in (0, 1) for step in close] + [(0, 0)]

    def piece_rows(side, step):
        more = 3 * days if (side, step) == (1, 0) else COLS if paired and (side, step) == (0, 3) else 0
        return half * days + TAIL + more

    operands = (send_list, send_count, target, swath, obs_mask, factor_space.reshape(rank * height, cells), factor_time)
    early = (0, n_lon - 1)
    sends.remove(early)
    first, total, seen, surface, space, time, *cols = call(
        functools.partial(route_kernel, half, early, paired),
        [shape((piece_rows(*early), cells), BF16), shape((2 * n_lon * half, days, cells)), shape((2 * n_lon * half + TAIL, LANES))]
        + [shape((rank, wide))]
        + [shape(ref.shape) for ref in operands[5:]]
        + [shape((COLS, LANES))] * (not paired),
        [pltpu.SMEM(ref.shape, jnp.int32) for ref in operands[:3]]
        + [pltpu.VMEM(ref.shape, ref.dtype) for ref in operands[3:5]]
        + [pltpu.SMEM((slots + 1,), jnp.int32), pltpu.SemaphoreType.DMA((len(operands) - 1 + SWATH_COPIES,))]
        + [pltpu.VMEM((COLS, LANES), F32)] * paired,
        hbm=len(operands),
    )(*operands)
    *pieces, edge_near, edge_far = call(
        functools.partial(pack_kernel, half, n_lon, sends),
        [shape((piece_rows(*key), cells), BF16) for key in sends]
        + [shape((rank, LANES)), shape((rank, LANES))],
    )(total, seen, space, time)

    def arrived(key, piece):
        side, step = key
        if side:
            return across(piece, ("lon", "ta"), 2 * step + 1)
        return across(piece, "lon", step) if step else piece

    pieces = dict(zip([early, *sends], [first, *pieces]))
    borders = ()
    if paired:
        near, far = (across(pieces.pop((side, 3)), "lon", 1) for side in (0, 1))
        borders = (near,)
        pieces[0, 2] = call(near_merge_kernel, shape(near.shape, BF16))(pieces[0, 2], near)
        outs = [shape(far.shape, BF16), shape(far.shape, BF16), shape(edge_far.shape)]
        pieces[1, 2], pieces[1, 1], edge_far = call(far_merge_kernel, outs)(pieces[1, 2], far, pieces[1, 1], edge_far)
    pieces = {key: arrived(key, piece) for key, piece in pieces.items()}
    order = list(pieces)

    def bands(edge):
        there = [(2 * band + 1, (2 * band + 2) % (2 * n_lat)) for band in range(n_lat)]
        return lax.ppermute(edge, ("lat", "ta"), there + [(b, a) for a, b in there])

    def swap():
        return lax.rem(lax.axis_index("lon"), 2) == 1 if paired else jnp.bool_(True)

    def columns(value):
        if paired:
            return across(value, "lon", 1), across(value, "lon", 3)
        ring = [(i, (i + 1) % n_lon) for i in range(n_lon)]
        return lax.ppermute(value, "lon", ring), lax.ppermute(value, "lon", [(b, a) for a, b in ring])

    predicted, packed, time_t = call(
        functools.partial(model_kernel, half),
        [shape((2 * days, wide)), shape((rank, wide), BF16), shape((rank, LANES))],
        [flip],
    )(surface, factor_time, pieces[1, 0])

    fresh, edge = shape((rank, wide)), shape((rank, LANES))
    sides = [[key for key in order if key[0] == side] for side in (0, 1)]
    side_out = [shape((days, wide)), shape((TAIL, LANES))]
    base, block, near, seen_near = call(
        functools.partial(near_kernel, half, days, sides[0], paired, swap),
        [fresh, edge, *side_out],
    )(surface, edge_near, predicted, packed, time_t, bands(edge_far), *[pieces[key] for key in sides[0]], *(borders if paired else columns(*cols)))
    surface, message, crossing, cols, edge_near, edge_far, far, seen_far = call(
        functools.partial(far_kernel, half, days, len(sides[1])),
        [fresh, shape((own_rows, LANES)), shape((own_rows, LANES)), shape((COLS, LANES)), edge, edge, *side_out],
    )(base, predicted, packed, time_t, block, *[pieces[key] for key in sides[1]])

    narrowed = shape((sum_rows + NORM, LANES), BF16)

    def add(mine, theirs):
        return call(add_kernel, shape(mine.shape))(mine, theirs)

    def doubled(total, axis, step):
        while step < lax.axis_size(axis):
            total = add(total, across(total, axis, step))
            step *= 2
        return total

    def over_lon(total):
        if paired:
            return [total] + [across(total, "lon", step) for step in (1, 2, 3)]
        return [doubled(total, "lon", 1)]

    def around(mine, core, both):
        return mine, across(core, "ta", 1), across(mine, "lat", 1), across(both, ("lat", "ta"), 3)

    total = call(core_sum_kernel, shape(crossing.shape))(message, across(crossing, "ta", 1))
    direct = paired and n_lat == 2
    band_sum = functools.partial(band_sum_kernel, half, swap)
    total, *again = call(band_sum, [shape(crossing.shape)] * (1 + direct))(total, across(total, "lat", 1), cols)
    if direct:
        parts = [total] + [across(value, "lon", step) for step, value in ((1, total), (2, again[0]), (3, again[0]))]
        cols = parts[1], parts[3]
    else:
        parts = [doubled(doubled(total, "lat", 2), "lon", 1)]
        cols = columns(cols)
    time_own, norm = call(functools.partial(own_kernel, len(parts)), [edge, shape((NORM, LANES))])(time_t, *parts)

    surface, time_t, message, outgoing = call(
        functools.partial(second_kernel, half, counts, direct, swap),
        [fresh, edge, narrowed, narrowed],
        [pltpu.VMEM((rank, wide), F32), pltpu.VMEM((rank, wide), F32), pltpu.VMEM((2 * days, wide), F32), pltpu.VMEM((rank, wide), BF16)],
    )(surface, time_own, across(time_own, "ta", 1), norm, near, far, seen_near, seen_far, across(edge_near, "ta", 1), bands(edge_far), *cols)

    other = across(surface, "ta", 1)
    total = narrowed if paired and n_lat == 2 else shape((sum_rows, LANES))
    total = call(functools.partial(all_sum_kernel, rank), total)(*around(message, outgoing, outgoing))
    parts = over_lon(doubled(total, "lat", 2))
    space, time = call(
        functools.partial(last_kernel, half, counts, len(parts)),
        [shape((rank * height, cells)), shape(factor_time.shape)],
        [flip],
    )(surface, other, time_t, *parts)
    return space.reshape(rank, height, cells), time


def solution(mesh):
    in_specs = (
        P(("grp", "lon", "lat"), "ta", None),
        P(("grp", "lon", "lat"), "ta"),
        P(("grp", "lon", "lat")),
        P(("grp", "lon", "lat"), None, None),
        P(("grp", "lon", "lat"), None),
        P(None, ("grp", "lat"), "lon"),
        P(("grp", "ta"), None),
    )
    out_specs = (P(None, ("grp", "lat"), "lon"), P(("grp", "ta"), None))
    return jax.shard_map(shards, mesh=mesh, in_specs=in_specs, out_specs=out_specs, check_vma=False)
```

```python
import functools
import math

import jax
import jax.numpy as jnp
from jax import lax
from jax.experimental import pallas as pl
from jax.experimental.pallas import tpu as pltpu
from jax.sharding import PartitionSpec as P

SMOOTH = 2.0
ETA_SPACE = 0.08
RIDGE = 1.0
EPSILON = 1e-06

F32 = jnp.float32
BF16 = jnp.bfloat16
LANES = 128
WIDTH = 512
TAIL = 16
COLS = 16
NORM = 8
SPARE = 2 * 1024 * 1024
SWATH_COPIES = 1
UNROLL = 4


def dot(a, b, contract):
    return lax.dot_general(a, b, ((contract[:1], contract[1:]), ((), ())), preferred_element_type=F32)


def route_kernel(half, early, paired, list_hbm, count_hbm, target_hbm, swath_hbm, mask_hbm, space_hbm, time_hbm, *rest):
    piece, total, seen, surface, space_ref, time_ref, *rest = rest
    cols = rest.pop(-1 if paired else 0)
    list_ref, count_ref, target_ref, swath_ref, mask_ref, place, arrived = rest
    me, core = lax.axis_index("lon"), lax.axis_index("ta")
    n_lon = list_ref.shape[1]
    slots, days, cells = swath_ref.shape
    chunk = slots // SWATH_COPIES
    small = [(list_hbm, list_ref), (count_hbm, count_ref), (target_hbm, target_ref), (mask_hbm, mask_ref)]
    large = [(swath_hbm.at[pl.ds(at, chunk)], swath_ref.at[pl.ds(at, chunk)]) for at in range(0, slots, chunk)]
    model = [(space_hbm, space_ref), (time_hbm, time_ref)]
    copies = [pltpu.make_async_copy(src, dst, arrived.at[i]) for i, (src, dst) in enumerate(small + model + large)]
    for copy in copies:
        copy.start()
    total[...] = jnp.zeros(total.shape, F32)
    seen[...] = jnp.zeros(seen.shape, F32)
    for copy in copies[: len(small)]:
        copy.wait()

    def owner(d, carry):
        first = jnp.bitwise_xor(d, me) * half
        count = count_ref[0, d]

        def entries(i, carry):
            for k in range(UNROLL):
                k = i * UNROLL + k
                slot = list_ref[0, d, k]
                row = target_ref[slot]
                far = jnp.bitwise_xor(lax.shift_right_logical(row, half.bit_length() - 1), core)
                place[jnp.where(k < count, slot, slots)] = far * (n_lon * half) + first + jnp.bitwise_and(row, half - 1)
            return carry

        return lax.fori_loop(0, lax.div(count + UNROLL - 1, UNROLL), entries, carry)

    lax.fori_loop(0, n_lon, owner, 0)
    for copy in copies[len(small):len(small) + len(model)]:
        copy.wait()
    rank = surface.shape[0]
    height = space_ref.shape[0] // rank
    for row in range(half):
        surface[:, row * LANES:(row + 1) * LANES] = space_ref[pl.ds(core * half + row, rank, stride=height), :]
    cols[...] = jnp.zeros(cols.shape, F32)
    cols[:, :rank] = border(surface[...], half)
    mask = mask_ref[...].astype(F32)
    by_day = mask.T.astype(BF16)
    for slot in range(slots):
        if slot % chunk == 0:
            copies[len(small) + len(model) + slot // chunk].wait()
        at = place[slot]
        total[at] += (swath_ref[slot] * by_day[:, slot:slot + 1]).astype(F32)
        seen[pl.ds(at, 1), :days] += mask[slot:slot + 1, :]
    pack(half, n_lon, early, total, seen, piece)
    end = half * days + TAIL
    if piece.shape[0] > end:
        piece[end:, :] = cols[...].astype(BF16)


def pack(half, n_lon, key, total, seen, out):
    side, step = key
    at = (side * n_lon + step) * half
    end = half * total.shape[1]
    out[:end, :] = total[at:at + half].reshape(end, LANES).astype(BF16)
    if side == 0:
        other = at + n_lon * half
        both = jnp.concatenate([seen[at:at + half, :], seen[other:other + half, :]], axis=0)
        out[end:end + TAIL, :] = both.astype(BF16)


def pack_kernel(half, n_lon, sends, total, seen, space_ref, time_ref, *rest):
    outs, (edge_near, edge_far) = rest[: len(sends)], rest[len(sends):]
    core = lax.axis_index("ta")
    days = total.shape[1]
    end = half * days
    rank = edge_near.shape[0]
    height = space_ref.shape[0] // rank
    edge_near[...] = space_ref[pl.ds(half - core, rank, stride=height), :]
    edge_far[...] = space_ref[pl.ds(core * (height - 1), rank, stride=height), :]
    for key, out in zip(sends, outs):
        pack(half, n_lon, key, total, seen, out)
        if key == (1, 0):
            left = time_ref[...]
            for part in range(end, end + 3 * days, days):
                value = left.astype(BF16)
                out[part:part + days, :] = jnp.zeros((days, LANES), BF16)
                out[part:part + days, :rank] = value
                left = left - value.astype(F32)


def row_of(surface, row):
    return surface[:, row * LANES:(row + 1) * LANES]


def diagonal(value, rank):
    row = lax.broadcasted_iota(jnp.int32, (rank, LANES), 0)
    lane = lax.broadcasted_iota(jnp.int32, (rank, LANES), 1)
    return jnp.where(row == lane, value, 0.0)


def column_as_row(column):
    row = jnp.sum(diagonal(column, column.shape[0]), axis=0, keepdims=True)
    return jnp.broadcast_to(row, (NORM, LANES))


def row_as_column(row, rank):
    return jnp.sum(diagonal(row, rank), axis=1, keepdims=True)


def border(surface, half):
    line = lax.broadcasted_iota(jnp.int32, (COLS, half * LANES), 0)
    lane = lax.broadcasted_iota(jnp.int32, (COLS, half * LANES), 1)
    pick_lane = jnp.where(line < half, line * LANES, (line - half) * LANES + LANES - 1)
    return dot((lane == pick_lane).astype(BF16), surface.astype(BF16), (1, 1))


def smoothed(surface, half, above, below, sides):
    lane = lax.broadcasted_iota(jnp.int32, above.shape, 1)
    strips = []
    for row in range(half):
        here = row_of(surface, row)
        up = above if row == 0 else row_of(surface, row - 1)
        down = below if row == half - 1 else row_of(surface, row + 1)
        left = jnp.where(lane == 0, 0.0, pltpu.roll(here, 1, 1))
        right = jnp.where(lane == LANES - 1, 0.0, pltpu.roll(here, LANES - 1, 1))
        lap = 4.0 * here - (up + down + left + right + row_of(sides, row))
        strips.append(here - (ETA_SPACE * SMOOTH) * lap)
    return strips


def pick(flag, a, b):
    return jnp.where(flag, a, b)


def in_order(odd, a, b):
    return pick(odd, a, b), pick(odd, b, a)


def model_kernel(half, surface, time_own, piece, predicted, packed, time_t, days_all):
    rank = surface.shape[0]
    days = time_own.shape[0]
    at = half * days
    high, middle, low = (piece[first:first + days, :].astype(F32) for first in range(at, at + 3 * days, days))
    days_all[...] = jnp.zeros(days_all.shape, F32)
    days_all[:days, :rank] = time_own[...]
    days_all[days:, :] = (high + middle) + low
    time_full = days_all[...]
    time_t[...] = time_full.T[:rank, :]
    packed[...] = surface[...].astype(BF16)
    time_bf = time_full[:, :rank].astype(BF16)
    for at in range(0, half * LANES, 2 * LANES):
        predicted[:, at:at + 2 * LANES] = dot(time_bf, packed[:, at:at + 2 * LANES], (1, 0))


def smooth(half, surface, edge_near, edge_far, left, right, scale, base):
    core = lax.axis_index("ta")
    rank = surface.shape[0]
    band = lax.axis_index("lat")
    outer = pick(core == 0, band == 0, band == lax.axis_size("lat") - 1)
    edge_far = jnp.where(outer, 0.0, edge_far)
    above = pick(core == 0, edge_far, edge_near)
    below = pick(core == 0, edge_near, edge_far)
    line = lax.broadcasted_iota(jnp.int32, (2 * half, half * LANES), 0)
    lane = lax.broadcasted_iota(jnp.int32, (2 * half, half * LANES), 1)
    place = jnp.where(line < half, line * LANES, (line - half) * LANES + LANES - 1)
    cols = jnp.concatenate([left, right], axis=0)
    sides = dot(cols[:, :rank].astype(BF16), (lane == place).astype(BF16), (0, 0))
    if scale is not None:
        above, below, sides = above * scale, below * scale, sides * scale
    for row, strip in enumerate(smoothed(surface, half, above, below, sides)):
        base[:, row * LANES:(row + 1) * LANES] = strip


def gradients(half, base, predicted, packed, time_t, seen, near, far, fresh):
    rank = time_t.shape[0]
    time_bf = time_t.astype(BF16)
    time_twice = jnp.concatenate([time_bf, time_bf], axis=1)
    seen_bf = seen.astype(BF16)
    width = WIDTH
    owner = lax.broadcasted_iota(jnp.int32, (TAIL, width), 0)
    lane = lax.broadcasted_iota(jnp.int32, (TAIL, width), 1)
    grad_time = jnp.zeros((rank, 2 * LANES), F32)
    grad_diag = jnp.zeros((rank, LANES), F32)
    norm = jnp.zeros((rank, 1), F32)
    for at in range(0, half * LANES, width):
        spread = (owner * LANES <= lane + at) & (lane + at < (owner + 1) * LANES)
        weight = dot(seen_bf, spread.astype(BF16), (0, 0))
        part = packed[:, at:at + width]
        summed = jnp.concatenate([near[:, at:at + width], far[:, at:at + width]], axis=0)
        residual = weight * predicted[:, at:at + width] - summed
        high = residual.astype(BF16)
        low = (residual - high.astype(F32)).astype(BF16)
        both = jnp.concatenate([high, low], axis=0)
        grad_space = dot(time_twice, both, (1, 0))
        grad_time = grad_time + dot(part, both, (1, 1))
        new = base[:, at:at + width] - ETA_SPACE * grad_space
        fresh[:, at:at + width] = new
        norm = norm + jnp.sum(new * new, axis=1, keepdims=True)
        wide = part.astype(F32)
        for row in range(width // LANES):
            strip = row_of(wide, row)
            square = jnp.sum(strip * strip, axis=1, keepdims=True)
            grad_diag = grad_diag + square * seen[at // LANES + row:at // LANES + row + 1, :]
    return grad_time[:, :LANES] + grad_time[:, LANES:], grad_diag, norm


def side_gradients(half, first, predicted, packed, time_t, seen, summed, take):
    rank, days = time_t.shape[0], summed.shape[0]
    below = lax.broadcasted_iota(jnp.int32, time_t.shape, 1) < days
    moved = pltpu.roll(time_t, days, 1)
    time_twice = (jnp.where(below, moved, time_t) if first else jnp.where(below, time_t, moved)).astype(BF16)
    seen_bf = seen[:, :days].astype(BF16)
    owner = lax.broadcasted_iota(jnp.int32, (TAIL, WIDTH), 0)
    lane = lax.broadcasted_iota(jnp.int32, (TAIL, WIDTH), 1)
    grad_time = jnp.zeros((rank, LANES), F32)
    grad_diag = jnp.zeros((rank, LANES), F32)
    for at in range(0, half * LANES, WIDTH):
        spread = (owner * LANES <= lane + at) & (lane + at < (owner + 1) * LANES)
        weight = dot(seen_bf, spread.astype(BF16), (0, 0))
        part = packed[:, at:at + WIDTH]
        residual = weight * predicted[first:first + days, at:at + WIDTH] - summed[:, at:at + WIDTH]
        high = residual.astype(BF16)
        low = (residual - high.astype(F32)).astype(BF16)
        both = jnp.concatenate([high, low], axis=0)
        take(at, dot(time_twice, both, (1, 0)))
        grad_time = grad_time + dot(part, both, (1, 1))
        wide = part.astype(F32)
        for row in range(WIDTH // LANES):
            strip = row_of(wide, row)
            square = jnp.sum(strip * strip, axis=1, keepdims=True)
            grad_diag = grad_diag + square * seen[at // LANES + row:at // LANES + row + 1, :]
    return jnp.where(below, grad_time + pltpu.roll(grad_time, days, 1), pltpu.roll(grad_diag, days, 1))


def add_up(parts, rows):
    value = parts[0][rows, :].astype(F32)
    for piece in parts[1:]:
        value = value + piece[rows, :].astype(F32)
    return value


def unpack_pieces(half, parts, summed):
    days = summed.shape[0]
    for row in range(half):
        summed[:, row * LANES:(row + 1) * LANES] = add_up(parts, slice(row * days, (row + 1) * days))


def narrow(value, rank):
    high = value[2 * rank:, :].astype(BF16)
    low = (value[2 * rank:, :] - high.astype(F32)).astype(BF16)
    return value[: 2 * rank, :].astype(BF16), jnp.concatenate([high.astype(F32), low.astype(F32)], axis=0).astype(BF16)


def widened(value, rank):
    value = value.astype(F32)
    return jnp.concatenate([value[: 2 * rank, :], value[2 * rank:2 * rank + NORM, :] + value[2 * rank + NORM:, :]], axis=0)


def post_all(sums, message, outgoing):
    grad_time, grad_diag, norm = sums
    rank = norm.shape[0]
    last = column_as_row(norm)
    for out, shift in ((message, 0), (outgoing, LANES // 2)):
        parts = [pltpu.roll(part, shift, 1) if shift else part for part in (grad_time, grad_diag)]
        out[: 2 * rank, :], out[2 * rank:, :] = narrow(jnp.concatenate([*parts, last], axis=0), rank)


def near_kernel(half, days, order, paired, swap, surface, edge_near, predicted, packed, time_t, edge_far, *rest):
    pieces, rest = dict(zip(order, rest)), rest[len(order):]
    cols, (base, block, summed, seen, beside) = rest[:-5], rest[-5:]
    if paired:
        at = half * days + TAIL
        cols = in_order(swap(), *[ref[at:, :].astype(F32) for ref in (cols[0], pieces[0, 2])])
    left, right = (ref[...] for ref in cols)
    smooth(half, surface[...], edge_near[...], edge_far[...], left[half:, :], right[:half, :], None, base)
    parts = [pieces[key] for key in sorted(pieces)]
    unpack_pieces(half, parts, summed)
    seen[...] = add_up(parts, slice(half * days, half * days + TAIL))
    beside[...] = jnp.concatenate([seen[half:, :], jnp.zeros((half, LANES), F32)], axis=0)

    def take(at, grad_space):
        base[:, at:at + WIDTH] = base[:, at:at + WIDTH] - ETA_SPACE * grad_space

    block[...] = side_gradients(half, 0, predicted, packed, time_t[...], seen, summed, take)


def far_kernel(half, days, n_lon, base, predicted, packed, time_t, block, *rest):
    parts, rest = rest[:n_lon], rest[n_lon:]
    seen, fresh, message, crossing, cols, edge_near, edge_far, summed = rest
    core = lax.axis_index("ta")
    rank = block.shape[0]
    unpack_pieces(half, parts, summed)

    def take(at, grad_space):
        fresh[:, at:at + WIDTH] = base[:, at:at + WIDTH] - ETA_SPACE * grad_space

    crossing[:rank, :] = side_gradients(half, days, predicted, packed, time_t[...], seen, summed, take)
    message[:rank, :] = block[...]
    new = fresh[...]
    norm = column_as_row(jnp.sum(new * new, axis=1, keepdims=True))
    message[rank:, :] = norm
    crossing[rank:, :] = norm
    cols[...] = jnp.zeros(cols.shape, F32)
    cols[:, :rank] = border(new, half)
    first_row, last_row = row_of(new, 0), row_of(new, half - 1)
    edge_near[...] = pick(core == 0, last_row, first_row)
    edge_far[...] = pick(core == 0, first_row, last_row)


def total_of(parts):
    total = parts[0][...].astype(F32)
    if len(parts) > 1:
        one, two, three = (part[...].astype(F32) for part in parts[1:])
        total = (total + one) + (two + three)
    return total


def packed_norm(norm, cols, rank):
    free = LANES - rank
    line = lax.broadcasted_iota(jnp.int32, cols.shape, 0)
    lane = lax.broadcasted_iota(jnp.int32, cols.shape, 1)
    for part in range(rank // free):
        moved = pltpu.roll(norm, rank - part * free, 1)
        cols = jnp.where((lane >= rank) & (line == part), moved, cols)
    return cols


def unpacked(block, rank):
    free = LANES - rank
    line = lax.broadcasted_iota(jnp.int32, block.shape, 0)
    lane = lax.broadcasted_iota(jnp.int32, block.shape, 1)
    norm = jnp.zeros(block.shape, F32)
    for part in range(rank // free):
        row = jnp.where((lane >= rank) & (line == part), block, 0.0)
        norm = norm + pltpu.roll(row, LANES - rank + part * free, 1)
    return jnp.broadcast_to(jnp.sum(norm, axis=0, keepdims=True), block.shape)


def own_kernel(n_parts, time_t, *rest):
    parts, (time_own, norm) = rest[:n_parts], rest[n_parts:]
    rank = time_t.shape[0]
    days = LANES // 2
    total = total_of(parts)
    block = total[:rank, :]
    own = lax.broadcasted_iota(jnp.int32, block.shape, 1) < days
    time_own[...] = jnp.where(own, time_t[...] - block / (pltpu.roll(block, days, 1) + RIDGE), 0.0)
    norm[...] = unpacked(total[rank:, :], rank) if n_parts > 1 else total[rank:, :]


def rescaling(counts, norm, time_new):
    day_count, cell_count = counts
    space_sq = row_as_column(norm[:1, :], time_new.shape[0])
    square = time_new * time_new
    time_sq = 0.5 * jnp.sum(square + pltpu.roll(square, LANES // 2, 1), axis=1, keepdims=True)
    ratio = (time_sq / day_count + EPSILON) / (space_sq / cell_count + EPSILON)
    return jnp.sqrt(jnp.sqrt(ratio))


def second_kernel(half, counts, paired, swap, surface, time_own, time_other, norm, near, far, seen_near, seen_far, edge_near, edge_far, cols_a, cols_b, *rest):
    fresh, time_out, message, outgoing, scaled, base, predicted, packed = rest
    rank = surface.shape[0]
    time_new = time_own[...] + pltpu.roll(time_other[...], LANES // 2, 1)
    scale = rescaling(counts, norm[...], time_new)
    time_now = time_new / scale
    time_out[...] = time_now
    scaled[...] = surface[...] * scale
    packed[...] = scaled[...].astype(BF16)
    time_bf = time_now.astype(BF16)
    for at in range(0, half * LANES, WIDTH):
        predicted[:, at:at + WIDTH] = dot(time_bf, packed[:, at:at + WIDTH], (0, 0))
    if paired:
        left, right = in_order(swap(), cols_a[rank:, :], cols_b[rank:, :])
    else:
        left, right = cols_a[half:, :], cols_b[:half, :]
    smooth(half, scaled[...], edge_near[...], edge_far[...], left, right, scale, base)
    seen = seen_near[...] + pltpu.roll(seen_far[...], LANES // 2, 1)
    sums = gradients(half, base, predicted, packed, time_now, seen, near, far, fresh)
    post_all(sums, message, outgoing)


def last_kernel(half, counts, n_parts, surface, other, time_t, *rest):
    parts = rest[:n_parts]
    space_out, time_out, flip = rest[n_parts:]
    core = lax.axis_index("ta")
    rank = surface.shape[0]
    height = space_out.shape[0] // rank
    total = total_of(parts)
    if parts[0].dtype == BF16:
        total = widened(total, rank)
    time_new = time_t[...] - total[:rank, :] / (total[rank:2 * rank, :] + RIDGE)
    scale = rescaling(counts, total[2 * rank:, :], time_new)
    flip[...] = jnp.zeros(flip.shape, F32)
    flip[:rank, :] = time_new / scale
    time_out[...] = flip[...].T[: time_out.shape[0], :rank]
    for row in range(half):
        at = row * LANES
        space_out[pl.ds(core * half + row, rank, stride=height), :] = surface[:, at:at + LANES] * scale
        space_out[pl.ds((1 - core) * half + row, rank, stride=height), :] = other[:, at:at + LANES] * scale


def near_merge_kernel(mine, theirs, out):
    rows = mine.shape[0]
    out[:rows, :] = (mine[...].astype(F32) + theirs[:rows, :].astype(F32)).astype(BF16)
    out[rows:, :] = theirs[rows:, :]


def far_merge_kernel(mine, theirs, piece_in, edge_in, out, piece_out, edge_out):
    piece_out[...] = piece_in[...]
    edge_out[...] = edge_in[...]
    out[...] = (mine[...].astype(F32) + theirs[...].astype(F32)).astype(BF16)


def add_kernel(mine, theirs, total):
    total[...] = mine[...] + theirs[...]


def core_sum_kernel(mine, core, total):
    total[...] = mine[: total.shape[0], :] + core[...]


def band_sum_kernel(half, swap, mine, band, cols, *totals):
    rank = mine.shape[0] - NORM
    value = mine[...] + band[...]
    borders = in_order(swap(), cols[:half, :], cols[half:, :])
    for total, lines in zip(totals, borders):
        total[:rank, :] = value[:rank, :]
        total[rank:, :] = value[rank:, :] if len(totals) == 1 else packed_norm(value[rank:, :], lines, rank)


def all_sum_kernel(rank, mine, core, band, both, total):
    one, two, three, four = (widened(part[...], rank) for part in (mine, core, band, both))
    value = (one + two) + (three + four)
    if total.dtype == BF16:
        total[: 2 * rank, :], total[2 * rank:, :] = narrow(value, rank)
    else:
        total[...] = value


def shape(dims, dtype=F32):
    return jax.ShapeDtypeStruct(tuple(dims), dtype)


def padded(ref):
    *outer, rows, lanes = (1, *ref.shape)
    return math.prod(outer) * -(-rows // 16) * 16 * -(-lanes // LANES) * LANES * jnp.dtype(ref.dtype).itemsize


def call(kernel, out_shape, scratch=(), hbm=0, after=0, flops=1_000_000):
    def run(*operands):
        operands = [pltpu.with_memory_space_constraint(x, pltpu.HBM) if i < hbm else x for i, x in enumerate(operands)]
        vmem = [*operands[hbm:len(operands) - after], *jax.tree.leaves(out_shape), *scratch]
        specs = [pltpu.HBM] * hbm + [pltpu.VMEM] * (len(operands) - hbm - after) + [pl.ANY] * after
        return pl.pallas_call(
            kernel,
            out_shape=out_shape,
            in_specs=[pl.BlockSpec(memory_space=space) for space in specs],
            out_specs=jax.tree.map(lambda _: pl.BlockSpec(memory_space=pltpu.VMEM), out_shape),
            scratch_shapes=list(scratch),
            compiler_params=pltpu.CompilerParams(vmem_limit_bytes=SPARE + sum(padded(ref) for ref in vmem if len(ref.shape) > 1)),
            cost_estimate=pl.CostEstimate(flops=flops, bytes_accessed=1_000_000, transcendentals=0),
        )(*operands)

    return run


def across(value, axis, step):
    return lax.ppermute(value, axis, [(i, i ^ step) for i in range(lax.axis_size(axis))])


def shards(swath, obs_mask, target, send_list, send_count, factor_space, factor_time):
    n_lon, n_lat, n_ta = (lax.axis_size(axis) for axis in ("lon", "lat", "ta"))
    slots, days, cells = swath.shape
    rank, height, _ = factor_space.shape
    half = height // n_ta
    wide = half * LANES
    counts = (float(days * n_ta), float(height * cells * n_lon * n_lat))
    own_rows, sum_rows = rank + NORM, 2 * rank + NORM
    flip = pltpu.VMEM((LANES, LANES), F32)

    paired = n_lon == 4

    distant, close = range(n_lon // 2, n_lon), range(1, n_lon // 2)
    sends = [(side, step) for step in reversed(distant) for side in (0, 1)] + [(1, 0)]
    sends += [(side, step) for side in (0, 1) for step in close] + [(0, 0)]

    def piece_rows(side, step):
        more = TAIL if side == 0 else 0
        more += 3 * days if (side, step) == (1, 0) else COLS if paired and (side, step) == (0, 3) else 0
        return half * days + more

    operands = (send_list, send_count, target, swath, obs_mask, factor_space.reshape(rank * height, cells), factor_time)
    early = (0, n_lon - 1)
    sends.remove(early)
    first, total, seen, surface, space, time, *cols = call(
        functools.partial(route_kernel, half, early, paired),
        [shape((piece_rows(*early), cells), BF16), shape((2 * n_lon * half, days, cells)), shape((2 * n_lon * half + TAIL, LANES))]
        + [shape((rank, wide))]
        + [shape(ref.shape) for ref in operands[5:]]
        + [shape((COLS, LANES))] * (not paired),
        [pltpu.SMEM(ref.shape, jnp.int32) for ref in operands[:3]]
        + [pltpu.VMEM(ref.shape, ref.dtype) for ref in operands[3:5]]
        + [pltpu.SMEM((slots + 1,), jnp.int32), pltpu.SemaphoreType.DMA((len(operands) - 1 + SWATH_COPIES,))]
        + [pltpu.VMEM((COLS, LANES), F32)] * paired,
        hbm=len(operands),
    )(*operands)
    *pieces, edge_near, edge_far = call(
        functools.partial(pack_kernel, half, n_lon, sends),
        [shape((piece_rows(*key), cells), BF16) for key in sends]
        + [shape((rank, LANES)), shape((rank, LANES))],
    )(total, seen, space, time)

    def arrived(key, piece):
        side, step = key
        if side:
            return across(piece, ("lon", "ta"), 2 * step + 1)
        return across(piece, "lon", step) if step else piece

    pieces = dict(zip([early, *sends], [first, *pieces]))
    borders = ()
    if paired:
        near, far = (across(pieces.pop((side, 3)), "lon", 1) for side in (0, 1))
        borders = (near,)
        pieces[0, 2] = call(near_merge_kernel, shape(near.shape, BF16))(pieces[0, 2], near)
        outs = [shape(far.shape, BF16), shape(far.shape, BF16), shape(edge_far.shape)]
        pieces[1, 2], pieces[1, 1], edge_far = call(far_merge_kernel, outs)(pieces[1, 2], far, pieces[1, 1], edge_far)
    pieces = {key: arrived(key, piece) for key, piece in pieces.items()}
    order = list(pieces)

    def bands(edge):
        there = [(2 * band + 1, (2 * band + 2) % (2 * n_lat)) for band in range(n_lat)]
        return lax.ppermute(edge, ("lat", "ta"), there + [(b, a) for a, b in there])

    def swap():
        return lax.rem(lax.axis_index("lon"), 2) == 1 if paired else jnp.bool_(True)

    def columns(value):
        if paired:
            return across(value, "lon", 1), across(value, "lon", 3)
        ring = [(i, (i + 1) % n_lon) for i in range(n_lon)]
        return lax.ppermute(value, "lon", ring), lax.ppermute(value, "lon", [(b, a) for a, b in ring])

    predicted, packed, time_t = call(
        functools.partial(model_kernel, half),
        [shape((2 * days, wide)), shape((rank, wide), BF16), shape((rank, LANES))],
        [flip],
    )(surface, factor_time, pieces[1, 0])

    fresh, edge = shape((rank, wide)), shape((rank, LANES))
    sides = [[key for key in order if key[0] == side] for side in (0, 1)]
    side_out = shape((days, wide))
    counts_out = shape((TAIL, LANES))
    base, block, near, seen_near, beside = call(
        functools.partial(near_kernel, half, days, sides[0], paired, swap),
        [fresh, edge, side_out, counts_out, counts_out],
    )(surface, edge_near, predicted, packed, time_t, bands(edge_far), *[pieces[key] for key in sides[0]], *(borders if paired else columns(*cols)))
    seen_far = across(beside, "ta", 1)
    surface, message, crossing, cols, edge_near, edge_far, far = call(
        functools.partial(far_kernel, half, days, len(sides[1])),
        [fresh, shape((own_rows, LANES)), shape((own_rows, LANES)), shape((COLS, LANES)), edge, edge, side_out],
    )(base, predicted, packed, time_t, block, *[pieces[key] for key in sides[1]], seen_far)

    narrowed = shape((sum_rows + NORM, LANES), BF16)

    def add(mine, theirs):
        return call(add_kernel, shape(mine.shape))(mine, theirs)

    def doubled(total, axis, step):
        while step < lax.axis_size(axis):
            total = add(total, across(total, axis, step))
            step *= 2
        return total

    def over_lon(total):
        if paired:
            return [total] + [across(total, "lon", step) for step in (1, 2, 3)]
        return [doubled(total, "lon", 1)]

    def around(mine, core, both):
        return mine, across(core, "ta", 1), across(mine, "lat", 1), across(both, ("lat", "ta"), 3)

    total = call(core_sum_kernel, shape(crossing.shape))(message, across(crossing, "ta", 1))
    direct = paired and n_lat == 2
    band_sum = functools.partial(band_sum_kernel, half, swap)
    total, *again = call(band_sum, [shape(crossing.shape)] * (1 + direct))(total, across(total, "lat", 1), cols)
    if direct:
        parts = [total] + [across(value, "lon", step) for step, value in ((1, total), (2, again[0]), (3, again[0]))]
        cols = parts[1], parts[3]
    else:
        parts = [doubled(doubled(total, "lat", 2), "lon", 1)]
        cols = columns(cols)
    time_own, norm = call(functools.partial(own_kernel, len(parts)), [edge, shape((NORM, LANES))])(time_t, *parts)

    surface, time_t, message, outgoing = call(
        functools.partial(second_kernel, half, counts, direct, swap),
        [fresh, edge, narrowed, narrowed],
        [pltpu.VMEM((rank, wide), F32), pltpu.VMEM((rank, wide), F32), pltpu.VMEM((2 * days, wide), F32), pltpu.VMEM((rank, wide), BF16)],
    )(surface, time_own, across(time_own, "ta", 1), norm, near, far, seen_near, seen_far, across(edge_near, "ta", 1), bands(edge_far), *cols)

    other = across(surface, "ta", 1)
    total = narrowed if paired and n_lat == 2 else shape((sum_rows, LANES))
    total = call(functools.partial(all_sum_kernel, rank), total)(*around(message, outgoing, outgoing))
    parts = over_lon(doubled(total, "lat", 2))
    space, time = call(
        functools.partial(last_kernel, half, counts, len(parts)),
        [shape((rank * height, cells)), shape(factor_time.shape)],
        [flip],
    )(surface, other, time_t, *parts)
    return space.reshape(rank, height, cells), time


def solution(mesh):
    in_specs = (
        P(("grp", "lon", "lat"), "ta", None),
        P(("grp", "lon", "lat"), "ta"),
        P(("grp", "lon", "lat")),
        P(("grp", "lon", "lat"), None, None),
        P(("grp", "lon", "lat"), None),
        P(None, ("grp", "lat"), "lon"),
        P(("grp", "ta"), None),
    )
    out_specs = (P(None, ("grp", "lat"), "lon"), P(("grp", "ta"), None))
    return jax.shard_map(shards, mesh=mesh, in_specs=in_specs, out_specs=out_specs, check_vma=False)
```

```python
import functools
import math

import jax
import jax.numpy as jnp
from jax import lax
from jax.experimental import pallas as pl
from jax.experimental.pallas import tpu as pltpu
from jax.sharding import PartitionSpec as P

SMOOTH = 2.0
ETA_SPACE = 0.08
RIDGE = 1.0
EPSILON = 1e-06

F32 = jnp.float32
BF16 = jnp.bfloat16
LANES = 128
WIDTH = 512
TAIL = 16
COLS = 16
NORM = 8
SPARE = 2 * 1024 * 1024
SWATH_COPIES = 1
UNROLL = 4


def dot(a, b, contract):
    return lax.dot_general(a, b, ((contract[:1], contract[1:]), ((), ())), preferred_element_type=F32)


def route_kernel(half, early, paired, list_hbm, count_hbm, target_hbm, swath_hbm, mask_hbm, space_hbm, time_hbm, *rest):
    piece, total, seen, surface, space_ref, time_ref, *rest = rest
    cols = rest.pop(-1 if paired else 0)
    list_ref, count_ref, target_ref, swath_ref, mask_ref, place, arrived = rest
    me, core = lax.axis_index("lon"), lax.axis_index("ta")
    n_lon = list_ref.shape[1]
    slots, days, cells = swath_ref.shape
    chunk = slots // SWATH_COPIES
    small = [(list_hbm, list_ref), (count_hbm, count_ref), (target_hbm, target_ref), (mask_hbm, mask_ref)]
    large = [(swath_hbm.at[pl.ds(at, chunk)], swath_ref.at[pl.ds(at, chunk)]) for at in range(0, slots, chunk)]
    model = [(space_hbm, space_ref), (time_hbm, time_ref)]
    copies = [pltpu.make_async_copy(src, dst, arrived.at[i]) for i, (src, dst) in enumerate(small + model + large)]
    for copy in copies:
        copy.start()
    total[...] = jnp.zeros(total.shape, F32)
    seen[...] = jnp.zeros(seen.shape, F32)
    for copy in copies[: len(small)]:
        copy.wait()

    def owner(d, carry):
        first = jnp.bitwise_xor(d, me) * half
        count = count_ref[0, d]

        def entries(i, carry):
            for k in range(UNROLL):
                k = i * UNROLL + k
                slot = list_ref[0, d, k]
                row = target_ref[slot]
                far = jnp.bitwise_xor(lax.shift_right_logical(row, half.bit_length() - 1), core)
                place[jnp.where(k < count, slot, slots)] = far * (n_lon * half) + first + jnp.bitwise_and(row, half - 1)
            return carry

        return lax.fori_loop(0, lax.div(count + UNROLL - 1, UNROLL), entries, carry)

    lax.fori_loop(0, n_lon, owner, 0)
    for copy in copies[len(small):len(small) + len(model)]:
        copy.wait()
    rank = surface.shape[0]
    height = space_ref.shape[0] // rank
    for row in range(half):
        surface[:, row * LANES:(row + 1) * LANES] = space_ref[pl.ds(core * half + row, rank, stride=height), :]
    cols[...] = jnp.zeros(cols.shape, F32)
    cols[:, :rank] = border(surface[...], half)
    mask = mask_ref[...].astype(F32)
    by_day = mask.T.astype(BF16)
    for slot in range(slots):
        if slot % chunk == 0:
            copies[len(small) + len(model) + slot // chunk].wait()
        at = place[slot]
        total[at] += (swath_ref[slot] * by_day[:, slot:slot + 1]).astype(F32)
        seen[pl.ds(at, 1), :days] += mask[slot:slot + 1, :]
    pack(half, n_lon, early, total, seen, piece)
    end = half * days + TAIL
    if piece.shape[0] > end:
        piece[end:, :] = cols[...].astype(BF16)


def pack(half, n_lon, key, total, seen, out):
    side, step = key
    at = (side * n_lon + step) * half
    end = half * total.shape[1]
    out[:end, :] = total[at:at + half].reshape(end, LANES).astype(BF16)
    if side == 0:
        other = at + n_lon * half
        both = jnp.concatenate([seen[at:at + half, :], seen[other:other + half, :]], axis=0)
        out[end:end + TAIL, :] = both.astype(BF16)


def pack_kernel(half, n_lon, sends, total, seen, space_ref, time_ref, *rest):
    outs, (edge_near, edge_far) = rest[: len(sends)], rest[len(sends):]
    core = lax.axis_index("ta")
    days = total.shape[1]
    end = half * days
    rank = edge_near.shape[0]
    height = space_ref.shape[0] // rank
    edge_near[...] = space_ref[pl.ds(half - core, rank, stride=height), :]
    edge_far[...] = space_ref[pl.ds(core * (height - 1), rank, stride=height), :]
    for key, out in zip(sends, outs):
        pack(half, n_lon, key, total, seen, out)
        if key == (1, 0):
            left = time_ref[...]
            for part in range(end, end + 3 * days, days):
                value = left.astype(BF16)
                out[part:part + days, :] = jnp.zeros((days, LANES), BF16)
                out[part:part + days, :rank] = value
                left = left - value.astype(F32)


def row_of(surface, row):
    return surface[:, row * LANES:(row + 1) * LANES]


def diagonal(value, rank):
    row = lax.broadcasted_iota(jnp.int32, (rank, LANES), 0)
    lane = lax.broadcasted_iota(jnp.int32, (rank, LANES), 1)
    return jnp.where(row == lane, value, 0.0)


def column_as_row(column):
    row = jnp.sum(diagonal(column, column.shape[0]), axis=0, keepdims=True)
    return jnp.broadcast_to(row, (NORM, LANES))


def row_as_column(row, rank):
    return jnp.sum(diagonal(row, rank), axis=1, keepdims=True)


def border(surface, half):
    line = lax.broadcasted_iota(jnp.int32, (COLS, half * LANES), 0)
    lane = lax.broadcasted_iota(jnp.int32, (COLS, half * LANES), 1)
    pick_lane = jnp.where(line < half, line * LANES, (line - half) * LANES + LANES - 1)
    return dot((lane == pick_lane).astype(BF16), surface.astype(BF16), (1, 1))


def smoothed(surface, half, above, below, sides):
    lane = lax.broadcasted_iota(jnp.int32, above.shape, 1)
    strips = []
    for row in range(half):
        here = row_of(surface, row)
        up = above if row == 0 else row_of(surface, row - 1)
        down = below if row == half - 1 else row_of(surface, row + 1)
        left = jnp.where(lane == 0, 0.0, pltpu.roll(here, 1, 1))
        right = jnp.where(lane == LANES - 1, 0.0, pltpu.roll(here, LANES - 1, 1))
        lap = 4.0 * here - (up + down + left + right + row_of(sides, row))
        strips.append(here - (ETA_SPACE * SMOOTH) * lap)
    return strips


def pick(flag, a, b):
    return jnp.where(flag, a, b)


def in_order(odd, a, b):
    return pick(odd, a, b), pick(odd, b, a)


def model_kernel(half, surface, time_own, piece, predicted, packed, time_t, days_all):
    rank = surface.shape[0]
    days = time_own.shape[0]
    at = half * days
    high, middle, low = (piece[first:first + days, :].astype(F32) for first in range(at, at + 3 * days, days))
    days_all[...] = jnp.zeros(days_all.shape, F32)
    days_all[:days, :rank] = time_own[...]
    days_all[days:, :] = (high + middle) + low
    time_full = days_all[...]
    time_t[...] = time_full.T[:rank, :]
    packed[...] = surface[...].astype(BF16)
    time_bf = time_full[:, :rank].astype(BF16)
    for at in range(0, half * LANES, 2 * LANES):
        predicted[:, at:at + 2 * LANES] = dot(time_bf, packed[:, at:at + 2 * LANES], (1, 0))


def smooth(half, surface, edge_near, edge_far, left, right, scale, base):
    core = lax.axis_index("ta")
    rank = surface.shape[0]
    band = lax.axis_index("lat")
    outer = pick(core == 0, band == 0, band == lax.axis_size("lat") - 1)
    edge_far = jnp.where(outer, 0.0, edge_far)
    above = pick(core == 0, edge_far, edge_near)
    below = pick(core == 0, edge_near, edge_far)
    line = lax.broadcasted_iota(jnp.int32, (2 * half, half * LANES), 0)
    lane = lax.broadcasted_iota(jnp.int32, (2 * half, half * LANES), 1)
    place = jnp.where(line < half, line * LANES, (line - half) * LANES + LANES - 1)
    cols = jnp.concatenate([left, right], axis=0)
    sides = dot(cols[:, :rank].astype(BF16), (lane == place).astype(BF16), (0, 0))
    if scale is not None:
        above, below, sides = above * scale, below * scale, sides * scale
    for row, strip in enumerate(smoothed(surface, half, above, below, sides)):
        base[:, row * LANES:(row + 1) * LANES] = strip


def gradients(half, base, predicted, packed, time_t, seen, near, far, fresh):
    rank = time_t.shape[0]
    time_bf = time_t.astype(BF16)
    time_twice = jnp.concatenate([time_bf, time_bf], axis=1)
    seen_bf = seen.astype(BF16)
    width = WIDTH
    owner = lax.broadcasted_iota(jnp.int32, (TAIL, width), 0)
    lane = lax.broadcasted_iota(jnp.int32, (TAIL, width), 1)
    grad_time = jnp.zeros((rank, 2 * LANES), F32)
    grad_diag = jnp.zeros((rank, LANES), F32)
    norm = jnp.zeros((rank, 1), F32)
    for at in range(0, half * LANES, width):
        spread = (owner * LANES <= lane + at) & (lane + at < (owner + 1) * LANES)
        weight = dot(seen_bf, spread.astype(BF16), (0, 0))
        part = packed[:, at:at + width]
        summed = jnp.concatenate([near[:, at:at + width], far[:, at:at + width]], axis=0)
        residual = weight * predicted[:, at:at + width] - summed
        high = residual.astype(BF16)
        low = (residual - high.astype(F32)).astype(BF16)
        both = jnp.concatenate([high, low], axis=0)
        grad_space = dot(time_twice, both, (1, 0))
        grad_time = grad_time + dot(part, both, (1, 1))
        new = base[:, at:at + width] - ETA_SPACE * grad_space
        fresh[:, at:at + width] = new
        norm = norm + jnp.sum(new * new, axis=1, keepdims=True)
        wide = part.astype(F32)
        for row in range(width // LANES):
            strip = row_of(wide, row)
            square = jnp.sum(strip * strip, axis=1, keepdims=True)
            grad_diag = grad_diag + square * seen[at // LANES + row:at // LANES + row + 1, :]
    return grad_time[:, :LANES] + grad_time[:, LANES:], grad_diag, norm


def side_gradients(half, first, predicted, packed, time_t, seen, summed, take):
    rank, days = time_t.shape[0], summed.shape[0]
    below = lax.broadcasted_iota(jnp.int32, time_t.shape, 1) < days
    moved = pltpu.roll(time_t, days, 1)
    time_twice = (jnp.where(below, moved, time_t) if first else jnp.where(below, time_t, moved)).astype(BF16)
    seen_bf = seen[:, :days].astype(BF16)
    owner = lax.broadcasted_iota(jnp.int32, (TAIL, 2 * WIDTH), 0)
    lane = lax.broadcasted_iota(jnp.int32, (TAIL, 2 * WIDTH), 1)
    grad_time = jnp.zeros((rank, LANES), F32)
    grad_diag = jnp.zeros((rank, LANES), F32)
    for at in range(0, half * LANES, 2 * WIDTH):
        spread = (owner * LANES <= lane + at) & (lane + at < (owner + 1) * LANES)
        weight = dot(seen_bf, spread.astype(BF16), (0, 0))
        part = packed[:, at:at + 2 * WIDTH]
        residual = weight * predicted[first:first + days, at:at + 2 * WIDTH] - summed[:, at:at + 2 * WIDTH]
        high = residual.astype(BF16)
        low = (residual - high.astype(F32)).astype(BF16)
        both = jnp.concatenate([high, low], axis=0)
        take(at, dot(time_twice, both, (1, 0)))
        grad_time = grad_time + dot(part, both, (1, 1))
        wide = part.astype(F32)
        for row in range(2 * WIDTH // LANES):
            strip = row_of(wide, row)
            square = jnp.sum(strip * strip, axis=1, keepdims=True)
            grad_diag = grad_diag + square * seen[at // LANES + row:at // LANES + row + 1, :]
    return jnp.where(below, grad_time + pltpu.roll(grad_time, days, 1), pltpu.roll(grad_diag, days, 1))


def add_up(parts, rows):
    value = parts[0][rows, :].astype(F32)
    for piece in parts[1:]:
        value = value + piece[rows, :].astype(F32)
    return value


def unpack_pieces(half, parts, summed):
    days = summed.shape[0]
    for row in range(half):
        summed[:, row * LANES:(row + 1) * LANES] = add_up(parts, slice(row * days, (row + 1) * days))


def narrow(value, rank):
    high = value[2 * rank:, :].astype(BF16)
    low = (value[2 * rank:, :] - high.astype(F32)).astype(BF16)
    return value[: 2 * rank, :].astype(BF16), jnp.concatenate([high.astype(F32), low.astype(F32)], axis=0).astype(BF16)


def widened(value, rank):
    value = value.astype(F32)
    return jnp.concatenate([value[: 2 * rank, :], value[2 * rank:2 * rank + NORM, :] + value[2 * rank + NORM:, :]], axis=0)


def post_all(sums, message, outgoing):
    grad_time, grad_diag, norm = sums
    rank = norm.shape[0]
    last = column_as_row(norm)
    for out, shift in ((message, 0), (outgoing, LANES // 2)):
        parts = [pltpu.roll(part, shift, 1) if shift else part for part in (grad_time, grad_diag)]
        out[: 2 * rank, :], out[2 * rank:, :] = narrow(jnp.concatenate([*parts, last], axis=0), rank)


def near_kernel(half, days, order, paired, swap, surface, edge_near, predicted, packed, time_t, edge_far, *rest):
    pieces, rest = dict(zip(order, rest)), rest[len(order):]
    cols, (base, block, summed, seen, beside) = rest[:-5], rest[-5:]
    if paired:
        at = half * days + TAIL
        cols = in_order(swap(), *[ref[at:, :].astype(F32) for ref in (cols[0], pieces[0, 2])])
    left, right = (ref[...] for ref in cols)
    smooth(half, surface[...], edge_near[...], edge_far[...], left[half:, :], right[:half, :], None, base)
    parts = [pieces[key] for key in sorted(pieces)]
    unpack_pieces(half, parts, summed)
    seen[...] = add_up(parts, slice(half * days, half * days + TAIL))
    beside[...] = jnp.concatenate([seen[half:, :], jnp.zeros((half, LANES), F32)], axis=0)

    def take(at, grad_space):
        base[:, at:at + 2 * WIDTH] = base[:, at:at + 2 * WIDTH] - ETA_SPACE * grad_space

    block[...] = side_gradients(half, 0, predicted, packed, time_t[...], seen, summed, take)


def far_kernel(half, days, n_lon, base, predicted, packed, time_t, block, *rest):
    parts, rest = rest[:n_lon], rest[n_lon:]
    seen, fresh, message, crossing, cols, edge_near, edge_far, summed = rest
    core = lax.axis_index("ta")
    rank = block.shape[0]
    unpack_pieces(half, parts, summed)

    def take(at, grad_space):
        fresh[:, at:at + 2 * WIDTH] = base[:, at:at + 2 * WIDTH] - ETA_SPACE * grad_space

    crossing[:rank, :] = side_gradients(half, days, predicted, packed, time_t[...], seen, summed, take)
    message[:rank, :] = block[...]
    new = fresh[...]
    norm = column_as_row(jnp.sum(new * new, axis=1, keepdims=True))
    message[rank:, :] = norm
    crossing[rank:, :] = norm
    cols[...] = jnp.zeros(cols.shape, F32)
    cols[:, :rank] = border(new, half)
    first_row, last_row = row_of(new, 0), row_of(new, half - 1)
    edge_near[...] = pick(core == 0, last_row, first_row)
    edge_far[...] = pick(core == 0, first_row, last_row)


def total_of(parts):
    total = parts[0][...].astype(F32)
    if len(parts) > 1:
        one, two, three = (part[...].astype(F32) for part in parts[1:])
        total = (total + one) + (two + three)
    return total


def packed_norm(norm, cols, rank):
    free = LANES - rank
    line = lax.broadcasted_iota(jnp.int32, cols.shape, 0)
    lane = lax.broadcasted_iota(jnp.int32, cols.shape, 1)
    for part in range(rank // free):
        moved = pltpu.roll(norm, rank - part * free, 1)
        cols = jnp.where((lane >= rank) & (line == part), moved, cols)
    return cols


def unpacked(block, rank):
    free = LANES - rank
    line = lax.broadcasted_iota(jnp.int32, block.shape, 0)
    lane = lax.broadcasted_iota(jnp.int32, block.shape, 1)
    norm = jnp.zeros(block.shape, F32)
    for part in range(rank // free):
        row = jnp.where((lane >= rank) & (line == part), block, 0.0)
        norm = norm + pltpu.roll(row, LANES - rank + part * free, 1)
    return jnp.broadcast_to(jnp.sum(norm, axis=0, keepdims=True), block.shape)


def own_kernel(n_parts, time_t, *rest):
    parts, (time_own, norm) = rest[:n_parts], rest[n_parts:]
    rank = time_t.shape[0]
    days = LANES // 2
    total = total_of(parts)
    block = total[:rank, :]
    own = lax.broadcasted_iota(jnp.int32, block.shape, 1) < days
    time_own[...] = jnp.where(own, time_t[...] - block / (pltpu.roll(block, days, 1) + RIDGE), 0.0)
    norm[...] = unpacked(total[rank:, :], rank) if n_parts > 1 else total[rank:, :]


def rescaling(counts, norm, time_new):
    day_count, cell_count = counts
    space_sq = row_as_column(norm[:1, :], time_new.shape[0])
    square = time_new * time_new
    time_sq = 0.5 * jnp.sum(square + pltpu.roll(square, LANES // 2, 1), axis=1, keepdims=True)
    ratio = (time_sq / day_count + EPSILON) / (space_sq / cell_count + EPSILON)
    return jnp.sqrt(jnp.sqrt(ratio))


def second_kernel(half, counts, paired, swap, surface, time_own, time_other, norm, near, far, seen_near, seen_far, edge_near, edge_far, cols_a, cols_b, *rest):
    fresh, time_out, message, outgoing, scaled, base, predicted, packed = rest
    rank = surface.shape[0]
    time_new = time_own[...] + pltpu.roll(time_other[...], LANES // 2, 1)
    scale = rescaling(counts, norm[...], time_new)
    time_now = time_new / scale
    time_out[...] = time_now
    scaled[...] = surface[...] * scale
    packed[...] = scaled[...].astype(BF16)
    time_bf = time_now.astype(BF16)
    for at in range(0, half * LANES, WIDTH):
        predicted[:, at:at + WIDTH] = dot(time_bf, packed[:, at:at + WIDTH], (0, 0))
    if paired:
        left, right = in_order(swap(), cols_a[rank:, :], cols_b[rank:, :])
    else:
        left, right = cols_a[half:, :], cols_b[:half, :]
    smooth(half, scaled[...], edge_near[...], edge_far[...], left, right, scale, base)
    seen = seen_near[...] + pltpu.roll(seen_far[...], LANES // 2, 1)
    sums = gradients(half, base, predicted, packed, time_now, seen, near, far, fresh)
    post_all(sums, message, outgoing)


def last_kernel(half, counts, n_parts, surface, other, time_t, *rest):
    parts = rest[:n_parts]
    space_out, time_out, flip = rest[n_parts:]
    core = lax.axis_index("ta")
    rank = surface.shape[0]
    height = space_out.shape[0] // rank
    total = total_of(parts)
    if parts[0].dtype == BF16:
        total = widened(total, rank)
    time_new = time_t[...] - total[:rank, :] / (total[rank:2 * rank, :] + RIDGE)
    scale = rescaling(counts, total[2 * rank:, :], time_new)
    flip[...] = jnp.zeros(flip.shape, F32)
    flip[:rank, :] = time_new / scale
    time_out[...] = flip[...].T[: time_out.shape[0], :rank]
    for row in range(half):
        at = row * LANES
        space_out[pl.ds(core * half + row, rank, stride=height), :] = surface[:, at:at + LANES] * scale
        space_out[pl.ds((1 - core) * half + row, rank, stride=height), :] = other[:, at:at + LANES] * scale


def near_merge_kernel(mine, theirs, out):
    rows = mine.shape[0]
    out[:rows, :] = (mine[...].astype(F32) + theirs[:rows, :].astype(F32)).astype(BF16)
    out[rows:, :] = theirs[rows:, :]


def far_merge_kernel(mine, theirs, piece_in, edge_in, out, piece_out, edge_out):
    piece_out[...] = piece_in[...]
    edge_out[...] = edge_in[...]
    out[...] = (mine[...].astype(F32) + theirs[...].astype(F32)).astype(BF16)


def add_kernel(mine, theirs, total):
    total[...] = mine[...] + theirs[...]


def core_sum_kernel(mine, core, total):
    total[...] = mine[: total.shape[0], :] + core[...]


def band_sum_kernel(half, swap, mine, band, cols, *totals):
    rank = mine.shape[0] - NORM
    value = mine[...] + band[...]
    borders = in_order(swap(), cols[:half, :], cols[half:, :])
    for total, lines in zip(totals, borders):
        total[:rank, :] = value[:rank, :]
        total[rank:, :] = value[rank:, :] if len(totals) == 1 else packed_norm(value[rank:, :], lines, rank)


def all_sum_kernel(rank, mine, core, band, both, total):
    one, two, three, four = (widened(part[...], rank) for part in (mine, core, band, both))
    value = (one + two) + (three + four)
    if total.dtype == BF16:
        total[: 2 * rank, :], total[2 * rank:, :] = narrow(value, rank)
    else:
        total[...] = value


def shape(dims, dtype=F32):
    return jax.ShapeDtypeStruct(tuple(dims), dtype)


def padded(ref):
    *outer, rows, lanes = (1, *ref.shape)
    return math.prod(outer) * -(-rows // 16) * 16 * -(-lanes // LANES) * LANES * jnp.dtype(ref.dtype).itemsize


def call(kernel, out_shape, scratch=(), hbm=0, after=0, flops=1_000_000):
    def run(*operands):
        operands = [pltpu.with_memory_space_constraint(x, pltpu.HBM) if i < hbm else x for i, x in enumerate(operands)]
        vmem = [*operands[hbm:len(operands) - after], *jax.tree.leaves(out_shape), *scratch]
        specs = [pltpu.HBM] * hbm + [pltpu.VMEM] * (len(operands) - hbm - after) + [pl.ANY] * after
        return pl.pallas_call(
            kernel,
            out_shape=out_shape,
            in_specs=[pl.BlockSpec(memory_space=space) for space in specs],
            out_specs=jax.tree.map(lambda _: pl.BlockSpec(memory_space=pltpu.VMEM), out_shape),
            scratch_shapes=list(scratch),
            compiler_params=pltpu.CompilerParams(vmem_limit_bytes=SPARE + sum(padded(ref) for ref in vmem if len(ref.shape) > 1)),
            cost_estimate=pl.CostEstimate(flops=flops, bytes_accessed=1_000_000, transcendentals=0),
        )(*operands)

    return run


def across(value, axis, step):
    return lax.ppermute(value, axis, [(i, i ^ step) for i in range(lax.axis_size(axis))])


def shards(swath, obs_mask, target, send_list, send_count, factor_space, factor_time):
    n_lon, n_lat, n_ta = (lax.axis_size(axis) for axis in ("lon", "lat", "ta"))
    slots, days, cells = swath.shape
    rank, height, _ = factor_space.shape
    half = height // n_ta
    wide = half * LANES
    counts = (float(days * n_ta), float(height * cells * n_lon * n_lat))
    own_rows, sum_rows = rank + NORM, 2 * rank + NORM
    flip = pltpu.VMEM((LANES, LANES), F32)

    paired = n_lon == 4

    distant, close = range(n_lon // 2, n_lon), range(1, n_lon // 2)
    sends = [(side, step) for step in reversed(distant) for side in (0, 1)] + [(1, 0)]
    sends += [(side, step) for side in (0, 1) for step in close] + [(0, 0)]

    def piece_rows(side, step):
        more = TAIL if side == 0 else 0
        more += 3 * days if (side, step) == (1, 0) else COLS if paired and (side, step) == (0, 3) else 0
        return half * days + more

    operands = (send_list, send_count, target, swath, obs_mask, factor_space.reshape(rank * height, cells), factor_time)
    early = (0, n_lon - 1)
    sends.remove(early)
    first, total, seen, surface, space, time, *cols = call(
        functools.partial(route_kernel, half, early, paired),
        [shape((piece_rows(*early), cells), BF16), shape((2 * n_lon * half, days, cells)), shape((2 * n_lon * half + TAIL, LANES))]
        + [shape((rank, wide))]
        + [shape(ref.shape) for ref in operands[5:]]
        + [shape((COLS, LANES))] * (not paired),
        [pltpu.SMEM(ref.shape, jnp.int32) for ref in operands[:3]]
        + [pltpu.VMEM(ref.shape, ref.dtype) for ref in operands[3:5]]
        + [pltpu.SMEM((slots + 1,), jnp.int32), pltpu.SemaphoreType.DMA((len(operands) - 1 + SWATH_COPIES,))]
        + [pltpu.VMEM((COLS, LANES), F32)] * paired,
        hbm=len(operands),
    )(*operands)
    *pieces, edge_near, edge_far = call(
        functools.partial(pack_kernel, half, n_lon, sends),
        [shape((piece_rows(*key), cells), BF16) for key in sends]
        + [shape((rank, LANES)), shape((rank, LANES))],
    )(total, seen, space, time)

    def arrived(key, piece):
        side, step = key
        if side:
            return across(piece, ("lon", "ta"), 2 * step + 1)
        return across(piece, "lon", step) if step else piece

    pieces = dict(zip([early, *sends], [first, *pieces]))
    borders = ()
    if paired:
        near, far = (across(pieces.pop((side, 3)), "lon", 1) for side in (0, 1))
        borders = (near,)
        pieces[0, 2] = call(near_merge_kernel, shape(near.shape, BF16))(pieces[0, 2], near)
        outs = [shape(far.shape, BF16), shape(far.shape, BF16), shape(edge_far.shape)]
        pieces[1, 2], pieces[1, 1], edge_far = call(far_merge_kernel, outs)(pieces[1, 2], far, pieces[1, 1], edge_far)
    pieces = {key: arrived(key, piece) for key, piece in pieces.items()}
    order = list(pieces)

    def bands(edge):
        there = [(2 * band + 1, (2 * band + 2) % (2 * n_lat)) for band in range(n_lat)]
        return lax.ppermute(edge, ("lat", "ta"), there + [(b, a) for a, b in there])

    def swap():
        return lax.rem(lax.axis_index("lon"), 2) == 1 if paired else jnp.bool_(True)

    def columns(value):
        if paired:
            return across(value, "lon", 1), across(value, "lon", 3)
        ring = [(i, (i + 1) % n_lon) for i in range(n_lon)]
        return lax.ppermute(value, "lon", ring), lax.ppermute(value, "lon", [(b, a) for a, b in ring])

    predicted, packed, time_t = call(
        functools.partial(model_kernel, half),
        [shape((2 * days, wide)), shape((rank, wide), BF16), shape((rank, LANES))],
        [flip],
    )(surface, factor_time, pieces[1, 0])

    fresh, edge = shape((rank, wide)), shape((rank, LANES))
    sides = [[key for key in order if key[0] == side] for side in (0, 1)]
    side_out = shape((days, wide))
    counts_out = shape((TAIL, LANES))
    base, block, near, seen_near, beside = call(
        functools.partial(near_kernel, half, days, sides[0], paired, swap),
        [fresh, edge, side_out, counts_out, counts_out],
    )(surface, edge_near, predicted, packed, time_t, bands(edge_far), *[pieces[key] for key in sides[0]], *(borders if paired else columns(*cols)))
    seen_far = across(beside, "ta", 1)
    surface, message, crossing, cols, edge_near, edge_far, far = call(
        functools.partial(far_kernel, half, days, len(sides[1])),
        [fresh, shape((own_rows, LANES)), shape((own_rows, LANES)), shape((COLS, LANES)), edge, edge, side_out],
    )(base, predicted, packed, time_t, block, *[pieces[key] for key in sides[1]], seen_far)

    narrowed = shape((sum_rows + NORM, LANES), BF16)

    def add(mine, theirs):
        return call(add_kernel, shape(mine.shape))(mine, theirs)

    def doubled(total, axis, step):
        while step < lax.axis_size(axis):
            total = add(total, across(total, axis, step))
            step *= 2
        return total

    def over_lon(total):
        if paired:
            return [total] + [across(total, "lon", step) for step in (1, 2, 3)]
        return [doubled(total, "lon", 1)]

    def around(mine, core, both):
        return mine, across(core, "ta", 1), across(mine, "lat", 1), across(both, ("lat", "ta"), 3)

    total = call(core_sum_kernel, shape(crossing.shape))(message, across(crossing, "ta", 1))
    direct = paired and n_lat == 2
    band_sum = functools.partial(band_sum_kernel, half, swap)
    total, *again = call(band_sum, [shape(crossing.shape)] * (1 + direct))(total, across(total, "lat", 1), cols)
    if direct:
        parts = [total] + [across(value, "lon", step) for step, value in ((1, total), (2, again[0]), (3, again[0]))]
        cols = parts[1], parts[3]
    else:
        parts = [doubled(doubled(total, "lat", 2), "lon", 1)]
        cols = columns(cols)
    time_own, norm = call(functools.partial(own_kernel, len(parts)), [edge, shape((NORM, LANES))])(time_t, *parts)

    surface, time_t, message, outgoing = call(
        functools.partial(second_kernel, half, counts, direct, swap),
        [fresh, edge, narrowed, narrowed],
        [pltpu.VMEM((rank, wide), F32), pltpu.VMEM((rank, wide), F32), pltpu.VMEM((2 * days, wide), F32), pltpu.VMEM((rank, wide), BF16)],
    )(surface, time_own, across(time_own, "ta", 1), norm, near, far, seen_near, seen_far, across(edge_near, "ta", 1), bands(edge_far), *cols)

    other = across(surface, "ta", 1)
    total = narrowed if paired and n_lat == 2 else shape((sum_rows, LANES))
    total = call(functools.partial(all_sum_kernel, rank), total)(*around(message, outgoing, outgoing))
    parts = over_lon(doubled(total, "lat", 2))
    space, time = call(
        functools.partial(last_kernel, half, counts, len(parts)),
        [shape((rank * height, cells)), shape(factor_time.shape)],
        [flip],
    )(surface, other, time_t, *parts)
    return space.reshape(rank, height, cells), time


def solution(mesh):
    in_specs = (
        P(("grp", "lon", "lat"), "ta", None),
        P(("grp", "lon", "lat"), "ta"),
        P(("grp", "lon", "lat")),
        P(("grp", "lon", "lat"), None, None),
        P(("grp", "lon", "lat"), None),
        P(None, ("grp", "lat"), "lon"),
        P(("grp", "ta"), None),
    )
    out_specs = (P(None, ("grp", "lat"), "lon"), P(("grp", "ta"), None))
    return jax.shard_map(shards, mesh=mesh, in_specs=in_specs, out_specs=out_specs, check_vma=False)
```

```python
import functools
import math

import jax
import jax.numpy as jnp
from jax import lax
from jax.experimental import pallas as pl
from jax.experimental.pallas import tpu as pltpu
from jax.sharding import PartitionSpec as P

SMOOTH = 2.0
ETA_SPACE = 0.08
RIDGE = 1.0
EPSILON = 1e-06

F32 = jnp.float32
BF16 = jnp.bfloat16
LANES = 128
WIDTH = 512
TAIL = 16
COLS = 16
NORM = 8
SPARE = 2 * 1024 * 1024
SWATH_COPIES = 1
UNROLL = 4


def dot(a, b, contract):
    return lax.dot_general(a, b, ((contract[:1], contract[1:]), ((), ())), preferred_element_type=F32)


def route_kernel(half, early, paired, list_hbm, count_hbm, target_hbm, swath_hbm, mask_hbm, space_hbm, time_hbm, *rest):
    piece, second, total, seen, surface, space_ref, time_ref, *rest = rest
    cols = rest.pop(-1 if paired else 0)
    list_ref, count_ref, target_ref, swath_ref, mask_ref, place, arrived = rest
    me, core = lax.axis_index("lon"), lax.axis_index("ta")
    n_lon = list_ref.shape[1]
    slots, days, cells = swath_ref.shape
    chunk = slots // SWATH_COPIES
    small = [(list_hbm, list_ref), (count_hbm, count_ref), (target_hbm, target_ref), (mask_hbm, mask_ref)]
    large = [(swath_hbm.at[pl.ds(at, chunk)], swath_ref.at[pl.ds(at, chunk)]) for at in range(0, slots, chunk)]
    model = [(space_hbm, space_ref), (time_hbm, time_ref)]
    copies = [pltpu.make_async_copy(src, dst, arrived.at[i]) for i, (src, dst) in enumerate(small + model + large)]
    for copy in copies:
        copy.start()
    total[...] = jnp.zeros(total.shape, F32)
    seen[...] = jnp.zeros(seen.shape, F32)
    for copy in copies[: len(small)]:
        copy.wait()

    def owner(d, carry):
        first = jnp.bitwise_xor(d, me) * half
        count = count_ref[0, d]

        def entries(i, carry):
            for k in range(UNROLL):
                k = i * UNROLL + k
                slot = list_ref[0, d, k]
                row = target_ref[slot]
                far = jnp.bitwise_xor(lax.shift_right_logical(row, half.bit_length() - 1), core)
                place[jnp.where(k < count, slot, slots)] = far * (n_lon * half) + first + jnp.bitwise_and(row, half - 1)
            return carry

        return lax.fori_loop(0, lax.div(count + UNROLL - 1, UNROLL), entries, carry)

    lax.fori_loop(0, n_lon, owner, 0)
    for copy in copies[len(small):len(small) + len(model)]:
        copy.wait()
    rank = surface.shape[0]
    height = space_ref.shape[0] // rank
    for row in range(half):
        surface[:, row * LANES:(row + 1) * LANES] = space_ref[pl.ds(core * half + row, rank, stride=height), :]
    cols[...] = jnp.zeros(cols.shape, F32)
    cols[:, :rank] = border(surface[...], half)
    mask = mask_ref[...].astype(F32)
    by_day = mask.T.astype(BF16)
    for slot in range(slots):
        if slot % chunk == 0:
            copies[len(small) + len(model) + slot // chunk].wait()
        at = place[slot]
        total[at] += (swath_ref[slot] * by_day[:, slot:slot + 1]).astype(F32)
        seen[pl.ds(at, 1), :days] += mask[slot:slot + 1, :]
    pack(half, n_lon, early, total, seen, piece)
    pack(half, n_lon, (1, early[1]), total, seen, second)
    end = half * days + TAIL
    if piece.shape[0] > end:
        piece[end:, :] = cols[...].astype(BF16)


def pack(half, n_lon, key, total, seen, out):
    side, step = key
    at = (side * n_lon + step) * half
    end = half * total.shape[1]
    out[:end, :] = total[at:at + half].reshape(end, LANES).astype(BF16)
    if side == 0:
        other = at + n_lon * half
        both = jnp.concatenate([seen[at:at + half, :], seen[other:other + half, :]], axis=0)
        out[end:end + TAIL, :] = both.astype(BF16)


def pack_kernel(half, n_lon, sends, total, seen, space_ref, time_ref, *rest):
    outs, (edge_near, edge_far) = rest[: len(sends)], rest[len(sends):]
    core = lax.axis_index("ta")
    days = total.shape[1]
    end = half * days
    rank = edge_near.shape[0]
    height = space_ref.shape[0] // rank
    edge_near[...] = space_ref[pl.ds(half - core, rank, stride=height), :]
    edge_far[...] = space_ref[pl.ds(core * (height - 1), rank, stride=height), :]
    for key, out in zip(sends, outs):
        pack(half, n_lon, key, total, seen, out)
        if key == (1, 0):
            left = time_ref[...]
            for part in range(end, end + 3 * days, days):
                value = left.astype(BF16)
                out[part:part + days, :] = jnp.zeros((days, LANES), BF16)
                out[part:part + days, :rank] = value
                left = left - value.astype(F32)


def row_of(surface, row):
    return surface[:, row * LANES:(row + 1) * LANES]


def diagonal(value, rank):
    row = lax.broadcasted_iota(jnp.int32, (rank, LANES), 0)
    lane = lax.broadcasted_iota(jnp.int32, (rank, LANES), 1)
    return jnp.where(row == lane, value, 0.0)


def column_as_row(column):
    row = jnp.sum(diagonal(column, column.shape[0]), axis=0, keepdims=True)
    return jnp.broadcast_to(row, (NORM, LANES))


def row_as_column(row, rank):
    return jnp.sum(diagonal(row, rank), axis=1, keepdims=True)


def border(surface, half):
    line = lax.broadcasted_iota(jnp.int32, (COLS, half * LANES), 0)
    lane = lax.broadcasted_iota(jnp.int32, (COLS, half * LANES), 1)
    pick_lane = jnp.where(line < half, line * LANES, (line - half) * LANES + LANES - 1)
    return dot((lane == pick_lane).astype(BF16), surface.astype(BF16), (1, 1))


def smoothed(surface, half, above, below, sides):
    lane = lax.broadcasted_iota(jnp.int32, above.shape, 1)
    strips = []
    for row in range(half):
        here = row_of(surface, row)
        up = above if row == 0 else row_of(surface, row - 1)
        down = below if row == half - 1 else row_of(surface, row + 1)
        left = jnp.where(lane == 0, 0.0, pltpu.roll(here, 1, 1))
        right = jnp.where(lane == LANES - 1, 0.0, pltpu.roll(here, LANES - 1, 1))
        lap = 4.0 * here - (up + down + left + right + row_of(sides, row))
        strips.append(here - (ETA_SPACE * SMOOTH) * lap)
    return strips


def pick(flag, a, b):
    return jnp.where(flag, a, b)


def in_order(odd, a, b):
    return pick(odd, a, b), pick(odd, b, a)


def model_kernel(half, surface, time_own, piece, predicted, packed, time_t, days_all):
    rank = surface.shape[0]
    days = time_own.shape[0]
    at = half * days
    high, middle, low = (piece[first:first + days, :].astype(F32) for first in range(at, at + 3 * days, days))
    days_all[...] = jnp.zeros(days_all.shape, F32)
    days_all[:days, :rank] = time_own[...]
    days_all[days:, :] = (high + middle) + low
    time_full = days_all[...]
    time_t[...] = time_full.T[:rank, :]
    packed[...] = surface[...].astype(BF16)
    time_bf = time_full[:, :rank].astype(BF16)
    for at in range(0, half * LANES, 2 * LANES):
        predicted[:, at:at + 2 * LANES] = dot(time_bf, packed[:, at:at + 2 * LANES], (1, 0))


def smooth(half, surface, edge_near, edge_far, left, right, scale, base):
    core = lax.axis_index("ta")
    rank = surface.shape[0]
    band = lax.axis_index("lat")
    outer = pick(core == 0, band == 0, band == lax.axis_size("lat") - 1)
    edge_far = jnp.where(outer, 0.0, edge_far)
    above = pick(core == 0, edge_far, edge_near)
    below = pick(core == 0, edge_near, edge_far)
    line = lax.broadcasted_iota(jnp.int32, (2 * half, half * LANES), 0)
    lane = lax.broadcasted_iota(jnp.int32, (2 * half, half * LANES), 1)
    place = jnp.where(line < half, line * LANES, (line - half) * LANES + LANES - 1)
    cols = jnp.concatenate([left, right], axis=0)
    sides = dot(cols[:, :rank].astype(BF16), (lane == place).astype(BF16), (0, 0))
    if scale is not None:
        above, below, sides = above * scale, below * scale, sides * scale
    for row, strip in enumerate(smoothed(surface, half, above, below, sides)):
        base[:, row * LANES:(row + 1) * LANES] = strip


def gradients(half, base, predicted, packed, time_t, seen, near, far, fresh):
    rank = time_t.shape[0]
    time_bf = time_t.astype(BF16)
    time_twice = jnp.concatenate([time_bf, time_bf], axis=1)
    seen_bf = seen.astype(BF16)
    width = WIDTH
    owner = lax.broadcasted_iota(jnp.int32, (TAIL, width), 0)
    lane = lax.broadcasted_iota(jnp.int32, (TAIL, width), 1)
    grad_time = jnp.zeros((rank, 2 * LANES), F32)
    grad_diag = jnp.zeros((rank, LANES), F32)
    norm = jnp.zeros((rank, 1), F32)
    for at in range(0, half * LANES, width):
        spread = (owner * LANES <= lane + at) & (lane + at < (owner + 1) * LANES)
        weight = dot(seen_bf, spread.astype(BF16), (0, 0))
        part = packed[:, at:at + width]
        summed = jnp.concatenate([near[:, at:at + width], far[:, at:at + width]], axis=0)
        residual = weight * predicted[:, at:at + width] - summed
        high = residual.astype(BF16)
        low = (residual - high.astype(F32)).astype(BF16)
        both = jnp.concatenate([high, low], axis=0)
        grad_space = dot(time_twice, both, (1, 0))
        grad_time = grad_time + dot(part, both, (1, 1))
        new = base[:, at:at + width] - ETA_SPACE * grad_space
        fresh[:, at:at + width] = new
        norm = norm + jnp.sum(new * new, axis=1, keepdims=True)
        wide = part.astype(F32)
        for row in range(width // LANES):
            strip = row_of(wide, row)
            square = jnp.sum(strip * strip, axis=1, keepdims=True)
            grad_diag = grad_diag + square * seen[at // LANES + row:at // LANES + row + 1, :]
    return grad_time[:, :LANES] + grad_time[:, LANES:], grad_diag, norm


def side_gradients(half, first, predicted, packed, time_t, seen, summed, take):
    rank, days = time_t.shape[0], summed.shape[0]
    below = lax.broadcasted_iota(jnp.int32, time_t.shape, 1) < days
    moved = pltpu.roll(time_t, days, 1)
    time_twice = (jnp.where(below, moved, time_t) if first else jnp.where(below, time_t, moved)).astype(BF16)
    seen_bf = seen[:, :days].astype(BF16)
    owner = lax.broadcasted_iota(jnp.int32, (TAIL, 2 * WIDTH), 0)
    lane = lax.broadcasted_iota(jnp.int32, (TAIL, 2 * WIDTH), 1)
    grad_time = jnp.zeros((rank, LANES), F32)
    grad_diag = jnp.zeros((rank, LANES), F32)
    for at in range(0, half * LANES, 2 * WIDTH):
        spread = (owner * LANES <= lane + at) & (lane + at < (owner + 1) * LANES)
        weight = dot(seen_bf, spread.astype(BF16), (0, 0))
        part = packed[:, at:at + 2 * WIDTH]
        residual = weight * predicted[first:first + days, at:at + 2 * WIDTH] - summed[:, at:at + 2 * WIDTH]
        high = residual.astype(BF16)
        low = (residual - high.astype(F32)).astype(BF16)
        both = jnp.concatenate([high, low], axis=0)
        take(at, dot(time_twice, both, (1, 0)))
        grad_time = grad_time + dot(part, both, (1, 1))
        wide = part.astype(F32)
        for row in range(2 * WIDTH // LANES):
            strip = row_of(wide, row)
            square = jnp.sum(strip * strip, axis=1, keepdims=True)
            grad_diag = grad_diag + square * seen[at // LANES + row:at // LANES + row + 1, :]
    return jnp.where(below, grad_time + pltpu.roll(grad_time, days, 1), pltpu.roll(grad_diag, days, 1))


def add_up(parts, rows):
    value = parts[0][rows, :].astype(F32)
    for piece in parts[1:]:
        value = value + piece[rows, :].astype(F32)
    return value


def unpack_pieces(half, parts, summed):
    days = summed.shape[0]
    for row in range(half):
        summed[:, row * LANES:(row + 1) * LANES] = add_up(parts, slice(row * days, (row + 1) * days))


def narrow(value, rank):
    high = value[2 * rank:, :].astype(BF16)
    low = (value[2 * rank:, :] - high.astype(F32)).astype(BF16)
    return value[: 2 * rank, :].astype(BF16), jnp.concatenate([high.astype(F32), low.astype(F32)], axis=0).astype(BF16)


def widened(value, rank):
    value = value.astype(F32)
    return jnp.concatenate([value[: 2 * rank, :], value[2 * rank:2 * rank + NORM, :] + value[2 * rank + NORM:, :]], axis=0)


def post_all(sums, message, outgoing):
    grad_time, grad_diag, norm = sums
    rank = norm.shape[0]
    last = column_as_row(norm)
    for out, shift in ((message, 0), (outgoing, LANES // 2)):
        parts = [pltpu.roll(part, shift, 1) if shift else part for part in (grad_time, grad_diag)]
        out[: 2 * rank, :], out[2 * rank:, :] = narrow(jnp.concatenate([*parts, last], axis=0), rank)


def near_kernel(half, days, order, paired, swap, surface, edge_near, predicted, packed, time_t, edge_far, *rest):
    pieces, rest = dict(zip(order, rest)), rest[len(order):]
    cols, (base, block, summed, seen, beside) = rest[:-5], rest[-5:]
    if paired:
        at = half * days + TAIL
        cols = in_order(swap(), *[ref[at:, :].astype(F32) for ref in (cols[0], pieces[0, 2])])
    left, right = (ref[...] for ref in cols)
    smooth(half, surface[...], edge_near[...], edge_far[...], left[half:, :], right[:half, :], None, base)
    parts = [pieces[key] for key in sorted(pieces)]
    unpack_pieces(half, parts, summed)
    seen[...] = add_up(parts, slice(half * days, half * days + TAIL))
    beside[...] = jnp.concatenate([seen[half:, :], jnp.zeros((half, LANES), F32)], axis=0)

    def take(at, grad_space):
        base[:, at:at + 2 * WIDTH] = base[:, at:at + 2 * WIDTH] - ETA_SPACE * grad_space

    block[...] = side_gradients(half, 0, predicted, packed, time_t[...], seen, summed, take)


def far_kernel(half, days, n_lon, base, predicted, packed, time_t, block, *rest):
    parts, rest = rest[:n_lon], rest[n_lon:]
    seen, fresh, message, crossing, cols, edge_near, edge_far, summed = rest
    core = lax.axis_index("ta")
    rank = block.shape[0]
    unpack_pieces(half, parts, summed)

    def take(at, grad_space):
        fresh[:, at:at + 2 * WIDTH] = base[:, at:at + 2 * WIDTH] - ETA_SPACE * grad_space

    crossing[:rank, :] = side_gradients(half, days, predicted, packed, time_t[...], seen, summed, take)
    message[:rank, :] = block[...]
    new = fresh[...]
    norm = column_as_row(jnp.sum(new * new, axis=1, keepdims=True))
    message[rank:, :] = norm
    crossing[rank:, :] = norm
    cols[...] = jnp.zeros(cols.shape, F32)
    cols[:, :rank] = border(new, half)
    first_row, last_row = row_of(new, 0), row_of(new, half - 1)
    edge_near[...] = pick(core == 0, last_row, first_row)
    edge_far[...] = pick(core == 0, first_row, last_row)


def total_of(parts):
    total = parts[0][...].astype(F32)
    if len(parts) > 1:
        one, two, three = (part[...].astype(F32) for part in parts[1:])
        total = (total + one) + (two + three)
    return total


def packed_norm(norm, cols, rank):
    free = LANES - rank
    line = lax.broadcasted_iota(jnp.int32, cols.shape, 0)
    lane = lax.broadcasted_iota(jnp.int32, cols.shape, 1)
    for part in range(rank // free):
        moved = pltpu.roll(norm, rank - part * free, 1)
        cols = jnp.where((lane >= rank) & (line == part), moved, cols)
    return cols


def unpacked(block, rank):
    free = LANES - rank
    line = lax.broadcasted_iota(jnp.int32, block.shape, 0)
    lane = lax.broadcasted_iota(jnp.int32, block.shape, 1)
    norm = jnp.zeros(block.shape, F32)
    for part in range(rank // free):
        row = jnp.where((lane >= rank) & (line == part), block, 0.0)
        norm = norm + pltpu.roll(row, LANES - rank + part * free, 1)
    return jnp.broadcast_to(jnp.sum(norm, axis=0, keepdims=True), block.shape)


def own_kernel(n_parts, time_t, *rest):
    parts, (time_own, norm) = rest[:n_parts], rest[n_parts:]
    rank = time_t.shape[0]
    days = LANES // 2
    total = total_of(parts)
    block = total[:rank, :]
    own = lax.broadcasted_iota(jnp.int32, block.shape, 1) < days
    time_own[...] = jnp.where(own, time_t[...] - block / (pltpu.roll(block, days, 1) + RIDGE), 0.0)
    norm[...] = unpacked(total[rank:, :], rank) if n_parts > 1 else total[rank:, :]


def rescaling(counts, norm, time_new):
    day_count, cell_count = counts
    space_sq = row_as_column(norm[:1, :], time_new.shape[0])
    square = time_new * time_new
    time_sq = 0.5 * jnp.sum(square + pltpu.roll(square, LANES // 2, 1), axis=1, keepdims=True)
    ratio = (time_sq / day_count + EPSILON) / (space_sq / cell_count + EPSILON)
    return jnp.sqrt(jnp.sqrt(ratio))


def second_kernel(half, counts, paired, swap, surface, time_own, time_other, norm, near, far, seen_near, seen_far, edge_near, edge_far, cols_a, cols_b, *rest):
    fresh, time_out, message, outgoing, scaled, base, predicted, packed = rest
    rank = surface.shape[0]
    time_new = time_own[...] + pltpu.roll(time_other[...], LANES // 2, 1)
    scale = rescaling(counts, norm[...], time_new)
    time_now = time_new / scale
    time_out[...] = time_now
    scaled[...] = surface[...] * scale
    packed[...] = scaled[...].astype(BF16)
    time_bf = time_now.astype(BF16)
    for at in range(0, half * LANES, WIDTH):
        predicted[:, at:at + WIDTH] = dot(time_bf, packed[:, at:at + WIDTH], (0, 0))
    if paired:
        left, right = in_order(swap(), cols_a[rank:, :], cols_b[rank:, :])
    else:
        left, right = cols_a[half:, :], cols_b[:half, :]
    smooth(half, scaled[...], edge_near[...], edge_far[...], left, right, scale, base)
    seen = seen_near[...] + pltpu.roll(seen_far[...], LANES // 2, 1)
    sums = gradients(half, base, predicted, packed, time_now, seen, near, far, fresh)
    post_all(sums, message, outgoing)


def last_kernel(half, counts, n_parts, surface, other, time_t, *rest):
    parts = rest[:n_parts]
    space_out, time_out, flip = rest[n_parts:]
    core = lax.axis_index("ta")
    rank = surface.shape[0]
    height = space_out.shape[0] // rank
    total = total_of(parts)
    if parts[0].dtype == BF16:
        total = widened(total, rank)
    time_new = time_t[...] - total[:rank, :] / (total[rank:2 * rank, :] + RIDGE)
    scale = rescaling(counts, total[2 * rank:, :], time_new)
    flip[...] = jnp.zeros(flip.shape, F32)
    flip[:rank, :] = time_new / scale
    time_out[...] = flip[...].T[: time_out.shape[0], :rank]
    for row in range(half):
        at = row * LANES
        space_out[pl.ds(core * half + row, rank, stride=height), :] = surface[:, at:at + LANES] * scale
        space_out[pl.ds((1 - core) * half + row, rank, stride=height), :] = other[:, at:at + LANES] * scale


def near_merge_kernel(mine, theirs, out):
    rows = mine.shape[0]
    out[:rows, :] = (mine[...].astype(F32) + theirs[:rows, :].astype(F32)).astype(BF16)
    out[rows:, :] = theirs[rows:, :]


def far_merge_kernel(mine, theirs, piece_in, edge_in, out, piece_out, edge_out):
    piece_out[...] = piece_in[...]
    edge_out[...] = edge_in[...]
    out[...] = (mine[...].astype(F32) + theirs[...].astype(F32)).astype(BF16)


def add_kernel(mine, theirs, total):
    total[...] = mine[...] + theirs[...]


def core_sum_kernel(mine, core, total):
    total[...] = mine[: total.shape[0], :] + core[...]


def band_sum_kernel(half, swap, mine, band, cols, *totals):
    rank = mine.shape[0] - NORM
    value = mine[...] + band[...]
    borders = in_order(swap(), cols[:half, :], cols[half:, :])
    for total, lines in zip(totals, borders):
        total[:rank, :] = value[:rank, :]
        total[rank:, :] = value[rank:, :] if len(totals) == 1 else packed_norm(value[rank:, :], lines, rank)


def all_sum_kernel(rank, mine, core, band, both, total):
    one, two, three, four = (widened(part[...], rank) for part in (mine, core, band, both))
    value = (one + two) + (three + four)
    if total.dtype == BF16:
        total[: 2 * rank, :], total[2 * rank:, :] = narrow(value, rank)
    else:
        total[...] = value


def shape(dims, dtype=F32):
    return jax.ShapeDtypeStruct(tuple(dims), dtype)


def padded(ref):
    *outer, rows, lanes = (1, *ref.shape)
    return math.prod(outer) * -(-rows // 16) * 16 * -(-lanes // LANES) * LANES * jnp.dtype(ref.dtype).itemsize


def call(kernel, out_shape, scratch=(), hbm=0, after=0, flops=1_000_000):
    def run(*operands):
        operands = [pltpu.with_memory_space_constraint(x, pltpu.HBM) if i < hbm else x for i, x in enumerate(operands)]
        vmem = [*operands[hbm:len(operands) - after], *jax.tree.leaves(out_shape), *scratch]
        specs = [pltpu.HBM] * hbm + [pltpu.VMEM] * (len(operands) - hbm - after) + [pl.ANY] * after
        return pl.pallas_call(
            kernel,
            out_shape=out_shape,
            in_specs=[pl.BlockSpec(memory_space=space) for space in specs],
            out_specs=jax.tree.map(lambda _: pl.BlockSpec(memory_space=pltpu.VMEM), out_shape),
            scratch_shapes=list(scratch),
            compiler_params=pltpu.CompilerParams(vmem_limit_bytes=SPARE + sum(padded(ref) for ref in vmem if len(ref.shape) > 1)),
            cost_estimate=pl.CostEstimate(flops=flops, bytes_accessed=1_000_000, transcendentals=0),
        )(*operands)

    return run


def across(value, axis, step):
    return lax.ppermute(value, axis, [(i, i ^ step) for i in range(lax.axis_size(axis))])


def shards(swath, obs_mask, target, send_list, send_count, factor_space, factor_time):
    n_lon, n_lat, n_ta = (lax.axis_size(axis) for axis in ("lon", "lat", "ta"))
    slots, days, cells = swath.shape
    rank, height, _ = factor_space.shape
    half = height // n_ta
    wide = half * LANES
    counts = (float(days * n_ta), float(height * cells * n_lon * n_lat))
    own_rows, sum_rows = rank + NORM, 2 * rank + NORM
    flip = pltpu.VMEM((LANES, LANES), F32)

    paired = n_lon == 4

    distant, close = range(n_lon // 2, n_lon), range(1, n_lon // 2)
    sends = [(side, step) for step in reversed(distant) for side in (0, 1)] + [(1, 0)]
    sends += [(side, step) for side in (0, 1) for step in close] + [(0, 0)]

    def piece_rows(side, step):
        more = TAIL if side == 0 else 0
        more += 3 * days if (side, step) == (1, 0) else COLS if paired and (side, step) == (0, 3) else 0
        return half * days + more

    operands = (send_list, send_count, target, swath, obs_mask, factor_space.reshape(rank * height, cells), factor_time)
    early = (0, n_lon - 1)
    sends.remove(early)
    sends.remove((1, n_lon - 1))
    first, second, total, seen, surface, space, time, *cols = call(
        functools.partial(route_kernel, half, early, paired),
        [shape((piece_rows(*early), cells), BF16), shape((piece_rows(1, n_lon - 1), cells), BF16), shape((2 * n_lon * half, days, cells)), shape((2 * n_lon * half + TAIL, LANES))]
        + [shape((rank, wide))]
        + [shape(ref.shape) for ref in operands[5:]]
        + [shape((COLS, LANES))] * (not paired),
        [pltpu.SMEM(ref.shape, jnp.int32) for ref in operands[:3]]
        + [pltpu.VMEM(ref.shape, ref.dtype) for ref in operands[3:5]]
        + [pltpu.SMEM((slots + 1,), jnp.int32), pltpu.SemaphoreType.DMA((len(operands) - 1 + SWATH_COPIES,))]
        + [pltpu.VMEM((COLS, LANES), F32)] * paired,
        hbm=len(operands),
    )(*operands)
    *pieces, edge_near, edge_far = call(
        functools.partial(pack_kernel, half, n_lon, sends),
        [shape((piece_rows(*key), cells), BF16) for key in sends]
        + [shape((rank, LANES)), shape((rank, LANES))],
    )(total, seen, space, time)

    def arrived(key, piece):
        side, step = key
        if side:
            return across(piece, ("lon", "ta"), 2 * step + 1)
        return across(piece, "lon", step) if step else piece

    pieces = dict(zip([early, (1, n_lon - 1), *sends], [first, second, *pieces]))
    borders = ()
    if paired:
        near, far = (across(pieces.pop((side, 3)), "lon", 1) for side in (0, 1))
        borders = (near,)
        pieces[0, 2] = call(near_merge_kernel, shape(near.shape, BF16))(pieces[0, 2], near)
        outs = [shape(far.shape, BF16), shape(far.shape, BF16), shape(edge_far.shape)]
        pieces[1, 2], pieces[1, 1], edge_far = call(far_merge_kernel, outs)(pieces[1, 2], far, pieces[1, 1], edge_far)
    pieces = {key: arrived(key, piece) for key, piece in pieces.items()}
    order = list(pieces)

    def bands(edge):
        there = [(2 * band + 1, (2 * band + 2) % (2 * n_lat)) for band in range(n_lat)]
        return lax.ppermute(edge, ("lat", "ta"), there + [(b, a) for a, b in there])

    def swap():
        return lax.rem(lax.axis_index("lon"), 2) == 1 if paired else jnp.bool_(True)

    def columns(value):
        if paired:
            return across(value, "lon", 1), across(value, "lon", 3)
        ring = [(i, (i + 1) % n_lon) for i in range(n_lon)]
        return lax.ppermute(value, "lon", ring), lax.ppermute(value, "lon", [(b, a) for a, b in ring])

    predicted, packed, time_t = call(
        functools.partial(model_kernel, half),
        [shape((2 * days, wide)), shape((rank, wide), BF16), shape((rank, LANES))],
        [flip],
    )(surface, factor_time, pieces[1, 0])

    fresh, edge = shape((rank, wide)), shape((rank, LANES))
    sides = [[key for key in order if key[0] == side] for side in (0, 1)]
    side_out = shape((days, wide))
    counts_out = shape((TAIL, LANES))
    base, block, near, seen_near, beside = call(
        functools.partial(near_kernel, half, days, sides[0], paired, swap),
        [fresh, edge, side_out, counts_out, counts_out],
    )(surface, edge_near, predicted, packed, time_t, bands(edge_far), *[pieces[key] for key in sides[0]], *(borders if paired else columns(*cols)))
    seen_far = across(beside, "ta", 1)
    surface, message, crossing, cols, edge_near, edge_far, far = call(
        functools.partial(far_kernel, half, days, len(sides[1])),
        [fresh, shape((own_rows, LANES)), shape((own_rows, LANES)), shape((COLS, LANES)), edge, edge, side_out],
    )(base, predicted, packed, time_t, block, *[pieces[key] for key in sides[1]], seen_far)

    narrowed = shape((sum_rows + NORM, LANES), BF16)

    def add(mine, theirs):
        return call(add_kernel, shape(mine.shape))(mine, theirs)

    def doubled(total, axis, step):
        while step < lax.axis_size(axis):
            total = add(total, across(total, axis, step))
            step *= 2
        return total

    def over_lon(total):
        if paired:
            return [total] + [across(total, "lon", step) for step in (1, 2, 3)]
        return [doubled(total, "lon", 1)]

    def around(mine, core, both):
        return mine, across(core, "ta", 1), across(mine, "lat", 1), across(both, ("lat", "ta"), 3)

    total = call(core_sum_kernel, shape(crossing.shape))(message, across(crossing, "ta", 1))
    direct = paired and n_lat == 2
    band_sum = functools.partial(band_sum_kernel, half, swap)
    total, *again = call(band_sum, [shape(crossing.shape)] * (1 + direct))(total, across(total, "lat", 1), cols)
    if direct:
        parts = [total] + [across(value, "lon", step) for step, value in ((1, total), (2, again[0]), (3, again[0]))]
        cols = parts[1], parts[3]
    else:
        parts = [doubled(doubled(total, "lat", 2), "lon", 1)]
        cols = columns(cols)
    time_own, norm = call(functools.partial(own_kernel, len(parts)), [edge, shape((NORM, LANES))])(time_t, *parts)

    surface, time_t, message, outgoing = call(
        functools.partial(second_kernel, half, counts, direct, swap),
        [fresh, edge, narrowed, narrowed],
        [pltpu.VMEM((rank, wide), F32), pltpu.VMEM((rank, wide), F32), pltpu.VMEM((2 * days, wide), F32), pltpu.VMEM((rank, wide), BF16)],
    )(surface, time_own, across(time_own, "ta", 1), norm, near, far, seen_near, seen_far, across(edge_near, "ta", 1), bands(edge_far), *cols)

    other = across(surface, "ta", 1)
    total = narrowed if paired and n_lat == 2 else shape((sum_rows, LANES))
    total = call(functools.partial(all_sum_kernel, rank), total)(*around(message, outgoing, outgoing))
    parts = over_lon(doubled(total, "lat", 2))
    space, time = call(
        functools.partial(last_kernel, half, counts, len(parts)),
        [shape((rank * height, cells)), shape(factor_time.shape)],
        [flip],
    )(surface, other, time_t, *parts)
    return space.reshape(rank, height, cells), time


def solution(mesh):
    in_specs = (
        P(("grp", "lon", "lat"), "ta", None),
        P(("grp", "lon", "lat"), "ta"),
        P(("grp", "lon", "lat")),
        P(("grp", "lon", "lat"), None, None),
        P(("grp", "lon", "lat"), None),
        P(None, ("grp", "lat"), "lon"),
        P(("grp", "ta"), None),
    )
    out_specs = (P(None, ("grp", "lat"), "lon"), P(("grp", "ta"), None))
    return jax.shard_map(shards, mesh=mesh, in_specs=in_specs, out_specs=out_specs, check_vma=False)
```
